32 devices in a mesh: pair: 4 (over y, x), wide: 8 (over z, core).
Axes of the slice: x: 2, y: 2, z: 4, core: 2. Of those that a mesh axis runs over, the one named last changes fastest.
Arguments:
- noisy: bfloat16 [4, 10, 2048], P('pair', None, 'wide'), may hold values from -6 to 6
- action_mask: int32 [10, 128], P(None, 'wide'), may hold values 0 or 1
- time_index: int32 [4, 128], P('pair', 'wide'), may hold values from 0 to 39
- obs_embed: bfloat16 [4, 32, 1024], P('pair', 'wide'), may hold values from -6 to 6
- obs_slot: int32 [128], P('wide'), may hold values from 0 to 15, as said below
- cotangent: float32 [4, 256, 2048], P('pair', None, 'wide'), may hold values from -6 to 6
- params: float32 [256, 12627], P('wide'), may hold values from -1.264911 to 1.8782971
- first_moment: float32 [256, 12627], P('wide'), may hold values from -0.0078125 to 0.0078125
- second_moment: float32 [256, 12627], P('wide'), may hold values from 3.0935692e-07 to 1.2374277e-06
Outputs:
- activations: bfloat16 [4, 256, 2048], P('pair', None, 'wide')
- noisy_grad: float32 [4, 10, 2048], P('pair', None, 'wide')
- observation_grad: float32 [4, 32, 1024], P('pair', 'wide')
- grad_norm: float32 [], replicated
- new_params: float32 [256, 12627], P('wide')
- new_first: float32 [256, 12627], P('wide')
- new_second: float32 [256, 12627], P('wide')
- params_copy: bfloat16 [256, 12627], P('wide')
The draws below stay inside these ranges and needn't reach their ends.
Inputs may be any that keep to these rules, and one draw needn't show every extreme that they name: `obs_slot`: in each aligned block of 16 samples the values are a permutation of 0 to 15.
All inputs are finite; a program needn't handle non-finite values. No bound on the sum of `action_mask` on one device may be relied on, other than what follows from the above.
Results may differ from the reference program's by a relative error of at most 0.014.
Values may be sent and summed in bfloat16 or wider, within the bound.
A program may use at most 128 MiB of HBM per device.

```python
import math
import jax
import jax.numpy as jnp
import numpy as np
from jax import lax

C = 256
OBS = 1024
TE = 128
TH = 512
ADIM = 10
FR = 16
KS = 5
GRP = 8
LEVELS = 40
ADAM_STEP = 7
SAMPLE_DEV = 16
COPIES = 4
SAMPLES = 128
SLOTS = 4
Q = 12627
N_WIDE = 8


def segment_table():
    cond_width = OBS + TE
    per_row = TH // C
    table = [(ADIM * KS, ADIM * KS), (C * KS, C * KS), (ADIM, ADIM), (2 * cond_width, cond_width), (3 * C, 3 * C), (4 * C, 2 * C), (2 * C * KS, 2 * C * KS), (C * KS, C * KS), (2 * C, 2 * C), (2 * cond_width, cond_width), (per_row * TE, TE), (per_row * TE, TH), (per_row, 0), (1, 0)]
    single_spans = [1, 1, 1, 2, 1, 1, 1, 1, 1, 1, 1, 1, 1, 2, 1, 1, 1, 1]
    flags = [0, -1, 0, 0, 0, -1, 0, 0, 0, 0, 0, -1, 0, 0, 0, -1, 0, 0]
    for span_cols, flag in zip(single_spans, flags):
        table.append((span_cols, flag))
    return table


def draw_obs_slot(key, part):
    key = jax.random.fold_in(key, 5)
    block_keys = jax.random.split(key, SAMPLES // SAMPLE_DEV)
    orders = jax.vmap(lambda block_key: jax.random.permutation(block_key, SAMPLE_DEV))(block_keys)
    return orders.reshape(SAMPLES).astype(jnp.int32)


def draw_params(key, part):
    key = jax.random.fold_in(key, 11)
    scale_list = []
    gain_flags = []
    for span_cols, fan_in in segment_table():
        if fan_in > 0:
            scale_list = scale_list + [fan_in ** (-0.5)] * span_cols
        else:
            scale_list = scale_list + [0.2] * span_cols
        gain_flags = gain_flags + [1.0 if fan_in < 0 else 0.0] * span_cols
    scale_row = jnp.asarray(np.array(scale_list, np.float32))[None, :]
    gain_row = jnp.asarray(np.array(gain_flags, np.float32))[None, :]
    key_base, key_spread = jax.random.split(key)
    entries = jnp.clip(jax.random.normal(key_base, (C, Q), jnp.float32), -4.0, 4.0)
    growth = 3.0 ** 0.5
    position = jnp.arange(C, dtype=jnp.float32)[:, None] / (C - 1)
    jitter = jax.random.uniform(key_spread, (C, Q), jnp.float32, 0.8, 1.2)
    gain_values = 0.7 * growth ** position * jitter
    return gain_row * gain_values + (1.0 - gain_row) * entries * scale_row


def plant(values, stream_key, low, largest):
    longest = values.shape.index(max(values.shape))
    spots = []
    for shift in (0, 1):
        where = [jax.random.randint(jax.random.fold_in(stream_key, axis), (), 0, length) for axis, length in enumerate(values.shape)]
        where[longest] = (where[longest] + shift) % values.shape[longest]
        spots.append(tuple(where))
    return values.at[spots[0]].set(low).at[spots[1]].set(largest)


def strengthened(drawn, key, source, target, blocks, factor):
    owner, partner = [(jnp.arange(drawn.shape[axis_at]) // (drawn.shape[axis_at] // blocks)).reshape([-1 if axis == axis_at else 1 for axis in range(drawn.ndim)]) for axis_at in (source, target)]
    chosen = jax.random.permutation(key, blocks)[partner]
    strong = (owner == chosen) | (owner == (partner + blocks // 2) % blocks)
    return jnp.where(strong, factor * drawn, drawn)


def block_levels(key, dims, cuts, smallest, high):
    factor_of, own = 1.0, jax.random.fold_in(key, 6)
    for dim, shards_of in cuts:
        heights = jnp.exp(jax.random.uniform(jax.random.fold_in(own, dim), (shards_of,), jnp.float32, smallest / len(cuts), high / len(cuts)))
        factor_of = factor_of * jnp.repeat(heights, dims[dim] // shards_of).reshape([-1 if axis == dim else 1 for axis in range(len(dims))])
    return factor_of


def gaussian(own_key, dims, scale, most, cuts=(), kind=jnp.bfloat16):
    loudness = block_levels(own_key, dims, cuts, -0.22, 0.18) if cuts else 1.0
    values = jax.random.normal(own_key, dims, jnp.float32) * scale * loudness
    return jnp.minimum(jnp.maximum(values, -most), most).astype(kind)


def noise_with(rng, dims, scale, bound, cuts, heavy, held_as=jnp.bfloat16):
    drawn = scale * jax.random.normal(rng, dims, jnp.float32)
    if cuts:
        drawn = drawn * block_levels(rng, dims, cuts, -0.22, 0.18)
    return jnp.clip(strengthened(drawn, jax.random.fold_in(rng, 3), *heavy), -bound, bound).astype(held_as)


def setup_inputs(seed: int = 0) -> dict:
    seeds = jax.random.split(jax.random.key(seed), 10)
    noisy = gaussian(seeds[0], (COPIES, ADIM, SAMPLES * FR), 1.0, 6.0, ((0, 4), (2, 8)))
    action_mask = plant((jax.random.randint(seeds[1], (ADIM, SAMPLES), 0, 4) < 3).astype(jnp.int32), jax.random.fold_in(seeds[1], 1), 0, 1)
    time_index = plant(jax.random.randint(seeds[2], (COPIES, SAMPLES), 0, LEVELS), jax.random.fold_in(seeds[2], 1), 0, LEVELS - 1).astype(jnp.int32)
    obs_embed = gaussian(seeds[3], (COPIES, SAMPLES // COPIES, OBS), 1.0, 6.0, ((0, 4), (1, 8)))
    obs_slot = draw_obs_slot(jax.random.fold_in(seeds[9], 71), 0)
    cotangent = noise_with(seeds[5], (COPIES, C, SAMPLES * FR), 1.0, 6.0, ((0, 4), (2, 8)), (2, 1, 8, 2.0), jnp.float32)
    params = draw_params(jax.random.fold_in(seeds[9], 71), 0)
    first_moment = gaussian(seeds[7], (C, Q), ((C * Q) ** -0.5), 0.0078125, ((0, 8),), jnp.float32)
    second_moment = jnp.clip(jnp.exp(math.log(1.2374276820992236e-06) - 1.3862944 * jax.random.uniform(seeds[8], (C, Q), jnp.float32) ** block_levels(seeds[8], (C, Q), ((0, 8),), -0.2, 0.2)), 3.093569205248059e-07, 1.2374276820992236e-06)
    return {"noisy": noisy, "action_mask": action_mask, "time_index": time_index, "obs_embed": obs_embed, "obs_slot": obs_slot, "cotangent": cotangent, "params": params, "first_moment": first_moment, "second_moment": second_moment}


@jax.custom_vjp
def low(v):
    return lax.optimization_barrier(v.astype(jnp.bfloat16)).astype(jnp.float32)

@jax.custom_vjp
def low_back(v):
    return v

def low_keep(v):
    return (low(v), None)

def low_pass(kept, grad):
    return (grad,)

def back_keep(v):
    return (v, None)

def back_low(kept, grad):
    return (low(grad),)
low.defvjp(low_keep, low_pass)
low_back.defvjp(back_keep, back_low)
highest = lax.Precision.HIGHEST
sigma_top = 80.0 ** (1.0 / 7.0)
sigma_low = 0.002 ** (1.0 / 7.0)
clip_limit = 1.0
learn_rate = 0.02
decay_first = 0.5
decay_second = 0.5
adam_eps = 1e-08
weight_decay = 0.01
norm_eps = 1e-05

def layout():
    cond_width = OBS + TE
    per_row = TH // C
    return [('down_first', ADIM * KS), ('down_second', C * KS), ('down_residual', ADIM), ('down_film', 2 * cond_width), ('pool_kernel', 3 * C), ('spread_kernel', 4 * C), ('up_first', 2 * C * KS), ('up_second', C * KS), ('up_residual', 2 * C), ('up_film', 2 * cond_width), ('time_inner', per_row * TE), ('time_outer', per_row * TE), ('time_bias', per_row), ('time_out_bias', 1), ('down_bias_first', 1), ('down_gain_first', 1), ('down_shift_first', 1), ('down_film_bias', 2), ('down_bias_second', 1), ('down_gain_second', 1), ('down_shift_second', 1), ('down_residual_bias', 1), ('pool_bias', 1), ('spread_bias', 1), ('up_bias_first', 1), ('up_gain_first', 1), ('up_shift_first', 1), ('up_film_bias', 2), ('up_bias_second', 1), ('up_gain_second', 1), ('up_shift_second', 1), ('up_residual_bias', 1)]

def unpack(flat):
    pieces = {}
    offset = 0
    for label, span in layout():
        pieces[label] = flat[:, offset:offset + span]
        offset = offset + span
    return pieces

def mish_curve(values):
    return values * jnp.tanh(jax.nn.softplus(values))

def time_features(levels):
    fraction = levels.astype(jnp.float32) / (LEVELS - 1)
    noise_time = 250.0 * 7.0 * jnp.log(sigma_top + fraction * (sigma_low - sigma_top))
    half_width = TE // 2
    frequency = jnp.exp(-math.log(10000.0) * jnp.arange(half_width, dtype=jnp.float32) / (half_width - 1))
    angles = noise_time[:, None] * frequency[None, :]
    return jnp.concatenate([jnp.sin(angles), jnp.cos(angles)], axis=1)

def shift_frames(values, step):
    frames = values.shape[-1]
    padding = [(0, 0)] * (values.ndim - 1)
    if step > 0:
        return jnp.pad(values[..., step:], padding + [(0, step)])
    if step < 0:
        return jnp.pad(values[..., :frames + step], padding + [(-step, 0)])
    return values

def mix_channels(kernel, source):
    return jnp.einsum('oi,bit->bot', kernel, source, precision=highest)

def conv_frames(kernel, source):
    reach = kernel.shape[2] // 2
    total = mix_channels(kernel[:, :, 0], shift_frames(source, -reach))
    for tap_index in range(1, kernel.shape[2]):
        total = total + mix_channels(kernel[:, :, tap_index], shift_frames(source, tap_index - reach))
    return total

def pool_frames(kernel, source):
    even_part = source[..., 0::2]
    odd_part = source[..., 1::2]
    total = mix_channels(kernel[:, :, 0], shift_frames(odd_part, -1))
    total = total + mix_channels(kernel[:, :, 1], even_part)
    return total + mix_channels(kernel[:, :, 2], odd_part)

def spread_frames(kernel, source):
    even_part = mix_channels(kernel[:, :, 1], source) + mix_channels(kernel[:, :, 3], shift_frames(source, -1))
    odd_part = mix_channels(kernel[:, :, 0], shift_frames(source, 1)) + mix_channels(kernel[:, :, 2], source)
    return jnp.stack([even_part, odd_part], axis=-1).reshape(source.shape[0], source.shape[1], -1)

def group_norm(before, gain_row, shifts):
    batch_rows, channels, frames = before.shape
    cube = before.reshape(batch_rows, GRP, channels // GRP, frames)
    center = lax.optimization_barrier(jnp.mean(cube, axis=(2, 3), keepdims=True))
    spread = lax.optimization_barrier(jnp.mean(jnp.square(cube - center), axis=(2, 3), keepdims=True))
    normal = ((cube - center) * lax.rsqrt(spread + norm_eps)).reshape(batch_rows, channels, frames)
    return normal * gain_row[None, :, None] + shifts[None, :, None]

def column(parts, label):
    return parts[label][:, 0][None, :, None]

def vector(parts, label):
    return parts[label][:, 0]

def film_rows(block):
    return block.reshape(C, 2, -1).transpose(1, 0, 2).reshape(2 * C, -1)

def forward(flat, seen_rows, actions, levels, keep_mask):
    parts = unpack(low(flat))
    inner_kernel = parts['time_inner'].reshape(TH, TE)
    outer_kernel = parts['time_outer'].reshape(TH, TE)
    feats = low(time_features(levels))
    hidden = low_back(jnp.einsum('be,he->bh', feats, inner_kernel, precision=highest)) + parts['time_bias'].reshape(TH)
    embed = low_back(jnp.einsum('bh,he->be', low(mish_curve(hidden)), outer_kernel, precision=highest))
    embed = embed + parts['time_out_bias'][:TE, 0]
    cond = low(mish_curve(jnp.concatenate([seen_rows, embed], axis=1)))
    film_kernel = jnp.concatenate([film_rows(parts['down_film']), film_rows(parts['up_film'])], axis=0)
    film_bias = jnp.concatenate([parts['down_film_bias'].T.reshape(-1), parts['up_film_bias'].T.reshape(-1)])
    film = low_back(jnp.einsum('bk,ok->bo', cond, film_kernel, precision=highest)) + film_bias
    start = actions * keep_mask[:, :, None]
    pre_one = low_back(conv_frames(parts['down_first'].reshape(C, ADIM, KS), start)) + column(parts, 'down_bias_first')
    mid_one = film[:, :C, None] * mish_curve(group_norm(pre_one, vector(parts, 'down_gain_first'), vector(parts, 'down_shift_first')))
    mid_one = mid_one + film[:, C:2 * C, None]
    pre_two = low_back(conv_frames(parts['down_second'].reshape(C, C, KS), low(mid_one))) + column(parts, 'down_bias_second')
    skip = mish_curve(group_norm(pre_two, vector(parts, 'down_gain_second'), vector(parts, 'down_shift_second')))
    skip = skip + low_back(mix_channels(parts['down_residual'], start)) + column(parts, 'down_residual_bias')
    skip = low(skip)
    pooled = low_back(pool_frames(parts['pool_kernel'].reshape(C, C, 3), skip)) + column(parts, 'pool_bias')
    spread = low_back(spread_frames(parts['spread_kernel'].reshape(C, C, 4), low(pooled))) + column(parts, 'spread_bias')
    joined = jnp.concatenate([low(spread), skip], axis=1)
    pre_three = low_back(conv_frames(parts['up_first'].reshape(C, 2 * C, KS), joined)) + column(parts, 'up_bias_first')
    mid_three = film[:, 2 * C:3 * C, None] * mish_curve(group_norm(pre_three, vector(parts, 'up_gain_first'), vector(parts, 'up_shift_first')))
    mid_three = mid_three + film[:, 3 * C:, None]
    pre_four = low_back(conv_frames(parts['up_second'].reshape(C, C, KS), low(mid_three))) + column(parts, 'up_bias_second')
    result = mish_curve(group_norm(pre_four, vector(parts, 'up_gain_second'), vector(parts, 'up_shift_second')))
    return result + low_back(mix_channels(parts['up_residual'], joined)) + column(parts, 'up_residual_bias')

def reference(noisy, action_mask, time_index, obs_embed, obs_slot, cotangent, params, first_moment, second_moment):
    blocks = COPIES * N_WIDE
    table = obs_embed.reshape(COPIES, N_WIDE, SLOTS, OBS).transpose(1, 0, 2, 3).reshape(N_WIDE, SAMPLE_DEV, OBS)
    slots = obs_slot.reshape(N_WIDE, SAMPLE_DEV)
    seen = jax.vmap(lambda rows_table, slot_row: rows_table[slot_row])(table, slots)
    acts = noisy.reshape(COPIES, ADIM, N_WIDE, SAMPLE_DEV, FR).transpose(0, 2, 3, 1, 4).reshape(blocks, SAMPLE_DEV, ADIM, FR)
    cots = cotangent.reshape(COPIES, C, N_WIDE, SAMPLE_DEV, FR).transpose(0, 2, 3, 1, 4).reshape(blocks, SAMPLE_DEV, C, FR)
    keeps = action_mask.reshape(ADIM, N_WIDE, SAMPLE_DEV).transpose(1, 2, 0)
    levels = time_index.reshape(blocks, SAMPLE_DEV)

    def step(carry, items):
        grads, seen_grads = carry
        act_block, cot_block, level_block, index = items
        place = index % N_WIDE
        keep_mask = keeps[place].astype(jnp.float32)

        def local(flat, seen_rows, actions):
            return forward(flat, seen_rows, actions, level_block, keep_mask)
        result, backward = jax.vjp(local, params, seen[place].astype(jnp.float32), act_block.astype(jnp.float32))
        flat_grad, seen_grad, act_grad = backward(cot_block.astype(jnp.float32))
        seen_grads = seen_grads.at[place].add(seen_grad)
        return ((grads + flat_grad, seen_grads), (result, act_grad))
    initial = (jnp.zeros_like(params), jnp.zeros((N_WIDE, SAMPLE_DEV, OBS), jnp.float32))
    (grads, seen_grads), (results, act_grads) = lax.scan(step, initial, (acts, cots, levels, jnp.arange(blocks, dtype=jnp.int32)))
    results_low = results.astype(jnp.bfloat16)
    activations = results_low.reshape(COPIES, N_WIDE, SAMPLE_DEV, C, FR).transpose(0, 3, 1, 2, 4).reshape(COPIES, C, SAMPLES * FR)
    noisy_grad = act_grads.reshape(COPIES, N_WIDE, SAMPLE_DEV, ADIM, FR).transpose(0, 3, 1, 2, 4).reshape(COPIES, ADIM, SAMPLES * FR)
    placed = jax.vmap(lambda grad_rows, slot_row: jnp.zeros_like(grad_rows).at[slot_row].set(grad_rows))(seen_grads, slots)
    observation_grad = placed.reshape(N_WIDE, COPIES, SLOTS, OBS).transpose(1, 0, 2, 3).reshape(COPIES, N_WIDE * SLOTS, OBS)
    grad_norm = jnp.sqrt(jnp.sum(grads * grads))
    clipped = grads * jnp.minimum(1.0, clip_limit / (grad_norm + 1e-06))
    new_first = decay_first * first_moment + (1.0 - decay_first) * clipped
    new_second = decay_second * second_moment + (1.0 - decay_second) * clipped * clipped
    first_hat = new_first / (1.0 - decay_first ** ADAM_STEP)
    second_hat = new_second / (1.0 - decay_second ** ADAM_STEP)
    new_params = params - learn_rate * (first_hat / (jnp.sqrt(second_hat) + adam_eps) + weight_decay * params)
    return (activations, noisy_grad, observation_grad, grad_norm, new_params, new_first, new_second, new_params.astype(jnp.bfloat16))
```

```python
import math

import jax
import jax.numpy as jnp
import numpy as np
from jax import lax
from jax.experimental import pallas as pl
from jax.experimental.pallas import tpu as pltpu
from jax.sharding import PartitionSpec as P

C = 256
OBS = 1024
TE = 128
TH = 512
ADIM = 10
FR = 16
LEVELS = 40
ADAM_STEP = 7
Q = 12627
SAM = 16
ROWS = 32
NB = 36

sigma_top = 80.0 ** (1.0 / 7.0)
sigma_low = 0.002 ** (1.0 / 7.0)
clip_limit = 1.0
learn_rate = 0.02
decay_first = 0.5
decay_second = 0.5
adam_eps = 1e-08
weight_decay = 0.01
norm_eps = 1e-05

f32 = jnp.float32
bf16 = jnp.bfloat16

AT_DOWN_RES = 1330
AT_TAIL = 12604
TAIL = 23
AT_FILM = (1340, 2492, 9788, 10940)
AT_TIME = (12092, 12348)
AT_UP_RES = 9276
B_MISC, B_INNER, B_OUTER, B_FILM = 0, 1, 2, 3
B_DS, B_POOL, B_SPREAD, B_UF, B_US, B_UR = 5, 10, 13, 17, 27, 32
LANE_TAIL = 64
CONVS = (
    (50, 5, 2, lambda t, h: B_DS + t),
    (5436, 5, 4, lambda t, h: B_UF + 2 * t + h // 2),
    (7996, 5, 2, lambda t, h: B_US + t),
    (3644, 3, 2, lambda t, h: B_POOL + t),
    (4412, 4, 2, lambda t, h: B_SPREAD + t),
)
(T_BIAS_A, T_BIAS_B, T_OUT, D_B1, D_G1, D_S1, D_FS, D_FO, D_B2, D_G2, D_S2, D_RB, PB, SB,
 U_B1, U_G1, U_S1, U_FS, U_FO, U_B2, U_G2, U_S2, U_RB) = range(TAIL)


def dot_nt(a, b):
    return lax.dot_general(a, b, (((1,), (1,)), ((), ())), preferred_element_type=f32)


def dot_nn(a, b):
    return lax.dot_general(a, b, (((1,), (0,)), ((), ())), preferred_element_type=f32)


def dot_tn(a, b):
    return lax.dot_general(a, b, (((0,), (0,)), ((), ())), preferred_element_type=f32)


def split2(v):
    high = v.astype(bf16)
    return high, (v - high.astype(f32)).astype(bf16)


def split3(v):
    high, rest = v.astype(bf16), None
    rest = v - high.astype(f32)
    mid = rest.astype(bf16)
    return high, mid, (rest - mid.astype(f32)).astype(bf16)


def tap_order(taps):
    n = 128 * taps
    row = lax.broadcasted_iota(jnp.int32, (n, n), 0)
    col = lax.broadcasted_iota(jnp.int32, (1, n), 1)
    source = (col & 127) * taps + (col >> 7)
    return jnp.where(row == source, 1.0, 0.0).astype(bf16)


def first_order():
    table = np.zeros((128, 128), np.float32)
    for i in range(ADIM):
        for t in range(5):
            table[i * 5 + t, t * ADIM + i] = 1.0
    return table


def level_table():
    levels = np.arange(LEVELS, dtype=np.float64)
    tau = 250.0 * 7.0 * np.log(sigma_top + levels / (LEVELS - 1) * (sigma_low - sigma_top))
    freq = np.exp(-math.log(10000.0) * np.arange(TE // 2) / (TE // 2 - 1))
    angles = tau[:, None] * freq[None, :]
    table = np.zeros((64, TE), np.float32)
    table[:LEVELS] = np.concatenate([np.sin(angles), np.cos(angles)], axis=1)
    return table


def pack_kernel(params_ref, order_ref, own_ref, film_ref):
    def low(start, width):
        return params_ref[:, start : start + width].astype(bf16)

    first = dot_nn(low(0, 128), order_ref[...])
    pieces = [
        first[:, :50],
        params_ref[:, AT_DOWN_RES : AT_DOWN_RES + ADIM],
        jnp.zeros((ROWS, LANE_TAIL - 60), f32),
        params_ref[:, AT_TAIL : AT_TAIL + TAIL],
        jnp.zeros((ROWS, 256 - LANE_TAIL - TAIL), f32),
    ]
    own_ref[B_MISC] = jnp.concatenate(pieces, axis=1).astype(bf16)
    own_ref[B_INNER] = low(AT_TIME[0], 256)
    own_ref[B_OUTER] = low(AT_TIME[1], 256)
    for q in range(4):
        film_ref[q * ROWS : (q + 1) * ROWS] = low(AT_FILM[q], OBS)
        own_ref[B_FILM + q // 2, :, (q % 2) * 128 : (q % 2) * 128 + 128] = low(AT_FILM[q] + OBS, TE)
    own_ref[B_UR] = low(AT_UP_RES, 256)
    own_ref[B_UR + 1] = low(AT_UP_RES + 256, 256)
    own_ref[NB - 2] = jnp.zeros((ROWS, 256), bf16)
    own_ref[NB - 1] = jnp.zeros((ROWS, 256), bf16)
    for taps in (5, 3, 4):
        places = [(at, h, block) for at, k, groups, block in CONVS if k == taps for h in range(groups)]
        stacked = jnp.concatenate([low(at + h * 128 * taps, 128 * taps) for at, h, _ in places], axis=0)
        moved = dot_nn(stacked, tap_order(taps)).astype(bf16)
        for n, (_, h, block) in enumerate(places):
            for t in range(taps):
                own_ref[block(t, h), :, (h % 2) * 128 : (h % 2) * 128 + 128] = moved[
                    n * ROWS : (n + 1) * ROWS, t * 128 : (t + 1) * 128
                ]


def pack(params):
    vmem = pl.BlockSpec(memory_space=pltpu.VMEM)
    return pl.pallas_call(
        pack_kernel,
        out_shape=(
            jax.ShapeDtypeStruct((NB, ROWS, 256), bf16),
            jax.ShapeDtypeStruct((4 * ROWS, OBS), bf16),
        ),
        in_specs=[vmem, vmem],
        out_specs=(vmem, vmem),
        compiler_params=pltpu.CompilerParams(vmem_limit_bytes=40 << 20),
        name="pack",
    )(params, jnp.asarray(first_order(), bf16))


def mish_parts(v):
    e = jnp.exp(jnp.minimum(v, 20.0))
    n = e * (e + 2.0)
    r = 1.0 / (n + 2.0)
    t = n * r
    return v * t, t + 4.0 * v * (e * r) * ((e + 1.0) * r)


def step_frames(v, step):
    if step == 0:
        return v
    zeros = jnp.zeros((SAM * abs(step), v.shape[1]), v.dtype)
    if step > 0:
        return jnp.concatenate([v[SAM * step :], zeros], axis=0)
    return jnp.concatenate([zeros, v[: SAM * step]], axis=0)


def over_frames(v):
    return jnp.sum(v.reshape(-1, SAM, v.shape[1]), axis=0)


def each_frame(v, s):
    return v.reshape(-1, SAM, v.shape[1]), s[None]


def group_means(values, ones):
    parts = [p for v in values for p in split3(v)]
    sums = dot_nn(jnp.concatenate(parts, axis=0), ones)
    out = []
    for i in range(len(values)):
        a, b, c = (sums[(3 * i + k) * SAM : (3 * i + k + 1) * SAM] for k in range(3))
        out.append((a + (b + c)) * (1.0 / (32 * FR)))
    return out


def minus(v, s):
    a, b = each_frame(v, s)
    return (a - b).reshape(v.shape)


def times(v, s):
    a, b = each_frame(v, s)
    return (a * b).reshape(v.shape)


def plus(v, s):
    a, b = each_frame(v, s)
    return (a + b).reshape(v.shape)


def norm_forward(before, gain, shift, ones):
    (center,) = group_means([over_frames(before)], ones)
    away = minus(before, center)
    (spread,) = group_means([over_frames(away * away)], ones)
    scale = lax.rsqrt(spread + norm_eps)
    normal = times(away, scale)
    act, slope = mish_parts(normal * gain + shift)
    return act, normal, slope, scale


def norm_backward(grad_act, normal, slope, scale, gain, ones):
    grad_out = grad_act * slope
    shift_rows = over_frames(grad_out)
    gain_rows = over_frames(grad_out * normal)
    mean_grad, mean_both = group_means([shift_rows * gain, gain_rows * gain], ones)
    inner = minus(grad_out * gain, mean_grad) - times(normal, mean_both)
    return (
        times(inner, scale),
        jnp.sum(gain_rows, axis=0, keepdims=True),
        jnp.sum(shift_rows, axis=0, keepdims=True),
    )


def conv_forward(source, weight):
    total = dot_nt(step_frames(source, -2), weight(0))
    for t in range(1, 5):
        total = total + dot_nt(step_frames(source, t - 2), weight(t))
    return total


def conv_source(grad_low, weight):
    total = dot_nn(step_frames(grad_low, 2), weight(0))
    for t in range(1, 5):
        total = total + dot_nn(step_frames(grad_low, 2 - t), weight(t))
    return total


def row_sum(v):
    return jnp.sum(over_frames(v), axis=0, keepdims=True)


def halves(v):
    cube = v.reshape(FR // 2, 2, SAM, v.shape[1])
    return cube[:, 0].reshape(-1, v.shape[1]), cube[:, 1].reshape(-1, v.shape[1])


def interleave(even, odd):
    width = even.shape[1]
    pair = [v.reshape(FR // 2, 1, SAM, width) for v in (even, odd)]
    return jnp.concatenate(pair, axis=1).reshape(FR * SAM, width)


def train_kernel(
    w_ref, seen_ref, slot_ref, noisy_ref, mask_ref, level_ref, cot_ref, table_ref,
    act_ref, noisy_grad_ref, grad_ref, film_grad_ref,
):
    iota = lambda shape, dim: lax.broadcasted_iota(jnp.int32, shape, dim)
    row = iota((256, 256), 0)
    col = iota((256, 256), 1)
    ones = jnp.where((row >> 5) == (col >> 5), 1.0, 0.0).astype(bf16)
    swap = jnp.where(col == ((row & 15) << 4) + (row >> 4), 1.0, 0.0).astype(bf16)
    misc = w_ref[B_MISC, :, :128]
    lane = iota((256, 128), 1)
    misc_first = jnp.where(lane < 50, misc, jnp.zeros_like(misc))
    misc_res = jnp.where((lane >= 50) & (lane < 60), misc, jnp.zeros_like(misc))
    singles = misc.astype(f32).T[LANE_TAIL : LANE_TAIL + 32]
    vec = lambda k: singles[k : k + 1]

    at_level = jnp.where(iota((64, SAM), 0) == level_ref[...], 1.0, 0.0).astype(bf16)
    feats = dot_tn(at_level, table_ref[...]).astype(bf16)
    inner = [w_ref[B_INNER, :, j * 128 : (j + 1) * 128] for j in range(2)]
    outer = [w_ref[B_OUTER, :, j * 128 : (j + 1) * 128] for j in range(2)]
    film_time = [w_ref[B_FILM + q // 2, :, (q % 2) * 128 : (q % 2) * 128 + 128] for q in range(4)]
    hidden = [mish_parts(dot_nt(feats, inner[j]) + vec(T_BIAS_A + j)) for j in range(2)]
    hidden_low = [h[0].astype(bf16) for h in hidden]
    embed = dot_nn(hidden_low[0], outer[0]) + dot_nn(hidden_low[1], outer[1]) + vec(T_OUT)[:, :TE]
    cond, cond_slope = mish_parts(embed)
    cond_low = cond.astype(bf16)
    at_slot = jnp.where(iota((SAM, SAM), 0) == slot_ref[...], 1.0, 0.0).astype(bf16)
    seen_parts = split3(seen_ref[...])
    seen_film = sum(dot_tn(at_slot, part) for part in seen_parts)
    film = [
        seen_film[:, q * C : (q + 1) * C] + dot_nt(cond_low, film_time[q]) + vec((D_FS, D_FO, U_FS, U_FO)[q])
        for q in range(4)
    ]

    spread_mask = jnp.where((iota((SAM, 256), 1) >> 4) == iota((SAM, 256), 0), 1.0, 0.0).astype(bf16)
    keep = dot_nn(mask_ref[...].astype(f32).astype(bf16), spread_mask)
    start_cols = noisy_ref[...].astype(f32) * keep
    start_cols = jnp.concatenate([start_cols, jnp.zeros((6, 256), f32)], axis=0).astype(bf16)
    start = dot_nt(swap, start_cols).astype(bf16)
    lane16 = iota((16, 128), 1)
    row16 = iota((16, 128), 0)
    inputs = jnp.zeros((256, 128), f32)
    for t in range(5):
        place = lane16 == row16 + t * ADIM
        if t == 2:
            place = place | (lane16 == row16 + 50)
        place = place & (row16 < ADIM)
        inputs = inputs + dot_nn(step_frames(start, t - 2), jnp.where(place, 1.0, 0.0).astype(bf16))
    inputs = inputs.astype(bf16)
    pre = dot_nt(inputs, misc_first) + vec(D_B1)
    act_one, normal_one, slope_one, scale_one = norm_forward(pre, vec(D_G1), vec(D_S1), ones)
    mid_one = plus(times(act_one, film[0]), film[1]).astype(bf16)
    down = lambda t: w_ref[B_DS + t]
    pre = conv_forward(mid_one, down) + vec(D_B2)
    act, normal_two, slope_two, scale_two = norm_forward(pre, vec(D_G2), vec(D_S2), ones)
    skip = (act + dot_nt(inputs, misc_res) + vec(D_RB)).astype(bf16)
    even, odd = halves(skip)
    odd_prev = step_frames(odd, -1)
    pool_sources = (odd_prev, even, odd)
    pooled = sum(dot_nt(s, w_ref[B_POOL + t]) for t, s in enumerate(pool_sources)) + vec(PB)
    pooled = pooled.astype(bf16)
    pooled_prev = step_frames(pooled, -1)
    pooled_next = step_frames(pooled, 1)
    even_out = dot_nt(pooled, w_ref[B_SPREAD + 1]) + dot_nt(pooled_prev, w_ref[B_SPREAD + 3])
    odd_out = dot_nt(pooled_next, w_ref[B_SPREAD]) + dot_nt(pooled, w_ref[B_SPREAD + 2])
    wide = (interleave(even_out, odd_out) + vec(SB)).astype(bf16)
    joined = (wide, skip)
    up_first = [lambda t, h=h: w_ref[B_UF + 2 * t + h] for h in range(2)]
    pre = conv_forward(wide, up_first[0]) + conv_forward(skip, up_first[1]) + vec(U_B1)
    act_three, normal_three, slope_three, scale_three = norm_forward(pre, vec(U_G1), vec(U_S1), ones)
    mid_three = plus(times(act_three, film[2]), film[3]).astype(bf16)
    up = lambda t: w_ref[B_US + t]
    pre = conv_forward(mid_three, up) + vec(U_B2)
    act, normal_four, slope_four, scale_four = norm_forward(pre, vec(U_G2), vec(U_S2), ones)
    result = act + dot_nt(wide, w_ref[B_UR]) + dot_nt(skip, w_ref[B_UR + 1]) + vec(U_RB)
    act_ref[...] = dot_tn(result.astype(bf16), swap).astype(bf16)

    single_grads = {}

    def conv_weights(grad_low, source, block):
        turned = grad_low.T
        for t in range(5):
            grad_ref[block(t)] = dot_nn(turned, step_frames(source, t - 2)).astype(bf16)

    cot_high, cot_low = split2(cot_ref[...])
    upstream = dot_nt(swap, cot_high) + dot_nt(swap, cot_low)
    grad, single_grads[U_G2], single_grads[U_S2] = norm_backward(
        upstream, normal_four, slope_four, scale_four, vec(U_G2), ones
    )
    single_grads[U_B2] = row_sum(grad)
    low = grad.astype(bf16)
    conv_weights(low, mid_three, lambda t: B_US + t)
    grad_mid = conv_source(low, up)
    shift_three = over_frames(grad_mid)
    gain_three = over_frames(grad_mid * act_three)
    grad, single_grads[U_G1], single_grads[U_S1] = norm_backward(
        times(grad_mid, film[2]), normal_three, slope_three, scale_three, vec(U_G1), ones
    )
    single_grads[U_B1] = row_sum(grad)
    low = grad.astype(bf16)
    for h in range(2):
        conv_weights(low, joined[h], lambda t, h=h: B_UF + 2 * t + h)
    single_grads[U_RB] = row_sum(upstream)
    upstream_low = upstream.astype(bf16)
    turned = upstream_low.T
    for h in range(2):
        grad_ref[B_UR + h] = dot_nn(turned, joined[h]).astype(bf16)
    grad_wide = conv_source(low, up_first[0]) + dot_nn(upstream_low, w_ref[B_UR])
    grad_skip = conv_source(low, up_first[1]) + dot_nn(upstream_low, w_ref[B_UR + 1])
    single_grads[SB] = row_sum(grad_wide)
    low_even, low_odd = halves(grad_wide.astype(bf16))
    turned_even, turned_odd = low_even.T, low_odd.T
    grad_ref[B_SPREAD] = dot_nn(turned_odd, pooled_next).astype(bf16)
    grad_ref[B_SPREAD + 1] = dot_nn(turned_even, pooled).astype(bf16)
    grad_ref[B_SPREAD + 2] = dot_nn(turned_odd, pooled).astype(bf16)
    grad_ref[B_SPREAD + 3] = dot_nn(turned_even, pooled_prev).astype(bf16)
    grad_pooled = dot_nn(low_even, w_ref[B_SPREAD + 1]) + dot_nn(low_odd, w_ref[B_SPREAD + 2])
    grad_pooled = grad_pooled + dot_nn(step_frames(low_even, 1), w_ref[B_SPREAD + 3])
    grad_pooled = grad_pooled + dot_nn(step_frames(low_odd, -1), w_ref[B_SPREAD])
    single_grads[PB] = row_sum(grad_pooled)
    low = grad_pooled.astype(bf16)
    turned = low.T
    for t in range(3):
        grad_ref[B_POOL + t] = dot_nn(turned, pool_sources[t]).astype(bf16)
    grad_even = dot_nn(low, w_ref[B_POOL + 1])
    grad_odd = dot_nn(low, w_ref[B_POOL + 2]) + dot_nn(step_frames(low, 1), w_ref[B_POOL])
    grad_skip = grad_skip + interleave(grad_even, grad_odd)
    single_grads[D_RB] = row_sum(grad_skip)
    skip_low = grad_skip.astype(bf16)
    misc_grad = jnp.where(lane < 50, 0.0, dot_nn(skip_low.T, inputs))
    back = dot_nn(skip_low, misc_res)
    grad, single_grads[D_G2], single_grads[D_S2] = norm_backward(
        grad_skip, normal_two, slope_two, scale_two, vec(D_G2), ones
    )
    single_grads[D_B2] = row_sum(grad)
    low = grad.astype(bf16)
    conv_weights(low, mid_one, lambda t: B_DS + t)
    grad_mid = conv_source(low, down)
    shift_one = over_frames(grad_mid)
    gain_one = over_frames(grad_mid * act_one)
    grad, single_grads[D_G1], single_grads[D_S1] = norm_backward(
        times(grad_mid, film[0]), normal_one, slope_one, scale_one, vec(D_G1), ones
    )
    single_grads[D_B1] = row_sum(grad)
    low = grad.astype(bf16)
    misc_grad = misc_grad + jnp.where(lane < 50, dot_nn(low.T, inputs), 0.0)
    back = back + dot_nn(low, misc_first)
    grad_start = back[:, 50:60]
    for t in range(5):
        grad_start = grad_start + step_frames(back[:, t * ADIM : (t + 1) * ADIM], 2 - t)
    grad_cols = sum(dot_tn(part, swap) for part in split3(jnp.concatenate([grad_start, jnp.zeros((256, 6), f32)], axis=1)))
    noisy_grad_ref[...] = grad_cols[:ADIM] * keep

    film_grads = (gain_one, shift_one, gain_three, shift_three)
    film_low = [g.astype(bf16) for g in film_grads]
    back_cond = None
    for q in range(4):
        single_grads[(D_FS, D_FO, U_FS, U_FO)[q]] = jnp.sum(film_grads[q], axis=0, keepdims=True)
        grad_ref[B_FILM + q // 2, :, (q % 2) * 128 : (q % 2) * 128 + 128] = dot_tn(film_low[q], cond_low).astype(bf16)
        part = dot_nn(film_low[q], film_time[q])
        back_cond = part if back_cond is None else back_cond + part
        film_grad_ref[:, q * C : (q + 1) * C] = dot_nn(at_slot, film_low[q]).astype(bf16)
    grad_embed = back_cond * cond_slope
    single_grads[T_OUT] = jnp.concatenate(
        [jnp.sum(grad_embed, axis=0, keepdims=True), jnp.zeros((1, C - TE), f32)], axis=1
    )
    embed_low = grad_embed.astype(bf16)
    for j in range(2):
        grad_ref[B_OUTER, :, j * 128 : (j + 1) * 128] = dot_tn(hidden_low[j], embed_low).astype(bf16)
        grad_hidden = dot_nt(embed_low, outer[j]) * hidden[j][1]
        single_grads[T_BIAS_A + j] = jnp.sum(grad_hidden, axis=0, keepdims=True)
        grad_ref[B_INNER, :, j * 128 : (j + 1) * 128] = dot_tn(grad_hidden.astype(bf16), feats).astype(bf16)
    stack = [jnp.zeros((LANE_TAIL, 256), f32)] + [single_grads[k] for k in range(TAIL)]
    stack = jnp.concatenate(stack + [jnp.zeros((128 - LANE_TAIL - TAIL, 256), f32)], axis=0)
    grad_ref[B_MISC, :, :128] = (misc_grad + stack.T).astype(bf16)
    grad_ref[B_MISC, :, 128:] = jnp.zeros((256, 128), bf16)
    for b in range(B_UR + 2, NB):
        grad_ref[b] = jnp.zeros((256, 256), bf16)


def train(weights, seen_film, slots, noisy, mask, levels, cotangent):
    vmem = pl.BlockSpec(memory_space=pltpu.VMEM)
    return pl.pallas_call(
        train_kernel,
        out_shape=(
            jax.ShapeDtypeStruct((C, 256), bf16),
            jax.ShapeDtypeStruct((ADIM, 256), f32),
            jax.ShapeDtypeStruct((NB, 256, 256), bf16),
            jax.ShapeDtypeStruct((SAM, 4 * C), bf16),
        ),
        in_specs=[vmem] * 8,
        out_specs=(vmem,) * 4,
        compiler_params=pltpu.CompilerParams(vmem_limit_bytes=48 << 20),
        name="train",
    )(weights, seen_film, slots, noisy, mask, levels, cotangent, jnp.asarray(level_table(), bf16))


def adam_kernel(
    own_ref, film_ref, square_ref, params_ref, first_ref, second_ref, order_ref,
    norm_ref, new_params_ref, new_first_ref, new_second_ref, copy_ref, grad_ref,
):
    norm = jnp.sqrt(jnp.sum(square_ref[...], axis=(0, 1), keepdims=True))
    norm_ref[...] = norm
    factor = jnp.minimum(1.0, clip_limit / (norm + 1e-06))
    misc = own_ref[B_MISC]
    first = dot_nt(misc[:, :128], order_ref[...])
    misc = misc.astype(f32)
    grad_ref[:, 0:50] = first[:, :50]
    grad_ref[:, AT_DOWN_RES : AT_DOWN_RES + ADIM] = misc[:, 50:60]
    grad_ref[:, AT_TAIL : AT_TAIL + TAIL] = misc[:, LANE_TAIL : LANE_TAIL + TAIL]
    grad_ref[:, AT_TIME[0] : AT_TIME[0] + 256] = own_ref[B_INNER].astype(f32)
    grad_ref[:, AT_TIME[1] : AT_TIME[1] + 256] = own_ref[B_OUTER].astype(f32)
    for q in range(4):
        grad_ref[:, AT_FILM[q] : AT_FILM[q] + OBS] = film_ref[q * ROWS : (q + 1) * ROWS]
        part = own_ref[B_FILM + q // 2, :, (q % 2) * 128 : (q % 2) * 128 + 128]
        grad_ref[:, AT_FILM[q] + OBS : AT_FILM[q] + OBS + TE] = part.astype(f32)
    grad_ref[:, AT_UP_RES : AT_UP_RES + 256] = own_ref[B_UR].astype(f32)
    grad_ref[:, AT_UP_RES + 256 : AT_UP_RES + 512] = own_ref[B_UR + 1].astype(f32)
    for taps in (5, 3, 4):
        places = [(at, h, block) for at, k, groups, block in CONVS if k == taps for h in range(groups)]
        stacked = jnp.concatenate(
            [
                jnp.concatenate(
                    [own_ref[block(t, h), :, (h % 2) * 128 : (h % 2) * 128 + 128] for t in range(taps)], axis=1
                )
                for _, h, block in places
            ],
            axis=0,
        )
        moved = dot_nt(stacked, tap_order(taps))
        for n, (at, h, _) in enumerate(places):
            begin = at + h * 128 * taps
            grad_ref[:, begin : begin + 128 * taps] = moved[n * ROWS : (n + 1) * ROWS]
    width = 1024
    for begin in range(0, Q, width):
        cols = slice(begin, min(begin + width, Q))
        clipped = grad_ref[:, cols] * factor
        new_first = decay_first * first_ref[:, cols] + (1.0 - decay_first) * clipped
        new_second = decay_second * second_ref[:, cols] + (1.0 - decay_second) * clipped * clipped
        first_hat = new_first * (1.0 / (1.0 - decay_first**ADAM_STEP))
        second_hat = new_second * (1.0 / (1.0 - decay_second**ADAM_STEP))
        old = params_ref[:, cols]
        new = old - learn_rate * (first_hat / (jnp.sqrt(second_hat) + adam_eps) + weight_decay * old)
        new_first_ref[:, cols] = new_first
        new_second_ref[:, cols] = new_second
        new_params_ref[:, cols] = new
        copy_ref[:, cols] = new.astype(bf16)


def adam(own, film, squares, params, first, second):
    vmem = pl.BlockSpec(memory_space=pltpu.VMEM)
    shape = jax.ShapeDtypeStruct((ROWS, Q), f32)
    return pl.pallas_call(
        adam_kernel,
        out_shape=(jax.ShapeDtypeStruct((1, 1), f32), shape, shape, shape, jax.ShapeDtypeStruct((ROWS, Q), bf16)),
        in_specs=[vmem] * 7,
        out_specs=(vmem,) * 5,
        scratch_shapes=[pltpu.VMEM((ROWS, Q), f32)],
        compiler_params=pltpu.CompilerParams(vmem_limit_bytes=56 << 20),
        name="adam",
    )(own, film, squares, params, first, second, jnp.asarray(first_order(), bf16))


def local_plain(noisy, action_mask, time_index, obs_embed, obs_slot, cotangent, params, first_moment, second_moment):
    rows = params.shape[0]
    padded = lambda v: jnp.pad(v, ((0, ROWS - rows), (0, 0))) if rows < ROWS else v
    if rows > ROWS:
        packed = [pack(params[r : r + ROWS]) for r in range(0, rows, ROWS)]
        own = jnp.concatenate([p[0] for p in packed], axis=1)
        film_own = jnp.concatenate([p[1].reshape(4, ROWS, OBS) for p in packed], axis=1)
    else:
        own, film_own = pack(padded(params))
        own = own[:, :rows]
        film_own = film_own.reshape(4, ROWS, OBS)[:, :rows]
    weights = lax.all_gather(own, "wide", axis=1, tiled=True)
    film_rows = lax.all_gather(film_own, "wide", axis=1, tiled=True).reshape(4 * C, OBS)
    seen = lax.all_gather(obs_embed, "pair", axis=0, tiled=True).reshape(-1, OBS).astype(f32)
    cond, slope = mish_parts(seen)
    cond = cond.astype(bf16)
    seen_film = dot_nt(cond, film_rows)
    act, noisy_grad, grads, film_grad = train(
        weights, seen_film, obs_slot[None], noisy[0], action_mask, time_index, cotangent[0]
    )
    film_total = lax.psum(dot_tn(film_grad, cond), ("pair", "wide")).reshape(4, C, OBS)
    back = lax.psum_scatter(
        (dot_nn(film_grad, film_rows) * slope).reshape(-1, obs_embed.shape[1], OBS),
        "pair", scatter_dimension=0, tiled=True,
    )
    total = lax.psum(grads.astype(f32), ("pair", "wide")).astype(bf16)
    squares = jnp.sum(jnp.square(total.astype(f32))) + jnp.sum(jnp.square(film_total))
    here = lax.axis_index("wide") * rows
    mine = lax.dynamic_slice_in_dim(total, here, rows, 1)
    film_mine = lax.dynamic_slice_in_dim(film_total, here, rows, 1)
    outs = []
    for r in range(0, rows, ROWS):
        take = lambda v: jnp.pad(v[:, r : r + ROWS], ((0, 0), (0, max(0, ROWS - rows)), (0, 0)))
        outs.append(
            adam(
                take(mine), take(film_mine).reshape(4 * ROWS, OBS), squares.reshape(1, 1),
                *(padded(v)[r : r + ROWS] for v in (params, first_moment, second_moment)),
            )
        )
    new = [jnp.concatenate([o[k] for o in outs], axis=0)[:rows] for k in range(1, 5)]
    return (act[None], noisy_grad[None], back, outs[0][0].reshape(()), *new)


def solution(mesh):
    in_specs = (
        P("pair", None, "wide"),
        P(None, "wide"),
        P("pair", "wide"),
        P("pair", "wide", None),
        P("wide"),
        P("pair", None, "wide"),
        P("wide", None),
        P("wide", None),
        P("wide", None),
    )
    out_specs = (
        P("pair", None, "wide"),
        P("pair", None, "wide"),
        P("pair", "wide", None),
        P(),
        P("wide", None),
        P("wide", None),
        P("wide", None),
        P("wide", None),
    )
    return jax.shard_map(local_plain, mesh=mesh, in_specs=in_specs, out_specs=out_specs, check_vma=False)
```

```python
import math

import jax
import jax.numpy as jnp
import numpy as np
from jax import lax
from jax.experimental import pallas as pl
from jax.experimental.pallas import tpu as pltpu
from jax.sharding import PartitionSpec as P

C = 256
OBS = 1024
TE = 128
TH = 512
ADIM = 10
FR = 16
LEVELS = 40
ADAM_STEP = 7
Q = 12627
SAM = 16
ROWS = 32
NB = 36

sigma_top = 80.0 ** (1.0 / 7.0)
sigma_low = 0.002 ** (1.0 / 7.0)
clip_limit = 1.0
learn_rate = 0.02
decay_first = 0.5
decay_second = 0.5
adam_eps = 1e-08
weight_decay = 0.01
norm_eps = 1e-05

f32 = jnp.float32
bf16 = jnp.bfloat16

AT_DOWN_RES = 1330
AT_TAIL = 12604
TAIL = 23
AT_FILM = (1340, 2492, 9788, 10940)
AT_TIME = (12092, 12348)
AT_UP_RES = 9276
B_MISC, B_INNER, B_OUTER, B_FILM = 0, 1, 2, 3
B_DS, B_POOL, B_SPREAD, B_UF, B_US, B_UR = 5, 10, 13, 17, 27, 32
LANE_TAIL = 64
CONVS = (
    (50, 5, 2, lambda t, h: B_DS + t),
    (5436, 5, 4, lambda t, h: B_UF + 2 * t + h // 2),
    (7996, 5, 2, lambda t, h: B_US + t),
    (3644, 3, 2, lambda t, h: B_POOL + t),
    (4412, 4, 2, lambda t, h: B_SPREAD + t),
)
(T_BIAS_A, T_BIAS_B, T_OUT, D_B1, D_G1, D_S1, D_FS, D_FO, D_B2, D_G2, D_S2, D_RB, PB, SB,
 U_B1, U_G1, U_S1, U_FS, U_FO, U_B2, U_G2, U_S2, U_RB) = range(TAIL)


def dot_nt(a, b):
    return lax.dot_general(a, b, (((1,), (1,)), ((), ())), preferred_element_type=f32)


def dot_nn(a, b):
    return lax.dot_general(a, b, (((1,), (0,)), ((), ())), preferred_element_type=f32)


def dot_tn(a, b):
    return lax.dot_general(a, b, (((0,), (0,)), ((), ())), preferred_element_type=f32)


def split2(v):
    high = v.astype(bf16)
    return high, (v - high.astype(f32)).astype(bf16)


def split3(v):
    high, rest = v.astype(bf16), None
    rest = v - high.astype(f32)
    mid = rest.astype(bf16)
    return high, mid, (rest - mid.astype(f32)).astype(bf16)


def tap_order(taps):
    n = 128 * taps
    row = lax.broadcasted_iota(jnp.int32, (n, n), 0)
    col = lax.broadcasted_iota(jnp.int32, (1, n), 1)
    source = (col & 127) * taps + (col >> 7)
    return jnp.where(row == source, 1.0, 0.0).astype(bf16)


def first_order():
    table = np.zeros((128, 128), np.float32)
    for i in range(ADIM):
        for t in range(5):
            table[i * 5 + t, t * ADIM + i] = 1.0
    return table


def level_table():
    levels = np.arange(LEVELS, dtype=np.float64)
    tau = 250.0 * 7.0 * np.log(sigma_top + levels / (LEVELS - 1) * (sigma_low - sigma_top))
    freq = np.exp(-math.log(10000.0) * np.arange(TE // 2) / (TE // 2 - 1))
    angles = tau[:, None] * freq[None, :]
    table = np.zeros((64, TE), np.float32)
    table[:LEVELS] = np.concatenate([np.sin(angles), np.cos(angles)], axis=1)
    return table


def pack_kernel(params_ref, order_ref, own_ref, film_ref):
    pack_rows(params_ref, order_ref, own_ref, film_ref)


class Blocks:
    def __init__(self, ref):
        self.ref = ref

    def _at(self, key):
        block, rest = (key[0], key[1:]) if isinstance(key, tuple) else (key, ())
        return (block // 4, block % 4) + rest

    def __getitem__(self, key):
        return self.ref[self._at(key)]

    def __setitem__(self, key, value):
        self.ref[self._at(key)] = value


def pack_rows(params_ref, order_ref, own_ref, film_ref):
    own_ref = Blocks(own_ref)

    def low(start, width):
        return params_ref[:, start : start + width].astype(bf16)

    first = dot_nn(low(0, 128), order_ref[...])
    pieces = [
        first[:, :50],
        params_ref[:, AT_DOWN_RES : AT_DOWN_RES + ADIM],
        jnp.zeros((ROWS, LANE_TAIL - 60), f32),
        params_ref[:, AT_TAIL : AT_TAIL + TAIL],
        jnp.zeros((ROWS, 256 - LANE_TAIL - TAIL), f32),
    ]
    own_ref[B_MISC] = jnp.concatenate(pieces, axis=1).astype(bf16)
    own_ref[B_INNER] = low(AT_TIME[0], 256)
    own_ref[B_OUTER] = low(AT_TIME[1], 256)
    for q in range(4):
        film_ref[q * ROWS : (q + 1) * ROWS] = low(AT_FILM[q], OBS)
        own_ref[B_FILM + q // 2, :, (q % 2) * 128 : (q % 2) * 128 + 128] = low(AT_FILM[q] + OBS, TE)
    own_ref[B_UR] = low(AT_UP_RES, 256)
    own_ref[B_UR + 1] = low(AT_UP_RES + 256, 256)
    own_ref[NB - 2] = jnp.zeros((ROWS, 256), bf16)
    own_ref[NB - 1] = jnp.zeros((ROWS, 256), bf16)
    for taps in (5, 3, 4):
        places = [(at, h, block) for at, k, groups, block in CONVS if k == taps for h in range(groups)]
        stacked = jnp.concatenate([low(at + h * 128 * taps, 128 * taps) for at, h, _ in places], axis=0)
        moved = dot_nn(stacked, tap_order(taps)).astype(bf16)
        for n, (_, h, block) in enumerate(places):
            for t in range(taps):
                own_ref[block(t, h), :, (h % 2) * 128 : (h % 2) * 128 + 128] = moved[
                    n * ROWS : (n + 1) * ROWS, t * 128 : (t + 1) * 128
                ]


def pack(params):
    vmem = pl.BlockSpec(memory_space=pltpu.VMEM)
    return pl.pallas_call(
        pack_kernel,
        out_shape=(
            jax.ShapeDtypeStruct((NB // 4, 4, ROWS, 256), bf16),
            jax.ShapeDtypeStruct((4 * ROWS, OBS), bf16),
        ),
        in_specs=[vmem, vmem],
        out_specs=(vmem, vmem),
        compiler_params=pltpu.CompilerParams(vmem_limit_bytes=40 << 20),
        name="pack",
    )(params, jnp.asarray(first_order(), bf16))


def mish_parts(v):
    e = jnp.exp(jnp.minimum(v, 20.0))
    n = e * (e + 2.0)
    r = 1.0 / (n + 2.0)
    t = n * r
    return v * t, t + 4.0 * v * (e * r) * ((e + 1.0) * r)


def step_frames(v, step):
    if step == 0:
        return v
    zeros = jnp.zeros((SAM * abs(step), v.shape[1]), v.dtype)
    if step > 0:
        return jnp.concatenate([v[SAM * step :], zeros], axis=0)
    return jnp.concatenate([zeros, v[: SAM * step]], axis=0)


def over_frames(v):
    return jnp.sum(v.reshape(-1, SAM, v.shape[1]), axis=0)


def each_frame(v, s):
    return v.reshape(-1, SAM, v.shape[1]), s[None]


def group_means(values, ones):
    parts = [p for v in values for p in split3(v)]
    sums = dot_nn(jnp.concatenate(parts, axis=0), ones)
    out = []
    for i in range(len(values)):
        a, b, c = (sums[(3 * i + k) * SAM : (3 * i + k + 1) * SAM] for k in range(3))
        out.append((a + (b + c)) * (1.0 / (32 * FR)))
    return out


def minus(v, s):
    a, b = each_frame(v, s)
    return (a - b).reshape(v.shape)


def times(v, s):
    a, b = each_frame(v, s)
    return (a * b).reshape(v.shape)


def plus(v, s):
    a, b = each_frame(v, s)
    return (a + b).reshape(v.shape)


def norm_forward(before, gain, shift, ones):
    (center,) = group_means([over_frames(before)], ones)
    away = minus(before, center)
    (spread,) = group_means([over_frames(away * away)], ones)
    scale = lax.rsqrt(spread + norm_eps)
    normal = times(away, scale)
    act, slope = mish_parts(normal * gain + shift)
    return act, normal, slope, scale


def norm_backward(grad_act, normal, slope, scale, gain, ones):
    grad_out = grad_act * slope
    shift_rows = over_frames(grad_out)
    gain_rows = over_frames(grad_out * normal)
    mean_grad, mean_both = group_means([shift_rows * gain, gain_rows * gain], ones)
    inner = minus(grad_out * gain, mean_grad) - times(normal, mean_both)
    return (
        times(inner, scale),
        jnp.sum(gain_rows, axis=0, keepdims=True),
        jnp.sum(shift_rows, axis=0, keepdims=True),
    )


def conv_forward(source, weight):
    total = dot_nt(step_frames(source, -2), weight(0))
    for t in range(1, 5):
        total = total + dot_nt(step_frames(source, t - 2), weight(t))
    return total


def conv_source(grad_low, weight):
    total = dot_nn(step_frames(grad_low, 2), weight(0))
    for t in range(1, 5):
        total = total + dot_nn(step_frames(grad_low, 2 - t), weight(t))
    return total


def row_sum(v):
    return jnp.sum(over_frames(v), axis=0, keepdims=True)


def halves(v):
    cube = v.reshape(FR // 2, 2, SAM, v.shape[1])
    return cube[:, 0].reshape(-1, v.shape[1]), cube[:, 1].reshape(-1, v.shape[1])


def interleave(even, odd):
    width = even.shape[1]
    pair = [v.reshape(FR // 2, 1, SAM, width) for v in (even, odd)]
    return jnp.concatenate(pair, axis=1).reshape(FR * SAM, width)


def train_kernel(
    w_ref, seen_ref, slot_ref, noisy_ref, mask_ref, level_ref, cot_ref, table_ref,
    act_ref, noisy_grad_ref, grad_ref, film_grad_ref,
):
    iota = lambda shape, dim: lax.broadcasted_iota(jnp.int32, shape, dim)
    row = iota((256, 256), 0)
    col = iota((256, 256), 1)
    ones = jnp.where((row >> 5) == (col >> 5), 1.0, 0.0).astype(bf16)
    swap = jnp.where(col == ((row & 15) << 4) + (row >> 4), 1.0, 0.0).astype(bf16)
    misc = w_ref[B_MISC, :, :128]
    lane = iota((256, 128), 1)
    misc_first = jnp.where(lane < 50, misc, jnp.zeros_like(misc))
    misc_res = jnp.where((lane >= 50) & (lane < 60), misc, jnp.zeros_like(misc))
    singles = misc.astype(f32).T[LANE_TAIL : LANE_TAIL + 32]
    vec = lambda k: singles[k : k + 1]

    at_level = jnp.where(iota((64, SAM), 0) == level_ref[...], 1.0, 0.0).astype(bf16)
    feats = dot_tn(at_level, table_ref[...]).astype(bf16)
    inner = [w_ref[B_INNER, :, j * 128 : (j + 1) * 128] for j in range(2)]
    outer = [w_ref[B_OUTER, :, j * 128 : (j + 1) * 128] for j in range(2)]
    film_time = [w_ref[B_FILM + q // 2, :, (q % 2) * 128 : (q % 2) * 128 + 128] for q in range(4)]
    hidden = [mish_parts(dot_nt(feats, inner[j]) + vec(T_BIAS_A + j)) for j in range(2)]
    hidden_low = [h[0].astype(bf16) for h in hidden]
    embed = dot_nn(hidden_low[0], outer[0]) + dot_nn(hidden_low[1], outer[1]) + vec(T_OUT)[:, :TE]
    cond, cond_slope = mish_parts(embed)
    cond_low = cond.astype(bf16)
    at_slot = jnp.where(iota((SAM, SAM), 0) == slot_ref[...], 1.0, 0.0).astype(bf16)
    line = iota((32, SAM), 0)
    at_line = ((line >> 3) * 4 + (line & 7) == slot_ref[...]) & ((line & 7) < 4)
    at_line = jnp.where(at_line, 1.0, 0.0).astype(bf16)
    seen_film = jnp.concatenate([seen_ref[:, k].reshape(32, 128) for k in range(8)], axis=1)
    seen_film = sum(dot_tn(at_line, part) for part in split3(seen_film))
    spans = lambda v, q: jnp.concatenate([v[:, k * 128 + q * 32 : k * 128 + q * 32 + 32] for k in range(8)], axis=1)
    film = [
        spans(seen_film, q) + dot_nt(cond_low, film_time[q]) + vec((D_FS, D_FO, U_FS, U_FO)[q])
        for q in range(4)
    ]

    spread_mask = jnp.where((iota((SAM, 256), 1) >> 4) == iota((SAM, 256), 0), 1.0, 0.0).astype(bf16)
    keep = dot_nn(mask_ref[...].astype(f32).astype(bf16), spread_mask)
    start_cols = noisy_ref[...].astype(f32) * keep
    start_cols = jnp.concatenate([start_cols, jnp.zeros((6, 256), f32)], axis=0).astype(bf16)
    start = dot_nt(swap, start_cols).astype(bf16)
    lane16 = iota((16, 128), 1)
    row16 = iota((16, 128), 0)
    inputs = jnp.zeros((256, 128), f32)
    for t in range(5):
        place = lane16 == row16 + t * ADIM
        if t == 2:
            place = place | (lane16 == row16 + 50)
        place = place & (row16 < ADIM)
        inputs = inputs + dot_nn(step_frames(start, t - 2), jnp.where(place, 1.0, 0.0).astype(bf16))
    inputs = inputs.astype(bf16)
    pre = dot_nt(inputs, misc_first) + vec(D_B1)
    act_one, normal_one, slope_one, scale_one = norm_forward(pre, vec(D_G1), vec(D_S1), ones)
    mid_one = plus(times(act_one, film[0]), film[1]).astype(bf16)
    down = lambda t: w_ref[B_DS + t]
    pre = conv_forward(mid_one, down) + vec(D_B2)
    act, normal_two, slope_two, scale_two = norm_forward(pre, vec(D_G2), vec(D_S2), ones)
    skip = (act + dot_nt(inputs, misc_res) + vec(D_RB)).astype(bf16)
    even, odd = halves(skip)
    odd_prev = step_frames(odd, -1)
    pool_sources = (odd_prev, even, odd)
    pooled = sum(dot_nt(s, w_ref[B_POOL + t]) for t, s in enumerate(pool_sources)) + vec(PB)
    pooled = pooled.astype(bf16)
    pooled_prev = step_frames(pooled, -1)
    pooled_next = step_frames(pooled, 1)
    even_out = dot_nt(pooled, w_ref[B_SPREAD + 1]) + dot_nt(pooled_prev, w_ref[B_SPREAD + 3])
    odd_out = dot_nt(pooled_next, w_ref[B_SPREAD]) + dot_nt(pooled, w_ref[B_SPREAD + 2])
    wide = (interleave(even_out, odd_out) + vec(SB)).astype(bf16)
    joined = (wide, skip)
    up_first = [lambda t, h=h: w_ref[B_UF + 2 * t + h] for h in range(2)]
    pre = conv_forward(wide, up_first[0]) + conv_forward(skip, up_first[1]) + vec(U_B1)
    act_three, normal_three, slope_three, scale_three = norm_forward(pre, vec(U_G1), vec(U_S1), ones)
    mid_three = plus(times(act_three, film[2]), film[3]).astype(bf16)
    up = lambda t: w_ref[B_US + t]
    pre = conv_forward(mid_three, up) + vec(U_B2)
    act, normal_four, slope_four, scale_four = norm_forward(pre, vec(U_G2), vec(U_S2), ones)
    result = act + dot_nt(wide, w_ref[B_UR]) + dot_nt(skip, w_ref[B_UR + 1]) + vec(U_RB)
    act_ref[...] = dot_tn(result.astype(bf16), swap).astype(bf16)

    single_grads = {}

    def conv_weights(grad_low, source, block):
        turned = grad_low.T
        for t in range(5):
            grad_ref[block(t)] = dot_nn(turned, step_frames(source, t - 2)).astype(bf16)

    cot_high, cot_low = split2(cot_ref[...])
    upstream = dot_nt(swap, cot_high) + dot_nt(swap, cot_low)
    grad, single_grads[U_G2], single_grads[U_S2] = norm_backward(
        upstream, normal_four, slope_four, scale_four, vec(U_G2), ones
    )
    single_grads[U_B2] = row_sum(grad)
    low = grad.astype(bf16)
    conv_weights(low, mid_three, lambda t: B_US + t)
    grad_mid = conv_source(low, up)
    shift_three = over_frames(grad_mid)
    gain_three = over_frames(grad_mid * act_three)
    grad, single_grads[U_G1], single_grads[U_S1] = norm_backward(
        times(grad_mid, film[2]), normal_three, slope_three, scale_three, vec(U_G1), ones
    )
    single_grads[U_B1] = row_sum(grad)
    low = grad.astype(bf16)
    for h in range(2):
        conv_weights(low, joined[h], lambda t, h=h: B_UF + 2 * t + h)
    single_grads[U_RB] = row_sum(upstream)
    upstream_low = upstream.astype(bf16)
    turned = upstream_low.T
    for h in range(2):
        grad_ref[B_UR + h] = dot_nn(turned, joined[h]).astype(bf16)
    grad_wide = conv_source(low, up_first[0]) + dot_nn(upstream_low, w_ref[B_UR])
    grad_skip = conv_source(low, up_first[1]) + dot_nn(upstream_low, w_ref[B_UR + 1])
    single_grads[SB] = row_sum(grad_wide)
    low_even, low_odd = halves(grad_wide.astype(bf16))
    turned_even, turned_odd = low_even.T, low_odd.T
    grad_ref[B_SPREAD] = dot_nn(turned_odd, pooled_next).astype(bf16)
    grad_ref[B_SPREAD + 1] = dot_nn(turned_even, pooled).astype(bf16)
    grad_ref[B_SPREAD + 2] = dot_nn(turned_odd, pooled).astype(bf16)
    grad_ref[B_SPREAD + 3] = dot_nn(turned_even, pooled_prev).astype(bf16)
    grad_pooled = dot_nn(low_even, w_ref[B_SPREAD + 1]) + dot_nn(low_odd, w_ref[B_SPREAD + 2])
    grad_pooled = grad_pooled + dot_nn(step_frames(low_even, 1), w_ref[B_SPREAD + 3])
    grad_pooled = grad_pooled + dot_nn(step_frames(low_odd, -1), w_ref[B_SPREAD])
    single_grads[PB] = row_sum(grad_pooled)
    low = grad_pooled.astype(bf16)
    turned = low.T
    for t in range(3):
        grad_ref[B_POOL + t] = dot_nn(turned, pool_sources[t]).astype(bf16)
    grad_even = dot_nn(low, w_ref[B_POOL + 1])
    grad_odd = dot_nn(low, w_ref[B_POOL + 2]) + dot_nn(step_frames(low, 1), w_ref[B_POOL])
    grad_skip = grad_skip + interleave(grad_even, grad_odd)
    single_grads[D_RB] = row_sum(grad_skip)
    skip_low = grad_skip.astype(bf16)
    misc_grad = jnp.where(lane < 50, 0.0, dot_nn(skip_low.T, inputs))
    back = dot_nn(skip_low, misc_res)
    grad, single_grads[D_G2], single_grads[D_S2] = norm_backward(
        grad_skip, normal_two, slope_two, scale_two, vec(D_G2), ones
    )
    single_grads[D_B2] = row_sum(grad)
    low = grad.astype(bf16)
    conv_weights(low, mid_one, lambda t: B_DS + t)
    grad_mid = conv_source(low, down)
    shift_one = over_frames(grad_mid)
    gain_one = over_frames(grad_mid * act_one)
    grad, single_grads[D_G1], single_grads[D_S1] = norm_backward(
        times(grad_mid, film[0]), normal_one, slope_one, scale_one, vec(D_G1), ones
    )
    single_grads[D_B1] = row_sum(grad)
    low = grad.astype(bf16)
    misc_grad = misc_grad + jnp.where(lane < 50, dot_nn(low.T, inputs), 0.0)
    back = back + dot_nn(low, misc_first)
    grad_start = back[:, 50:60]
    for t in range(5):
        grad_start = grad_start + step_frames(back[:, t * ADIM : (t + 1) * ADIM], 2 - t)
    grad_cols = sum(dot_tn(part, swap) for part in split3(jnp.concatenate([grad_start, jnp.zeros((256, 6), f32)], axis=1)))
    noisy_grad_ref[...] = grad_cols[:ADIM] * keep

    film_grads = (gain_one, shift_one, gain_three, shift_three)
    film_low = [g.astype(bf16) for g in film_grads]
    back_cond = None
    for q in range(4):
        single_grads[(D_FS, D_FO, U_FS, U_FO)[q]] = jnp.sum(film_grads[q], axis=0, keepdims=True)
        grad_ref[B_FILM + q // 2, :, (q % 2) * 128 : (q % 2) * 128 + 128] = dot_tn(film_low[q], cond_low).astype(bf16)
        part = dot_nn(film_low[q], film_time[q])
        back_cond = part if back_cond is None else back_cond + part
    at_slots = [dot_nn(at_slot, v) for v in film_low]
    for k in range(8):
        film_grad_ref[k] = jnp.concatenate([v[:, k * 32 : (k + 1) * 32] for v in at_slots], axis=1).astype(bf16)
    grad_embed = back_cond * cond_slope
    single_grads[T_OUT] = jnp.concatenate(
        [jnp.sum(grad_embed, axis=0, keepdims=True), jnp.zeros((1, C - TE), f32)], axis=1
    )
    embed_low = grad_embed.astype(bf16)
    for j in range(2):
        grad_ref[B_OUTER, :, j * 128 : (j + 1) * 128] = dot_tn(hidden_low[j], embed_low).astype(bf16)
        grad_hidden = dot_nt(embed_low, outer[j]) * hidden[j][1]
        single_grads[T_BIAS_A + j] = jnp.sum(grad_hidden, axis=0, keepdims=True)
        grad_ref[B_INNER, :, j * 128 : (j + 1) * 128] = dot_tn(grad_hidden.astype(bf16), feats).astype(bf16)
    stack = [jnp.zeros((LANE_TAIL, 256), f32)] + [single_grads[k] for k in range(TAIL)]
    stack = jnp.concatenate(stack + [jnp.zeros((128 - LANE_TAIL - TAIL, 256), f32)], axis=0)
    grad_ref[B_MISC, :, :128] = (misc_grad + stack.T).astype(bf16)
    grad_ref[B_MISC, :, 128:] = jnp.zeros((256, 128), bf16)
    for b in range(B_UR + 2, NB):
        grad_ref[b] = jnp.zeros((256, 256), bf16)


def train(weights, seen_film, slots, noisy, mask, levels, cotangent):
    vmem = pl.BlockSpec(memory_space=pltpu.VMEM)
    return pl.pallas_call(
        train_kernel,
        out_shape=(
            jax.ShapeDtypeStruct((C, 256), bf16),
            jax.ShapeDtypeStruct((ADIM, 256), f32),
            jax.ShapeDtypeStruct((NB, 256, 256), bf16),
            jax.ShapeDtypeStruct((8, SAM, 128), bf16),
        ),
        in_specs=[vmem] * 8,
        out_specs=(vmem,) * 4,
        compiler_params=pltpu.CompilerParams(vmem_limit_bytes=48 << 20),
        name="train",
    )(weights, seen_film, slots, noisy, mask, levels, cotangent, jnp.asarray(level_table(), bf16))


def adam_kernel(
    own_ref, film_ref, square_ref, params_ref, first_ref, second_ref, order_ref,
    norm_ref, new_params_ref, new_first_ref, new_second_ref, copy_ref, grad_ref,
):
    norm = jnp.sqrt(jnp.sum(square_ref[...], axis=(0, 1), keepdims=True))
    norm_ref[...] = norm
    factor = jnp.minimum(1.0, clip_limit / (norm + 1e-06))
    misc = own_ref[B_MISC]
    first = dot_nt(misc[:, :128], order_ref[...])
    misc = misc.astype(f32)
    grad_ref[:, 0:50] = first[:, :50]
    grad_ref[:, AT_DOWN_RES : AT_DOWN_RES + ADIM] = misc[:, 50:60]
    grad_ref[:, AT_TAIL : AT_TAIL + TAIL] = misc[:, LANE_TAIL : LANE_TAIL + TAIL]
    grad_ref[:, AT_TIME[0] : AT_TIME[0] + 256] = own_ref[B_INNER].astype(f32)
    grad_ref[:, AT_TIME[1] : AT_TIME[1] + 256] = own_ref[B_OUTER].astype(f32)
    for q in range(4):
        grad_ref[:, AT_FILM[q] : AT_FILM[q] + OBS] = film_ref[q * ROWS : (q + 1) * ROWS]
        part = own_ref[B_FILM + q // 2, :, (q % 2) * 128 : (q % 2) * 128 + 128]
        grad_ref[:, AT_FILM[q] + OBS : AT_FILM[q] + OBS + TE] = part.astype(f32)
    grad_ref[:, AT_UP_RES : AT_UP_RES + 256] = own_ref[B_UR].astype(f32)
    grad_ref[:, AT_UP_RES + 256 : AT_UP_RES + 512] = own_ref[B_UR + 1].astype(f32)
    for taps in (5, 3, 4):
        places = [(at, h, block) for at, k, groups, block in CONVS if k == taps for h in range(groups)]
        stacked = jnp.concatenate(
            [
                jnp.concatenate(
                    [own_ref[block(t, h), :, (h % 2) * 128 : (h % 2) * 128 + 128] for t in range(taps)], axis=1
                )
                for _, h, block in places
            ],
            axis=0,
        )
        moved = dot_nt(stacked, tap_order(taps))
        for n, (at, h, _) in enumerate(places):
            begin = at + h * 128 * taps
            grad_ref[:, begin : begin + 128 * taps] = moved[n * ROWS : (n + 1) * ROWS]
    width = 1024
    for begin in range(0, Q, width):
        cols = slice(begin, min(begin + width, Q))
        clipped = grad_ref[:, cols] * factor
        new_first = decay_first * first_ref[:, cols] + (1.0 - decay_first) * clipped
        new_second = decay_second * second_ref[:, cols] + (1.0 - decay_second) * clipped * clipped
        first_hat = new_first * (1.0 / (1.0 - decay_first**ADAM_STEP))
        second_hat = new_second * (1.0 / (1.0 - decay_second**ADAM_STEP))
        old = params_ref[:, cols]
        new = old - learn_rate * (first_hat / (jnp.sqrt(second_hat) + adam_eps) + weight_decay * old)
        new_first_ref[:, cols] = new_first
        new_second_ref[:, cols] = new_second
        new_params_ref[:, cols] = new
        copy_ref[:, cols] = new.astype(bf16)


def adam(own, film, squares, params, first, second):
    vmem = pl.BlockSpec(memory_space=pltpu.VMEM)
    shape = jax.ShapeDtypeStruct((ROWS, Q), f32)
    return pl.pallas_call(
        adam_kernel,
        out_shape=(jax.ShapeDtypeStruct((1, 1), f32), shape, shape, shape, jax.ShapeDtypeStruct((ROWS, Q), bf16)),
        in_specs=[vmem] * 7,
        out_specs=(vmem,) * 5,
        scratch_shapes=[pltpu.VMEM((ROWS, Q), f32)],
        compiler_params=pltpu.CompilerParams(vmem_limit_bytes=56 << 20),
        name="adam",
    )(own, film, squares, params, first, second, jnp.asarray(first_order(), bf16))


def local_plain(noisy, action_mask, time_index, obs_embed, obs_slot, cotangent, params, first_moment, second_moment):
    rows = params.shape[0]
    padded = lambda v: jnp.pad(v, ((0, ROWS - rows), (0, 0))) if rows < ROWS else v
    if rows > ROWS:
        packed = [pack(params[r : r + ROWS]) for r in range(0, rows, ROWS)]
        own = jnp.concatenate([p[0].reshape(NB, ROWS, 256) for p in packed], axis=1)
        film_own = jnp.concatenate([p[1].reshape(4, ROWS, OBS) for p in packed], axis=1)
    else:
        own, film_own = pack(padded(params))
        own = own.reshape(NB, ROWS, 256)[:, :rows]
        film_own = film_own.reshape(4, ROWS, OBS)[:, :rows]
    weights = lax.all_gather(own, "wide", axis=1, tiled=True)
    film_rows = lax.all_gather(film_own, "wide", axis=1, tiled=True).reshape(4 * C, OBS)
    seen = lax.all_gather(obs_embed, "pair", axis=0, tiled=True).reshape(-1, OBS).astype(f32)
    cond, slope = mish_parts(seen)
    cond = cond.astype(bf16)
    seen_film = dot_nt(cond, film_rows).reshape(4, 4, 4, 8, 32).transpose(0, 3, 1, 2, 4).reshape(4, 8, 4, 128)
    seen_film = jnp.pad(seen_film, ((0, 0), (0, 0), (0, 4), (0, 0)))
    act, noisy_grad, grads, film_grad = train(
        weights, seen_film, obs_slot[None], noisy[0], action_mask, time_index, cotangent[0]
    )
    film_grad = film_grad.reshape(8, SAM, 4, 32).transpose(1, 2, 0, 3).reshape(SAM, 4 * C)
    film_total = lax.psum(dot_tn(film_grad, cond), ("pair", "wide")).reshape(4, C, OBS)
    back = lax.psum_scatter(
        (dot_nn(film_grad, film_rows) * slope).reshape(-1, obs_embed.shape[1], OBS),
        "pair", scatter_dimension=0, tiled=True,
    )
    total = lax.psum(grads.astype(f32), ("pair", "wide")).astype(bf16)
    squares = jnp.sum(jnp.square(total.astype(f32))) + jnp.sum(jnp.square(film_total))
    here = lax.axis_index("wide") * rows
    mine = lax.dynamic_slice_in_dim(total, here, rows, 1)
    film_mine = lax.dynamic_slice_in_dim(film_total, here, rows, 1)
    outs = []
    for r in range(0, rows, ROWS):
        take = lambda v: jnp.pad(v[:, r : r + ROWS], ((0, 0), (0, max(0, ROWS - rows)), (0, 0)))
        outs.append(
            adam(
                take(mine), take(film_mine).reshape(4 * ROWS, OBS), squares.reshape(1, 1),
                *(padded(v)[r : r + ROWS] for v in (params, first_moment, second_moment)),
            )
        )
    new = [jnp.concatenate([o[k] for o in outs], axis=0)[:rows] for k in range(1, 5)]
    return (act[None], noisy_grad[None], back, outs[0][0].reshape(()), *new)


MESH = pl.DeviceIdType.MESH
GROUPS = 3
EACH = NB // 4 // GROUPS


def flipped(v, bits):
    out = v
    for k in range(3):
        if bits >> k & 1:
            bit = (v // (1 << k)) % 2
            out = out + (1 << k) * (1 - 2 * bit)
    return out


class Place:
    def __init__(self):
        self.p = lax.axis_index("pair")
        self.w = lax.axis_index("wide")
        self.x, self.y = self.p % 2, self.p // 2
        self.c, self.z = self.w % 2, self.w // 2

    def line(self, l):
        return (self.p, flipped(self.w, l))

    def plane(self, k):
        return (flipped(self.p, k), self.w)


def meet(me):
    barrier = pltpu.get_barrier_semaphore()
    for l in range(1, 8):
        pl.semaphore_signal(barrier, inc=1, device_id=me.line(l), device_id_type=MESH)
    for k in range(1, 4):
        pl.semaphore_signal(barrier, inc=1, device_id=me.plane(k), device_id_type=MESH)
    pl.semaphore_wait(barrier, 10)


def send(source, target, sems, at, device):
    copy = pltpu.make_async_remote_copy(
        src_ref=source, dst_ref=target, send_sem=sems[0].at[at], recv_sem=sems[1].at[at],
        device_id=device, device_id_type=MESH,
    )
    copy.start()
    return copy


def fold_rows(v):
    return jnp.concatenate([v[:, q * 256 : (q + 1) * 256] for q in range(4)], axis=0)


def unfold_rows(v):
    return jnp.concatenate([v[q * 4 : (q + 1) * 4] for q in range(4)], axis=1)


def iota(shape, dim):
    return lax.broadcasted_iota(jnp.int32, shape, dim)


def one_hot(condition):
    return jnp.where(condition, 1.0, 0.0).astype(bf16)


def quarter_rows(parts):
    quarter = (iota(parts[0].shape, 0) >> 2) & 3
    return sum(jnp.where(quarter == q, part, 0.0) for q, part in enumerate(parts))


def gather_kernel(
    params_ref, order_ref, obs_ref,
    w_ref, seen_ref, obs_all_ref, film_ref,
    own_ref, film_part, film_line,
    obs_sems, obs_sems2, part_sems, part_sems2, film_sems, film_sems2, more_sems, more_sems2,
    z_sems, z_sems2, x_sems, x_sems2, y_sems, y_sems2, f_sems, f_sems2, c_sems, c_sems2, local_sem,
):
    me = Place()
    obs_sems, part_sems, film_sems, more_sems = (
        (obs_sems, obs_sems2), (part_sems, part_sems2), (film_sems, film_sems2), (more_sems, more_sems2)
    )
    z_sems, x_sems, y_sems, f_sems, c_sems = (
        (z_sems, z_sems2), (x_sems, x_sems2), (y_sems, y_sems2), (f_sems, f_sems2), (c_sems, c_sems2)
    )
    obs_all_ref[me.p, me.w] = fold_rows(obs_ref[0].astype(f32)).astype(bf16)
    meet(me)
    obs_copies = [
        send(obs_all_ref.at[me.p, me.w], obs_all_ref.at[me.p, me.w], obs_sems, l - 1, me.line(l)) for l in range(1, 8)
    ]
    pack_rows(params_ref, order_ref, own_ref, film_ref)
    group = lambda g: pl.ds(g * EACH, EACH)
    z_copies = [
        [
            send(own_ref.at[group(g), me.p], w_ref.at[group(g), me.p, me.z, me.c], z_sems, g * 3 + k - 1, me.line(2 * k))
            for k in range(1, 4)
        ]
        for g in range(GROUPS)
    ]
    local = pltpu.make_async_copy(own_ref, w_ref.at[:, :, me.z, me.c], local_sem)
    local.start()

    for copy in obs_copies:
        copy.wait_recv()
    cond = mish_parts(obs_all_ref[me.p].reshape(128, 256).astype(f32))[0].astype(bf16)
    film = quarter_rows([dot_nt(cond, film_ref[:, q * 256 : (q + 1) * 256]) for q in range(4)])
    row, col = iota((64, 128), 0), iota((64, 128), 1)
    gather = one_hot(((row >> 3) == (col >> 4)) & ((row & 7) == (col & 3)))
    film = sum(dot_nn(gather, part) for part in split3(film))
    film_part[...] = film.reshape(8, 8, 128)
    part_copies = [
        send(film_part.at[flipped(me.w, l)], film_line.at[me.w], part_sems, l - 1, me.line(l)) for l in range(1, 8)
    ]
    film_line[me.w] = film_part[me.w]

    x_copies, y_copies, f_copies, c_copies = {}, {}, {}, {}
    film_copies, more_copies = [], []

    def first_hop(g):
        for k in range(1, 4):
            z_copies[g][k - 1].wait_recv()
            piece = w_ref.at[group(g), me.p, flipped(me.z, k), me.c]
            x_copies[g, k] = send(piece, piece, x_sems, g * 3 + k - 1, me.plane(1))
            y_copies[g, k] = send(piece, piece, y_sems, g * 3 + k - 1, me.plane(2))

    def second_hop(g):
        for k in range(1, 4):
            x_copies[g, k].wait_recv()
            y_copies[g, k].wait_recv()
            along_y = (g + k) % 2 == 0
            piece = w_ref.at[group(g), flipped(me.p, 1 if along_y else 2), flipped(me.z, k), me.c]
            f_copies[g, k] = send(piece, piece, f_sems, g * 3 + k - 1, me.plane(2 if along_y else 1))

    def last_hop(g):
        for k in range(1, 4):
            f_copies[g, k].wait_recv()
        piece = w_ref.at[group(g), :, :, me.c]
        c_copies[g] = send(piece, piece, c_sems, g, me.line(1))

    def film_hop():
        for copy in part_copies:
            copy.wait()
        seen_ref[me.p] = film_line[...]
        for k in range(1, 4):
            film_copies.append(send(seen_ref.at[me.p], seen_ref.at[me.p], film_sems, k - 1, me.plane(k)))
        for k in range(1, 4):
            more_copies.append(send(obs_all_ref.at[me.p], obs_all_ref.at[me.p], more_sems, k - 1, me.plane(k)))

    for step in range(GROUPS + 2):
        if step < GROUPS:
            first_hop(step)
        if step == 0:
            film_hop()
        if 0 <= step - 1 < GROUPS:
            second_hop(step - 1)
        if 0 <= step - 2 < GROUPS:
            if step == 2:
                local.wait()
            last_hop(step - 2)
    for copy in film_copies + more_copies + list(c_copies.values()):
        copy.wait()
    for copy in obs_copies + [c for row in z_copies for c in row]:
        copy.wait_send()
    for copies in (x_copies, y_copies, f_copies):
        for copy in copies.values():
            copy.wait_send()


def gather(params, obs):
    vmem = pl.BlockSpec(memory_space=pltpu.VMEM)
    pair = lambda n: [pltpu.SemaphoreType.DMA((n,))] * 2
    n = 3 * GROUPS
    return pl.pallas_call(
        gather_kernel,
        out_shape=(
            jax.ShapeDtypeStruct((NB // 4, 4, 4, 2, ROWS, 256), bf16),
            jax.ShapeDtypeStruct((4, 8, 8, 128), f32),
            jax.ShapeDtypeStruct((4, 8, 16, 256), bf16),
            jax.ShapeDtypeStruct((4 * ROWS, OBS), bf16),
        ),
        in_specs=[vmem] * 3,
        out_specs=(vmem,) * 4,
        scratch_shapes=[
            pltpu.VMEM((NB // 4, 4, ROWS, 256), bf16),
            pltpu.VMEM((8, 8, 128), f32),
            pltpu.VMEM((8, 8, 128), f32),
            *pair(7), *pair(7), *pair(3), *pair(3),
            *pair(n), *pair(n), *pair(n), *pair(n), *pair(GROUPS),
            pltpu.SemaphoreType.DMA,
        ],
        compiler_params=pltpu.CompilerParams(collective_id=0, has_side_effects=True, vmem_limit_bytes=56 << 20),
        name="gather",
    )(params, jnp.asarray(first_order(), bf16), obs)


def scatter_kernel(
    grad_ref, film_grad_ref, obs_all_ref, film_ref,
    out_ref, film_out_ref, back_ref, square_ref,
    half_ref, core_ref, x_ref, y_ref, u_ref, v_ref, z_ref, film_all, back_part, back_line, line_squares,
    g_sems, g_sems2, h_sems, h_sems2, b_sems, b_sems2,
    c_sems, c_sems2, x_sems, x_sems2, y_sems, y_sems2, u_sems, u_sems2, v_sems, v_sems2,
    z_sems, z_sems2, r_sems, r_sems2, n_sems, n_sems2, m_sems, m_sems2,
):
    me = Place()
    x, y, z, c = me.x, me.y, me.z, me.c
    group = lambda g: pl.ds(g * EACH, EACH)
    meet(me)
    c_copies = [
        send(grad_ref.at[group(g), :, :, 1 - c], core_ref.at[group(g)], (c_sems, c_sems2), g, me.line(1))
        for g in range(GROUPS)
    ]
    film_all[me.p, me.w] = film_grad_ref[me.w]
    g_copies = [
        send(film_grad_ref.at[flipped(me.w, l)], film_all.at[me.p, me.w], (g_sems, g_sems2), l - 1, me.line(l))
        for l in range(1, 8)
    ]
    x_copies, y_copies, u_copies, v_copies, z_copies, r_copies = {}, {}, {}, {}, {}, {}
    low_z, high_z = pl.ds(0, 2), pl.ds(2, 2)

    def core_sum(g):
        c_copies[g].wait_recv()

        def add(i, _):
            j, q = g * EACH + i // 4, i % 4
            total = grad_ref[j, q, :, c].astype(f32) + core_ref[j, q].astype(f32)
            half_ref[j, q // 2, q % 2] = total.astype(bf16)
            return 0

        lax.fori_loop(0, EACH * 4, add, 0)
        x_copies[g] = send(
            half_ref.at[group(g), :, 1 - x, low_z], x_ref.at[group(g)], (x_sems, x_sems2), g, me.plane(1)
        )
        y_copies[g] = send(
            half_ref.at[group(g), 1 - y, :, high_z], y_ref.at[group(g)], (y_sems, y_sems2), g, me.plane(2)
        )

    def first_sum(g):
        x_copies[g].wait_recv()

        def add_x(i, _):
            j, q = g * EACH + i // 2, i % 2
            total = half_ref[j, q, x, low_z].astype(f32) + x_ref[j, q].astype(f32)
            half_ref[j, q, x, low_z] = total.astype(bf16)
            return 0

        lax.fori_loop(0, EACH * 2, add_x, 0)
        y_copies[g].wait_recv()

        def add_y(i, _):
            j, q = g * EACH + i // 2, i % 2
            total = half_ref[j, y, q, high_z].astype(f32) + y_ref[j, q].astype(f32)
            half_ref[j, y, q, high_z] = total.astype(bf16)
            return 0

        lax.fori_loop(0, EACH * 2, add_y, 0)
        x_copies[g].wait_send()
        y_copies[g].wait_send()
        u_copies[g] = send(
            half_ref.at[group(g), 1 - y, x, low_z], u_ref.at[group(g)], (u_sems, u_sems2), g, me.plane(2)
        )
        v_copies[g] = send(
            half_ref.at[group(g), y, 1 - x, high_z], v_ref.at[group(g)], (v_sems, v_sems2), g, me.plane(1)
        )

    def second_sum(g):
        u_copies[g].wait_recv()
        v_copies[g].wait_recv()
        for j in range(g * EACH, (g + 1) * EACH):
            total = half_ref[j, y, x, low_z].astype(f32) + u_ref[j].astype(f32)
            half_ref[j, y, x, low_z] = total.astype(bf16)
            total = half_ref[j, y, x, high_z].astype(f32) + v_ref[j].astype(f32)
            half_ref[j, y, x, high_z] = total.astype(bf16)
        for k in range(1, 4):
            z_copies[g, k] = send(
                half_ref.at[group(g), y, x, flipped(z, k)], z_ref.at[k - 1, group(g)],
                (z_sems, z_sems2), g * 3 + k - 1, me.line(2 * k),
            )

    squares = []

    def last_sum(g):
        for k in range(1, 4):
            z_copies[g, k].wait_recv()
        for j in range(g * EACH, (g + 1) * EACH):
            total = half_ref[j, y, x, z].astype(f32)
            for k in range(3):
                total = total + z_ref[k, j].astype(f32)
            total = total.astype(bf16)
            out_ref[j, me.p] = total
            squares.append(jnp.sum(jnp.square(total.astype(f32)).reshape(4, 8, 256), axis=0))
        piece = out_ref.at[group(g), me.p]
        for k in range(1, 4):
            r_copies[g, k] = send(piece, piece, (r_sems, r_sems2), g * 3 + k - 1, me.plane(k))

    h_copies, b_copies = [], []

    def film_line():
        for copy in g_copies:
            copy.wait()
        piece = film_all.at[me.p]
        for k in range(1, 4):
            h_copies.append(send(piece, piece, (h_sems, h_sems2), k - 1, me.plane(k)))

    def film_plane():
        for copy in h_copies:
            copy.wait()
        copies = [film_all[k].reshape(128, 128) for k in range(4)]
        row, col = iota((128, 512), 0), iota((128, 512), 1)
        same = ((row >> 4) == ((col >> 4) & 7)) & (((row >> 2) & 3) == (col >> 7)) & ((row & 3) == (col & 3))
        seen_all = obs_all_ref[...].reshape(512, 256)
        for q in range(4):
            pick = one_hot(same & (((col >> 2) & 3) == q))
            cond = mish_parts(dot_nn(pick, seen_all))[0].astype(bf16)
            total = sum(dot_tn(piece, cond) for piece in copies)
            film_out_ref[:, q * 256 : (q + 1) * 256] = total
        row, col = iota((128, 128), 0), iota((128, 128), 1)
        mine = one_hot(((row >> 4) == (col >> 4)) & ((col & 15) == 4 * me.p + (row & 3)))
        rows = [dot_nn(mine, piece).astype(bf16) for piece in copies]
        parts = [sum(dot_nn(r, film_ref[:, q * 256 : (q + 1) * 256]) for r in rows) for q in range(4)]
        back_part[...] = quarter_rows(parts).astype(bf16).reshape(8, 16, 256)
        for l in range(1, 8):
            b_copies.append(
                send(back_part.at[flipped(me.w, l)], back_line.at[me.w], (b_sems, b_sems2), l - 1, me.line(l))
            )
        back_line[me.w] = back_part[me.w]

    def film_back():
        for copy in b_copies:
            copy.wait()
        total = jnp.sum(back_line[...].astype(f32), axis=0)
        slope = mish_parts(obs_all_ref[me.p, me.w].astype(f32))[1]
        back_ref[0] = unfold_rows(total * slope)

    for step in range(GROUPS + 3):
        if step < GROUPS:
            core_sum(step)
        if step == 0:
            film_line()
        if 0 <= step - 1 < GROUPS:
            first_sum(step - 1)
        if step == 1:
            film_plane()
        if 0 <= step - 2 < GROUPS:
            second_sum(step - 2)
        if step == 2:
            film_back()
        if 0 <= step - 3 < GROUPS:
            last_sum(step - 3)

    film_square = jnp.zeros((8, 256), f32)
    for q in range(4):
        part = jnp.square(film_out_ref[:, q * 256 : (q + 1) * 256])
        film_square = film_square + jnp.sum(part.reshape(16, 8, 256), axis=0)
    total = sum(squares) + 0.25 * film_square
    line_squares[me.p, me.w] = total[:, :128] + total[:, 128:]
    m_copies = [
        send(line_squares.at[me.p, me.w], line_squares.at[me.p, me.w], (m_sems, m_sems2), l - 1, me.line(l))
        for l in range(1, 8)
    ]
    for copy in m_copies:
        copy.wait()
    n_copies = [
        send(line_squares.at[me.p], line_squares.at[me.p], (n_sems, n_sems2), k - 1, me.plane(k)) for k in range(1, 4)
    ]
    for copy in n_copies + list(r_copies.values()):
        copy.wait()
    square_ref[...] = jnp.sum(line_squares[...].reshape(32, 8, 128), axis=0)
    for copies in (u_copies, v_copies, z_copies):
        for copy in copies.values():
            copy.wait_send()
    for copy in c_copies:
        copy.wait_send()


def scatter(grads, film_grad, obs_all, film_own):
    vmem = pl.BlockSpec(memory_space=pltpu.VMEM)
    pair = lambda n: [pltpu.SemaphoreType.DMA((n,))] * 2
    n = NB // 4
    return pl.pallas_call(
        scatter_kernel,
        out_shape=(
            jax.ShapeDtypeStruct((n, 4, ROWS, 256), bf16),
            jax.ShapeDtypeStruct((4 * ROWS, OBS), f32),
            jax.ShapeDtypeStruct((1, 4, OBS), f32),
            jax.ShapeDtypeStruct((8, 128), f32),
        ),
        in_specs=[vmem] * 4,
        out_specs=(vmem,) * 4,
        scratch_shapes=[
            pltpu.VMEM((n, 2, 2, 4, ROWS, 256), bf16),
            pltpu.VMEM((n, 4, 4, ROWS, 256), bf16),
            pltpu.VMEM((n, 2, 2, ROWS, 256), bf16),
            pltpu.VMEM((n, 2, 2, ROWS, 256), bf16),
            pltpu.VMEM((n, 2, ROWS, 256), bf16),
            pltpu.VMEM((n, 2, ROWS, 256), bf16),
            pltpu.VMEM((3, n, ROWS, 256), bf16),
            pltpu.VMEM((4, 8, 16, 128), bf16),
            pltpu.VMEM((8, 16, 256), bf16),
            pltpu.VMEM((8, 16, 256), bf16),
            pltpu.VMEM((4, 8, 8, 128), f32),
            *pair(7), *pair(3), *pair(7),
            *pair(GROUPS), *pair(GROUPS), *pair(GROUPS), *pair(GROUPS), *pair(GROUPS),
            *pair(3 * GROUPS), *pair(3 * GROUPS), *pair(3), *pair(7),
        ],
        compiler_params=pltpu.CompilerParams(collective_id=1, has_side_effects=True, vmem_limit_bytes=56 << 20),
        name="scatter",
    )(grads, film_grad, obs_all, film_own)


def local_fast(noisy, action_mask, time_index, obs_embed, obs_slot, cotangent, params, first_moment, second_moment):
    weights, seen_film, obs_all, film_own = gather(params, obs_embed)
    act, noisy_grad, grads, film_grad = train(
        weights.reshape(NB, C, 256), seen_film.reshape(4, 8, 8, 128), obs_slot[None], noisy[0], action_mask, time_index, cotangent[0]
    )
    total, film_total, back, squares = scatter(
        grads.reshape(NB // 4, 4, 4, 2, ROWS, 256), film_grad, obs_all, film_own
    )
    norm, *new = adam(
        total.reshape(NB, ROWS, 256), film_total, squares, params, first_moment, second_moment
    )
    return (act[None], noisy_grad[None], back, norm.reshape(()), *new)


def solution(mesh):
    in_specs = (
        P("pair", None, "wide"),
        P(None, "wide"),
        P("pair", "wide"),
        P("pair", "wide", None),
        P("wide"),
        P("pair", None, "wide"),
        P("wide", None),
        P("wide", None),
        P("wide", None),
    )
    out_specs = (
        P("pair", None, "wide"),
        P("pair", None, "wide"),
        P("pair", "wide", None),
        P(),
        P("wide", None),
        P("wide", None),
        P("wide", None),
        P("wide", None),
    )
    fast = mesh.shape["pair"] == 4 and mesh.shape["wide"] == 8
    return jax.shard_map(local_fast if fast else local_plain, mesh=mesh, in_specs=in_specs, out_specs=out_specs, check_vma=False)
```

```python
import math

import jax
import jax.numpy as jnp
import numpy as np
from jax import lax
from jax.experimental import pallas as pl
from jax.experimental.pallas import tpu as pltpu
from jax.sharding import PartitionSpec as P

C = 256
OBS = 1024
TE = 128
TH = 512
ADIM = 10
FR = 16
LEVELS = 40
ADAM_STEP = 7
Q = 12627
SAM = 16
ROWS = 32
NB = 36

sigma_top = 80.0 ** (1.0 / 7.0)
sigma_low = 0.002 ** (1.0 / 7.0)
clip_limit = 1.0
learn_rate = 0.02
decay_first = 0.5
decay_second = 0.5
adam_eps = 1e-08
weight_decay = 0.01
norm_eps = 1e-05

f32 = jnp.float32
bf16 = jnp.bfloat16

AT_DOWN_RES = 1330
AT_TAIL = 12604
TAIL = 23
AT_FILM = (1340, 2492, 9788, 10940)
AT_TIME = (12092, 12348)
AT_UP_RES = 9276
B_MISC, B_INNER, B_OUTER, B_FILM = 0, 1, 2, 3
B_DS, B_POOL, B_SPREAD, B_UF, B_US, B_UR = 5, 10, 13, 18, 28, 33
B_NONE = (17, 35)
LANE_TAIL = 64
CONVS = (
    (50, 5, 2, lambda t, h: B_DS + t),
    (5436, 5, 4, lambda t, h: B_UF + 2 * t + h // 2),
    (7996, 5, 2, lambda t, h: B_US + t),
    (3644, 3, 2, lambda t, h: B_POOL + t),
    (4412, 4, 2, lambda t, h: B_SPREAD + t),
)
(T_BIAS_A, T_BIAS_B, T_OUT, D_B1, D_G1, D_S1, D_FS, D_FO, D_B2, D_G2, D_S2, D_RB, PB, SB,
 U_B1, U_G1, U_S1, U_FS, U_FO, U_B2, U_G2, U_S2, U_RB) = range(TAIL)


def dot_nt(a, b):
    return lax.dot_general(a, b, (((1,), (1,)), ((), ())), preferred_element_type=f32)


def dot_nn(a, b):
    return lax.dot_general(a, b, (((1,), (0,)), ((), ())), preferred_element_type=f32)


def dot_tn(a, b):
    return lax.dot_general(a, b, (((0,), (0,)), ((), ())), preferred_element_type=f32)


def split2(v):
    high = v.astype(bf16)
    return high, (v - high.astype(f32)).astype(bf16)


def split3(v):
    high, rest = v.astype(bf16), None
    rest = v - high.astype(f32)
    mid = rest.astype(bf16)
    return high, mid, (rest - mid.astype(f32)).astype(bf16)


def iota(shape, dim):
    return lax.broadcasted_iota(jnp.int32, shape, dim)


def one_hot(condition):
    return jnp.where(condition, 1.0, 0.0).astype(bf16)


def tap_order(taps):
    n = 128 * taps
    row = lax.broadcasted_iota(jnp.int32, (n, n), 0)
    col = lax.broadcasted_iota(jnp.int32, (1, n), 1)
    source = (col & 127) * taps + (col >> 7)
    return jnp.where(row == source, 1.0, 0.0).astype(bf16)


def first_order():
    table = np.zeros((128, 128), np.float32)
    for i in range(ADIM):
        for t in range(5):
            table[i * 5 + t, t * ADIM + i] = 1.0
    return table


def level_table():
    levels = np.arange(LEVELS, dtype=np.float64)
    tau = 250.0 * 7.0 * np.log(sigma_top + levels / (LEVELS - 1) * (sigma_low - sigma_top))
    freq = np.exp(-math.log(10000.0) * np.arange(TE // 2) / (TE // 2 - 1))
    angles = tau[:, None] * freq[None, :]
    table = np.zeros((64, TE), np.float32)
    table[:LEVELS] = np.concatenate([np.sin(angles), np.cos(angles)], axis=1)
    return table


def pack_kernel(params_ref, order_ref, own_ref, film_ref):
    pack_rows(params_ref, order_ref, own_ref, film_ref)


class Blocks:
    def __init__(self, ref):
        self.ref = ref

    def _at(self, key):
        block, rest = (key[0], key[1:]) if isinstance(key, tuple) else (key, ())
        return (block // 4, block % 4) + rest

    def __getitem__(self, key):
        return self.ref[self._at(key)]

    def __setitem__(self, key, value):
        self.ref[self._at(key)] = value


def pack_rows(params_ref, order_ref, own_ref, film_ref):
    own_ref = Blocks(own_ref)

    def low(start, width):
        return params_ref[:, start : start + width].astype(bf16)

    first = dot_nn(low(0, 128), order_ref[...])
    pieces = [
        first[:, :50],
        params_ref[:, AT_DOWN_RES : AT_DOWN_RES + ADIM],
        jnp.zeros((ROWS, LANE_TAIL - 60), f32),
        params_ref[:, AT_TAIL : AT_TAIL + TAIL],
        jnp.zeros((ROWS, 256 - LANE_TAIL - TAIL), f32),
    ]
    own_ref[B_MISC] = jnp.concatenate(pieces, axis=1).astype(bf16)
    own_ref[B_INNER] = low(AT_TIME[0], 256)
    own_ref[B_OUTER] = low(AT_TIME[1], 256)
    for q in range(4):
        film_ref[q * ROWS : (q + 1) * ROWS] = low(AT_FILM[q], OBS)
        own_ref[B_FILM + q // 2, :, (q % 2) * 128 : (q % 2) * 128 + 128] = low(AT_FILM[q] + OBS, TE)
    own_ref[B_UR] = low(AT_UP_RES, 256)
    own_ref[B_UR + 1] = low(AT_UP_RES + 256, 256)
    for b in B_NONE:
        own_ref[b] = jnp.zeros((ROWS, 256), bf16)
    for taps in (5, 3, 4):
        places = [(at, h, block) for at, k, groups, block in CONVS if k == taps for h in range(groups)]
        stacked = jnp.concatenate([low(at + h * 128 * taps, 128 * taps) for at, h, _ in places], axis=0)
        moved = dot_nn(stacked, tap_order(taps)).astype(bf16)
        for n, (_, h, block) in enumerate(places):
            for t in range(taps):
                own_ref[block(t, h), :, (h % 2) * 128 : (h % 2) * 128 + 128] = moved[
                    n * ROWS : (n + 1) * ROWS, t * 128 : (t + 1) * 128
                ]


def pack(params):
    vmem = pl.BlockSpec(memory_space=pltpu.VMEM)
    return pl.pallas_call(
        pack_kernel,
        out_shape=(
            jax.ShapeDtypeStruct((NB // 4, 4, ROWS, 256), bf16),
            jax.ShapeDtypeStruct((4 * ROWS, OBS), bf16),
        ),
        in_specs=[vmem, vmem],
        out_specs=(vmem, vmem),
        compiler_params=pltpu.CompilerParams(vmem_limit_bytes=40 << 20),
        name="pack",
    )(params, jnp.asarray(first_order(), bf16))


def mish_parts(v):
    e = jnp.exp(jnp.minimum(v, 20.0))
    n = e * (e + 2.0)
    r = 1.0 / (n + 2.0)
    t = n * r
    return v * t, t + 4.0 * v * (e * r) * ((e + 1.0) * r)


def step_frames(v, step):
    if step == 0:
        return v
    zeros = jnp.zeros((SAM * abs(step), v.shape[1]), v.dtype)
    if step > 0:
        return jnp.concatenate([v[SAM * step :], zeros], axis=0)
    return jnp.concatenate([zeros, v[: SAM * step]], axis=0)


def over_frames(v):
    return jnp.sum(v.reshape(-1, SAM, v.shape[1]), axis=0)


def each_frame(v, s):
    return v.reshape(-1, SAM, v.shape[1]), s[None]


def group_means(values, ones):
    parts = [p for v in values for p in split3(v)]
    sums = dot_nn(jnp.concatenate(parts, axis=0), ones)
    out = []
    for i in range(len(values)):
        a, b, c = (sums[(3 * i + k) * SAM : (3 * i + k + 1) * SAM] for k in range(3))
        out.append((a + (b + c)) * (1.0 / (32 * FR)))
    return out


def minus(v, s):
    a, b = each_frame(v, s)
    return (a - b).reshape(v.shape)


def times(v, s):
    a, b = each_frame(v, s)
    return (a * b).reshape(v.shape)


def plus(v, s):
    a, b = each_frame(v, s)
    return (a + b).reshape(v.shape)


def norm_forward(before, gain, shift, ones):
    (center,) = group_means([over_frames(before)], ones)
    away = minus(before, center)
    (spread,) = group_means([over_frames(away * away)], ones)
    scale = lax.rsqrt(spread + norm_eps)
    normal = times(away, scale)
    act, slope = mish_parts(normal * gain + shift)
    return act, normal, slope, scale


def norm_backward(grad_act, normal, slope, scale, gain, ones):
    grad_out = grad_act * slope
    shift_rows = over_frames(grad_out)
    gain_rows = over_frames(grad_out * normal)
    mean_grad, mean_both = group_means([shift_rows * gain, gain_rows * gain], ones)
    inner = minus(grad_out * gain, mean_grad) - times(normal, mean_both)
    return (
        times(inner, scale),
        jnp.sum(gain_rows, axis=0, keepdims=True),
        jnp.sum(shift_rows, axis=0, keepdims=True),
    )


def conv_forward(source, weight):
    total = dot_nt(step_frames(source, -2), weight(0))
    for t in range(1, 5):
        total = total + dot_nt(step_frames(source, t - 2), weight(t))
    return total


def conv_source(grad_low, weight):
    total = dot_nn(step_frames(grad_low, 2), weight(0))
    for t in range(1, 5):
        total = total + dot_nn(step_frames(grad_low, 2 - t), weight(t))
    return total


def row_sum(v):
    return jnp.sum(over_frames(v), axis=0, keepdims=True)


def halves(v):
    cube = v.reshape(FR // 2, 2, SAM, v.shape[1])
    return cube[:, 0].reshape(-1, v.shape[1]), cube[:, 1].reshape(-1, v.shape[1])


def interleave(even, odd):
    width = even.shape[1]
    pair = [v.reshape(FR // 2, 1, SAM, width) for v in (even, odd)]
    return jnp.concatenate(pair, axis=1).reshape(FR * SAM, width)


def train_kernel(*refs):
    train_body(*refs, lambda point: None)


def train_body(
    w_ref, seen_ref, slot_ref, noisy_ref, mask_ref, level_ref, cot_ref, table_ref,
    act_ref, noisy_grad_ref, grad_ref, film_grad_ref, reach,
):
    row = iota((256, 256), 0)
    col = iota((256, 256), 1)
    ones = jnp.where((row >> 5) == (col >> 5), 1.0, 0.0).astype(bf16)
    swap = jnp.where(col == ((row & 15) << 4) + (row >> 4), 1.0, 0.0).astype(bf16)
    for b in B_NONE:
        grad_ref[b] = jnp.zeros((256, 256), bf16)
    spread_mask = one_hot((iota((SAM, 256), 1) >> 4) == iota((SAM, 256), 0))
    keep = dot_nn(mask_ref[...].astype(f32).astype(bf16), spread_mask)
    start_cols = noisy_ref[...].astype(f32) * keep
    start_cols = jnp.concatenate([start_cols, jnp.zeros((6, 256), f32)], axis=0).astype(bf16)
    start = dot_nt(swap, start_cols).astype(bf16)
    lane16 = iota((16, 128), 1)
    row16 = iota((16, 128), 0)
    inputs = jnp.zeros((256, 128), f32)
    for t in range(5):
        place = lane16 == row16 + t * ADIM
        if t == 2:
            place = place | (lane16 == row16 + 50)
        inputs = inputs + dot_nn(step_frames(start, t - 2), one_hot(place & (row16 < ADIM)))
    inputs = inputs.astype(bf16)
    cot_high, cot_low = split2(cot_ref[...])
    upstream = dot_nt(swap, cot_high) + dot_nt(swap, cot_low)
    upstream_low = upstream.astype(bf16)
    at_level = one_hot(iota((64, SAM), 0) == level_ref[...])
    feats = dot_tn(at_level, table_ref[...]).astype(bf16)
    reach(0)
    misc = w_ref[B_MISC, :, :128]
    lane = iota((256, 128), 1)
    misc_first = jnp.where(lane < 50, misc, jnp.zeros_like(misc))
    misc_res = jnp.where((lane >= 50) & (lane < 60), misc, jnp.zeros_like(misc))
    singles = misc.astype(f32).T[LANE_TAIL : LANE_TAIL + 32]
    vec = lambda k: singles[k : k + 1]

    inner = [w_ref[B_INNER, :, j * 128 : (j + 1) * 128] for j in range(2)]
    outer = [w_ref[B_OUTER, :, j * 128 : (j + 1) * 128] for j in range(2)]
    film_time = lambda q: w_ref[B_FILM + q // 2, :, (q % 2) * 128 : (q % 2) * 128 + 128]
    hidden = [mish_parts(dot_nt(feats, inner[j]) + vec(T_BIAS_A + j)) for j in range(2)]
    hidden_low = [h[0].astype(bf16) for h in hidden]
    embed = dot_nn(hidden_low[0], outer[0]) + dot_nn(hidden_low[1], outer[1]) + vec(T_OUT)[:, :TE]
    cond, cond_slope = mish_parts(embed)
    cond_low = cond.astype(bf16)
    pre = dot_nt(inputs, misc_first) + vec(D_B1)
    act_one, normal_one, slope_one, scale_one = norm_forward(pre, vec(D_G1), vec(D_S1), ones)
    reach(1)
    at_slot = one_hot(iota((SAM, SAM), 0) == slot_ref[...])
    line = iota((32, SAM), 0)
    seen_film = jnp.concatenate([seen_ref[:, k].reshape(32, 128) for k in range(4)], axis=1)
    seen_film = split3(seen_film)
    sides = []
    for side in range(2):
        at_line = one_hot(((line >> 3) * 4 + (line & 3) == slot_ref[...]) & ((line >> 2) & 1 == side))
        sides.append(sum(dot_tn(at_line, part) for part in seen_film))
    seen_film = jnp.concatenate(
        [sides[k % 2][:, (k // 2) * 128 : (k // 2) * 128 + 128] for k in range(8)], axis=1
    )
    spans = lambda v, q: jnp.concatenate([v[:, k * 128 + q * 32 : k * 128 + q * 32 + 32] for k in range(8)], axis=1)
    film_of = lambda q: spans(seen_film, q) + dot_nt(cond_low, film_time(q)) + vec((D_FS, D_FO, U_FS, U_FO)[q])
    film = [film_of(0), film_of(1)]
    mid_one = plus(times(act_one, film[0]), film[1]).astype(bf16)
    reach(2)
    down = lambda t: w_ref[B_DS + t]
    pre = conv_forward(mid_one, down) + vec(D_B2)
    act, normal_two, slope_two, scale_two = norm_forward(pre, vec(D_G2), vec(D_S2), ones)
    skip = (act + dot_nt(inputs, misc_res) + vec(D_RB)).astype(bf16)
    reach(3)
    even, odd = halves(skip)
    odd_prev = step_frames(odd, -1)
    pool_sources = (odd_prev, even, odd)
    pooled = sum(dot_nt(s, w_ref[B_POOL + t]) for t, s in enumerate(pool_sources)) + vec(PB)
    pooled = pooled.astype(bf16)
    reach(4)
    pooled_prev = step_frames(pooled, -1)
    pooled_next = step_frames(pooled, 1)
    even_out = dot_nt(pooled, w_ref[B_SPREAD + 1]) + dot_nt(pooled_prev, w_ref[B_SPREAD + 3])
    odd_out = dot_nt(pooled_next, w_ref[B_SPREAD]) + dot_nt(pooled, w_ref[B_SPREAD + 2])
    wide = (interleave(even_out, odd_out) + vec(SB)).astype(bf16)
    joined = (wide, skip)
    reach(5)
    up_first = [lambda t, h=h: w_ref[B_UF + 2 * t + h] for h in range(2)]
    pre = conv_forward(wide, up_first[0]) + conv_forward(skip, up_first[1]) + vec(U_B1)
    act_three, normal_three, slope_three, scale_three = norm_forward(pre, vec(U_G1), vec(U_S1), ones)
    film += [film_of(2), film_of(3)]
    mid_three = plus(times(act_three, film[2]), film[3]).astype(bf16)
    reach(6)
    up = lambda t: w_ref[B_US + t]
    pre = conv_forward(mid_three, up) + vec(U_B2)
    act, normal_four, slope_four, scale_four = norm_forward(pre, vec(U_G2), vec(U_S2), ones)
    result = act + dot_nt(wide, w_ref[B_UR]) + dot_nt(skip, w_ref[B_UR + 1]) + vec(U_RB)
    act_ref[...] = dot_tn(result.astype(bf16), swap).astype(bf16)

    single_grads = {}

    def conv_weights(grad_low, source, block):
        turned = grad_low.T
        for t in range(5):
            grad_ref[block(t)] = dot_nn(turned, step_frames(source, t - 2)).astype(bf16)

    reach(7)
    grad, single_grads[U_G2], single_grads[U_S2] = norm_backward(
        upstream, normal_four, slope_four, scale_four, vec(U_G2), ones
    )
    single_grads[U_B2] = row_sum(grad)
    low = grad.astype(bf16)
    conv_weights(low, mid_three, lambda t: B_US + t)
    turned = upstream_low.T
    for h in range(2):
        grad_ref[B_UR + h] = dot_nn(turned, joined[h]).astype(bf16)
    reach(8)
    grad_mid = conv_source(low, up)
    shift_three = over_frames(grad_mid)
    gain_three = over_frames(grad_mid * act_three)
    grad, single_grads[U_G1], single_grads[U_S1] = norm_backward(
        times(grad_mid, film[2]), normal_three, slope_three, scale_three, vec(U_G1), ones
    )
    single_grads[U_B1] = row_sum(grad)
    low = grad.astype(bf16)
    for h in range(2):
        conv_weights(low, joined[h], lambda t, h=h: B_UF + 2 * t + h)
    single_grads[U_RB] = row_sum(upstream)
    reach(9)
    grad_wide = conv_source(low, up_first[0]) + dot_nn(upstream_low, w_ref[B_UR])
    grad_skip = conv_source(low, up_first[1]) + dot_nn(upstream_low, w_ref[B_UR + 1])
    single_grads[SB] = row_sum(grad_wide)
    low_even, low_odd = halves(grad_wide.astype(bf16))
    turned_even, turned_odd = low_even.T, low_odd.T
    grad_ref[B_SPREAD] = dot_nn(turned_odd, pooled_next).astype(bf16)
    grad_ref[B_SPREAD + 1] = dot_nn(turned_even, pooled).astype(bf16)
    grad_ref[B_SPREAD + 2] = dot_nn(turned_odd, pooled).astype(bf16)
    grad_ref[B_SPREAD + 3] = dot_nn(turned_even, pooled_prev).astype(bf16)
    reach(10)
    grad_pooled = dot_nn(low_even, w_ref[B_SPREAD + 1]) + dot_nn(low_odd, w_ref[B_SPREAD + 2])
    grad_pooled = grad_pooled + dot_nn(step_frames(low_even, 1), w_ref[B_SPREAD + 3])
    grad_pooled = grad_pooled + dot_nn(step_frames(low_odd, -1), w_ref[B_SPREAD])
    single_grads[PB] = row_sum(grad_pooled)
    low = grad_pooled.astype(bf16)
    turned = low.T
    for t in range(3):
        grad_ref[B_POOL + t] = dot_nn(turned, pool_sources[t]).astype(bf16)
    reach(11)
    grad_even = dot_nn(low, w_ref[B_POOL + 1])
    grad_odd = dot_nn(low, w_ref[B_POOL + 2]) + dot_nn(step_frames(low, 1), w_ref[B_POOL])
    grad_skip = grad_skip + interleave(grad_even, grad_odd)
    single_grads[D_RB] = row_sum(grad_skip)
    skip_low = grad_skip.astype(bf16)
    misc_grad = jnp.where(lane < 50, 0.0, dot_nn(skip_low.T, inputs))
    back = dot_nn(skip_low, misc_res)
    grad, single_grads[D_G2], single_grads[D_S2] = norm_backward(
        grad_skip, normal_two, slope_two, scale_two, vec(D_G2), ones
    )
    single_grads[D_B2] = row_sum(grad)
    low = grad.astype(bf16)
    conv_weights(low, mid_one, lambda t: B_DS + t)
    reach(12)
    grad_mid = conv_source(low, down)
    shift_one = over_frames(grad_mid)
    gain_one = over_frames(grad_mid * act_one)
    grad, single_grads[D_G1], single_grads[D_S1] = norm_backward(
        times(grad_mid, film[0]), normal_one, slope_one, scale_one, vec(D_G1), ones
    )
    single_grads[D_B1] = row_sum(grad)
    low = grad.astype(bf16)
    misc_grad = misc_grad + jnp.where(lane < 50, dot_nn(low.T, inputs), 0.0)
    film_grads = (gain_one, shift_one, gain_three, shift_three)
    film_low = [g.astype(bf16) for g in film_grads]
    back_cond = None
    for q in range(4):
        single_grads[(D_FS, D_FO, U_FS, U_FO)[q]] = jnp.sum(film_grads[q], axis=0, keepdims=True)
        grad_ref[B_FILM + q // 2, :, (q % 2) * 128 : (q % 2) * 128 + 128] = dot_tn(film_low[q], cond_low).astype(bf16)
        part = dot_nn(film_low[q], film_time(q))
        back_cond = part if back_cond is None else back_cond + part
    at_slots = [dot_nn(at_slot, v) for v in film_low]
    for k in range(8):
        film_grad_ref[k] = jnp.concatenate([v[:, k * 32 : (k + 1) * 32] for v in at_slots], axis=1).astype(bf16)
    reach(13)
    back = back + dot_nn(low, misc_first)
    grad_start = back[:, 50:60]
    for t in range(5):
        grad_start = grad_start + step_frames(back[:, t * ADIM : (t + 1) * ADIM], 2 - t)
    grad_cols = sum(dot_tn(part, swap) for part in split3(jnp.concatenate([grad_start, jnp.zeros((256, 6), f32)], axis=1)))
    noisy_grad_ref[...] = grad_cols[:ADIM] * keep

    grad_embed = back_cond * cond_slope
    single_grads[T_OUT] = jnp.concatenate(
        [jnp.sum(grad_embed, axis=0, keepdims=True), jnp.zeros((1, C - TE), f32)], axis=1
    )
    embed_low = grad_embed.astype(bf16)
    for j in range(2):
        grad_ref[B_OUTER, :, j * 128 : (j + 1) * 128] = dot_tn(hidden_low[j], embed_low).astype(bf16)
        grad_hidden = dot_nt(embed_low, outer[j]) * hidden[j][1]
        single_grads[T_BIAS_A + j] = jnp.sum(grad_hidden, axis=0, keepdims=True)
        grad_ref[B_INNER, :, j * 128 : (j + 1) * 128] = dot_tn(grad_hidden.astype(bf16), feats).astype(bf16)
    stack = [jnp.zeros((LANE_TAIL, 256), f32)] + [single_grads[k] for k in range(TAIL)]
    stack = jnp.concatenate(stack + [jnp.zeros((128 - LANE_TAIL - TAIL, 256), f32)], axis=0)
    grad_ref[B_MISC, :, :128] = (misc_grad + stack.T).astype(bf16)
    grad_ref[B_MISC, :, 128:] = jnp.zeros((256, 128), bf16)


def train(weights, seen_film, slots, noisy, mask, levels, cotangent):
    vmem = pl.BlockSpec(memory_space=pltpu.VMEM)
    return pl.pallas_call(
        train_kernel,
        out_shape=(
            jax.ShapeDtypeStruct((C, 256), bf16),
            jax.ShapeDtypeStruct((ADIM, 256), f32),
            jax.ShapeDtypeStruct((NB, 256, 256), bf16),
            jax.ShapeDtypeStruct((8, SAM, 128), bf16),
        ),
        in_specs=[vmem] * 8,
        out_specs=(vmem,) * 4,
        compiler_params=pltpu.CompilerParams(vmem_limit_bytes=48 << 20),
        name="train",
    )(weights, seen_film, slots, noisy, mask, levels, cotangent, jnp.asarray(level_table(), bf16))


def adam_kernel(
    own_ref, film_ref, square_ref, params_ref, first_ref, second_ref, order_ref,
    norm_ref, new_params_ref, new_first_ref, new_second_ref, copy_ref, grad_ref,
):
    norm = jnp.sqrt(jnp.sum(square_ref[...], axis=(0, 1), keepdims=True))
    norm_ref[...] = norm
    factor = jnp.minimum(1.0, clip_limit / (norm + 1e-06))
    misc = own_ref[B_MISC]
    first = dot_nt(misc[:, :128], order_ref[...])
    misc = misc.astype(f32)
    grad_ref[:, 0:50] = first[:, :50]
    grad_ref[:, AT_DOWN_RES : AT_DOWN_RES + ADIM] = misc[:, 50:60]
    grad_ref[:, AT_TAIL : AT_TAIL + TAIL] = misc[:, LANE_TAIL : LANE_TAIL + TAIL]
    grad_ref[:, AT_TIME[0] : AT_TIME[0] + 256] = own_ref[B_INNER].astype(f32)
    grad_ref[:, AT_TIME[1] : AT_TIME[1] + 256] = own_ref[B_OUTER].astype(f32)
    for q in range(4):
        grad_ref[:, AT_FILM[q] : AT_FILM[q] + OBS] = film_ref[q * ROWS : (q + 1) * ROWS]
        part = own_ref[B_FILM + q // 2, :, (q % 2) * 128 : (q % 2) * 128 + 128]
        grad_ref[:, AT_FILM[q] + OBS : AT_FILM[q] + OBS + TE] = part.astype(f32)
    grad_ref[:, AT_UP_RES : AT_UP_RES + 256] = own_ref[B_UR].astype(f32)
    grad_ref[:, AT_UP_RES + 256 : AT_UP_RES + 512] = own_ref[B_UR + 1].astype(f32)
    for taps in (5, 3, 4):
        places = [(at, h, block) for at, k, groups, block in CONVS if k == taps for h in range(groups)]
        stacked = jnp.concatenate(
            [
                jnp.concatenate(
                    [own_ref[block(t, h), :, (h % 2) * 128 : (h % 2) * 128 + 128] for t in range(taps)], axis=1
                )
                for _, h, block in places
            ],
            axis=0,
        )
        moved = dot_nt(stacked, tap_order(taps))
        for n, (at, h, _) in enumerate(places):
            begin = at + h * 128 * taps
            grad_ref[:, begin : begin + 128 * taps] = moved[n * ROWS : (n + 1) * ROWS]
    width = 1024
    for begin in range(0, Q, width):
        cols = slice(begin, min(begin + width, Q))
        clipped = grad_ref[:, cols] * factor
        new_first = decay_first * first_ref[:, cols] + (1.0 - decay_first) * clipped
        new_second = decay_second * second_ref[:, cols] + (1.0 - decay_second) * clipped * clipped
        first_hat = new_first * (1.0 / (1.0 - decay_first**ADAM_STEP))
        second_hat = new_second * (1.0 / (1.0 - decay_second**ADAM_STEP))
        old = params_ref[:, cols]
        new = old - learn_rate * (first_hat / (jnp.sqrt(second_hat) + adam_eps) + weight_decay * old)
        new_first_ref[:, cols] = new_first
        new_second_ref[:, cols] = new_second
        new_params_ref[:, cols] = new
        copy_ref[:, cols] = new.astype(bf16)


def adam(own, film, squares, params, first, second):
    vmem = pl.BlockSpec(memory_space=pltpu.VMEM)
    shape = jax.ShapeDtypeStruct((ROWS, Q), f32)
    return pl.pallas_call(
        adam_kernel,
        out_shape=(jax.ShapeDtypeStruct((1, 1), f32), shape, shape, shape, jax.ShapeDtypeStruct((ROWS, Q), bf16)),
        in_specs=[vmem] * 7,
        out_specs=(vmem,) * 5,
        scratch_shapes=[pltpu.VMEM((ROWS, Q), f32)],
        compiler_params=pltpu.CompilerParams(vmem_limit_bytes=56 << 20),
        name="adam",
    )(own, film, squares, params, first, second, jnp.asarray(first_order(), bf16))


def local_plain(noisy, action_mask, time_index, obs_embed, obs_slot, cotangent, params, first_moment, second_moment):
    rows = params.shape[0]
    padded = lambda v: jnp.pad(v, ((0, ROWS - rows), (0, 0))) if rows < ROWS else v
    if rows > ROWS:
        packed = [pack(params[r : r + ROWS]) for r in range(0, rows, ROWS)]
        own = jnp.concatenate([p[0].reshape(NB, ROWS, 256) for p in packed], axis=1)
        film_own = jnp.concatenate([p[1].reshape(4, ROWS, OBS) for p in packed], axis=1)
    else:
        own, film_own = pack(padded(params))
        own = own.reshape(NB, ROWS, 256)[:, :rows]
        film_own = film_own.reshape(4, ROWS, OBS)[:, :rows]
    weights = lax.all_gather(own, "wide", axis=1, tiled=True)
    film_rows = lax.all_gather(film_own, "wide", axis=1, tiled=True).reshape(4 * C, OBS)
    seen = lax.all_gather(obs_embed, "pair", axis=0, tiled=True).reshape(-1, OBS).astype(f32)
    cond, slope = mish_parts(seen)
    cond = cond.astype(bf16)
    seen_film = dot_nt(cond, film_rows).reshape(4, 4, 4, 8, 32).transpose(0, 3, 1, 2, 4).reshape(4, 8, 4, 128)
    seen_film = seen_film.reshape(4, 4, 8, 128)
    act, noisy_grad, grads, film_grad = train(
        weights, seen_film, obs_slot[None], noisy[0], action_mask, time_index, cotangent[0]
    )
    film_grad = film_grad.reshape(8, SAM, 4, 32).transpose(1, 2, 0, 3).reshape(SAM, 4 * C)
    film_total = lax.psum(dot_tn(film_grad, cond), ("pair", "wide")).reshape(4, C, OBS)
    back = lax.psum_scatter(
        (dot_nn(film_grad, film_rows) * slope).reshape(-1, obs_embed.shape[1], OBS),
        "pair", scatter_dimension=0, tiled=True,
    )
    total = lax.psum(grads.astype(f32), ("pair", "wide")).astype(bf16)
    squares = jnp.sum(jnp.square(total.astype(f32))) + jnp.sum(jnp.square(film_total))
    here = lax.axis_index("wide") * rows
    mine = lax.dynamic_slice_in_dim(total, here, rows, 1)
    film_mine = lax.dynamic_slice_in_dim(film_total, here, rows, 1)
    outs = []
    for r in range(0, rows, ROWS):
        take = lambda v: jnp.pad(v[:, r : r + ROWS], ((0, 0), (0, max(0, ROWS - rows)), (0, 0)))
        outs.append(
            adam(
                take(mine), take(film_mine).reshape(4 * ROWS, OBS), squares.reshape(1, 1),
                *(padded(v)[r : r + ROWS] for v in (params, first_moment, second_moment)),
            )
        )
    new = [jnp.concatenate([o[k] for o in outs], axis=0)[:rows] for k in range(1, 5)]
    return (act[None], noisy_grad[None], back, outs[0][0].reshape(()), *new)


MESH = pl.DeviceIdType.MESH


def flipped(v, bits):
    out = v
    for k in range(3):
        if bits >> k & 1:
            bit = (v // (1 << k)) % 2
            out = out + (1 << k) * (1 - 2 * bit)
    return out


class Place:
    def __init__(self):
        self.p = lax.axis_index("pair")
        self.w = lax.axis_index("wide")
        self.x, self.y = self.p % 2, self.p // 2
        self.c, self.z = self.w % 2, self.w // 2

    def line(self, l):
        return (self.p, flipped(self.w, l))

    def plane(self, k):
        return (flipped(self.p, k), self.w)


def greet(me):
    barrier = pltpu.get_barrier_semaphore()
    for l in range(1, 8):
        pl.semaphore_signal(barrier, inc=1, device_id=me.line(l), device_id_type=MESH)
    for k in range(1, 4):
        pl.semaphore_signal(barrier, inc=1, device_id=me.plane(k), device_id_type=MESH)


def meet(me):
    pl.semaphore_wait(pltpu.get_barrier_semaphore(), 10)


def send(source, target, sems, at, device):
    copy = pltpu.make_async_remote_copy(
        src_ref=source, dst_ref=target, send_sem=sems[0].at[at], recv_sem=sems[1].at[at],
        device_id=device, device_id_type=MESH,
    )
    copy.start()
    return copy


def fold_rows(v):
    return jnp.concatenate([v[:, q * 256 : (q + 1) * 256] for q in range(4)], axis=0)


def unfold_rows(v):
    return jnp.concatenate([v[q * 4 : (q + 1) * 4] for q in range(4)], axis=1)


def quarter_rows(parts):
    quarter = (iota(parts[0].shape, 0) >> 2) & 3
    return sum(jnp.where(quarter == q, part, 0.0) for q, part in enumerate(parts))


class Gather:
    def __init__(self, me, own, weights, seen, obs_all, film, film_part, film_line, sems):
        self.me, self.own, self.weights, self.seen, self.obs_all, self.film = me, own, weights, seen, obs_all, film
        self.film_part, self.film_line = film_part, film_line
        (self.obs_sems, self.part_sems, self.film_sems, self.more_sems,
         self.z_sems, self.x_sems, self.y_sems, self.f_sems, self.c_sems, self.local_sem) = sems
        self.z, self.x, self.y, self.f, self.c = {}, {}, {}, {}, {}

    def start_obs(self):
        me = self.me
        piece = self.obs_all.at[me.p, me.w]
        self.obs_copies = [send(piece, piece, self.obs_sems, l - 1, me.line(l)) for l in range(1, 8)]

    def start_rows(self, g):
        me = self.me
        for k in range(1, 4):
            self.z[g, k] = send(
                self.own.at[gather_group(g), me.p], self.weights.at[gather_group(g), me.p, me.z, me.c],
                self.z_sems, g * 3 + k - 1, me.line(2 * k),
            )
        if g == 0:
            self.local = pltpu.make_async_copy(self.own, self.weights.at[:, :, me.z, me.c], self.local_sem)
            self.local.start()

    def film_product(self):
        me = self.me
        for copy in self.obs_copies:
            copy.wait()
        cond = mish_parts(self.obs_all[me.p].reshape(128, 256).astype(f32))[0].astype(bf16)
        film = quarter_rows([dot_nt(cond, self.film[:, q * 256 : (q + 1) * 256]) for q in range(4)])
        row, col = iota((64, 128), 0), iota((64, 128), 1)
        pick = one_hot(((row >> 3) == (col >> 4)) & ((row & 7) == (col & 3)))
        self.film_part[...] = sum(dot_nn(pick, part) for part in split3(film)).reshape(8, 8, 128)
        self.part_copies = [
            send(self.film_part.at[flipped(me.w, l)], self.film_line.at[me.w], self.part_sems, l - 1, me.line(l))
            for l in range(1, 8)
        ]
        self.film_line[me.w] = self.film_part[me.w]

    def film_hop(self):
        me = self.me
        for copy in self.part_copies:
            copy.wait()
        for k in range(4):
            self.seen[me.p, k] = self.film_line[2 * k] + pltpu.roll(self.film_line[2 * k + 1], 4, 0)
        piece = self.seen.at[me.p]
        self.film_copies = [send(piece, piece, self.film_sems, k - 1, me.plane(k)) for k in range(1, 4)]

    def obs_hop(self):
        me = self.me
        piece = self.obs_all.at[me.p]
        self.more_copies = [send(piece, piece, self.more_sems, k - 1, me.plane(k)) for k in range(1, 4)]

    def film_done(self):
        for copy in self.film_copies:
            copy.wait()

    def first_hop(self, g):
        me = self.me
        for k in range(1, 4):
            self.z[g, k].wait_recv()
            piece = self.weights.at[gather_group(g), me.p, flipped(me.z, k), me.c]
            self.x[g, k] = send(piece, piece, self.x_sems, g * 3 + k - 1, me.plane(1))
            self.y[g, k] = send(piece, piece, self.y_sems, g * 3 + k - 1, me.plane(2))
            if g in GATHER_DIRECT:
                self.f[g, k] = send(piece, piece, self.f_sems, g * 3 + k - 1, me.plane(3))

    def second_hop(self, g):
        me = self.me
        for k in range(1, 4):
            self.x[g, k].wait_recv()
            self.y[g, k].wait_recv()
            if g in GATHER_DIRECT:
                continue
            along_y = (g + k) % 2 == 0
            piece = self.weights.at[gather_group(g), flipped(me.p, 1 if along_y else 2), flipped(me.z, k), me.c]
            self.f[g, k] = send(piece, piece, self.f_sems, g * 3 + k - 1, me.plane(2 if along_y else 1))

    def last_hop(self, g):
        if g == 0:
            self.local.wait()
        if g in GATHER_DIRECT:
            self.second_hop(g)
        for k in range(1, 4):
            self.f[g, k].wait_recv()
        piece = self.weights.at[gather_group(g), :, :, self.me.c]
        self.c[g] = send(piece, piece, self.c_sems, g, self.me.line(1))

    def arrived(self, g):
        self.c[g].wait_recv()

    def finish(self):
        for copy in self.more_copies:
            copy.wait()
        for copies in (self.z, self.x, self.y, self.f, self.c):
            for copy in copies.values():
                copy.wait_send()


class Scatter:
    def __init__(self, me, grad, film_grad, obs_all, film, out, film_out, back, square, buffers, sems):
        self.me, self.grad, self.film_grad, self.obs_all, self.film = me, grad, film_grad, obs_all, film
        self.out, self.film_out, self.back, self.square = out, film_out, back, square
        (self.half, self.core, self.xb, self.yb, self.ub, self.vb, self.zb,
         self.film_all, self.back_part, self.back_line, self.all_squares) = buffers
        (self.g_sems, self.h_sems, self.b_sems, self.c_sems, self.x_sems, self.y_sems, self.u_sems, self.v_sems,
         self.z_sems, self.r_sems, self.n_sems, self.m_sems) = sems
        self.x, self.y, self.u, self.v, self.z, self.r, self.c = {}, {}, {}, {}, {}, {}, {}
        self.squares = []

    def start(self, g):
        me = self.me
        self.c[g] = send(
            self.grad.at[group(g), :, :, 1 - me.c], self.core.at[group(g)], self.c_sems, g, me.line(1)
        )

    def core_sum(self, g):
        me, (first, last) = self.me, GROUPS[g]
        self.c[g].wait_recv()

        def add(i, _):
            j, q = first + i // 4, i % 4
            total = self.grad[j, q, :, me.c].astype(f32) + self.core[j, q].astype(f32)
            self.half[j, q // 2, q % 2] = total.astype(bf16)
            return 0

        lax.fori_loop(0, (last - first) * 4, add, 0)
        self.x[g] = send(
            self.half.at[group(g), :, 1 - me.x, LOW], self.xb.at[group(g)], self.x_sems, g, me.plane(1)
        )
        self.y[g] = send(
            self.half.at[group(g), 1 - me.y, :, HIGH], self.yb.at[group(g)], self.y_sems, g, me.plane(2)
        )

    def first_sum(self, g):
        me, half, (first, last) = self.me, self.half, GROUPS[g]
        self.x[g].wait_recv()

        def add_x(i, _):
            j, q = first + i // 2, i % 2
            total = half[j, q, me.x, LOW].astype(f32) + self.xb[j, q].astype(f32)
            half[j, q, me.x, LOW] = total.astype(bf16)
            return 0

        lax.fori_loop(0, (last - first) * 2, add_x, 0)
        self.u[g] = send(half.at[group(g), 1 - me.y, me.x, LOW], self.ub.at[group(g)], self.u_sems, g, me.plane(2))
        self.y[g].wait_recv()

        def add_y(i, _):
            j, q = first + i // 2, i % 2
            total = half[j, me.y, q, HIGH].astype(f32) + self.yb[j, q].astype(f32)
            half[j, me.y, q, HIGH] = total.astype(bf16)
            return 0

        lax.fori_loop(0, (last - first) * 2, add_y, 0)
        self.v[g] = send(half.at[group(g), me.y, 1 - me.x, HIGH], self.vb.at[group(g)], self.v_sems, g, me.plane(1))

    def second_sum(self, g):
        me, half = self.me, self.half
        self.u[g].wait_recv()
        self.v[g].wait_recv()
        for j in range(*GROUPS[g]):
            total = half[j, me.y, me.x, LOW].astype(f32) + self.ub[j].astype(f32)
            half[j, me.y, me.x, LOW] = total.astype(bf16)
            total = half[j, me.y, me.x, HIGH].astype(f32) + self.vb[j].astype(f32)
            half[j, me.y, me.x, HIGH] = total.astype(bf16)
        for k in range(1, 4):
            self.z[g, k] = send(
                half.at[group(g), me.y, me.x, flipped(me.z, k)], self.zb.at[k - 1, group(g)],
                self.z_sems, g * 3 + k - 1, me.line(2 * k),
            )

    def last_sum(self, g):
        me = self.me
        for k in range(1, 4):
            self.z[g, k].wait_recv()
        for j in range(*GROUPS[g]):
            total = self.half[j, me.y, me.x, me.z].astype(f32)
            for k in range(3):
                total = total + self.zb[k, j].astype(f32)
            total = total.astype(bf16)
            self.out[j, me.p] = total
            self.squares.append(jnp.sum(jnp.square(total.astype(f32)).reshape(4, 8, 256), axis=0))
        piece = self.out.at[group(g), me.p]
        for k in range(1, 4):
            self.r[g, k] = send(piece, piece, self.r_sems, g * 3 + k - 1, me.plane(k))

    def film_start(self):
        me = self.me
        self.film_all[me.p, me.w] = self.film_grad[me.w]
        self.g = [
            send(self.film_grad.at[flipped(me.w, l)], self.film_all.at[me.p, me.w], self.g_sems, l - 1, me.line(l))
            for l in range(1, 8)
        ]

    def film_hop(self):
        me = self.me
        for copy in self.g:
            copy.wait()
        piece = self.film_all.at[me.p]
        self.h = [send(piece, piece, self.h_sems, k - 1, me.plane(k)) for k in range(1, 4)]

    def film_products(self):
        me = self.me
        for copy in self.h:
            copy.wait()
        copies = [self.film_all[k].reshape(128, 128) for k in range(4)]
        row, col = iota((128, 128), 0), iota((128, 128), 1)
        mine = one_hot(((row >> 4) == (col >> 4)) & ((col & 15) == 4 * me.p + (row & 3)))
        rows = [dot_nn(mine, piece).astype(bf16) for piece in copies]
        parts = [sum(dot_nn(r, self.film[:, q * 256 : (q + 1) * 256]) for r in rows) for q in range(4)]
        self.back_part[...] = quarter_rows(parts).astype(bf16).reshape(8, 16, 256)
        self.b = [
            send(self.back_part.at[flipped(me.w, l)], self.back_line.at[me.w], self.b_sems, l - 1, me.line(l))
            for l in range(1, 8)
        ]
        self.back_line[me.w] = self.back_part[me.w]
        row, col = iota((128, 512), 0), iota((128, 512), 1)
        same = ((row >> 4) == ((col >> 4) & 7)) & (((row >> 2) & 3) == (col >> 7)) & ((row & 3) == (col & 3))
        seen_all = self.obs_all[...].reshape(512, 256)
        square = jnp.zeros((8, 256), f32)
        for q in range(4):
            pick = one_hot(same & (((col >> 2) & 3) == q))
            cond = mish_parts(dot_nn(pick, seen_all))[0].astype(bf16)
            total = sum(dot_tn(piece, cond) for piece in copies)
            self.film_out[:, q * 256 : (q + 1) * 256] = total
            square = square + jnp.sum(jnp.square(total).reshape(16, 8, 256), axis=0)
        self.squares.append(0.25 * square)

    def film_back(self):
        me = self.me
        for copy in self.b:
            copy.wait()
        total = jnp.sum(self.back_line[...].astype(f32), axis=0)
        slope = mish_parts(self.obs_all[me.p, me.w].astype(f32))[1]
        self.back[0] = unfold_rows(total * slope)

    def norm(self):
        me = self.me
        total = sum(self.squares)
        piece = self.all_squares.at[me.p, me.w]
        self.all_squares[me.p, me.w] = total[:, :128] + total[:, 128:]
        copies = [send(piece, piece, self.m_sems, l - 1, me.line(l)) for l in range(1, 8)]
        for copy in copies:
            copy.wait()
        piece = self.all_squares.at[me.p]
        copies = [send(piece, piece, self.n_sems, k - 1, me.plane(k)) for k in range(1, 4)]
        for copy in copies + list(self.r.values()):
            copy.wait()
        self.square[...] = jnp.sum(self.all_squares[...].reshape(32, 8, 128), axis=0)
        for copies in (self.c, self.x, self.y, self.u, self.v, self.z):
            for copy in copies.values():
                copy.wait_send()


GATHER_GROUPS = ((0, 1), (1, 3), (3, 5), (5, 7), (7, 9))
GATHER_DIRECT = (3, 4)
GROUPS = ((0, 1), (1, 3), (3, 5), (5, 7), (7, 9))
LOW, HIGH = pl.ds(0, 2), pl.ds(2, 2)


def group(g):
    return pl.ds(GROUPS[g][0], GROUPS[g][1] - GROUPS[g][0])


def gather_group(g):
    return pl.ds(GATHER_GROUPS[g][0], GATHER_GROUPS[g][1] - GATHER_GROUPS[g][0])


def step_kernel(*refs):
    (params, order, obs, slots, noisy, mask, levels, cotangent, table,
     act, noisy_grad, back, out, film_out, square,
     own, weights, seen, obs_all, film, film_part, film_line, grad, film_grad) = refs[:24]
    buffers, sems = refs[24:35], refs[35:]
    pairs = [(sems[2 * i], sems[2 * i + 1]) for i in range(21)]
    me = Place()
    gather = Gather(me, own, weights, seen, obs_all, film, film_part, film_line, pairs[:9] + [sems[42]])
    scatter = Scatter(me, grad, film_grad, obs_all, film, out, film_out, back, square, buffers, pairs[9:])
    obs_all[me.p, me.w] = fold_rows(obs[0].astype(f32)).astype(bf16)
    greet(me)
    pack_rows(params, order, own, film)
    meet(me)
    gather.start_obs()
    gather.start_rows(0)
    gather.start_rows(1)

    def reach(point):
        if point == 0:
            gather.film_product()
            gather.start_rows(2)
            gather.start_rows(3)
            gather.start_rows(4)
            gather.first_hop(0)
            gather.first_hop(1)
            gather.second_hop(0)
            gather.film_hop()
            gather.first_hop(2)
            gather.second_hop(1)
            gather.last_hop(0)
            gather.first_hop(3)
            gather.second_hop(2)
            gather.last_hop(1)
            gather.arrived(0)
        if point == 1:
            gather.film_done()
        if point == 2:
            gather.first_hop(4)
            gather.arrived(1)
        if point == 3:
            gather.last_hop(2)
            gather.last_hop(3)
            gather.arrived(2)
        if point == 5:
            gather.last_hop(4)
            gather.arrived(3)
        if point == 6:
            gather.obs_hop()
            gather.arrived(4)
        if point == 8:
            scatter.start(4)
        if point == 9:
            scatter.core_sum(4)
            scatter.start(3)
        if point == 10:
            scatter.core_sum(3)
        if point == 11:
            scatter.start(2)
        if point == 12:
            scatter.core_sum(2)
        if point == 13:
            scatter.film_start()
            scatter.start(1)

    train_body(
        Stacked(weights), seen, slots, noisy, mask, levels, cotangent, table,
        act, noisy_grad, Stacked(grad), film_grad, reach,
    )
    scatter.start(0)
    scatter.core_sum(1)
    scatter.first_sum(4)
    scatter.core_sum(0)
    scatter.film_hop()
    scatter.first_sum(3)
    scatter.second_sum(4)
    scatter.first_sum(2)
    scatter.second_sum(3)
    scatter.first_sum(1)
    scatter.first_sum(0)
    scatter.second_sum(2)
    gather.finish()
    scatter.film_products()
    scatter.second_sum(1)
    scatter.second_sum(0)
    scatter.last_sum(4)
    scatter.last_sum(3)
    scatter.film_back()
    scatter.last_sum(2)
    scatter.last_sum(1)
    scatter.last_sum(0)
    scatter.norm()


class Stacked:
    def __init__(self, ref):
        self.ref = ref

    def _split(self, key):
        if not isinstance(key, tuple):
            return key, slice(None)
        return key[0], key[2]

    def __getitem__(self, key):
        block, cols = self._split(key)
        value = self.ref[block // 4, block % 4, :, :, :, cols]
        return value.reshape(256, value.shape[-1])

    def __setitem__(self, key, value):
        block, cols = self._split(key)
        self.ref[block // 4, block % 4, :, :, :, cols] = value.reshape(4, 2, ROWS, value.shape[-1])


def step(params, obs, slots, noisy, mask, levels, cotangent):
    vmem = pl.BlockSpec(memory_space=pltpu.VMEM)
    pair = lambda n: [pltpu.SemaphoreType.DMA((n,))] * 2
    n, count, parts = NB // 4, len(GROUPS), len(GATHER_GROUPS)
    low = lambda *shape: pltpu.VMEM(shape, bf16)
    return pl.pallas_call(
        step_kernel,
        out_shape=(
            jax.ShapeDtypeStruct((C, 256), bf16),
            jax.ShapeDtypeStruct((ADIM, 256), f32),
            jax.ShapeDtypeStruct((1, 4, OBS), f32),
            jax.ShapeDtypeStruct((n, 4, ROWS, 256), bf16),
            jax.ShapeDtypeStruct((4 * ROWS, OBS), f32),
            jax.ShapeDtypeStruct((8, 128), f32),
        ),
        in_specs=[vmem] * 9,
        out_specs=(vmem,) * 6,
        scratch_shapes=[
            low(n, 4, ROWS, 256),
            low(n, 4, 4, 2, ROWS, 256),
            pltpu.VMEM((4, 4, 8, 128), f32),
            low(4, 8, 16, 256),
            low(4 * ROWS, OBS),
            pltpu.VMEM((8, 8, 128), f32),
            pltpu.VMEM((8, 8, 128), f32),
            low(n, 4, 4, 2, ROWS, 256),
            low(8, SAM, 128),
            low(n, 2, 2, 4, ROWS, 256),
            low(n, 4, 4, ROWS, 256),
            low(n, 2, 2, ROWS, 256),
            low(n, 2, 2, ROWS, 256),
            low(n, 2, ROWS, 256),
            low(n, 2, ROWS, 256),
            low(3, n, ROWS, 256),
            low(4, 8, 16, 128),
            low(8, 16, 256),
            low(8, 16, 256),
            pltpu.VMEM((4, 8, 8, 128), f32),
            *pair(7), *pair(7), *pair(3), *pair(3),
            *pair(3 * parts), *pair(3 * parts), *pair(3 * parts), *pair(3 * parts), *pair(parts),
            *pair(7), *pair(3), *pair(7),
            *pair(count), *pair(count), *pair(count), *pair(count), *pair(count),
            *pair(3 * count), *pair(3 * count), *pair(3), *pair(7),
            pltpu.SemaphoreType.DMA,
        ],
        compiler_params=pltpu.CompilerParams(collective_id=0, has_side_effects=True, vmem_limit_bytes=60 << 20),
        name="step",
    )(params, jnp.asarray(first_order(), bf16), obs, slots, noisy, mask, levels, cotangent, jnp.asarray(level_table(), bf16))


def local_fast(noisy, action_mask, time_index, obs_embed, obs_slot, cotangent, params, first_moment, second_moment):
    act, noisy_grad, back, total, film_total, squares = step(
        params, obs_embed, obs_slot[None], noisy[0], action_mask, time_index, cotangent[0]
    )
    norm, *new = adam(
        total.reshape(NB, ROWS, 256), film_total, squares, params, first_moment, second_moment
    )
    return (act[None], noisy_grad[None], back, norm.reshape(()), *new)


def solution(mesh):
    in_specs = (
        P("pair", None, "wide"),
        P(None, "wide"),
        P("pair", "wide"),
        P("pair", "wide", None),
        P("wide"),
        P("pair", None, "wide"),
        P("wide", None),
        P("wide", None),
        P("wide", None),
    )
    out_specs = (
        P("pair", None, "wide"),
        P("pair", None, "wide"),
        P("pair", "wide", None),
        P(),
        P("wide", None),
        P("wide", None),
        P("wide", None),
        P("wide", None),
    )
    fast = mesh.shape["pair"] == 4 and mesh.shape["wide"] == 8
    return jax.shard_map(local_fast if fast else local_plain, mesh=mesh, in_specs=in_specs, out_specs=out_specs, check_vma=False)
```

```python
import functools
import math

import jax
import jax.numpy as jnp
import numpy as np
from jax import lax
from jax.experimental import pallas as pl
from jax.experimental.pallas import tpu as pltpu
from jax.sharding import PartitionSpec as P

C = 256
OBS = 1024
TE = 128
TH = 512
ADIM = 10
FR = 16
LEVELS = 40
ADAM_STEP = 7
Q = 12627
SAM = 16
ROWS = 32
NB = 36

sigma_top = 80.0 ** (1.0 / 7.0)
sigma_low = 0.002 ** (1.0 / 7.0)
clip_limit = 1.0
learn_rate = 0.02
decay_first = 0.5
decay_second = 0.5
adam_eps = 1e-08
weight_decay = 0.01
norm_eps = 1e-05

f32 = jnp.float32
bf16 = jnp.bfloat16

AT_DOWN_RES = 1330
AT_TAIL = 12604
TAIL = 23
AT_FILM = (1340, 2492, 9788, 10940)
AT_TIME = (12092, 12348)
AT_UP_RES = 9276
B_MISC, B_INNER, B_OUTER, B_FILM = 0, 1, 2, 3
B_DS, B_POOL, B_SPREAD, B_UF, B_US, B_UR = 5, 10, 13, 18, 28, 33
B_NONE = (17, 35)
LANE_TAIL = 64
CONVS = (
    (50, 5, 2, lambda t, h: B_DS + t),
    (5436, 5, 4, lambda t, h: B_UF + 2 * t + h // 2),
    (7996, 5, 2, lambda t, h: B_US + t),
    (3644, 3, 2, lambda t, h: B_POOL + t),
    (4412, 4, 2, lambda t, h: B_SPREAD + t),
)
(T_BIAS_A, T_BIAS_B, T_OUT, D_B1, D_G1, D_S1, D_FS, D_FO, D_B2, D_G2, D_S2, D_RB, PB, SB,
 U_B1, U_G1, U_S1, U_FS, U_FO, U_B2, U_G2, U_S2, U_RB) = range(TAIL)


def dot_nt(a, b):
    return lax.dot_general(a, b, (((1,), (1,)), ((), ())), preferred_element_type=f32)


def dot_nn(a, b):
    return lax.dot_general(a, b, (((1,), (0,)), ((), ())), preferred_element_type=f32)


def dot_tn(a, b):
    return lax.dot_general(a, b, (((0,), (0,)), ((), ())), preferred_element_type=f32)


def split2(v):
    high = v.astype(bf16)
    return high, (v - high.astype(f32)).astype(bf16)


def split3(v):
    high, rest = v.astype(bf16), None
    rest = v - high.astype(f32)
    mid = rest.astype(bf16)
    return high, mid, (rest - mid.astype(f32)).astype(bf16)


def iota(shape, dim):
    return lax.broadcasted_iota(jnp.int32, shape, dim)


def one_hot(condition):
    return jnp.where(condition, 1.0, 0.0).astype(bf16)


def tap_order(taps):
    n = 128 * taps
    row = lax.broadcasted_iota(jnp.int32, (n, n), 0)
    col = lax.broadcasted_iota(jnp.int32, (1, n), 1)
    source = (col & 127) * taps + (col >> 7)
    return jnp.where(row == source, 1.0, 0.0).astype(bf16)


def first_order():
    table = np.zeros((128, 128), np.float32)
    for i in range(ADIM):
        for t in range(5):
            table[i * 5 + t, t * ADIM + i] = 1.0
    return table


def level_table():
    levels = np.arange(LEVELS, dtype=np.float64)
    tau = 250.0 * 7.0 * np.log(sigma_top + levels / (LEVELS - 1) * (sigma_low - sigma_top))
    freq = np.exp(-math.log(10000.0) * np.arange(TE // 2) / (TE // 2 - 1))
    angles = tau[:, None] * freq[None, :]
    table = np.zeros((64, TE), np.float32)
    table[:LEVELS] = np.concatenate([np.sin(angles), np.cos(angles)], axis=1)
    return table


def pack_kernel(params_ref, order_ref, own_ref, film_ref):
    pack_rows(params_ref, order_ref, own_ref, film_ref)


class Blocks:
    def __init__(self, ref):
        self.ref = ref

    def _at(self, key):
        block, rest = (key[0], key[1:]) if isinstance(key, tuple) else (key, ())
        return (block // 4, block % 4) + rest

    def __getitem__(self, key):
        return self.ref[self._at(key)]

    def __setitem__(self, key, value):
        self.ref[self._at(key)] = value


def pack_rows(params_ref, order_ref, own_ref, film_ref):
    own_ref = Blocks(own_ref)

    def low(start, width):
        return params_ref[:, start : start + width].astype(bf16)

    first = dot_nn(low(0, 128), order_ref[...])
    pieces = [
        first[:, :50],
        params_ref[:, AT_DOWN_RES : AT_DOWN_RES + ADIM],
        jnp.zeros((ROWS, LANE_TAIL - 60), f32),
        params_ref[:, AT_TAIL : AT_TAIL + TAIL],
        jnp.zeros((ROWS, 256 - LANE_TAIL - TAIL), f32),
    ]
    own_ref[B_MISC] = jnp.concatenate(pieces, axis=1).astype(bf16)
    own_ref[B_INNER] = low(AT_TIME[0], 256)
    own_ref[B_OUTER] = low(AT_TIME[1], 256)
    for q in range(4):
        film_ref[q * ROWS : (q + 1) * ROWS] = low(AT_FILM[q], OBS)
        own_ref[B_FILM + q // 2, :, (q % 2) * 128 : (q % 2) * 128 + 128] = low(AT_FILM[q] + OBS, TE)
    own_ref[B_UR] = low(AT_UP_RES, 256)
    own_ref[B_UR + 1] = low(AT_UP_RES + 256, 256)
    for b in B_NONE:
        own_ref[b] = jnp.zeros((ROWS, 256), bf16)
    for taps in (5, 3, 4):
        places = [(at, h, block) for at, k, groups, block in CONVS if k == taps for h in range(groups)]
        stacked = jnp.concatenate([low(at + h * 128 * taps, 128 * taps) for at, h, _ in places], axis=0)
        moved = dot_nn(stacked, tap_order(taps)).astype(bf16)
        for n, (_, h, block) in enumerate(places):
            for t in range(taps):
                own_ref[block(t, h), :, (h % 2) * 128 : (h % 2) * 128 + 128] = moved[
                    n * ROWS : (n + 1) * ROWS, t * 128 : (t + 1) * 128
                ]


def pack(params):
    vmem = pl.BlockSpec(memory_space=pltpu.VMEM)
    return pl.pallas_call(
        pack_kernel,
        out_shape=(
            jax.ShapeDtypeStruct((NB // 4, 4, ROWS, 256), bf16),
            jax.ShapeDtypeStruct((4 * ROWS, OBS), bf16),
        ),
        in_specs=[vmem, vmem],
        out_specs=(vmem, vmem),
        compiler_params=pltpu.CompilerParams(vmem_limit_bytes=40 << 20),
        name="pack",
    )(params, jnp.asarray(first_order(), bf16))


def mish_parts(v):
    e = jnp.exp(jnp.minimum(v, 20.0))
    n = e * (e + 2.0)
    r = 1.0 / (n + 2.0)
    t = n * r
    return v * t, t + 4.0 * v * (e * r) * ((e + 1.0) * r)


def step_frames(v, step):
    if step == 0:
        return v
    zeros = jnp.zeros((SAM * abs(step), v.shape[1]), v.dtype)
    if step > 0:
        return jnp.concatenate([v[SAM * step :], zeros], axis=0)
    return jnp.concatenate([zeros, v[: SAM * step]], axis=0)


def over_frames(v):
    return jnp.sum(v.reshape(-1, SAM, v.shape[1]), axis=0)


def each_frame(v, s):
    return v.reshape(-1, SAM, v.shape[1]), s[None]


def group_means(values, ones):
    parts = [p for v in values for p in split3(v)]
    sums = dot_nn(jnp.concatenate(parts, axis=0), ones)
    out = []
    for i in range(len(values)):
        a, b, c = (sums[(3 * i + k) * SAM : (3 * i + k + 1) * SAM] for k in range(3))
        out.append((a + (b + c)) * (1.0 / (32 * FR)))
    return out


def minus(v, s):
    a, b = each_frame(v, s)
    return (a - b).reshape(v.shape)


def times(v, s):
    a, b = each_frame(v, s)
    return (a * b).reshape(v.shape)


def plus(v, s):
    a, b = each_frame(v, s)
    return (a + b).reshape(v.shape)


def norm_forward(before, gain, shift, ones):
    (center,) = group_means([over_frames(before)], ones)
    away = minus(before, center)
    (spread,) = group_means([over_frames(away * away)], ones)
    scale = lax.rsqrt(spread + norm_eps)
    normal = times(away, scale)
    act, slope = mish_parts(normal * gain + shift)
    return act, normal, slope, scale


def norm_backward(grad_act, normal, slope, scale, gain, ones):
    grad_out = grad_act * slope
    shift_rows = over_frames(grad_out)
    gain_rows = over_frames(grad_out * normal)
    mean_grad, mean_both = group_means([shift_rows * gain, gain_rows * gain], ones)
    inner = minus(grad_out * gain, mean_grad) - times(normal, mean_both)
    return (
        times(inner, scale),
        jnp.sum(gain_rows, axis=0, keepdims=True),
        jnp.sum(shift_rows, axis=0, keepdims=True),
    )


def conv_forward(source, weight):
    total = dot_nt(step_frames(source, -2), weight(0))
    for t in range(1, 5):
        total = total + dot_nt(step_frames(source, t - 2), weight(t))
    return total


def conv_source(grad_low, weight):
    total = dot_nn(step_frames(grad_low, 2), weight(0))
    for t in range(1, 5):
        total = total + dot_nn(step_frames(grad_low, 2 - t), weight(t))
    return total


def row_sum(v):
    return jnp.sum(over_frames(v), axis=0, keepdims=True)


def halves(v):
    cube = v.reshape(FR // 2, 2, SAM, v.shape[1])
    return cube[:, 0].reshape(-1, v.shape[1]), cube[:, 1].reshape(-1, v.shape[1])


def interleave(even, odd):
    width = even.shape[1]
    pair = [v.reshape(FR // 2, 1, SAM, width) for v in (even, odd)]
    return jnp.concatenate(pair, axis=1).reshape(FR * SAM, width)


def train_kernel(*refs):
    train_body(*refs, lambda point: None)


def train_body(
    w_ref, seen_ref, slot_ref, noisy_ref, mask_ref, level_ref, cot_ref, table_ref,
    act_ref, noisy_grad_ref, grad_ref, film_grad_ref, reach,
):
    row = iota((256, 256), 0)
    col = iota((256, 256), 1)
    ones = jnp.where((row >> 5) == (col >> 5), 1.0, 0.0).astype(bf16)
    swap = jnp.where(col == ((row & 15) << 4) + (row >> 4), 1.0, 0.0).astype(bf16)
    for b in B_NONE:
        grad_ref[b] = jnp.zeros((256, 256), bf16)
    spread_mask = one_hot((iota((SAM, 256), 1) >> 4) == iota((SAM, 256), 0))
    keep = dot_nn(mask_ref[...].astype(f32).astype(bf16), spread_mask)
    start_cols = noisy_ref[...].astype(f32) * keep
    start_cols = jnp.concatenate([start_cols, jnp.zeros((6, 256), f32)], axis=0).astype(bf16)
    start = dot_nt(swap, start_cols).astype(bf16)
    lane16 = iota((16, 128), 1)
    row16 = iota((16, 128), 0)
    inputs = jnp.zeros((256, 128), f32)
    for t in range(5):
        place = lane16 == row16 + t * ADIM
        if t == 2:
            place = place | (lane16 == row16 + 50)
        inputs = inputs + dot_nn(step_frames(start, t - 2), one_hot(place & (row16 < ADIM)))
    inputs = inputs.astype(bf16)
    cot_high, cot_low = split2(cot_ref[...])
    upstream = dot_nt(swap, cot_high) + dot_nt(swap, cot_low)
    upstream_low = upstream.astype(bf16)
    at_level = one_hot(iota((64, SAM), 0) == level_ref[...])
    feats = dot_tn(at_level, table_ref[...]).astype(bf16)
    reach(0)
    misc = w_ref[B_MISC, :, :128]
    lane = iota((256, 128), 1)
    misc_first = jnp.where(lane < 50, misc, jnp.zeros_like(misc))
    misc_res = jnp.where((lane >= 50) & (lane < 60), misc, jnp.zeros_like(misc))
    singles = misc.astype(f32).T[LANE_TAIL : LANE_TAIL + 32]
    vec = lambda k: singles[k : k + 1]

    inner = [w_ref[B_INNER, :, j * 128 : (j + 1) * 128] for j in range(2)]
    outer = [w_ref[B_OUTER, :, j * 128 : (j + 1) * 128] for j in range(2)]
    film_time = lambda q: w_ref[B_FILM + q // 2, :, (q % 2) * 128 : (q % 2) * 128 + 128]
    hidden = [mish_parts(dot_nt(feats, inner[j]) + vec(T_BIAS_A + j)) for j in range(2)]
    hidden_low = [h[0].astype(bf16) for h in hidden]
    embed = dot_nn(hidden_low[0], outer[0]) + dot_nn(hidden_low[1], outer[1]) + vec(T_OUT)[:, :TE]
    cond, cond_slope = mish_parts(embed)
    cond_low = cond.astype(bf16)
    pre = dot_nt(inputs, misc_first) + vec(D_B1)
    act_one, normal_one, slope_one, scale_one = norm_forward(pre, vec(D_G1), vec(D_S1), ones)
    reach(1)
    at_slot = one_hot(iota((SAM, SAM), 0) == slot_ref[...])
    line = iota((32, SAM), 0)
    seen_film = jnp.concatenate([seen_ref[:, k].reshape(32, 128) for k in range(4)], axis=1)
    seen_film = split3(seen_film)
    sides = []
    for side in range(2):
        at_line = one_hot(((line >> 3) * 4 + (line & 3) == slot_ref[...]) & ((line >> 2) & 1 == side))
        sides.append(sum(dot_tn(at_line, part) for part in seen_film))
    seen_film = jnp.concatenate(
        [sides[k % 2][:, (k // 2) * 128 : (k // 2) * 128 + 128] for k in range(8)], axis=1
    )
    spans = lambda v, q: jnp.concatenate([v[:, k * 128 + q * 32 : k * 128 + q * 32 + 32] for k in range(8)], axis=1)
    film_of = lambda q: spans(seen_film, q) + dot_nt(cond_low, film_time(q)) + vec((D_FS, D_FO, U_FS, U_FO)[q])
    film = [film_of(0), film_of(1)]
    mid_one = plus(times(act_one, film[0]), film[1]).astype(bf16)
    reach(2)
    down = lambda t: w_ref[B_DS + t]
    pre = conv_forward(mid_one, down) + vec(D_B2)
    act, normal_two, slope_two, scale_two = norm_forward(pre, vec(D_G2), vec(D_S2), ones)
    skip = (act + dot_nt(inputs, misc_res) + vec(D_RB)).astype(bf16)
    reach(3)
    even, odd = halves(skip)
    odd_prev = step_frames(odd, -1)
    pool_sources = (odd_prev, even, odd)
    pooled = sum(dot_nt(s, w_ref[B_POOL + t]) for t, s in enumerate(pool_sources)) + vec(PB)
    pooled = pooled.astype(bf16)
    reach(4)
    pooled_prev = step_frames(pooled, -1)
    pooled_next = step_frames(pooled, 1)
    even_out = dot_nt(pooled, w_ref[B_SPREAD + 1]) + dot_nt(pooled_prev, w_ref[B_SPREAD + 3])
    odd_out = dot_nt(pooled_next, w_ref[B_SPREAD]) + dot_nt(pooled, w_ref[B_SPREAD + 2])
    wide = (interleave(even_out, odd_out) + vec(SB)).astype(bf16)
    joined = (wide, skip)
    reach(5)
    up_first = [lambda t, h=h: w_ref[B_UF + 2 * t + h] for h in range(2)]
    pre = conv_forward(wide, up_first[0]) + conv_forward(skip, up_first[1]) + vec(U_B1)
    act_three, normal_three, slope_three, scale_three = norm_forward(pre, vec(U_G1), vec(U_S1), ones)
    film += [film_of(2), film_of(3)]
    mid_three = plus(times(act_three, film[2]), film[3]).astype(bf16)
    reach(6)
    up = lambda t: w_ref[B_US + t]
    pre = conv_forward(mid_three, up) + vec(U_B2)
    act, normal_four, slope_four, scale_four = norm_forward(pre, vec(U_G2), vec(U_S2), ones)
    result = act + dot_nt(wide, w_ref[B_UR]) + dot_nt(skip, w_ref[B_UR + 1]) + vec(U_RB)
    act_ref[...] = dot_tn(result.astype(bf16), swap).astype(bf16)

    single_grads = {}

    def conv_weights(grad_low, source, block):
        turned = grad_low.T
        for t in range(5):
            grad_ref[block(t)] = dot_nn(turned, step_frames(source, t - 2)).astype(bf16)

    reach(7)
    grad, single_grads[U_G2], single_grads[U_S2] = norm_backward(
        upstream, normal_four, slope_four, scale_four, vec(U_G2), ones
    )
    single_grads[U_B2] = row_sum(grad)
    low = grad.astype(bf16)
    conv_weights(low, mid_three, lambda t: B_US + t)
    turned = upstream_low.T
    for h in range(2):
        grad_ref[B_UR + h] = dot_nn(turned, joined[h]).astype(bf16)
    reach(8)
    grad_mid = conv_source(low, up)
    shift_three = over_frames(grad_mid)
    gain_three = over_frames(grad_mid * act_three)
    grad, single_grads[U_G1], single_grads[U_S1] = norm_backward(
        times(grad_mid, film[2]), normal_three, slope_three, scale_three, vec(U_G1), ones
    )
    single_grads[U_B1] = row_sum(grad)
    low = grad.astype(bf16)
    for h in range(2):
        conv_weights(low, joined[h], lambda t, h=h: B_UF + 2 * t + h)
    single_grads[U_RB] = row_sum(upstream)
    reach(9)
    grad_wide = conv_source(low, up_first[0]) + dot_nn(upstream_low, w_ref[B_UR])
    grad_skip = conv_source(low, up_first[1]) + dot_nn(upstream_low, w_ref[B_UR + 1])
    single_grads[SB] = row_sum(grad_wide)
    low_even, low_odd = halves(grad_wide.astype(bf16))
    turned_even, turned_odd = low_even.T, low_odd.T
    grad_ref[B_SPREAD] = dot_nn(turned_odd, pooled_next).astype(bf16)
    grad_ref[B_SPREAD + 1] = dot_nn(turned_even, pooled).astype(bf16)
    grad_ref[B_SPREAD + 2] = dot_nn(turned_odd, pooled).astype(bf16)
    grad_ref[B_SPREAD + 3] = dot_nn(turned_even, pooled_prev).astype(bf16)
    reach(10)
    grad_pooled = dot_nn(low_even, w_ref[B_SPREAD + 1]) + dot_nn(low_odd, w_ref[B_SPREAD + 2])
    grad_pooled = grad_pooled + dot_nn(step_frames(low_even, 1), w_ref[B_SPREAD + 3])
    grad_pooled = grad_pooled + dot_nn(step_frames(low_odd, -1), w_ref[B_SPREAD])
    single_grads[PB] = row_sum(grad_pooled)
    low = grad_pooled.astype(bf16)
    turned = low.T
    for t in range(3):
        grad_ref[B_POOL + t] = dot_nn(turned, pool_sources[t]).astype(bf16)
    reach(11)
    grad_even = dot_nn(low, w_ref[B_POOL + 1])
    grad_odd = dot_nn(low, w_ref[B_POOL + 2]) + dot_nn(step_frames(low, 1), w_ref[B_POOL])
    grad_skip = grad_skip + interleave(grad_even, grad_odd)
    single_grads[D_RB] = row_sum(grad_skip)
    skip_low = grad_skip.astype(bf16)
    misc_grad = jnp.where(lane < 50, 0.0, dot_nn(skip_low.T, inputs))
    back = dot_nn(skip_low, misc_res)
    grad, single_grads[D_G2], single_grads[D_S2] = norm_backward(
        grad_skip, normal_two, slope_two, scale_two, vec(D_G2), ones
    )
    single_grads[D_B2] = row_sum(grad)
    low = grad.astype(bf16)
    conv_weights(low, mid_one, lambda t: B_DS + t)
    reach(12)
    grad_mid = conv_source(low, down)
    shift_one = over_frames(grad_mid)
    gain_one = over_frames(grad_mid * act_one)
    grad, single_grads[D_G1], single_grads[D_S1] = norm_backward(
        times(grad_mid, film[0]), normal_one, slope_one, scale_one, vec(D_G1), ones
    )
    single_grads[D_B1] = row_sum(grad)
    low = grad.astype(bf16)
    misc_grad = misc_grad + jnp.where(lane < 50, dot_nn(low.T, inputs), 0.0)
    film_grads = (gain_one, shift_one, gain_three, shift_three)
    film_low = [g.astype(bf16) for g in film_grads]
    back_cond = None
    for q in range(4):
        single_grads[(D_FS, D_FO, U_FS, U_FO)[q]] = jnp.sum(film_grads[q], axis=0, keepdims=True)
        grad_ref[B_FILM + q // 2, :, (q % 2) * 128 : (q % 2) * 128 + 128] = dot_tn(film_low[q], cond_low).astype(bf16)
        part = dot_nn(film_low[q], film_time(q))
        back_cond = part if back_cond is None else back_cond + part
    at_slots = [dot_nn(at_slot, v) for v in film_low]
    for k in range(8):
        film_grad_ref[k] = jnp.concatenate([v[:, k * 32 : (k + 1) * 32] for v in at_slots], axis=1).astype(bf16)
    reach(13)
    back = back + dot_nn(low, misc_first)
    grad_start = back[:, 50:60]
    for t in range(5):
        grad_start = grad_start + step_frames(back[:, t * ADIM : (t + 1) * ADIM], 2 - t)
    grad_cols = sum(dot_tn(part, swap) for part in split3(jnp.concatenate([grad_start, jnp.zeros((256, 6), f32)], axis=1)))
    noisy_grad_ref[...] = grad_cols[:ADIM] * keep

    grad_embed = back_cond * cond_slope
    single_grads[T_OUT] = jnp.concatenate(
        [jnp.sum(grad_embed, axis=0, keepdims=True), jnp.zeros((1, C - TE), f32)], axis=1
    )
    embed_low = grad_embed.astype(bf16)
    for j in range(2):
        grad_ref[B_OUTER, :, j * 128 : (j + 1) * 128] = dot_tn(hidden_low[j], embed_low).astype(bf16)
        grad_hidden = dot_nt(embed_low, outer[j]) * hidden[j][1]
        single_grads[T_BIAS_A + j] = jnp.sum(grad_hidden, axis=0, keepdims=True)
        grad_ref[B_INNER, :, j * 128 : (j + 1) * 128] = dot_tn(grad_hidden.astype(bf16), feats).astype(bf16)
    stack = [jnp.zeros((LANE_TAIL, 256), f32)] + [single_grads[k] for k in range(TAIL)]
    stack = jnp.concatenate(stack + [jnp.zeros((128 - LANE_TAIL - TAIL, 256), f32)], axis=0)
    grad_ref[B_MISC, :, :128] = (misc_grad + stack.T).astype(bf16)
    grad_ref[B_MISC, :, 128:] = jnp.zeros((256, 128), bf16)


def train(weights, seen_film, slots, noisy, mask, levels, cotangent):
    vmem = pl.BlockSpec(memory_space=pltpu.VMEM)
    return pl.pallas_call(
        train_kernel,
        out_shape=(
            jax.ShapeDtypeStruct((C, 256), bf16),
            jax.ShapeDtypeStruct((ADIM, 256), f32),
            jax.ShapeDtypeStruct((NB, 256, 256), bf16),
            jax.ShapeDtypeStruct((8, SAM, 128), bf16),
        ),
        in_specs=[vmem] * 8,
        out_specs=(vmem,) * 4,
        compiler_params=pltpu.CompilerParams(vmem_limit_bytes=48 << 20),
        name="train",
    )(weights, seen_film, slots, noisy, mask, levels, cotangent, jnp.asarray(level_table(), bf16))


HALF = ROWS // 2


def native_grads(own_ref, film_ref, order_ref, grad_ref):
    misc = own_ref[B_MISC]
    first = dot_nt(misc[:, :128], order_ref[...])
    misc = misc.astype(f32)
    grad_ref[:, 0:50] = first[:, :50]
    grad_ref[:, AT_DOWN_RES : AT_DOWN_RES + ADIM] = misc[:, 50:60]
    grad_ref[:, AT_TAIL : AT_TAIL + TAIL] = misc[:, LANE_TAIL : LANE_TAIL + TAIL]
    grad_ref[:, AT_TIME[0] : AT_TIME[0] + 256] = own_ref[B_INNER].astype(f32)
    grad_ref[:, AT_TIME[1] : AT_TIME[1] + 256] = own_ref[B_OUTER].astype(f32)
    for q in range(4):
        grad_ref[:, AT_FILM[q] : AT_FILM[q] + OBS] = film_ref[q * ROWS : (q + 1) * ROWS]
        part = own_ref[B_FILM + q // 2, :, (q % 2) * 128 : (q % 2) * 128 + 128]
        grad_ref[:, AT_FILM[q] + OBS : AT_FILM[q] + OBS + TE] = part.astype(f32)
    grad_ref[:, AT_UP_RES : AT_UP_RES + 256] = own_ref[B_UR].astype(f32)
    grad_ref[:, AT_UP_RES + 256 : AT_UP_RES + 512] = own_ref[B_UR + 1].astype(f32)
    for taps in (5, 3, 4):
        places = [(at, h, block) for at, k, groups, block in CONVS if k == taps for h in range(groups)]
        stacked = jnp.concatenate(
            [
                jnp.concatenate(
                    [own_ref[block(t, h), :, (h % 2) * 128 : (h % 2) * 128 + 128] for t in range(taps)], axis=1
                )
                for _, h, block in places
            ],
            axis=0,
        )
        moved = dot_nt(stacked, tap_order(taps))
        for n, (at, h, _) in enumerate(places):
            begin = at + h * 128 * taps
            grad_ref[:, begin : begin + 128 * taps] = moved[n * ROWS : (n + 1) * ROWS]


def adam_kernel(count, *refs):
    own_ref, film_ref, square_ref, order_ref = refs[:4]
    old_hbm, extra_in = refs[4:7], refs[7 : 7 + count]
    norm_ref, new_hbm, extra_out = refs[7 + count], refs[8 + count : 12 + count], refs[12 + count : 12 + 2 * count]
    grad_ref, old, new, in_sems, out_sems = refs[12 + 2 * count], refs[13 + 2 * count : 16 + 2 * count], refs[
        16 + 2 * count : 20 + 2 * count
    ], refs[-2], refs[-1]
    rows = [pl.ds(h * HALF, HALF) for h in range(2)]
    loads = [
        [pltpu.make_async_copy(old_hbm[n].at[rows[h]], old[n].at[rows[h]], in_sems.at[h, n]) for n in range(3)]
        for h in range(2)
    ]
    stores = [
        [pltpu.make_async_copy(new[n].at[rows[h]], new_hbm[n].at[rows[h]], out_sems.at[h, n]) for n in range(4)]
        for h in range(2)
    ]
    for half in loads:
        for copy in half:
            copy.start()
    norm = jnp.sqrt(jnp.sum(square_ref[...], axis=(0, 1), keepdims=True))
    norm_ref[...] = norm
    factor = jnp.minimum(1.0, clip_limit / (norm + 1e-06))
    for source, target in zip(extra_in, extra_out):
        target[...] = source[...].reshape(target.shape)
    native_grads(own_ref, film_ref, order_ref, grad_ref)
    width = 1024
    for h in range(2):
        for copy in loads[h]:
            copy.wait()
        for begin in range(0, Q, width):
            at = (rows[h], slice(begin, min(begin + width, Q)))
            clipped = grad_ref[at] * factor
            new_first = decay_first * old[1][at] + (1.0 - decay_first) * clipped
            new_second = decay_second * old[2][at] + (1.0 - decay_second) * clipped * clipped
            first_hat = new_first * (1.0 / (1.0 - decay_first**ADAM_STEP))
            second_hat = new_second * (1.0 / (1.0 - decay_second**ADAM_STEP))
            before = old[0][at]
            after = before - learn_rate * (first_hat / (jnp.sqrt(second_hat) + adam_eps) + weight_decay * before)
            new[0][at] = after
            new[1][at] = new_first
            new[2][at] = new_second
            new[3][at] = after.astype(bf16)
        for copy in stores[h]:
            copy.start()
    for half in stores:
        for copy in half:
            copy.wait()


def adam(own, film, squares, params, first, second, extras=(), extra_shapes=()):
    vmem = pl.BlockSpec(memory_space=pltpu.VMEM)
    hbm = pl.BlockSpec(memory_space=pl.ANY)
    shape = jax.ShapeDtypeStruct((ROWS, Q), f32)
    count = len(extras)
    return pl.pallas_call(
        functools.partial(adam_kernel, count),
        out_shape=(
            jax.ShapeDtypeStruct((1, 1), f32),
            shape, shape, shape, jax.ShapeDtypeStruct((ROWS, Q), bf16),
            *(jax.ShapeDtypeStruct(dims, v.dtype) for dims, v in zip(extra_shapes, extras)),
        ),
        in_specs=[vmem] * 4 + [hbm] * 3 + [vmem] * count,
        out_specs=(vmem,) + (hbm,) * 4 + (vmem,) * count,
        scratch_shapes=[pltpu.VMEM((ROWS, Q), f32)] * 7
        + [pltpu.VMEM((ROWS, Q), bf16), pltpu.SemaphoreType.DMA((2, 3)), pltpu.SemaphoreType.DMA((2, 4))],
        compiler_params=pltpu.CompilerParams(vmem_limit_bytes=56 << 20),
        name="adam",
    )(own, film, squares, jnp.asarray(first_order(), bf16), params, first, second, *extras)


def local_plain(noisy, action_mask, time_index, obs_embed, obs_slot, cotangent, params, first_moment, second_moment):
    rows = params.shape[0]
    padded = lambda v: jnp.pad(v, ((0, ROWS - rows), (0, 0))) if rows < ROWS else v
    if rows > ROWS:
        packed = [pack(params[r : r + ROWS]) for r in range(0, rows, ROWS)]
        own = jnp.concatenate([p[0].reshape(NB, ROWS, 256) for p in packed], axis=1)
        film_own = jnp.concatenate([p[1].reshape(4, ROWS, OBS) for p in packed], axis=1)
    else:
        own, film_own = pack(padded(params))
        own = own.reshape(NB, ROWS, 256)[:, :rows]
        film_own = film_own.reshape(4, ROWS, OBS)[:, :rows]
    weights = lax.all_gather(own, "wide", axis=1, tiled=True)
    film_rows = lax.all_gather(film_own, "wide", axis=1, tiled=True).reshape(4 * C, OBS)
    seen = lax.all_gather(obs_embed, "pair", axis=0, tiled=True).reshape(-1, OBS).astype(f32)
    cond, slope = mish_parts(seen)
    cond = cond.astype(bf16)
    seen_film = dot_nt(cond, film_rows).reshape(4, 4, 4, 8, 32).transpose(0, 3, 1, 2, 4).reshape(4, 8, 4, 128)
    seen_film = seen_film.reshape(4, 4, 8, 128)
    act, noisy_grad, grads, film_grad = train(
        weights, seen_film, obs_slot[None], noisy[0], action_mask, time_index, cotangent[0]
    )
    film_grad = film_grad.reshape(8, SAM, 4, 32).transpose(1, 2, 0, 3).reshape(SAM, 4 * C)
    film_total = lax.psum(dot_tn(film_grad, cond), ("pair", "wide")).reshape(4, C, OBS)
    back = lax.psum_scatter(
        (dot_nn(film_grad, film_rows) * slope).reshape(-1, obs_embed.shape[1], OBS),
        "pair", scatter_dimension=0, tiled=True,
    )
    total = lax.psum(grads.astype(f32), ("pair", "wide")).astype(bf16)
    squares = jnp.sum(jnp.square(total.astype(f32))) + jnp.sum(jnp.square(film_total))
    here = lax.axis_index("wide") * rows
    mine = lax.dynamic_slice_in_dim(total, here, rows, 1)
    film_mine = lax.dynamic_slice_in_dim(film_total, here, rows, 1)
    outs = []
    for r in range(0, rows, ROWS):
        take = lambda v: jnp.pad(v[:, r : r + ROWS], ((0, 0), (0, max(0, ROWS - rows)), (0, 0)))
        outs.append(
            adam(
                take(mine), take(film_mine).reshape(4 * ROWS, OBS), squares.reshape(1, 1),
                *(padded(v)[r : r + ROWS] for v in (params, first_moment, second_moment)),
            )
        )
    new = [jnp.concatenate([o[k] for o in outs], axis=0)[:rows] for k in range(1, 5)]
    return (act[None], noisy_grad[None], back, outs[0][0].reshape(()), *new)


MESH = pl.DeviceIdType.MESH


def flipped(v, bits):
    out = v
    for k in range(3):
        if bits >> k & 1:
            bit = (v // (1 << k)) % 2
            out = out + (1 << k) * (1 - 2 * bit)
    return out


class Place:
    def __init__(self):
        self.p = lax.axis_index("pair")
        self.w = lax.axis_index("wide")
        self.x, self.y = self.p % 2, self.p // 2
        self.c, self.z = self.w % 2, self.w // 2

    def line(self, l):
        return (self.p, flipped(self.w, l))

    def others(self):
        return [(flipped(self.p, k), flipped(self.w, l)) for k in range(1, 4) for l in range(1, 8)]

    def plane(self, k):
        return (flipped(self.p, k), self.w)


def greet(me):
    barrier = pltpu.get_barrier_semaphore()
    for l in range(1, 8):
        pl.semaphore_signal(barrier, inc=1, device_id=me.line(l), device_id_type=MESH)
    for k in range(1, 4):
        pl.semaphore_signal(barrier, inc=1, device_id=me.plane(k), device_id_type=MESH)


def meet(me):
    pl.semaphore_wait(pltpu.get_barrier_semaphore(), 10)


def send(source, target, sems, at, device):
    copy = pltpu.make_async_remote_copy(
        src_ref=source, dst_ref=target, send_sem=sems[0].at[at], recv_sem=sems[1].at[at],
        device_id=device, device_id_type=MESH,
    )
    copy.start()
    return copy


def fold_rows(v):
    return jnp.concatenate([v[:, q * 256 : (q + 1) * 256] for q in range(4)], axis=0)


def unfold_rows(v):
    return jnp.concatenate([v[q * 4 : (q + 1) * 4] for q in range(4)], axis=1)


def quarter_rows(parts):
    quarter = (iota(parts[0].shape, 0) >> 2) & 3
    return sum(jnp.where(quarter == q, part, 0.0) for q, part in enumerate(parts))


class Gather:
    def __init__(self, me, own, weights, seen, obs_all, film, film_part, film_line, sems):
        self.me, self.own, self.weights, self.seen, self.obs_all, self.film = me, own, weights, seen, obs_all, film
        self.film_part, self.film_line = film_part, film_line
        (self.obs_sems, self.part_sems, self.film_sems, self.more_sems,
         self.z_sems, self.x_sems, self.y_sems, self.f_sems, self.c_sems, self.local_sem) = sems
        self.z, self.x, self.y, self.f, self.c = {}, {}, {}, {}, {}

    def start_obs(self):
        me = self.me
        piece = self.obs_all.at[me.p, me.w]
        self.obs_copies = [send(piece, piece, self.obs_sems, l - 1, me.line(l)) for l in range(1, 8)]

    def start_rows(self, g):
        me = self.me
        for k in range(1, 4):
            self.z[g, k] = send(
                self.own.at[gather_group(g), me.p], self.weights.at[gather_group(g), me.p, me.z, me.c],
                self.z_sems, g * 3 + k - 1, me.line(2 * k),
            )
        if g == 0:
            self.local = pltpu.make_async_copy(self.own, self.weights.at[:, :, me.z, me.c], self.local_sem)
            self.local.start()

    def film_product(self):
        me = self.me
        for copy in self.obs_copies:
            copy.wait()
        cond = mish_parts(self.obs_all[me.p].reshape(128, 256).astype(f32))[0].astype(bf16)
        film = quarter_rows([dot_nt(cond, self.film[:, q * 256 : (q + 1) * 256]) for q in range(4)])
        row, col = iota((64, 128), 0), iota((64, 128), 1)
        pick = one_hot(((row >> 3) == (col >> 4)) & ((row & 7) == (col & 3)))
        self.film_part[...] = sum(dot_nn(pick, part) for part in split3(film)).reshape(8, 8, 128)
        self.part_copies = [
            send(self.film_part.at[flipped(me.w, l)], self.film_line.at[me.w], self.part_sems, l - 1, me.line(l))
            for l in range(1, 8)
        ]
        self.film_line[me.w] = self.film_part[me.w]

    def film_hop(self):
        me = self.me
        for copy in self.part_copies:
            copy.wait()
        for k in range(4):
            self.seen[me.p, k] = self.film_line[2 * k] + pltpu.roll(self.film_line[2 * k + 1], 4, 0)
        piece = self.seen.at[me.p]
        self.film_copies = [send(piece, piece, self.film_sems, k - 1, me.plane(k)) for k in range(1, 4)]

    def obs_hop(self):
        me = self.me
        piece = self.obs_all.at[me.p]
        self.more_copies = [send(piece, piece, self.more_sems, k - 1, me.plane(k)) for k in range(1, 4)]

    def film_done(self):
        for copy in self.film_copies:
            copy.wait()

    def first_hop(self, g):
        me = self.me
        for k in range(1, 4):
            self.z[g, k].wait_recv()
            piece = self.weights.at[gather_group(g), me.p, flipped(me.z, k), me.c]
            self.x[g, k] = send(piece, piece, self.x_sems, g * 3 + k - 1, me.plane(1))
            self.y[g, k] = send(piece, piece, self.y_sems, g * 3 + k - 1, me.plane(2))
            if g in GATHER_DIRECT:
                self.f[g, k] = send(piece, piece, self.f_sems, g * 3 + k - 1, me.plane(3))

    def second_hop(self, g):
        me = self.me
        for k in range(1, 4):
            self.x[g, k].wait_recv()
            self.y[g, k].wait_recv()
            if g in GATHER_DIRECT:
                continue
            along_y = (g + k) % 2 == 0
            piece = self.weights.at[gather_group(g), flipped(me.p, 1 if along_y else 2), flipped(me.z, k), me.c]
            self.f[g, k] = send(piece, piece, self.f_sems, g * 3 + k - 1, me.plane(2 if along_y else 1))

    def last_hop(self, g):
        if g == 0:
            self.local.wait()
        if g in GATHER_DIRECT:
            self.second_hop(g)
        for k in range(1, 4):
            self.f[g, k].wait_recv()
        piece = self.weights.at[gather_group(g), :, :, self.me.c]
        self.c[g] = send(piece, piece, self.c_sems, g, self.me.line(1))

    def arrived(self, g):
        self.c[g].wait_recv()

    def finish(self):
        for copy in self.more_copies:
            copy.wait()
        for copies in (self.z, self.x, self.y, self.f, self.c):
            for copy in copies.values():
                copy.wait_send()


class Scatter:
    def __init__(self, me, grad, film_grad, obs_all, film, out, film_out, back, square, buffers, sems):
        self.me, self.grad, self.film_grad, self.obs_all, self.film = me, grad, film_grad, obs_all, film
        self.out, self.film_out, self.back, self.square = out, film_out, back, square
        (self.half, self.core, self.xb, self.yb, self.ub, self.vb, self.zb, self.zq, self.pq,
         self.film_all, self.back_part, self.back_line, self.cond, self.all_squares) = buffers
        (self.g_sems, self.h_sems, self.b_sems, self.c_sems, self.x_sems, self.y_sems, self.u_sems, self.v_sems,
         self.z_sems, self.r_sems, self.n_sems) = sems
        self.x, self.y, self.u, self.v, self.z, self.r, self.c, self.q = {}, {}, {}, {}, {}, {}, {}, {}
        self.squares = []

    def start(self, g):
        me = self.me
        self.c[g] = send(
            self.grad.at[group(g), :, :, 1 - me.c], self.core.at[group(g)], self.c_sems, g, me.line(1)
        )

    def core_sum(self, g):
        me, (first, last) = self.me, GROUPS[g]
        self.c[g].wait_recv()

        def add(i, _):
            j, q = first + i // 4, i % 4
            total = self.grad[j, q, :, me.c].astype(f32) + self.core[j, q].astype(f32)
            self.half[j, q // 2, q % 2] = total.astype(bf16)
            return 0

        lax.fori_loop(0, (last - first) * 4, add, 0)
        if g == Z_FIRST:
            for k in range(1, 4):
                self.z[g, k] = send(
                    self.half.at[group(g), :, :, flipped(me.z, k)], self.zq.at[k - 1],
                    self.z_sems, g * 3 + k - 1, me.line(2 * k),
                )
            return
        self.x[g] = send(
            self.half.at[group(g), :, 1 - me.x, LOW], self.xb.at[group(g)], self.x_sems, g, me.plane(1)
        )
        self.y[g] = send(
            self.half.at[group(g), 1 - me.y, :, HIGH], self.yb.at[group(g)], self.y_sems, g, me.plane(2)
        )

    def z_sum(self, g):
        me, half, (first, last) = self.me, self.half, GROUPS[g]
        for k in range(1, 4):
            self.z[g, k].wait_recv()
        for j in range(first, last):
            total = half[j, :, :, me.z].astype(f32)
            for k in range(3):
                total = total + self.zq[k, j - first].astype(f32)
            half[j, :, :, me.z] = total.astype(bf16)
        for k, sems in enumerate((self.x_sems, self.y_sems, self.u_sems)):
            other = flipped(me.p, k + 1)
            self.q[k] = send(
                half.at[group(g), other // 2, other % 2, me.z], self.pq.at[k], sems, g, me.plane(k + 1)
            )

    def plane_sum(self, g):
        for k in range(3):
            self.q[k].wait_recv()
        self.finish_sum(g, [lambda j, k=k: self.pq[k, j - GROUPS[g][0]] for k in range(3)])

    def first_sum(self, g):
        me, half, (first, last) = self.me, self.half, GROUPS[g]
        self.x[g].wait_recv()

        def add_x(i, _):
            j, q = first + i // 2, i % 2
            total = half[j, q, me.x, LOW].astype(f32) + self.xb[j, q].astype(f32)
            half[j, q, me.x, LOW] = total.astype(bf16)
            return 0

        lax.fori_loop(0, (last - first) * 2, add_x, 0)
        self.u[g] = send(half.at[group(g), 1 - me.y, me.x, LOW], self.ub.at[group(g)], self.u_sems, g, me.plane(2))
        self.y[g].wait_recv()

        def add_y(i, _):
            j, q = first + i // 2, i % 2
            total = half[j, me.y, q, HIGH].astype(f32) + self.yb[j, q].astype(f32)
            half[j, me.y, q, HIGH] = total.astype(bf16)
            return 0

        lax.fori_loop(0, (last - first) * 2, add_y, 0)
        self.v[g] = send(half.at[group(g), me.y, 1 - me.x, HIGH], self.vb.at[group(g)], self.v_sems, g, me.plane(1))

    def second_sum(self, g):
        me, half = self.me, self.half
        self.u[g].wait_recv()
        self.v[g].wait_recv()
        for j in range(*GROUPS[g]):
            total = half[j, me.y, me.x, LOW].astype(f32) + self.ub[j].astype(f32)
            half[j, me.y, me.x, LOW] = total.astype(bf16)
            total = half[j, me.y, me.x, HIGH].astype(f32) + self.vb[j].astype(f32)
            half[j, me.y, me.x, HIGH] = total.astype(bf16)
        for k in range(1, 4):
            self.z[g, k] = send(
                half.at[group(g), me.y, me.x, flipped(me.z, k)], self.zb.at[k - 1, group(g)],
                self.z_sems, g * 3 + k - 1, me.line(2 * k),
            )

    def last_sum(self, g):
        for k in range(1, 4):
            self.z[g, k].wait_recv()
        self.finish_sum(g, [lambda j, k=k: self.zb[k, j] for k in range(3)])

    def finish_sum(self, g, terms):
        me = self.me
        for j in range(*GROUPS[g]):
            total = self.half[j, me.y, me.x, me.z].astype(f32)
            for term in terms:
                total = total + term(j).astype(f32)
            total = total.astype(bf16)
            self.out[j, me.p] = total
            self.squares.append(jnp.sum(jnp.square(total.astype(f32)).reshape(4, 8, 256), axis=0))
        piece = self.out.at[group(g), me.p]
        for k in range(1, 4):
            self.r[g, k] = send(piece, piece, self.r_sems, g * 3 + k - 1, me.plane(k))

    def film_start(self):
        me = self.me
        self.film_all[me.p, me.w] = self.film_grad[me.w]
        self.g = [
            send(self.film_grad.at[flipped(me.w, l)], self.film_all.at[me.p, me.w], self.g_sems, l - 1, me.line(l))
            for l in range(1, 8)
        ]

    def film_hop(self):
        me = self.me
        for copy in self.g:
            copy.wait()
        piece = self.film_all.at[me.p]
        self.h = [send(piece, piece, self.h_sems, k - 1, me.plane(k)) for k in range(1, 4)]

    def film_inputs(self):
        row, col = iota((128, 512), 0), iota((128, 512), 1)
        same = ((row >> 4) == ((col >> 4) & 7)) & (((row >> 2) & 3) == (col >> 7)) & ((row & 3) == (col & 3))
        seen_all = self.obs_all[...].reshape(512, 256)
        for q in range(4):
            pick = one_hot(same & (((col >> 2) & 3) == q))
            self.cond[q] = mish_parts(dot_nn(pick, seen_all))[0].astype(bf16)

    def film_products(self):
        me = self.me
        for copy in self.h:
            copy.wait()
        copies = [self.film_all[k].reshape(128, 128).astype(f32) for k in range(4)]
        total = split2((copies[0] + copies[1]) + (copies[2] + copies[3]))
        row, col = iota((128, 128), 0), iota((128, 128), 1)
        mine = one_hot(((row >> 4) == (col >> 4)) & ((col & 15) == 4 * me.p + (row & 3)))
        rows = [dot_nn(mine, part).astype(bf16) for part in total]
        parts = [
            dot_nn(rows[0], self.film[:, q * 256 : (q + 1) * 256])
            + dot_nn(rows[1], self.film[:, q * 256 : (q + 1) * 256])
            for q in range(4)
        ]
        self.back_part[...] = quarter_rows(parts).astype(bf16).reshape(8, 16, 256)
        self.b = [
            send(self.back_part.at[flipped(me.w, l)], self.back_line.at[me.w], self.b_sems, l - 1, me.line(l))
            for l in range(1, 8)
        ]
        self.back_line[me.w] = self.back_part[me.w]
        square = jnp.zeros((8, 256), f32)
        turned = [part.T for part in total]
        for q in range(4):
            cond = self.cond[q]
            product = dot_nn(turned[0], cond) + dot_nn(turned[1], cond)
            self.film_out[:, q * 256 : (q + 1) * 256] = product
            square = square + jnp.sum(jnp.square(product).reshape(16, 8, 256), axis=0)
        self.squares.append(0.25 * square)

    def film_back(self):
        me = self.me
        for copy in self.b:
            copy.wait()
        total = jnp.sum(self.back_line[...].astype(f32), axis=0)
        slope = mish_parts(self.obs_all[me.p, me.w].astype(f32))[1]
        self.back[0] = unfold_rows(total * slope)

    def norm(self, hello):
        me = self.me
        total = sum(self.squares)
        piece = self.all_squares.at[me.p, me.w]
        self.all_squares[me.p, me.w] = jnp.sum(total[:, :128] + total[:, 128:], axis=0, keepdims=True)
        pl.semaphore_wait(hello, len(me.others()))
        copies = [
            send(piece, piece, self.n_sems, i - 1, (flipped(me.p, i % 4), flipped(me.w, i // 4))) for i in range(1, 32)
        ]
        for copy in copies + list(self.r.values()):
            copy.wait()
        self.square[...] = jnp.sum(self.all_squares[...].reshape(32, 128), axis=0, keepdims=True)
        for copies in (self.c, self.x, self.y, self.u, self.v, self.z, self.q):
            for copy in copies.values():
                copy.wait_send()


GATHER_GROUPS = ((0, 1), (1, 3), (3, 5), (5, 7), (7, 9))
GATHER_DIRECT = (3, 4)
GROUPS = ((0, 1), (1, 3), (3, 5), (5, 7), (7, 9))
Z_FIRST = 4
LOW, HIGH = pl.ds(0, 2), pl.ds(2, 2)


def group(g):
    return pl.ds(GROUPS[g][0], GROUPS[g][1] - GROUPS[g][0])


def gather_group(g):
    return pl.ds(GATHER_GROUPS[g][0], GATHER_GROUPS[g][1] - GATHER_GROUPS[g][0])


def step_kernel(*refs):
    (params, order, obs, slots, noisy, mask, levels, cotangent, table,
     act, noisy_grad, back, out, film_out, square,
     own, weights, seen, obs_all, film, film_part, film_line, grad, film_grad) = refs[:24]
    buffers, sems, hello = refs[24:38], refs[38:-1], refs[-1]
    pairs = [(sems[2 * i], sems[2 * i + 1]) for i in range(20)]
    me = Place()
    gather = Gather(me, own, weights, seen, obs_all, film, film_part, film_line, pairs[:9] + [sems[40]])
    scatter = Scatter(me, grad, film_grad, obs_all, film, out, film_out, back, square, buffers, pairs[9:])
    obs_all[me.p, me.w] = fold_rows(obs[0].astype(f32)).astype(bf16)
    greet(me)
    pack_rows(params, order, own, film)
    meet(me)
    gather.start_obs()
    gather.start_rows(0)
    gather.start_rows(1)

    def reach(point):
        if point == 0:
            gather.first_hop(0)
            gather.film_product()
            for g in range(2, len(GATHER_GROUPS)):
                gather.start_rows(g)
            gather.first_hop(1)
            gather.second_hop(0)
            gather.film_hop()
            gather.first_hop(2)
            gather.second_hop(1)
            gather.last_hop(0)
            for device in me.others():
                pl.semaphore_signal(hello, inc=1, device_id=device, device_id_type=MESH)
            gather.first_hop(3)
            gather.second_hop(2)
            gather.last_hop(1)
            gather.arrived(0)
        if point == 1:
            gather.film_done()
        if point == 2:
            gather.first_hop(4)
            gather.arrived(1)
        if point == 3:
            gather.last_hop(2)
            gather.last_hop(3)
            gather.arrived(2)
        if point == 5:
            gather.last_hop(4)
            gather.arrived(3)
        if point == 6:
            gather.obs_hop()
            gather.arrived(4)
        if point == 8:
            scatter.start(4)
        if point == 9:
            scatter.core_sum(4)
            scatter.start(3)
        if point == 10:
            scatter.core_sum(3)
        if point == 11:
            scatter.start(2)
        if point == 12:
            scatter.core_sum(2)
            scatter.first_sum(3)
        if point == 13:
            scatter.film_start()
            scatter.start(1)

    train_body(
        Stacked(weights), seen, slots, noisy, mask, levels, cotangent, table,
        act, noisy_grad, Stacked(grad), film_grad, reach,
    )
    scatter.start(0)
    scatter.core_sum(1)
    scatter.first_sum(2)
    scatter.core_sum(0)
    scatter.second_sum(3)
    scatter.z_sum(4)
    scatter.first_sum(1)
    scatter.film_hop()
    scatter.second_sum(2)
    scatter.first_sum(0)
    gather.finish()
    scatter.film_inputs()
    scatter.plane_sum(4)
    scatter.second_sum(1)
    scatter.film_products()
    scatter.second_sum(0)
    scatter.last_sum(3)
    scatter.last_sum(2)
    scatter.last_sum(1)
    scatter.film_back()
    scatter.last_sum(0)
    scatter.norm(hello)


class Stacked:
    def __init__(self, ref):
        self.ref = ref

    def _split(self, key):
        if not isinstance(key, tuple):
            return key, slice(None)
        return key[0], key[2]

    def __getitem__(self, key):
        block, cols = self._split(key)
        value = self.ref[block // 4, block % 4, :, :, :, cols]
        return value.reshape(256, value.shape[-1])

    def __setitem__(self, key, value):
        block, cols = self._split(key)
        self.ref[block // 4, block % 4, :, :, :, cols] = value.reshape(4, 2, ROWS, value.shape[-1])


def step(params, obs, slots, noisy, mask, levels, cotangent):
    vmem = pl.BlockSpec(memory_space=pltpu.VMEM)
    pair = lambda n: [pltpu.SemaphoreType.DMA((n,))] * 2
    n, count, parts = NB // 4, len(GROUPS), len(GATHER_GROUPS)
    low = lambda *shape: pltpu.VMEM(shape, bf16)
    return pl.pallas_call(
        step_kernel,
        out_shape=(
            jax.ShapeDtypeStruct((C, 256), bf16),
            jax.ShapeDtypeStruct((ADIM, 256), f32),
            jax.ShapeDtypeStruct((1, 4, OBS), f32),
            jax.ShapeDtypeStruct((n, 4, ROWS, 256), bf16),
            jax.ShapeDtypeStruct((4 * ROWS, OBS), f32),
            jax.ShapeDtypeStruct((1, 128), f32),
        ),
        in_specs=[vmem] * 9,
        out_specs=(vmem,) * 6,
        scratch_shapes=[
            low(n, 4, ROWS, 256),
            low(n, 4, 4, 2, ROWS, 256),
            pltpu.VMEM((4, 4, 8, 128), f32),
            low(4, 8, 16, 256),
            low(4 * ROWS, OBS),
            pltpu.VMEM((8, 8, 128), f32),
            pltpu.VMEM((8, 8, 128), f32),
            low(n, 4, 4, 2, ROWS, 256),
            low(8, SAM, 128),
            low(n, 2, 2, 4, ROWS, 256),
            low(n, 4, 4, ROWS, 256),
            low(n, 2, 2, ROWS, 256),
            low(n, 2, 2, ROWS, 256),
            low(n, 2, ROWS, 256),
            low(n, 2, ROWS, 256),
            low(3, n, ROWS, 256),
            low(3, GROUPS[Z_FIRST][1] - GROUPS[Z_FIRST][0], 2, 2, ROWS, 256),
            low(3, GROUPS[Z_FIRST][1] - GROUPS[Z_FIRST][0], ROWS, 256),
            low(4, 8, 16, 128),
            low(8, 16, 256),
            low(8, 16, 256),
            low(4, 128, 256),
            pltpu.VMEM((4, 8, 1, 128), f32),
            *pair(7), *pair(7), *pair(3), *pair(3),
            *pair(3 * parts), *pair(3 * parts), *pair(3 * parts), *pair(3 * parts), *pair(parts),
            *pair(7), *pair(3), *pair(7),
            *pair(count), *pair(count), *pair(count), *pair(count), *pair(count),
            *pair(3 * count), *pair(3 * count), *pair(31),
            pltpu.SemaphoreType.DMA,
            pltpu.SemaphoreType.REGULAR,
        ],
        compiler_params=pltpu.CompilerParams(collective_id=0, has_side_effects=True, vmem_limit_bytes=60 << 20),
        name="step",
    )(params, jnp.asarray(first_order(), bf16), obs, slots, noisy, mask, levels, cotangent, jnp.asarray(level_table(), bf16))


def local_fast(noisy, action_mask, time_index, obs_embed, obs_slot, cotangent, params, first_moment, second_moment):
    act, noisy_grad, back, total, film_total, squares = step(
        params, obs_embed, obs_slot[None], noisy[0], action_mask, time_index, cotangent[0]
    )
    norm, *new, act, noisy_grad, back = adam(
        total.reshape(NB, ROWS, 256), film_total, squares, params, first_moment, second_moment,
        (act, noisy_grad, back), ((1, C, 256), (ADIM, 1, 256), (1, 4, OBS)),
    )
    return (act, noisy_grad.transpose(1, 0, 2), back, norm.reshape(()), *new)


def solution(mesh):
    in_specs = (
        P("pair", None, "wide"),
        P(None, "wide"),
        P("pair", "wide"),
        P("pair", "wide", None),
        P("wide"),
        P("pair", None, "wide"),
        P("wide", None),
        P("wide", None),
        P("wide", None),
    )
    out_specs = (
        P("pair", None, "wide"),
        P("pair", None, "wide"),
        P("pair", "wide", None),
        P(),
        P("wide", None),
        P("wide", None),
        P("wide", None),
        P("wide", None),
    )
    fast = mesh.shape["pair"] == 4 and mesh.shape["wide"] == 8
    return jax.shard_map(local_fast if fast else local_plain, mesh=mesh, in_specs=in_specs, out_specs=out_specs, check_vma=False)
```

```python
import functools
import math

import jax
import jax.numpy as jnp
import numpy as np
from jax import lax
from jax.experimental import pallas as pl
from jax.experimental.pallas import tpu as pltpu
from jax.sharding import PartitionSpec as P

C = 256
OBS = 1024
TE = 128
TH = 512
ADIM = 10
FR = 16
LEVELS = 40
ADAM_STEP = 7
Q = 12627
SAM = 16
ROWS = 32
NB = 36

sigma_top = 80.0 ** (1.0 / 7.0)
sigma_low = 0.002 ** (1.0 / 7.0)
clip_limit = 1.0
learn_rate = 0.02
decay_first = 0.5
decay_second = 0.5
adam_eps = 1e-08
weight_decay = 0.01
norm_eps = 1e-05

f32 = jnp.float32
bf16 = jnp.bfloat16

AT_DOWN_RES = 1330
AT_TAIL = 12604
TAIL = 23
AT_FILM = (1340, 2492, 9788, 10940)
AT_TIME = (12092, 12348)
AT_UP_RES = 9276
B_MISC, B_INNER, B_OUTER, B_FILM = 0, 1, 2, 3
B_DS, B_POOL, B_SPREAD, B_UF, B_US, B_UR = 5, 10, 13, 17, 27, 32
B_NONE = (34, 35)
LANE_TAIL = 64
CONVS = (
    (50, 5, 2, lambda t, h: B_DS + t),
    (5436, 5, 4, lambda t, h: B_UF + 2 * t + h // 2),
    (7996, 5, 2, lambda t, h: B_US + t),
    (3644, 3, 2, lambda t, h: B_POOL + t),
    (4412, 4, 2, lambda t, h: B_SPREAD + t),
)
(T_BIAS_A, T_BIAS_B, T_OUT, D_B1, D_G1, D_S1, D_FS, D_FO, D_B2, D_G2, D_S2, D_RB, PB, SB,
 U_B1, U_G1, U_S1, U_FS, U_FO, U_B2, U_G2, U_S2, U_RB) = range(TAIL)


def dot_nt(a, b):
    return lax.dot_general(a, b, (((1,), (1,)), ((), ())), preferred_element_type=f32)


def dot_nn(a, b):
    return lax.dot_general(a, b, (((1,), (0,)), ((), ())), preferred_element_type=f32)


def dot_tn(a, b):
    return lax.dot_general(a, b, (((0,), (0,)), ((), ())), preferred_element_type=f32)


def split2(v):
    high = v.astype(bf16)
    return high, (v - high.astype(f32)).astype(bf16)


def split3(v):
    high, rest = v.astype(bf16), None
    rest = v - high.astype(f32)
    mid = rest.astype(bf16)
    return high, mid, (rest - mid.astype(f32)).astype(bf16)


def iota(shape, dim):
    return lax.broadcasted_iota(jnp.int32, shape, dim)


def one_hot(condition):
    return jnp.where(condition, 1.0, 0.0).astype(bf16)


def tap_order(taps):
    n = 128 * taps
    row = lax.broadcasted_iota(jnp.int32, (n, n), 0)
    col = lax.broadcasted_iota(jnp.int32, (1, n), 1)
    source = (col & 127) * taps + (col >> 7)
    return jnp.where(row == source, 1.0, 0.0).astype(bf16)


def first_order():
    table = np.zeros((128, 128), np.float32)
    for i in range(ADIM):
        for t in range(5):
            table[i * 5 + t, t * ADIM + i] = 1.0
    return table


def level_table():
    levels = np.arange(LEVELS, dtype=np.float64)
    tau = 250.0 * 7.0 * np.log(sigma_top + levels / (LEVELS - 1) * (sigma_low - sigma_top))
    freq = np.exp(-math.log(10000.0) * np.arange(TE // 2) / (TE // 2 - 1))
    angles = tau[:, None] * freq[None, :]
    table = np.zeros((64, TE), np.float32)
    table[:LEVELS] = np.concatenate([np.sin(angles), np.cos(angles)], axis=1)
    return table


def pack_kernel(params_ref, order_ref, own_ref, film_ref):
    pack_rows(params_ref, order_ref, own_ref, film_ref)


class Blocks:
    def __init__(self, ref):
        self.ref = ref

    def _at(self, key):
        block, rest = (key[0], key[1:]) if isinstance(key, tuple) else (key, ())
        return (block // 4, block % 4) + rest

    def __getitem__(self, key):
        return self.ref[self._at(key)]

    def __setitem__(self, key, value):
        self.ref[self._at(key)] = value


def pack_rows(params_ref, order_ref, own_ref, film_ref):
    pack_first(params_ref, order_ref, own_ref)
    pack_rest(params_ref, own_ref, film_ref)


def pack_first(params_ref, order_ref, own_ref):
    own_ref = Blocks(own_ref)

    def low(start, width):
        return params_ref[:, start : start + width].astype(bf16)

    first = dot_nn(low(0, 128), order_ref[...])
    pieces = [
        first[:, :50],
        params_ref[:, AT_DOWN_RES : AT_DOWN_RES + ADIM],
        jnp.zeros((ROWS, LANE_TAIL - 60), f32),
        params_ref[:, AT_TAIL : AT_TAIL + TAIL],
        jnp.zeros((ROWS, 256 - LANE_TAIL - TAIL), f32),
    ]
    own_ref[B_MISC] = jnp.concatenate(pieces, axis=1).astype(bf16)
    own_ref[B_INNER] = low(AT_TIME[0], 256)
    own_ref[B_OUTER] = low(AT_TIME[1], 256)
    for q in range(4):
        own_ref[B_FILM + q // 2, :, (q % 2) * 128 : (q % 2) * 128 + 128] = low(AT_FILM[q] + OBS, TE)


def pack_rest(params_ref, own_ref, film_ref):
    own_ref = Blocks(own_ref)

    def low(start, width):
        return params_ref[:, start : start + width].astype(bf16)

    for q in range(4):
        film_ref[q * ROWS : (q + 1) * ROWS] = low(AT_FILM[q], OBS)
    own_ref[B_UR] = low(AT_UP_RES, 256)
    own_ref[B_UR + 1] = low(AT_UP_RES + 256, 256)
    for b in B_NONE:
        own_ref[b] = jnp.zeros((ROWS, 256), bf16)
    for taps in (5, 3, 4):
        places = [(at, h, block) for at, k, groups, block in CONVS if k == taps for h in range(groups)]
        stacked = jnp.concatenate([low(at + h * 128 * taps, 128 * taps) for at, h, _ in places], axis=0)
        moved = dot_nn(stacked, tap_order(taps)).astype(bf16)
        for n, (_, h, block) in enumerate(places):
            for t in range(taps):
                own_ref[block(t, h), :, (h % 2) * 128 : (h % 2) * 128 + 128] = moved[
                    n * ROWS : (n + 1) * ROWS, t * 128 : (t + 1) * 128
                ]


def pack(params):
    vmem = pl.BlockSpec(memory_space=pltpu.VMEM)
    return pl.pallas_call(
        pack_kernel,
        out_shape=(
            jax.ShapeDtypeStruct((NB // 4, 4, ROWS, 256), bf16),
            jax.ShapeDtypeStruct((4 * ROWS, OBS), bf16),
        ),
        in_specs=[vmem, vmem],
        out_specs=(vmem, vmem),
        compiler_params=pltpu.CompilerParams(vmem_limit_bytes=40 << 20),
        name="pack",
    )(params, jnp.asarray(first_order(), bf16))


def mish_parts(v):
    e = jnp.exp(jnp.minimum(v, 20.0))
    n = e * (e + 2.0)
    r = 1.0 / (n + 2.0)
    t = n * r
    return v * t, t + 4.0 * v * (e * r) * ((e + 1.0) * r)


def step_frames(v, step):
    if step == 0:
        return v
    zeros = jnp.zeros((SAM * abs(step), v.shape[1]), v.dtype)
    if step > 0:
        return jnp.concatenate([v[SAM * step :], zeros], axis=0)
    return jnp.concatenate([zeros, v[: SAM * step]], axis=0)


def over_frames(v):
    return jnp.sum(v.reshape(-1, SAM, v.shape[1]), axis=0)


def each_frame(v, s):
    return v.reshape(-1, SAM, v.shape[1]), s[None]


def group_means(values, ones):
    parts = [p for v in values for p in split3(v)]
    sums = dot_nn(jnp.concatenate(parts, axis=0), ones)
    out = []
    for i in range(len(values)):
        a, b, c = (sums[(3 * i + k) * SAM : (3 * i + k + 1) * SAM] for k in range(3))
        out.append((a + (b + c)) * (1.0 / (32 * FR)))
    return out


def minus(v, s):
    a, b = each_frame(v, s)
    return (a - b).reshape(v.shape)


def times(v, s):
    a, b = each_frame(v, s)
    return (a * b).reshape(v.shape)


def plus(v, s):
    a, b = each_frame(v, s)
    return (a + b).reshape(v.shape)


def norm_forward(before, gain, shift, ones):
    center, square = group_means([over_frames(before), over_frames(before * before)], ones)
    scale = lax.rsqrt(jnp.maximum(square - center * center, 0.0) + norm_eps)
    away = minus(before, center)
    normal = times(away, scale)
    act, slope = mish_parts(normal * gain + shift)
    return act, normal, slope, scale


def norm_backward(grad_act, normal, slope, scale, gain, ones):
    grad_out = grad_act * slope
    shift_rows = over_frames(grad_out)
    gain_rows = over_frames(grad_out * normal)
    mean_grad, mean_both = group_means([shift_rows * gain, gain_rows * gain], ones)
    inner = minus(grad_out * gain, mean_grad) - times(normal, mean_both)
    return (
        times(inner, scale),
        jnp.sum(gain_rows, axis=0, keepdims=True),
        jnp.sum(shift_rows, axis=0, keepdims=True),
    )


def conv_forward(source, weight):
    total = dot_nt(step_frames(source, -2), weight(0))
    for t in range(1, 5):
        total = total + dot_nt(step_frames(source, t - 2), weight(t))
    return total


def conv_source(grad_low, weight):
    total = dot_nn(step_frames(grad_low, 2), weight(0))
    for t in range(1, 5):
        total = total + dot_nn(step_frames(grad_low, 2 - t), weight(t))
    return total


def row_sum(v):
    return jnp.sum(over_frames(v), axis=0, keepdims=True)


def halves(v):
    cube = v.reshape(FR // 2, 2, SAM, v.shape[1])
    return cube[:, 0].reshape(-1, v.shape[1]), cube[:, 1].reshape(-1, v.shape[1])


def interleave(even, odd):
    width = even.shape[1]
    pair = [v.reshape(FR // 2, 1, SAM, width) for v in (even, odd)]
    return jnp.concatenate(pair, axis=1).reshape(FR * SAM, width)


def train_kernel(*refs):
    train_body(*refs, lambda point: None)


def train_body(
    w_ref, seen_ref, slot_ref, noisy_ref, mask_ref, level_ref, cot_ref, table_ref,
    act_ref, noisy_grad_ref, grad_ref, film_grad_ref, reach,
):
    row = iota((256, 256), 0)
    col = iota((256, 256), 1)
    ones = jnp.where((row >> 5) == (col >> 5), 1.0, 0.0).astype(bf16)
    swap = jnp.where(col == ((row & 15) << 4) + (row >> 4), 1.0, 0.0).astype(bf16)
    for b in B_NONE:
        grad_ref[b] = jnp.zeros((256, 256), bf16)
    spread_mask = one_hot((iota((SAM, 256), 1) >> 4) == iota((SAM, 256), 0))
    keep = dot_nn(mask_ref[...].astype(f32).astype(bf16), spread_mask)
    start_cols = noisy_ref[...].astype(f32) * keep
    start_cols = jnp.concatenate([start_cols, jnp.zeros((6, 256), f32)], axis=0).astype(bf16)
    start = dot_nt(swap, start_cols).astype(bf16)
    lane16 = iota((16, 128), 1)
    row16 = iota((16, 128), 0)
    inputs = jnp.zeros((256, 128), f32)
    for t in range(5):
        place = lane16 == row16 + t * ADIM
        if t == 2:
            place = place | (lane16 == row16 + 50)
        inputs = inputs + dot_nn(step_frames(start, t - 2), one_hot(place & (row16 < ADIM)))
    inputs = inputs.astype(bf16)
    cot_high, cot_low = split2(cot_ref[...])
    upstream = dot_nt(swap, cot_high) + dot_nt(swap, cot_low)
    upstream_low = upstream.astype(bf16)
    at_level = one_hot(iota((64, SAM), 0) == level_ref[...])
    feats = dot_tn(at_level, table_ref[...]).astype(bf16)
    reach(0)
    misc = w_ref[B_MISC, :, :128]
    lane = iota((256, 128), 1)
    misc_first = jnp.where(lane < 50, misc, jnp.zeros_like(misc))
    misc_res = jnp.where((lane >= 50) & (lane < 60), misc, jnp.zeros_like(misc))
    singles = misc.astype(f32).T[LANE_TAIL : LANE_TAIL + 32]
    vec = lambda k: singles[k : k + 1]

    inner = [w_ref[B_INNER, :, j * 128 : (j + 1) * 128] for j in range(2)]
    outer = [w_ref[B_OUTER, :, j * 128 : (j + 1) * 128] for j in range(2)]
    film_time = lambda q: w_ref[B_FILM + q // 2, :, (q % 2) * 128 : (q % 2) * 128 + 128]
    hidden = [mish_parts(dot_nt(feats, inner[j]) + vec(T_BIAS_A + j)) for j in range(2)]
    hidden_low = [h[0].astype(bf16) for h in hidden]
    embed = dot_nn(hidden_low[0], outer[0]) + dot_nn(hidden_low[1], outer[1]) + vec(T_OUT)[:, :TE]
    cond, cond_slope = mish_parts(embed)
    cond_low = cond.astype(bf16)
    pre = dot_nt(inputs, misc_first) + vec(D_B1)
    act_one, normal_one, slope_one, scale_one = norm_forward(pre, vec(D_G1), vec(D_S1), ones)
    reach(1)
    at_slot = one_hot(iota((SAM, SAM), 0) == slot_ref[...])
    line = iota((32, SAM), 0)
    seen_film = jnp.concatenate([seen_ref[:, k].reshape(32, 128) for k in range(4)], axis=1)
    seen_film = split3(seen_film)
    sides = []
    for side in range(2):
        at_line = one_hot(((line >> 3) * 4 + (line & 3) == slot_ref[...]) & ((line >> 2) & 1 == side))
        sides.append(sum(dot_tn(at_line, part) for part in seen_film))
    seen_film = jnp.concatenate(
        [sides[k % 2][:, (k // 2) * 128 : (k // 2) * 128 + 128] for k in range(8)], axis=1
    )
    spans = lambda v, q: jnp.concatenate([v[:, k * 128 + q * 32 : k * 128 + q * 32 + 32] for k in range(8)], axis=1)
    film_of = lambda q: spans(seen_film, q) + dot_nt(cond_low, film_time(q)) + vec((D_FS, D_FO, U_FS, U_FO)[q])
    film = [film_of(0), film_of(1)]
    mid_one = plus(times(act_one, film[0]), film[1]).astype(bf16)
    reach(2)
    down = lambda t: w_ref[B_DS + t]
    pre = conv_forward(mid_one, down) + vec(D_B2)
    act, normal_two, slope_two, scale_two = norm_forward(pre, vec(D_G2), vec(D_S2), ones)
    skip = (act + dot_nt(inputs, misc_res) + vec(D_RB)).astype(bf16)
    reach(3)
    even, odd = halves(skip)
    odd_prev = step_frames(odd, -1)
    pool_sources = (odd_prev, even, odd)
    pooled = sum(dot_nt(s, w_ref[B_POOL + t]) for t, s in enumerate(pool_sources)) + vec(PB)
    pooled = pooled.astype(bf16)
    reach(4)
    pooled_prev = step_frames(pooled, -1)
    pooled_next = step_frames(pooled, 1)
    even_out = dot_nt(pooled, w_ref[B_SPREAD + 1]) + dot_nt(pooled_prev, w_ref[B_SPREAD + 3])
    odd_out = dot_nt(pooled_next, w_ref[B_SPREAD]) + dot_nt(pooled, w_ref[B_SPREAD + 2])
    wide = (interleave(even_out, odd_out) + vec(SB)).astype(bf16)
    joined = (wide, skip)
    turned = upstream_low.T
    for h in range(2):
        grad_ref[B_UR + h] = dot_nn(turned, joined[h]).astype(bf16)
    reach(5)
    up_first = [lambda t, h=h: w_ref[B_UF + 2 * t + h] for h in range(2)]
    pre = conv_forward(wide, up_first[0]) + conv_forward(skip, up_first[1]) + vec(U_B1)
    act_three, normal_three, slope_three, scale_three = norm_forward(pre, vec(U_G1), vec(U_S1), ones)
    film += [film_of(2), film_of(3)]
    mid_three = plus(times(act_three, film[2]), film[3]).astype(bf16)
    reach(6)
    up = lambda t: w_ref[B_US + t]
    pre = conv_forward(mid_three, up) + vec(U_B2)
    act, normal_four, slope_four, scale_four = norm_forward(pre, vec(U_G2), vec(U_S2), ones)
    act_four = act

    single_grads = {}

    def conv_weights(grad_low, source, block):
        turned = grad_low.T
        for t in range(5):
            grad_ref[block(t)] = dot_nn(turned, step_frames(source, t - 2)).astype(bf16)

    reach(7)
    grad, single_grads[U_G2], single_grads[U_S2] = norm_backward(
        upstream, normal_four, slope_four, scale_four, vec(U_G2), ones
    )
    single_grads[U_B2] = row_sum(grad)
    low = grad.astype(bf16)
    conv_weights(low, mid_three, lambda t: B_US + t)
    reach(8)
    grad_mid = conv_source(low, up)
    shift_three = over_frames(grad_mid)
    gain_three = over_frames(grad_mid * act_three)
    grad, single_grads[U_G1], single_grads[U_S1] = norm_backward(
        times(grad_mid, film[2]), normal_three, slope_three, scale_three, vec(U_G1), ones
    )
    single_grads[U_B1] = row_sum(grad)
    low = grad.astype(bf16)
    reach(15)
    for h in range(2):
        conv_weights(low, joined[h], lambda t, h=h: B_UF + 2 * t + h)
    single_grads[U_RB] = row_sum(upstream)
    reach(9)
    grad_wide = conv_source(low, up_first[0]) + dot_nn(upstream_low, w_ref[B_UR])
    grad_skip = conv_source(low, up_first[1]) + dot_nn(upstream_low, w_ref[B_UR + 1])
    single_grads[SB] = row_sum(grad_wide)
    low_even, low_odd = halves(grad_wide.astype(bf16))
    turned_even, turned_odd = low_even.T, low_odd.T
    grad_ref[B_SPREAD] = dot_nn(turned_odd, pooled_next).astype(bf16)
    grad_ref[B_SPREAD + 1] = dot_nn(turned_even, pooled).astype(bf16)
    grad_ref[B_SPREAD + 2] = dot_nn(turned_odd, pooled).astype(bf16)
    grad_ref[B_SPREAD + 3] = dot_nn(turned_even, pooled_prev).astype(bf16)
    reach(10)
    grad_pooled = dot_nn(low_even, w_ref[B_SPREAD + 1]) + dot_nn(low_odd, w_ref[B_SPREAD + 2])
    grad_pooled = grad_pooled + dot_nn(step_frames(low_even, 1), w_ref[B_SPREAD + 3])
    grad_pooled = grad_pooled + dot_nn(step_frames(low_odd, -1), w_ref[B_SPREAD])
    single_grads[PB] = row_sum(grad_pooled)
    low = grad_pooled.astype(bf16)
    turned = low.T
    for t in range(3):
        grad_ref[B_POOL + t] = dot_nn(turned, pool_sources[t]).astype(bf16)
    reach(11)
    grad_even = dot_nn(low, w_ref[B_POOL + 1])
    grad_odd = dot_nn(low, w_ref[B_POOL + 2]) + dot_nn(step_frames(low, 1), w_ref[B_POOL])
    grad_skip = grad_skip + interleave(grad_even, grad_odd)
    single_grads[D_RB] = row_sum(grad_skip)
    skip_low = grad_skip.astype(bf16)
    misc_grad = jnp.where(lane < 50, 0.0, dot_nn(skip_low.T, inputs))
    back = dot_nn(skip_low, misc_res)
    grad, single_grads[D_G2], single_grads[D_S2] = norm_backward(
        grad_skip, normal_two, slope_two, scale_two, vec(D_G2), ones
    )
    single_grads[D_B2] = row_sum(grad)
    low = grad.astype(bf16)
    conv_weights(low, mid_one, lambda t: B_DS + t)
    reach(12)
    grad_mid = conv_source(low, down)
    shift_one = over_frames(grad_mid)
    gain_one = over_frames(grad_mid * act_one)
    grad, single_grads[D_G1], single_grads[D_S1] = norm_backward(
        times(grad_mid, film[0]), normal_one, slope_one, scale_one, vec(D_G1), ones
    )
    single_grads[D_B1] = row_sum(grad)
    low = grad.astype(bf16)
    misc_grad = misc_grad + jnp.where(lane < 50, dot_nn(low.T, inputs), 0.0)
    film_grads = (gain_one, shift_one, gain_three, shift_three)
    film_low = [g.astype(bf16) for g in film_grads]
    back_cond = None
    for q in range(4):
        single_grads[(D_FS, D_FO, U_FS, U_FO)[q]] = jnp.sum(film_grads[q], axis=0, keepdims=True)
        grad_ref[B_FILM + q // 2, :, (q % 2) * 128 : (q % 2) * 128 + 128] = dot_tn(film_low[q], cond_low).astype(bf16)
        part = dot_nn(film_low[q], film_time(q))
        back_cond = part if back_cond is None else back_cond + part
    at_slots = [dot_nn(at_slot, v) for v in film_low]
    for k in range(8):
        film_grad_ref[k] = jnp.concatenate([v[:, k * 32 : (k + 1) * 32] for v in at_slots], axis=1).astype(bf16)
    reach(13)
    grad_embed = back_cond * cond_slope
    single_grads[T_OUT] = jnp.concatenate(
        [jnp.sum(grad_embed, axis=0, keepdims=True), jnp.zeros((1, C - TE), f32)], axis=1
    )
    embed_low = grad_embed.astype(bf16)
    for j in range(2):
        grad_ref[B_OUTER, :, j * 128 : (j + 1) * 128] = dot_tn(hidden_low[j], embed_low).astype(bf16)
        grad_hidden = dot_nt(embed_low, outer[j]) * hidden[j][1]
        single_grads[T_BIAS_A + j] = jnp.sum(grad_hidden, axis=0, keepdims=True)
        grad_ref[B_INNER, :, j * 128 : (j + 1) * 128] = dot_tn(grad_hidden.astype(bf16), feats).astype(bf16)
    stack = [jnp.zeros((LANE_TAIL, 256), f32)] + [single_grads[k] for k in range(TAIL)]
    stack = jnp.concatenate(stack + [jnp.zeros((128 - LANE_TAIL - TAIL, 256), f32)], axis=0)
    grad_ref[B_MISC, :, :128] = (misc_grad + stack.T).astype(bf16)
    grad_ref[B_MISC, :, 128:] = jnp.zeros((256, 128), bf16)
    reach(14)
    result = act_four + dot_nt(wide, w_ref[B_UR]) + dot_nt(skip, w_ref[B_UR + 1]) + vec(U_RB)
    act_ref[...] = dot_tn(result.astype(bf16), swap).astype(bf16)
    back = back + dot_nn(low, misc_first)
    grad_start = back[:, 50:60]
    for t in range(5):
        grad_start = grad_start + step_frames(back[:, t * ADIM : (t + 1) * ADIM], 2 - t)
    grad_cols = sum(dot_tn(part, swap) for part in split3(jnp.concatenate([grad_start, jnp.zeros((256, 6), f32)], axis=1)))
    noisy_grad_ref[...] = grad_cols[:ADIM] * keep


def train(weights, seen_film, slots, noisy, mask, levels, cotangent):
    vmem = pl.BlockSpec(memory_space=pltpu.VMEM)
    return pl.pallas_call(
        train_kernel,
        out_shape=(
            jax.ShapeDtypeStruct((C, 256), bf16),
            jax.ShapeDtypeStruct((ADIM, 256), f32),
            jax.ShapeDtypeStruct((NB, 256, 256), bf16),
            jax.ShapeDtypeStruct((8, SAM, 128), bf16),
        ),
        in_specs=[vmem] * 8,
        out_specs=(vmem,) * 4,
        compiler_params=pltpu.CompilerParams(vmem_limit_bytes=48 << 20),
        name="train",
    )(weights, seen_film, slots, noisy, mask, levels, cotangent, jnp.asarray(level_table(), bf16))


HALF = ROWS // 2


def native_grads(own_ref, film_ref, order_ref, grad_ref):
    misc = own_ref[B_MISC]
    first = dot_nt(misc[:, :128], order_ref[...])
    misc = misc.astype(f32)
    grad_ref[:, 0:50] = first[:, :50]
    grad_ref[:, AT_DOWN_RES : AT_DOWN_RES + ADIM] = misc[:, 50:60]
    grad_ref[:, AT_TAIL : AT_TAIL + TAIL] = misc[:, LANE_TAIL : LANE_TAIL + TAIL]
    grad_ref[:, AT_TIME[0] : AT_TIME[0] + 256] = own_ref[B_INNER].astype(f32)
    grad_ref[:, AT_TIME[1] : AT_TIME[1] + 256] = own_ref[B_OUTER].astype(f32)
    for q in range(4):
        grad_ref[:, AT_FILM[q] : AT_FILM[q] + OBS] = film_ref[q * ROWS : (q + 1) * ROWS]
        part = own_ref[B_FILM + q // 2, :, (q % 2) * 128 : (q % 2) * 128 + 128]
        grad_ref[:, AT_FILM[q] + OBS : AT_FILM[q] + OBS + TE] = part.astype(f32)
    grad_ref[:, AT_UP_RES : AT_UP_RES + 256] = own_ref[B_UR].astype(f32)
    grad_ref[:, AT_UP_RES + 256 : AT_UP_RES + 512] = own_ref[B_UR + 1].astype(f32)
    for taps in (5, 3, 4):
        places = [(at, h, block) for at, k, groups, block in CONVS if k == taps for h in range(groups)]
        stacked = jnp.concatenate(
            [
                jnp.concatenate(
                    [own_ref[block(t, h), :, (h % 2) * 128 : (h % 2) * 128 + 128] for t in range(taps)], axis=1
                )
                for _, h, block in places
            ],
            axis=0,
        )
        moved = dot_nt(stacked, tap_order(taps))
        for n, (at, h, _) in enumerate(places):
            begin = at + h * 128 * taps
            grad_ref[:, begin : begin + 128 * taps] = moved[n * ROWS : (n + 1) * ROWS]


def unpack_kernel(own_ref, film_ref, order_ref, grad_ref):
    native_grads(own_ref, film_ref, order_ref, grad_ref)


def unpack(own, film):
    vmem = pl.BlockSpec(memory_space=pltpu.VMEM)
    return pl.pallas_call(
        unpack_kernel,
        out_shape=jax.ShapeDtypeStruct((ROWS, Q), f32),
        in_specs=[vmem] * 3,
        out_specs=vmem,
        compiler_params=pltpu.CompilerParams(vmem_limit_bytes=30 << 20),
        name="unpack",
    )(own, film, jnp.asarray(first_order(), bf16))


def adam_kernel(count, *refs):
    grad_ref, square_ref = refs[:2]
    old, extra_in = refs[2:5], refs[5 : 5 + count]
    norm_ref, new_hbm, extra_out = refs[5 + count], refs[6 + count : 10 + count], refs[10 + count : 10 + 2 * count]
    new, sems = refs[10 + 2 * count : 14 + 2 * count], refs[-1]
    norm = jnp.sqrt(jnp.sum(square_ref[...], axis=(0, 1), keepdims=True))
    norm_ref[...] = norm
    factor = jnp.minimum(1.0, clip_limit / (norm + 1e-06))
    stores = {}

    def store(n, height, at):
        rows = pl.ds(at, height)
        stores[n, at] = pltpu.make_async_copy(new[n].at[rows], new_hbm[n].at[rows], sems.at[n, at // 8])
        stores[n, at].start()

    width = 1024
    for row in range(0, ROWS, 16):
        for begin in range(0, Q, width):
            cols = slice(begin, min(begin + width, Q))
            at = (slice(row, row + 16), cols)
            clipped = grad_ref[at] * factor
            new_first = decay_first * old[1][at] + (1.0 - decay_first) * clipped
            new_second = decay_second * old[2][at] + (1.0 - decay_second) * clipped * clipped
            first_hat = new_first * (1.0 / (1.0 - decay_first**ADAM_STEP))
            second_hat = new_second * (1.0 / (1.0 - decay_second**ADAM_STEP))
            before = old[0][at]
            after = before - learn_rate * (first_hat / (jnp.sqrt(second_hat) + adam_eps) + weight_decay * before)
            new[0][at] = after
            new[1][at] = new_first
            new[2][at] = new_second
            new[3][at] = after.astype(bf16)
        for n in range(4):
            store(n, 16, row)
    for source, target in zip(extra_in, extra_out):
        target[...] = source[...].reshape(target.shape)
    for copy in stores.values():
        copy.wait()


def adam(grads, squares, params, first, second, extras=(), extra_shapes=()):
    vmem = pl.BlockSpec(memory_space=pltpu.VMEM)
    hbm = pl.BlockSpec(memory_space=pl.ANY)
    shape = jax.ShapeDtypeStruct((ROWS, Q), f32)
    count = len(extras)
    return pl.pallas_call(
        functools.partial(adam_kernel, count),
        out_shape=(
            jax.ShapeDtypeStruct((1, 1), f32),
            shape, shape, shape, jax.ShapeDtypeStruct((ROWS, Q), bf16),
            *(jax.ShapeDtypeStruct(dims, v.dtype) for dims, v in zip(extra_shapes, extras)),
        ),
        in_specs=[vmem] * (5 + count),
        out_specs=(vmem,) + (hbm,) * 4 + (vmem,) * count,
        scratch_shapes=[pltpu.VMEM((ROWS, Q), f32)] * 3
        + [pltpu.VMEM((ROWS, Q), bf16), pltpu.SemaphoreType.DMA((4, ROWS // 8))],
        compiler_params=pltpu.CompilerParams(vmem_limit_bytes=30 << 20),
        name="adam",
    )(grads, squares, params, first, second, *extras)


def local_plain(noisy, action_mask, time_index, obs_embed, obs_slot, cotangent, params, first_moment, second_moment):
    rows = params.shape[0]
    padded = lambda v: jnp.pad(v, ((0, ROWS - rows), (0, 0))) if rows < ROWS else v
    if rows > ROWS:
        packed = [pack(params[r : r + ROWS]) for r in range(0, rows, ROWS)]
        own = jnp.concatenate([p[0].reshape(NB, ROWS, 256) for p in packed], axis=1)
        film_own = jnp.concatenate([p[1].reshape(4, ROWS, OBS) for p in packed], axis=1)
    else:
        own, film_own = pack(padded(params))
        own = own.reshape(NB, ROWS, 256)[:, :rows]
        film_own = film_own.reshape(4, ROWS, OBS)[:, :rows]
    weights = lax.all_gather(own, "wide", axis=1, tiled=True)
    film_rows = lax.all_gather(film_own, "wide", axis=1, tiled=True).reshape(4 * C, OBS)
    seen = lax.all_gather(obs_embed, "pair", axis=0, tiled=True).reshape(-1, OBS).astype(f32)
    cond, slope = mish_parts(seen)
    cond = cond.astype(bf16)
    seen_film = dot_nt(cond, film_rows).reshape(4, 4, 4, 8, 32).transpose(0, 3, 1, 2, 4).reshape(4, 8, 4, 128)
    seen_film = seen_film.reshape(4, 4, 8, 128)
    act, noisy_grad, grads, film_grad = train(
        weights, seen_film, obs_slot[None], noisy[0], action_mask, time_index, cotangent[0]
    )
    film_grad = film_grad.reshape(8, SAM, 4, 32).transpose(1, 2, 0, 3).reshape(SAM, 4 * C)
    film_total = lax.psum(dot_tn(film_grad, cond), ("pair", "wide")).reshape(4, C, OBS)
    back = lax.psum_scatter(
        (dot_nn(film_grad, film_rows) * slope).reshape(-1, obs_embed.shape[1], OBS),
        "pair", scatter_dimension=0, tiled=True,
    )
    total = lax.psum(grads.astype(f32), ("pair", "wide")).astype(bf16)
    squares = jnp.sum(jnp.square(total.astype(f32))) + jnp.sum(jnp.square(film_total))
    here = lax.axis_index("wide") * rows
    mine = lax.dynamic_slice_in_dim(total, here, rows, 1)
    film_mine = lax.dynamic_slice_in_dim(film_total, here, rows, 1)
    outs = []
    for r in range(0, rows, ROWS):
        take = lambda v: jnp.pad(v[:, r : r + ROWS], ((0, 0), (0, max(0, ROWS - rows)), (0, 0)))
        outs.append(
            adam(
                unpack(take(mine), take(film_mine).reshape(4 * ROWS, OBS)), squares.reshape(1, 1),
                *(padded(v)[r : r + ROWS] for v in (params, first_moment, second_moment)),
            )
        )
    new = [jnp.concatenate([o[k] for o in outs], axis=0)[:rows] for k in range(1, 5)]
    return (act[None], noisy_grad[None], back, outs[0][0].reshape(()), *new)


MESH = pl.DeviceIdType.MESH


class Place:
    def __init__(self):
        p = lax.axis_index("pair")
        w = lax.axis_index("wide")
        self.p, self.w = p, w
        self.x, self.y = lax.rem(p, 2), lax.div(p, 2)
        self.c, self.z = lax.rem(w, 2), lax.div(w, 2)
        turn = [1 - 2 * self.x, 2 - 4 * self.y]
        self.p_flip = [p, p + turn[0], p + turn[1], p + (turn[0] + turn[1])]
        z_turn = [1 - 2 * lax.rem(self.z, 2), 2 - 4 * lax.div(self.z, 2)]
        self.z_flip = [self.z, self.z + z_turn[0], self.z + z_turn[1], self.z + (z_turn[0] + z_turn[1])]
        self.w_flip = []
        for z in self.z_flip:
            self.w_flip += [2 * z + self.c, 2 * z + (1 - self.c)]
        self.w_flip[0] = w
        self.x_of = [lax.rem(v, 2) for v in self.p_flip]
        self.y_of = [lax.div(v, 2) for v in self.p_flip]

    def line(self, l):
        return (self.p, self.w_flip[l])

    def others(self):
        return [(self.p_flip[k], self.w_flip[l]) for k in range(1, 4) for l in range(1, 8)]

    def plane(self, k):
        return (self.p_flip[k], self.w)


def greet(me):
    barrier = pltpu.get_barrier_semaphore()
    for l in range(1, 8):
        pl.semaphore_signal(barrier, inc=1, device_id=me.line(l), device_id_type=MESH)
    for k in range(1, 4):
        pl.semaphore_signal(barrier, inc=1, device_id=me.plane(k), device_id_type=MESH)


def meet(me):
    pl.semaphore_wait(pltpu.get_barrier_semaphore(), 10)


def drain(size, semaphore):
    pltpu.make_async_copy(size, size, semaphore).wait()


class Pool:
    def __init__(self, ref):
        self.ref, self.used = ref, 0

    def new(self):
        self.used += 1
        return self.ref.at[self.used - 1]

    def several(self, keys):
        return {key: self.new() for key in keys}


class Lane:
    def __init__(self, pool):
        self.sent, self.bytes = pool.new(), 0

    def send(self, source, target, arrival, device):
        pltpu.make_async_remote_copy(
            src_ref=source, dst_ref=target, send_sem=self.sent, recv_sem=arrival,
            device_id=device, device_id_type=MESH,
        ).start()
        self.bytes += math.prod(source.shape) * source.dtype.itemsize

    def finish(self, size):
        assert math.prod(size.shape) * size.dtype.itemsize == self.bytes
        drain(size, self.sent)


def fold_rows(v):
    return jnp.concatenate([v[:, q * 256 : (q + 1) * 256] for q in range(4)], axis=0)


def unfold_rows(v):
    return jnp.concatenate([v[q * 4 : (q + 1) * 4] for q in range(4)], axis=1)


def quarter_rows(parts):
    quarter = (iota(parts[0].shape, 0) >> 2) & 3
    return sum(jnp.where(quarter == q, part, 0.0) for q, part in enumerate(parts))


class Gather:
    def __init__(self, me, own, weights, seen, obs_all, film, film_part, film_line, pool, local_sem):
        self.me, self.own, self.weights, self.seen, self.obs_all, self.film = me, own, weights, seen, obs_all, film
        self.film_part, self.film_line, self.local_sem = film_part, film_line, local_sem
        self.z, self.x, self.y, self.f, self.c, self.small = (Lane(pool) for _ in range(6))
        self.parts, self.films, self.more = (Lane(pool) for _ in range(3))
        pieces = [(g, k) for g in range(len(GATHER_GROUPS)) for k in range(1, 4)]
        self.z_in = pool.several(pieces)
        near = [(g, k) for g, k in pieces if g not in GATHER_DIRECT] + list(GATHER_DIRECT)
        self.x_in, self.y_in = pool.several(near), pool.several(near)
        self.f_in = pool.several(range(len(GATHER_GROUPS)))
        self.c_in = pool.several(range(len(GATHER_GROUPS)))
        self.obs_in, self.part_in, self.film_in, self.more_in = (pool.new() for _ in range(4))

    def start_obs(self):
        me = self.me
        piece = self.obs_all.at[me.p, me.w]
        for l in range(1, 8):
            self.small.send(piece, piece, self.obs_in, me.line(l))

    def start_rows(self, g):
        me = self.me
        for k in range(1, 4):
            self.z.send(
                self.own.at[gather_group(g), me.p], self.weights.at[gather_group(g), me.p, me.z, me.c],
                self.z_in[g, k], me.line(2 * k),
            )

    def start_local(self):
        self.local = pltpu.make_async_copy(self.own, self.weights.at[:, :, self.me.z, self.me.c], self.local_sem)
        self.local.start()

    def film_product(self):
        me = self.me
        drain(self.obs_all.at[0, 0:7], self.obs_in)
        cond = mish_parts(self.obs_all[me.p].reshape(128, 256).astype(f32))[0].astype(bf16)
        film = quarter_rows([dot_nt(cond, self.film[:, q * 256 : (q + 1) * 256]) for q in range(4)])
        row, col = iota((64, 128), 0), iota((64, 128), 1)
        pick = one_hot(((row >> 3) == (col >> 4)) & ((row & 7) == (col & 3)))
        self.film_part[...] = sum(dot_nn(pick, part) for part in split3(film)).reshape(8, 8, 128)
        for l in range(1, 8):
            self.parts.send(self.film_part.at[me.w_flip[l]], self.film_line.at[me.w], self.part_in, me.line(l))
        self.film_line[me.w] = self.film_part[me.w]

    def film_hop(self):
        me = self.me
        drain(self.film_line.at[0:7], self.part_in)
        for k in range(4):
            self.seen[me.p, k] = self.film_line[2 * k] + pltpu.roll(self.film_line[2 * k + 1], 4, 0)
        piece = self.seen.at[me.p]
        for k in range(1, 4):
            self.films.send(piece, piece, self.film_in, me.plane(k))

    def obs_hop(self):
        me = self.me
        piece = self.obs_all.at[me.p]
        for k in range(1, 4):
            self.more.send(piece, piece, self.more_in, me.plane(k))

    def film_done(self):
        drain(self.seen.at[0:3], self.film_in)

    def first_hop(self, g):
        me = self.me
        for k in range(1, 4):
            piece = self.weights.at[gather_group(g), me.p, me.z_flip[k], me.c]
            drain(piece, self.z_in[g, k])
            key = g if g in GATHER_DIRECT else (g, k)
            self.x.send(piece, piece, self.x_in[key], me.plane(1))
            self.y.send(piece, piece, self.y_in[key], me.plane(2))
            if g in GATHER_DIRECT:
                self.f.send(piece, piece, self.f_in[g], me.plane(3))

    def second_hop(self, g):
        me = self.me
        if g in GATHER_DIRECT:
            three = self.weights.at[gather_group(g), 0, 0:3, 0]
            drain(three, self.x_in[g])
            drain(three, self.y_in[g])
            return
        for k in range(1, 4):
            one = self.weights.at[gather_group(g), 0, 0, 0]
            drain(one, self.x_in[g, k])
            drain(one, self.y_in[g, k])
            along_y = (g + k) % 2 == 0
            piece = self.weights.at[gather_group(g), me.p_flip[1 if along_y else 2], me.z_flip[k], me.c]
            self.f.send(piece, piece, self.f_in[g], me.plane(2 if along_y else 1))

    def last_hop(self, g):
        if g == 0:
            self.local.wait()
        if g in GATHER_DIRECT:
            self.second_hop(g)
        drain(self.weights.at[gather_group(g), 0, 0:3, 0], self.f_in[g])
        piece = self.weights.at[gather_group(g), :, :, self.me.c]
        self.c.send(piece, piece, self.c_in[g], self.me.line(1))

    def arrived(self, g):
        drain(self.weights.at[gather_group(g), :, :, 0], self.c_in[g])

    def obs_done(self):
        drain(self.obs_all.at[0:3], self.more_in)

    def finish(self):
        three = self.weights.at[:, 0, 0:3, 0]
        for lane in (self.z, self.x, self.y, self.f):
            lane.finish(three)
        self.c.finish(self.weights.at[:, :, :, 0])
        self.small.finish(self.obs_all.at[0, 0:7])
        self.parts.finish(self.film_line.at[0:7])
        self.films.finish(self.seen.at[0:3])
        self.more.finish(self.obs_all.at[0:3])


class Scatter:
    def __init__(self, me, grad, film_grad, obs_all, film, out, film_out, back, square, buffers, pool):
        self.me, self.grad, self.film_grad, self.obs_all, self.film = me, grad, film_grad, obs_all, film
        self.out, self.film_out, self.back, self.square = out, film_out, back, square
        (self.half, self.core, self.xb, self.yb, self.ub, self.vb, self.zb, self.zq, self.pq, self.db,
         self.film_all, self.back_part, self.back_line, self.cond, self.all_squares) = buffers
        self.c, self.x, self.y, self.u, self.v, self.z = (Lane(pool) for _ in range(6))
        self.zf, self.q, self.d, self.r, self.g, self.h, self.b, self.n = (Lane(pool) for _ in range(8))
        groups = range(len(GROUPS))
        self.staged = [g for g in groups if g != Z_FIRST and g not in PLANE_DIRECT]
        self.c_in = pool.several(groups)
        self.x_in, self.y_in, self.u_in, self.v_in = (pool.several(self.staged) for _ in range(4))
        self.d_in = pool.several(PLANE_DIRECT)
        self.z_in = pool.several(g for g in groups if g != Z_FIRST)
        self.zf_in, self.q_in, self.r_in, self.g_in, self.h_in, self.b_in, self.n_in = (pool.new() for _ in range(7))
        self.squares = []

    def start(self, g):
        me = self.me
        self.c.send(self.grad.at[group(g), :, :, 1 - me.c], self.core.at[group(g)], self.c_in[g], me.line(1))

    def core_sum(self, g):
        me, half, (first, last) = self.me, self.half, GROUPS[g]
        drain(self.core.at[group(g)], self.c_in[g])

        def add(i, _):
            j, q = first + i // 4, i % 4
            total = self.grad[j, q, :, me.c].astype(f32) + self.core[j, q].astype(f32)
            half[j, q // 2, q % 2] = total.astype(bf16)
            return 0

        lax.fori_loop(0, (last - first) * 4, add, 0)
        if g == Z_FIRST:
            self.z_send(g, 0)
        elif g in PLANE_DIRECT:
            for k in range(1, 4):
                piece = half.at[group(g), me.y_of[k], me.x_of[k]]
                self.d.send(piece, self.db.at[k - 1, group(g)], self.d_in[g], me.plane(k))
        else:
            self.x.send(half.at[group(g), :, 1 - me.x, LOW], self.xb.at[group(g)], self.x_in[g], me.plane(1))
            self.y.send(half.at[group(g), 1 - me.y, :, HIGH], self.yb.at[group(g)], self.y_in[g], me.plane(2))

    def z_send(self, g, n):
        me = self.me
        for k in range(1, 4):
            self.zf.send(
                self.half.at[GROUPS[g][0] + n, :, :, me.z_flip[k]], self.zq.at[k - 1, n], self.zf_in, me.line(2 * k)
            )

    def z_sum(self, g):
        me, half, (first, last) = self.me, self.half, GROUPS[g]
        drain(self.zq, self.zf_in)
        for j in range(first, last):
            total = half[j, :, :, me.z].astype(f32)
            for k in range(3):
                total = total + self.zq[k, j - first].astype(f32)
            half[j, :, :, me.z] = total.astype(bf16)
        for k in range(1, 4):
            piece = half.at[group(g), me.y_of[k], me.x_of[k], me.z]
            self.q.send(piece, self.pq.at[k - 1], self.q_in, me.plane(k))

    def plane_sum(self, g):
        drain(self.pq, self.q_in)
        self.finish_sum(g, [lambda j, k=k: self.pq[k, j - GROUPS[g][0]] for k in range(3)])

    def first_sum(self, g):
        me, half, (first, last) = self.me, self.half, GROUPS[g]
        drain(self.xb.at[group(g)], self.x_in[g])

        def add_x(i, _):
            j, q = first + i // 2, i % 2
            total = half[j, q, me.x, LOW].astype(f32) + self.xb[j, q].astype(f32)
            half[j, q, me.x, LOW] = total.astype(bf16)
            return 0

        lax.fori_loop(0, (last - first) * 2, add_x, 0)
        self.u.send(half.at[group(g), 1 - me.y, me.x, LOW], self.ub.at[group(g)], self.u_in[g], me.plane(2))
        drain(self.yb.at[group(g)], self.y_in[g])

        def add_y(i, _):
            j, q = first + i // 2, i % 2
            total = half[j, me.y, q, HIGH].astype(f32) + self.yb[j, q].astype(f32)
            half[j, me.y, q, HIGH] = total.astype(bf16)
            return 0

        lax.fori_loop(0, (last - first) * 2, add_y, 0)
        self.v.send(half.at[group(g), me.y, 1 - me.x, HIGH], self.vb.at[group(g)], self.v_in[g], me.plane(1))

    def direct_sum(self, g):
        me, half = self.me, self.half
        drain(self.db.at[:, group(g)], self.d_in[g])
        for j in range(*GROUPS[g]):
            total = half[j, me.y, me.x].astype(f32)
            for k in range(3):
                total = total + self.db[k, j].astype(f32)
            half[j, me.y, me.x] = total.astype(bf16)
        self.send_z(g)

    def second_sum(self, g):
        me, half = self.me, self.half
        drain(self.ub.at[group(g)], self.u_in[g])
        drain(self.vb.at[group(g)], self.v_in[g])
        for j in range(*GROUPS[g]):
            total = half[j, me.y, me.x, LOW].astype(f32) + self.ub[j].astype(f32)
            half[j, me.y, me.x, LOW] = total.astype(bf16)
            total = half[j, me.y, me.x, HIGH].astype(f32) + self.vb[j].astype(f32)
            half[j, me.y, me.x, HIGH] = total.astype(bf16)
        self.send_z(g)

    def send_z(self, g):
        me = self.me
        for k in range(1, 4):
            piece = self.half.at[group(g), me.y, me.x, me.z_flip[k]]
            self.z.send(piece, self.zb.at[k - 1, group(g)], self.z_in[g], me.line(2 * k))

    def last_sum(self, g):
        drain(self.zb.at[:, group(g)], self.z_in[g])
        self.finish_sum(g, [lambda j, k=k: self.zb[k, j] for k in range(3)])

    def finish_sum(self, g, terms):
        me = self.me
        for j in range(*GROUPS[g]):
            total = self.half[j, me.y, me.x, me.z].astype(f32)
            for term in terms:
                total = total + term(j).astype(f32)
            total = total.astype(bf16)
            self.out[j, me.p] = total
            self.squares.append(jnp.sum(jnp.square(total.astype(f32)).reshape(4, 8, 256), axis=0))
        piece = self.out.at[group(g), me.p]
        for k in range(1, 4):
            self.r.send(piece, piece, self.r_in, me.plane(k))

    def film_start(self):
        me = self.me
        self.film_all[me.p, me.w] = self.film_grad[me.w]
        for l in range(1, 8):
            self.g.send(self.film_grad.at[me.w_flip[l]], self.film_all.at[me.p, me.w], self.g_in, me.line(l))

    def film_hop(self):
        me = self.me
        drain(self.film_all.at[0, 0:7], self.g_in)
        piece = self.film_all.at[me.p]
        for k in range(1, 4):
            self.h.send(piece, piece, self.h_in, me.plane(k))

    def film_inputs(self):
        row, col = iota((128, 512), 0), iota((128, 512), 1)
        same = ((row >> 4) == ((col >> 4) & 7)) & (((row >> 2) & 3) == (col >> 7)) & ((row & 3) == (col & 3))
        seen_all = self.obs_all[...].reshape(512, 256)
        for q in range(4):
            pick = one_hot(same & (((col >> 2) & 3) == q))
            self.cond[q] = mish_parts(dot_nn(pick, seen_all))[0].astype(bf16)

    def film_products(self):
        me = self.me
        drain(self.film_all.at[0:3], self.h_in)
        copies = [self.film_all[k].reshape(128, 128).astype(f32) for k in range(4)]
        total = split2((copies[0] + copies[1]) + (copies[2] + copies[3]))
        row, col = iota((128, 128), 0), iota((128, 128), 1)
        mine = one_hot(((row >> 4) == (col >> 4)) & ((col & 15) == 4 * me.p + (row & 3)))
        rows = [dot_nn(mine, part).astype(bf16) for part in total]
        parts = [
            dot_nn(rows[0], self.film[:, q * 256 : (q + 1) * 256])
            + dot_nn(rows[1], self.film[:, q * 256 : (q + 1) * 256])
            for q in range(4)
        ]
        self.back_part[...] = quarter_rows(parts).astype(bf16).reshape(8, 16, 256)
        for l in range(1, 8):
            self.b.send(self.back_part.at[me.w_flip[l]], self.back_line.at[me.w], self.b_in, me.line(l))
        self.back_line[me.w] = self.back_part[me.w]
        square = jnp.zeros((8, 256), f32)
        turned = [part.T for part in total]
        for q in range(4):
            cond = self.cond[q]
            product = dot_nn(turned[0], cond) + dot_nn(turned[1], cond)
            self.film_out[:, q * 256 : (q + 1) * 256] = product
            square = square + jnp.sum(jnp.square(product).reshape(16, 8, 256), axis=0)
        self.squares.append(0.25 * square)

    def film_back(self):
        me = self.me
        drain(self.back_line.at[0:7], self.b_in)
        total = jnp.sum(self.back_line[...].astype(f32), axis=0)
        slope = mish_parts(self.obs_all[me.p, me.w].astype(f32))[1]
        self.back[0] = unfold_rows(total * slope)

    def norm(self, hello, native):
        me = self.me
        total = sum(self.squares)
        here = me.p * 8 + me.w
        piece = self.all_squares.at[here]
        self.all_squares[here] = jnp.sum(total[:, :128] + total[:, 128:], axis=0, keepdims=True)
        pl.semaphore_wait(hello, len(me.others()))
        for i in range(1, 32):
            self.n.send(piece, piece, self.n_in, (me.p_flip[i % 4], me.w_flip[i // 4]))
        drain(self.zb, self.r_in)
        native()
        drain(self.all_squares.at[0:31], self.n_in)
        self.square[...] = jnp.sum(self.all_squares[...].reshape(32, 128), axis=0, keepdims=True)

    def finish(self):
        size = lambda gs: sum(GROUPS[g][1] - GROUPS[g][0] for g in gs)
        staged = size(self.staged)
        self.c.finish(self.grad.at[:, :, :, 0])
        self.x.finish(self.xb.at[0:staged])
        self.y.finish(self.yb.at[0:staged])
        self.u.finish(self.ub.at[0:staged])
        self.v.finish(self.vb.at[0:staged])
        self.d.finish(self.db.at[:, 0 : size(PLANE_DIRECT)])
        self.z.finish(self.zb.at[:, 0 : staged + size(PLANE_DIRECT)])
        self.zf.finish(self.zq)
        self.q.finish(self.pq)
        self.r.finish(self.zb)
        self.g.finish(self.film_all.at[0, 0:7])
        self.h.finish(self.film_all.at[0:3])
        self.b.finish(self.back_line.at[0:7])
        self.n.finish(self.all_squares.at[0:31])


GATHER_GROUPS = ((0, 1), (1, 3), (3, 5), (5, 7), (7, 9))
GATHER_DIRECT = (3, 4)
GROUPS = ((0, 1), (1, 3), (3, 5), (5, 7), (7, 8), (8, 9))
Z_FIRST = 3
PLANE_DIRECT = (0,)
SEMAPHORES = 109
LOW, HIGH = pl.ds(0, 2), pl.ds(2, 2)


def group(g):
    return pl.ds(GROUPS[g][0], GROUPS[g][1] - GROUPS[g][0])


def gather_group(g):
    return pl.ds(GATHER_GROUPS[g][0], GATHER_GROUPS[g][1] - GATHER_GROUPS[g][0])


def step_kernel(*refs):
    params_out = refs[16]
    targets = (params_out,) + refs[19:27]
    loads = [
        pltpu.make_async_copy(source, target, refs[-2].at[i])
        for i, (source, target) in enumerate(zip(refs[:11], targets + refs[17:19]))
    ]
    for i in (0, 2, 1, 3, 4, 5, 6, 7, 8):
        loads[i].start()
    refs = targets + refs[9:11] + refs[11:16] + refs[17:19] + refs[27:-2] + refs[-1:]
    (params, order, obs, slots, noisy, mask, levels, cotangent, table, first, second,
     act, noisy_grad, back, native, square, first_out, second_out,
     own, weights, seen, obs_all, film, film_part, film_line, grad, film_grad, out, film_out) = refs[:29]
    buffers, (semaphores, local_sem, hello) = refs[29:44], refs[44:]
    pool = Pool(semaphores)
    me = Place()
    gather = Gather(me, own, weights, seen, obs_all, film, film_part, film_line, pool, local_sem)
    scatter = Scatter(me, grad, film_grad, obs_all, film, out, film_out, back, square, buffers, pool)
    greet(me)
    loads[0].wait()
    loads[1].wait()
    pack_first(params, order, own)
    loads[2].wait()
    obs_all[me.p, me.w] = fold_rows(obs[0].astype(f32)).astype(bf16)
    meet(me)
    gather.start_rows(0)
    gather.start_obs()
    pack_rest(params, own, film)
    gather.start_local()
    gather.start_rows(1)
    for i in range(3, 9):
        loads[i].wait()

    def reach(point):
        if point == 0:
            gather.first_hop(0)
            gather.film_product()
            for g in range(2, len(GATHER_GROUPS)):
                gather.start_rows(g)
            gather.first_hop(1)
            gather.second_hop(0)
            gather.film_hop()
            gather.first_hop(2)
            gather.second_hop(1)
            gather.last_hop(0)
            for device in me.others():
                pl.semaphore_signal(hello, inc=1, device_id=device, device_id_type=MESH)
            gather.arrived(0)
        if point == 1:
            gather.first_hop(3)
            gather.second_hop(2)
            gather.last_hop(1)
            gather.film_done()
        if point == 2:
            gather.first_hop(4)
            gather.arrived(1)
        if point == 3:
            gather.last_hop(2)
            gather.last_hop(3)
            gather.arrived(2)
        if point == 5:
            gather.last_hop(4)
            gather.arrived(3)
        if point == 6:
            gather.obs_hop()
            loads[9].start()
            loads[10].start()
            gather.arrived(4)
        if point == 8:
            scatter.start(5)
            scatter.start(4)
        if point == 15:
            scatter.core_sum(5)
            scatter.core_sum(4)
        if point == 9:
            scatter.start(3)
        if point == 10:
            scatter.core_sum(3)
        if point == 11:
            scatter.start(2)
        if point == 12:
            scatter.core_sum(2)
            scatter.first_sum(5)
            scatter.first_sum(4)
        if point == 13:
            scatter.film_start()
            scatter.z_send(Z_FIRST, 1)
            scatter.start(1)
        if point == 14:
            scatter.start(0)
            scatter.core_sum(1)
            scatter.second_sum(5)
            scatter.second_sum(4)
            scatter.core_sum(0)
            scatter.first_sum(2)

    train_body(
        Stacked(weights), seen, slots, noisy, mask, levels, cotangent, table,
        act, noisy_grad, Stacked(grad), film_grad, reach,
    )
    scatter.film_hop()
    scatter.first_sum(1)
    gather.obs_done()
    scatter.film_inputs()
    scatter.second_sum(2)
    scatter.z_sum(3)
    scatter.film_products()
    scatter.second_sum(1)
    scatter.direct_sum(0)
    scatter.plane_sum(3)
    scatter.last_sum(5)
    scatter.last_sum(4)
    scatter.last_sum(2)
    scatter.last_sum(1)
    scatter.film_back()
    scatter.last_sum(0)
    loads[9].wait()
    loads[10].wait()
    scatter.norm(hello, lambda: native_grads(Blocks(out), film_out, order, native))
    gather.finish()
    scatter.finish()
    assert pool.used <= SEMAPHORES


class Stacked:
    def __init__(self, ref):
        self.ref = ref

    def _split(self, key):
        if not isinstance(key, tuple):
            return key, slice(None)
        return key[0], key[2]

    def __getitem__(self, key):
        block, cols = self._split(key)
        value = self.ref[block // 4, block % 4, :, :, :, cols]
        return value.reshape(256, value.shape[-1])

    def __setitem__(self, key, value):
        block, cols = self._split(key)
        self.ref[block // 4, block % 4, :, :, :, cols] = value.reshape(4, 2, ROWS, value.shape[-1])


def step(params, obs, slots, noisy, mask, levels, cotangent, first, second):
    vmem = pl.BlockSpec(memory_space=pltpu.VMEM)
    n = NB // 4
    inputs = (
        params, jnp.asarray(first_order(), bf16), obs, slots, noisy, mask, levels, cotangent,
        jnp.asarray(level_table(), bf16), first, second,
    )
    inputs = tuple(pltpu.with_memory_space_constraint(v, pltpu.HBM) for v in inputs)
    low = lambda *shape: pltpu.VMEM(shape, bf16)
    return pl.pallas_call(
        step_kernel,
        out_shape=(
            jax.ShapeDtypeStruct((C, 256), bf16),
            jax.ShapeDtypeStruct((ADIM, 256), f32),
            jax.ShapeDtypeStruct((1, 4, OBS), f32),
            jax.ShapeDtypeStruct((ROWS, Q), f32),
            jax.ShapeDtypeStruct((1, 128), f32),
            *[jax.ShapeDtypeStruct((ROWS, Q), f32)] * 3,
        ),
        in_specs=[pl.BlockSpec(memory_space=pltpu.HBM)] * 11,
        out_specs=(vmem,) * 8,
        scratch_shapes=[
            *(pltpu.VMEM(v.shape, v.dtype) for v in inputs[1:9]),
            low(n, 4, ROWS, 256),
            low(n, 4, 4, 2, ROWS, 256),
            pltpu.VMEM((4, 4, 8, 128), f32),
            low(4, 8, 16, 256),
            low(4 * ROWS, OBS),
            pltpu.VMEM((8, 8, 128), f32),
            pltpu.VMEM((8, 8, 128), f32),
            low(n, 4, 4, 2, ROWS, 256),
            low(8, SAM, 128),
            low(n, 4, ROWS, 256),
            pltpu.VMEM((4 * ROWS, OBS), f32),
            low(n, 2, 2, 4, ROWS, 256),
            low(n, 4, 4, ROWS, 256),
            low(n, 2, 2, ROWS, 256),
            low(n, 2, 2, ROWS, 256),
            low(n, 2, ROWS, 256),
            low(n, 2, ROWS, 256),
            low(3, n, ROWS, 256),
            low(3, GROUPS[Z_FIRST][1] - GROUPS[Z_FIRST][0], 2, 2, ROWS, 256),
            low(3, GROUPS[Z_FIRST][1] - GROUPS[Z_FIRST][0], ROWS, 256),
            low(3, GROUPS[max(PLANE_DIRECT)][1], 4, ROWS, 256),
            low(4, 8, 16, 128),
            low(8, 16, 256),
            low(8, 16, 256),
            low(4, 128, 256),
            pltpu.VMEM((32, 1, 128), f32),
            pltpu.SemaphoreType.DMA((SEMAPHORES,)),
            pltpu.SemaphoreType.DMA,
            pltpu.SemaphoreType.DMA((11,)),
            pltpu.SemaphoreType.REGULAR,
        ],
        compiler_params=pltpu.CompilerParams(collective_id=0, has_side_effects=True, vmem_limit_bytes=34 << 20),
        cost_estimate=pl.CostEstimate(flops=3 * 10**9, bytes_accessed=200 * 10**6, transcendentals=10**6),
        name="step",
    )(*inputs)


def local_fast(noisy, action_mask, time_index, obs_embed, obs_slot, cotangent, params, first_moment, second_moment):
    act, noisy_grad, back, native, squares, params, first_moment, second_moment = step(
        params, obs_embed, obs_slot[None], noisy[0], action_mask, time_index, cotangent[0],
        first_moment, second_moment,
    )
    norm, *new, act, noisy_grad, back = adam(
        native, squares, params, first_moment, second_moment,
        (act, noisy_grad, back), ((1, C, 256), (ADIM, 1, 256), (1, 4, OBS)),
    )
    return (act, noisy_grad.transpose(1, 0, 2), back, norm.reshape(()), *new)


def solution(mesh):
    in_specs = (
        P("pair", None, "wide"),
        P(None, "wide"),
        P("pair", "wide"),
        P("pair", "wide", None),
        P("wide"),
        P("pair", None, "wide"),
        P("wide", None),
        P("wide", None),
        P("wide", None),
    )
    out_specs = (
        P("pair", None, "wide"),
        P("pair", None, "wide"),
        P("pair", "wide", None),
        P(),
        P("wide", None),
        P("wide", None),
        P("wide", None),
        P("wide", None),
    )
    fast = mesh.shape["pair"] == 4 and mesh.shape["wide"] == 8
    return jax.shard_map(local_fast if fast else local_plain, mesh=mesh, in_specs=in_specs, out_specs=out_specs, check_vma=False)
```

```python
import functools
import math

import jax
import jax.numpy as jnp
import numpy as np
from jax import lax
from jax.experimental import pallas as pl
from jax.experimental.pallas import tpu as pltpu
from jax.sharding import PartitionSpec as P

C = 256
OBS = 1024
TE = 128
TH = 512
ADIM = 10
FR = 16
LEVELS = 40
ADAM_STEP = 7
Q = 12627
SAM = 16
ROWS = 32
NB = 36

sigma_top = 80.0 ** (1.0 / 7.0)
sigma_low = 0.002 ** (1.0 / 7.0)
clip_limit = 1.0
learn_rate = 0.02
decay_first = 0.5
decay_second = 0.5
adam_eps = 1e-08
weight_decay = 0.01
norm_eps = 1e-05

f32 = jnp.float32
bf16 = jnp.bfloat16

AT_DOWN_RES = 1330
AT_TAIL = 12604
TAIL = 23
AT_FILM = (1340, 2492, 9788, 10940)
AT_TIME = (12092, 12348)
AT_UP_RES = 9276
B_MISC, B_INNER, B_OUTER, B_FILM = 0, 1, 2, 3
B_DS, B_POOL, B_SPREAD, B_UF, B_US, B_UR = 5, 10, 13, 17, 27, 32
LANE_TAIL = 64
CONVS = (
    (50, 5, 2, lambda t, h: B_DS + t),
    (5436, 5, 4, lambda t, h: B_UF + 2 * t + h // 2),
    (7996, 5, 2, lambda t, h: B_US + t),
    (3644, 3, 2, lambda t, h: B_POOL + t),
    (4412, 4, 2, lambda t, h: B_SPREAD + t),
)
(T_BIAS_A, T_BIAS_B, T_OUT, D_B1, D_G1, D_S1, D_FS, D_FO, D_B2, D_G2, D_S2, D_RB, PB, SB,
 U_B1, U_G1, U_S1, U_FS, U_FO, U_B2, U_G2, U_S2, U_RB) = range(TAIL)


def dot_nt(a, b):
    return lax.dot_general(a, b, (((1,), (1,)), ((), ())), preferred_element_type=f32)


def dot_nn(a, b):
    return lax.dot_general(a, b, (((1,), (0,)), ((), ())), preferred_element_type=f32)


def dot_tn(a, b):
    return lax.dot_general(a, b, (((0,), (0,)), ((), ())), preferred_element_type=f32)


def split2(v):
    high = v.astype(bf16)
    return high, (v - high.astype(f32)).astype(bf16)


def split3(v):
    high, rest = v.astype(bf16), None
    rest = v - high.astype(f32)
    mid = rest.astype(bf16)
    return high, mid, (rest - mid.astype(f32)).astype(bf16)


def iota(shape, dim):
    return lax.broadcasted_iota(jnp.int32, shape, dim)


def one_hot(condition):
    return jnp.where(condition, 1.0, 0.0).astype(bf16)


def tap_order(taps):
    n = 128 * taps
    row = lax.broadcasted_iota(jnp.int32, (n, n), 0)
    col = lax.broadcasted_iota(jnp.int32, (1, n), 1)
    source = (col & 127) * taps + (col >> 7)
    return jnp.where(row == source, 1.0, 0.0).astype(bf16)


def first_order():
    table = np.zeros((128, 128), np.float32)
    for i in range(ADIM):
        for t in range(5):
            table[i * 5 + t, t * ADIM + i] = 1.0
    return table


def level_table():
    levels = np.arange(LEVELS, dtype=np.float64)
    tau = 250.0 * 7.0 * np.log(sigma_top + levels / (LEVELS - 1) * (sigma_low - sigma_top))
    freq = np.exp(-math.log(10000.0) * np.arange(TE // 2) / (TE // 2 - 1))
    angles = tau[:, None] * freq[None, :]
    table = np.zeros((64, TE), np.float32)
    table[:LEVELS] = np.concatenate([np.sin(angles), np.cos(angles)], axis=1)
    return table


def pack_kernel(params_ref, order_ref, own_ref, film_ref):
    pack_rows(params_ref, order_ref, own_ref, film_ref)


class Blocks:
    def __init__(self, ref):
        self.ref = ref

    def _at(self, key):
        block, rest = (key[0], key[1:]) if isinstance(key, tuple) else (key, ())
        return (block // 4, block % 4) + rest

    def __getitem__(self, key):
        return self.ref[self._at(key)]

    def __setitem__(self, key, value):
        self.ref[self._at(key)] = value


def pack_rows(params_ref, order_ref, own_ref, film_ref):
    pack_first(params_ref, order_ref, own_ref)
    pack_rest(params_ref, own_ref, film_ref)


def pack_first(params_ref, order_ref, own_ref):
    own_ref = Blocks(own_ref)

    def low(start, width):
        return params_ref[:, start : start + width].astype(bf16)

    first = dot_nn(low(0, 128), order_ref[...])
    pieces = [
        first[:, :50],
        params_ref[:, AT_DOWN_RES : AT_DOWN_RES + ADIM],
        jnp.zeros((ROWS, LANE_TAIL - 60), f32),
        params_ref[:, AT_TAIL : AT_TAIL + TAIL],
        jnp.zeros((ROWS, 256 - LANE_TAIL - TAIL), f32),
    ]
    own_ref[B_MISC] = jnp.concatenate(pieces, axis=1).astype(bf16)
    own_ref[B_INNER] = low(AT_TIME[0], 256)
    own_ref[B_OUTER] = low(AT_TIME[1], 256)
    for q in range(4):
        own_ref[B_FILM + q // 2, :, (q % 2) * 128 : (q % 2) * 128 + 128] = low(AT_FILM[q] + OBS, TE)


def pack_rest(params_ref, own_ref, film_ref):
    own_ref = Blocks(own_ref)

    def low(start, width):
        return params_ref[:, start : start + width].astype(bf16)

    for q in range(4):
        film_ref[q * ROWS : (q + 1) * ROWS] = low(AT_FILM[q], OBS)
    for i in range(4):
        own_ref[B_UR + i, :, 0:128] = low(AT_UP_RES + i * 128, 128)
    for taps in (5, 3, 4):
        places = [(at, h, block) for at, k, groups, block in CONVS if k == taps for h in range(groups)]
        stacked = jnp.concatenate([low(at + h * 128 * taps, 128 * taps) for at, h, _ in places], axis=0)
        moved = dot_nn(stacked, tap_order(taps)).astype(bf16)
        for n, (_, h, block) in enumerate(places):
            for t in range(taps):
                own_ref[block(t, h), :, (h % 2) * 128 : (h % 2) * 128 + 128] = moved[
                    n * ROWS : (n + 1) * ROWS, t * 128 : (t + 1) * 128
                ]


def pack(params):
    vmem = pl.BlockSpec(memory_space=pltpu.VMEM)
    return pl.pallas_call(
        pack_kernel,
        out_shape=(
            jax.ShapeDtypeStruct((NB // 4, 4, ROWS, 256), bf16),
            jax.ShapeDtypeStruct((4 * ROWS, OBS), bf16),
        ),
        in_specs=[vmem, vmem],
        out_specs=(vmem, vmem),
        compiler_params=pltpu.CompilerParams(vmem_limit_bytes=40 << 20),
        name="pack",
    )(params, jnp.asarray(first_order(), bf16))


def mish_parts(v):
    e = jnp.exp(jnp.minimum(v, 20.0))
    n = e * (e + 2.0)
    r = 1.0 / (n + 2.0)
    t = n * r
    return v * t, t + 4.0 * v * (e * r) * ((e + 1.0) * r)


def step_frames(v, step):
    if step == 0:
        return v
    zeros = jnp.zeros((SAM * abs(step), v.shape[1]), v.dtype)
    if step > 0:
        return jnp.concatenate([v[SAM * step :], zeros], axis=0)
    return jnp.concatenate([zeros, v[: SAM * step]], axis=0)


def over_frames(v):
    return jnp.sum(v.reshape(-1, SAM, v.shape[1]), axis=0)


def each_frame(v, s):
    return v.reshape(-1, SAM, v.shape[1]), s[None]


def group_means(values, ones):
    parts = [p for v in values for p in split3(v)]
    sums = dot_nn(jnp.concatenate(parts, axis=0), ones)
    out = []
    for i in range(len(values)):
        a, b, c = (sums[(3 * i + k) * SAM : (3 * i + k + 1) * SAM] for k in range(3))
        out.append((a + (b + c)) * (1.0 / (32 * FR)))
    return out


def minus(v, s):
    a, b = each_frame(v, s)
    return (a - b).reshape(v.shape)


def times(v, s):
    a, b = each_frame(v, s)
    return (a * b).reshape(v.shape)


def plus(v, s):
    a, b = each_frame(v, s)
    return (a + b).reshape(v.shape)


def norm_forward(before, gain, shift, ones):
    center, square = group_means([over_frames(before), over_frames(before * before)], ones)
    scale = lax.rsqrt(jnp.maximum(square - center * center, 0.0) + norm_eps)
    away = minus(before, center)
    normal = times(away, scale)
    act, slope = mish_parts(normal * gain + shift)
    return act, normal, slope, scale


def norm_backward(grad_act, normal, slope, scale, gain, ones):
    grad_out = grad_act * slope
    shift_rows = over_frames(grad_out)
    gain_rows = over_frames(grad_out * normal)
    mean_grad, mean_both = group_means([shift_rows * gain, gain_rows * gain], ones)
    inner = minus(grad_out * gain, mean_grad) - times(normal, mean_both)
    return (
        times(inner, scale),
        jnp.sum(gain_rows, axis=0, keepdims=True),
        jnp.sum(shift_rows, axis=0, keepdims=True),
    )


def conv_forward(source, weight):
    total = dot_nt(step_frames(source, -2), weight(0))
    for t in range(1, 5):
        total = total + dot_nt(step_frames(source, t - 2), weight(t))
    return total


def conv_source(grad_low, weight):
    total = dot_nn(step_frames(grad_low, 2), weight(0))
    for t in range(1, 5):
        total = total + dot_nn(step_frames(grad_low, 2 - t), weight(t))
    return total


def row_sum(v):
    return jnp.sum(over_frames(v), axis=0, keepdims=True)


def halves(v):
    cube = v.reshape(FR // 2, 2, SAM, v.shape[1])
    return cube[:, 0].reshape(-1, v.shape[1]), cube[:, 1].reshape(-1, v.shape[1])


def interleave(even, odd):
    width = even.shape[1]
    pair = [v.reshape(FR // 2, 1, SAM, width) for v in (even, odd)]
    return jnp.concatenate(pair, axis=1).reshape(FR * SAM, width)


def train_kernel(*refs):
    for b in range(B_UR, NB):
        refs[10][b, :, 128:] = jnp.zeros((256, 128), bf16)
    train_body(*refs, lambda point: None)


def train_body(
    w_ref, seen_ref, slot_ref, noisy_ref, mask_ref, level_ref, cot_ref, table_ref,
    act_ref, noisy_grad_ref, grad_ref, film_grad_ref, reach,
):
    row = iota((256, 256), 0)
    col = iota((256, 256), 1)
    ones = jnp.where((row >> 5) == (col >> 5), 1.0, 0.0).astype(bf16)
    swap = jnp.where(col == ((row & 15) << 4) + (row >> 4), 1.0, 0.0).astype(bf16)
    spread_mask = one_hot((iota((SAM, 256), 1) >> 4) == iota((SAM, 256), 0))
    keep = dot_nn(mask_ref[...].astype(f32).astype(bf16), spread_mask)
    start_cols = noisy_ref[...].astype(f32) * keep
    start_cols = jnp.concatenate([start_cols, jnp.zeros((6, 256), f32)], axis=0).astype(bf16)
    start = dot_nt(swap, start_cols).astype(bf16)
    lane16 = iota((16, 128), 1)
    row16 = iota((16, 128), 0)
    inputs = jnp.zeros((256, 128), f32)
    for t in range(5):
        place = lane16 == row16 + t * ADIM
        if t == 2:
            place = place | (lane16 == row16 + 50)
        inputs = inputs + dot_nn(step_frames(start, t - 2), one_hot(place & (row16 < ADIM)))
    inputs = inputs.astype(bf16)
    cot_high, cot_low = split2(cot_ref[...])
    upstream = dot_nt(swap, cot_high) + dot_nt(swap, cot_low)
    upstream_low = upstream.astype(bf16)
    at_level = one_hot(iota((64, SAM), 0) == level_ref[...])
    feats = dot_tn(at_level, table_ref[...]).astype(bf16)
    reach(0)
    misc = w_ref[B_MISC, :, :128]
    lane = iota((256, 128), 1)
    misc_first = jnp.where(lane < 50, misc, jnp.zeros_like(misc))
    misc_res = jnp.where((lane >= 50) & (lane < 60), misc, jnp.zeros_like(misc))
    singles = misc.astype(f32).T[LANE_TAIL : LANE_TAIL + 32]
    vec = lambda k: singles[k : k + 1]

    inner = [w_ref[B_INNER, :, j * 128 : (j + 1) * 128] for j in range(2)]
    outer = [w_ref[B_OUTER, :, j * 128 : (j + 1) * 128] for j in range(2)]
    film_time = lambda q: w_ref[B_FILM + q // 2, :, (q % 2) * 128 : (q % 2) * 128 + 128]
    hidden = [mish_parts(dot_nt(feats, inner[j]) + vec(T_BIAS_A + j)) for j in range(2)]
    hidden_low = [h[0].astype(bf16) for h in hidden]
    embed = dot_nn(hidden_low[0], outer[0]) + dot_nn(hidden_low[1], outer[1]) + vec(T_OUT)[:, :TE]
    cond, cond_slope = mish_parts(embed)
    cond_low = cond.astype(bf16)
    pre = dot_nt(inputs, misc_first) + vec(D_B1)
    act_one, normal_one, slope_one, scale_one = norm_forward(pre, vec(D_G1), vec(D_S1), ones)
    reach(1)
    at_slot = one_hot(iota((SAM, SAM), 0) == slot_ref[...])
    line = iota((32, SAM), 0)
    seen_film = jnp.concatenate([seen_ref[:, k].reshape(32, 128) for k in range(4)], axis=1)
    seen_film = split3(seen_film)
    sides = []
    for side in range(2):
        at_line = one_hot(((line >> 3) * 4 + (line & 3) == slot_ref[...]) & ((line >> 2) & 1 == side))
        sides.append(sum(dot_tn(at_line, part) for part in seen_film))
    seen_film = jnp.concatenate(
        [sides[k % 2][:, (k // 2) * 128 : (k // 2) * 128 + 128] for k in range(8)], axis=1
    )
    spans = lambda v, q: jnp.concatenate([v[:, k * 128 + q * 32 : k * 128 + q * 32 + 32] for k in range(8)], axis=1)
    film_of = lambda q: spans(seen_film, q) + dot_nt(cond_low, film_time(q)) + vec((D_FS, D_FO, U_FS, U_FO)[q])
    film = [film_of(0), film_of(1)]
    mid_one = plus(times(act_one, film[0]), film[1]).astype(bf16)
    reach(2)
    down = lambda t: w_ref[B_DS + t]
    pre = conv_forward(mid_one, down) + vec(D_B2)
    act, normal_two, slope_two, scale_two = norm_forward(pre, vec(D_G2), vec(D_S2), ones)
    skip = (act + dot_nt(inputs, misc_res) + vec(D_RB)).astype(bf16)
    reach(3)
    even, odd = halves(skip)
    odd_prev = step_frames(odd, -1)
    pool_sources = (odd_prev, even, odd)
    pooled = sum(dot_nt(s, w_ref[B_POOL + t]) for t, s in enumerate(pool_sources)) + vec(PB)
    pooled = pooled.astype(bf16)
    reach(4)
    pooled_prev = step_frames(pooled, -1)
    pooled_next = step_frames(pooled, 1)
    even_out = dot_nt(pooled, w_ref[B_SPREAD + 1]) + dot_nt(pooled_prev, w_ref[B_SPREAD + 3])
    odd_out = dot_nt(pooled_next, w_ref[B_SPREAD]) + dot_nt(pooled, w_ref[B_SPREAD + 2])
    wide = (interleave(even_out, odd_out) + vec(SB)).astype(bf16)
    joined = (wide, skip)
    up_res = lambda h: jnp.concatenate([w_ref[B_UR + 2 * h + i, :, 0:128] for i in range(2)], axis=1)
    turned = upstream_low.T
    for h in range(2):
        product = dot_nn(turned, joined[h]).astype(bf16)
        for i in range(2):
            grad_ref[B_UR + 2 * h + i, :, 0:128] = product[:, i * 128 : (i + 1) * 128]
    reach(5)
    up_first = [lambda t, h=h: w_ref[B_UF + 2 * t + h] for h in range(2)]
    pre = conv_forward(wide, up_first[0]) + conv_forward(skip, up_first[1]) + vec(U_B1)
    act_three, normal_three, slope_three, scale_three = norm_forward(pre, vec(U_G1), vec(U_S1), ones)
    film += [film_of(2), film_of(3)]
    mid_three = plus(times(act_three, film[2]), film[3]).astype(bf16)
    reach(6)
    up = lambda t: w_ref[B_US + t]
    pre = conv_forward(mid_three, up) + vec(U_B2)
    act, normal_four, slope_four, scale_four = norm_forward(pre, vec(U_G2), vec(U_S2), ones)
    act_four = act

    single_grads = {}

    def conv_weights(grad_low, source, block):
        turned = grad_low.T
        for t in range(5):
            grad_ref[block(t)] = dot_nn(turned, step_frames(source, t - 2)).astype(bf16)

    reach(7)
    grad, single_grads[U_G2], single_grads[U_S2] = norm_backward(
        upstream, normal_four, slope_four, scale_four, vec(U_G2), ones
    )
    single_grads[U_B2] = row_sum(grad)
    low = grad.astype(bf16)
    conv_weights(low, mid_three, lambda t: B_US + t)
    reach(8)
    grad_mid = conv_source(low, up)
    shift_three = over_frames(grad_mid)
    gain_three = over_frames(grad_mid * act_three)
    grad, single_grads[U_G1], single_grads[U_S1] = norm_backward(
        times(grad_mid, film[2]), normal_three, slope_three, scale_three, vec(U_G1), ones
    )
    single_grads[U_B1] = row_sum(grad)
    low = grad.astype(bf16)
    reach(15)
    for h in range(2):
        conv_weights(low, joined[h], lambda t, h=h: B_UF + 2 * t + h)
    single_grads[U_RB] = row_sum(upstream)
    reach(9)
    grad_wide = conv_source(low, up_first[0]) + dot_nn(upstream_low, up_res(0))
    grad_skip = conv_source(low, up_first[1]) + dot_nn(upstream_low, up_res(1))
    single_grads[SB] = row_sum(grad_wide)
    low_even, low_odd = halves(grad_wide.astype(bf16))
    turned_even, turned_odd = low_even.T, low_odd.T
    grad_ref[B_SPREAD] = dot_nn(turned_odd, pooled_next).astype(bf16)
    grad_ref[B_SPREAD + 1] = dot_nn(turned_even, pooled).astype(bf16)
    grad_ref[B_SPREAD + 2] = dot_nn(turned_odd, pooled).astype(bf16)
    grad_ref[B_SPREAD + 3] = dot_nn(turned_even, pooled_prev).astype(bf16)
    reach(10)
    grad_pooled = dot_nn(low_even, w_ref[B_SPREAD + 1]) + dot_nn(low_odd, w_ref[B_SPREAD + 2])
    grad_pooled = grad_pooled + dot_nn(step_frames(low_even, 1), w_ref[B_SPREAD + 3])
    grad_pooled = grad_pooled + dot_nn(step_frames(low_odd, -1), w_ref[B_SPREAD])
    single_grads[PB] = row_sum(grad_pooled)
    low = grad_pooled.astype(bf16)
    turned = low.T
    for t in range(3):
        grad_ref[B_POOL + t] = dot_nn(turned, pool_sources[t]).astype(bf16)
    reach(11)
    grad_even = dot_nn(low, w_ref[B_POOL + 1])
    grad_odd = dot_nn(low, w_ref[B_POOL + 2]) + dot_nn(step_frames(low, 1), w_ref[B_POOL])
    grad_skip = grad_skip + interleave(grad_even, grad_odd)
    single_grads[D_RB] = row_sum(grad_skip)
    skip_low = grad_skip.astype(bf16)
    misc_grad = jnp.where(lane < 50, 0.0, dot_nn(skip_low.T, inputs))
    back = dot_nn(skip_low, misc_res)
    grad, single_grads[D_G2], single_grads[D_S2] = norm_backward(
        grad_skip, normal_two, slope_two, scale_two, vec(D_G2), ones
    )
    single_grads[D_B2] = row_sum(grad)
    low = grad.astype(bf16)
    conv_weights(low, mid_one, lambda t: B_DS + t)
    reach(12)
    grad_mid = conv_source(low, down)
    shift_one = over_frames(grad_mid)
    gain_one = over_frames(grad_mid * act_one)
    grad, single_grads[D_G1], single_grads[D_S1] = norm_backward(
        times(grad_mid, film[0]), normal_one, slope_one, scale_one, vec(D_G1), ones
    )
    single_grads[D_B1] = row_sum(grad)
    low = grad.astype(bf16)
    misc_grad = misc_grad + jnp.where(lane < 50, dot_nn(low.T, inputs), 0.0)
    film_grads = (gain_one, shift_one, gain_three, shift_three)
    film_low = [g.astype(bf16) for g in film_grads]
    back_cond = None
    for q in range(4):
        single_grads[(D_FS, D_FO, U_FS, U_FO)[q]] = jnp.sum(film_grads[q], axis=0, keepdims=True)
        grad_ref[B_FILM + q // 2, :, (q % 2) * 128 : (q % 2) * 128 + 128] = dot_tn(film_low[q], cond_low).astype(bf16)
        part = dot_nn(film_low[q], film_time(q))
        back_cond = part if back_cond is None else back_cond + part
    at_slots = [dot_nn(at_slot, v) for v in film_low]
    for k in range(8):
        film_grad_ref[k] = jnp.concatenate([v[:, k * 32 : (k + 1) * 32] for v in at_slots], axis=1).astype(bf16)
    reach(13)
    grad_embed = back_cond * cond_slope
    single_grads[T_OUT] = jnp.concatenate(
        [jnp.sum(grad_embed, axis=0, keepdims=True), jnp.zeros((1, C - TE), f32)], axis=1
    )
    embed_low = grad_embed.astype(bf16)
    for j in range(2):
        grad_ref[B_OUTER, :, j * 128 : (j + 1) * 128] = dot_tn(hidden_low[j], embed_low).astype(bf16)
        grad_hidden = dot_nt(embed_low, outer[j]) * hidden[j][1]
        single_grads[T_BIAS_A + j] = jnp.sum(grad_hidden, axis=0, keepdims=True)
        grad_ref[B_INNER, :, j * 128 : (j + 1) * 128] = dot_tn(grad_hidden.astype(bf16), feats).astype(bf16)
    stack = [jnp.zeros((LANE_TAIL, 256), f32)] + [single_grads[k] for k in range(TAIL)]
    stack = jnp.concatenate(stack + [jnp.zeros((128 - LANE_TAIL - TAIL, 256), f32)], axis=0)
    grad_ref[B_MISC, :, :128] = (misc_grad + stack.T).astype(bf16)
    grad_ref[B_MISC, :, 128:] = jnp.zeros((256, 128), bf16)
    reach(14)
    result = act_four + dot_nt(wide, up_res(0)) + dot_nt(skip, up_res(1)) + vec(U_RB)
    act_ref[...] = dot_tn(result.astype(bf16), swap).astype(bf16)
    back = back + dot_nn(low, misc_first)
    grad_start = back[:, 50:60]
    for t in range(5):
        grad_start = grad_start + step_frames(back[:, t * ADIM : (t + 1) * ADIM], 2 - t)
    grad_cols = sum(dot_tn(part, swap) for part in split3(jnp.concatenate([grad_start, jnp.zeros((256, 6), f32)], axis=1)))
    noisy_grad_ref[...] = grad_cols[:ADIM] * keep


def train(weights, seen_film, slots, noisy, mask, levels, cotangent):
    vmem = pl.BlockSpec(memory_space=pltpu.VMEM)
    return pl.pallas_call(
        train_kernel,
        out_shape=(
            jax.ShapeDtypeStruct((C, 256), bf16),
            jax.ShapeDtypeStruct((ADIM, 256), f32),
            jax.ShapeDtypeStruct((NB, 256, 256), bf16),
            jax.ShapeDtypeStruct((8, SAM, 128), bf16),
        ),
        in_specs=[vmem] * 8,
        out_specs=(vmem,) * 4,
        compiler_params=pltpu.CompilerParams(vmem_limit_bytes=48 << 20),
        name="train",
    )(weights, seen_film, slots, noisy, mask, levels, cotangent, jnp.asarray(level_table(), bf16))


HALF = ROWS // 2


def native_grads(own_ref, film_ref, order_ref, grad_ref):
    native_most(own_ref, film_ref, grad_ref)
    native_rest(own_ref, order_ref, grad_ref)


def native_rest(own_ref, order_ref, grad_ref):
    misc = own_ref[B_MISC]
    first = dot_nt(misc[:, :128], order_ref[...])
    misc = misc.astype(f32)
    grad_ref[:, 0:50] = first[:, :50]
    grad_ref[:, AT_DOWN_RES : AT_DOWN_RES + ADIM] = misc[:, 50:60]
    grad_ref[:, AT_TAIL : AT_TAIL + TAIL] = misc[:, LANE_TAIL : LANE_TAIL + TAIL]
    grad_ref[:, AT_TIME[0] : AT_TIME[0] + 256] = own_ref[B_INNER].astype(f32)
    grad_ref[:, AT_TIME[1] : AT_TIME[1] + 256] = own_ref[B_OUTER].astype(f32)
    native_film(own_ref, grad_ref, 0)


def native_film(own_ref, grad_ref, side):
    for q in (2 * side, 2 * side + 1):
        part = own_ref[B_FILM + side, :, (q % 2) * 128 : (q % 2) * 128 + 128]
        grad_ref[:, AT_FILM[q] + OBS : AT_FILM[q] + OBS + TE] = part.astype(f32)


def native_most(own_ref, film_ref, grad_ref):
    for q in range(4):
        grad_ref[:, AT_FILM[q] : AT_FILM[q] + OBS] = film_ref[q * ROWS : (q + 1) * ROWS]
    native_film(own_ref, grad_ref, 1)
    for i in range(4):
        begin = AT_UP_RES + i * 128
        grad_ref[:, begin : begin + 128] = own_ref[B_UR + i, :, 0:128].astype(f32)
    for taps in (5, 3, 4):
        places = [(at, h, block) for at, k, groups, block in CONVS if k == taps for h in range(groups)]
        stacked = jnp.concatenate(
            [
                jnp.concatenate(
                    [own_ref[block(t, h), :, (h % 2) * 128 : (h % 2) * 128 + 128] for t in range(taps)], axis=1
                )
                for _, h, block in places
            ],
            axis=0,
        )
        moved = dot_nt(stacked, tap_order(taps))
        for n, (at, h, _) in enumerate(places):
            begin = at + h * 128 * taps
            grad_ref[:, begin : begin + 128 * taps] = moved[n * ROWS : (n + 1) * ROWS]


def unpack_kernel(own_ref, film_ref, order_ref, grad_ref):
    native_grads(own_ref, film_ref, order_ref, grad_ref)


def unpack(own, film):
    vmem = pl.BlockSpec(memory_space=pltpu.VMEM)
    return pl.pallas_call(
        unpack_kernel,
        out_shape=jax.ShapeDtypeStruct((ROWS, Q), f32),
        in_specs=[vmem] * 3,
        out_specs=vmem,
        compiler_params=pltpu.CompilerParams(vmem_limit_bytes=30 << 20),
        name="unpack",
    )(own, film, jnp.asarray(first_order(), bf16))


def adam_kernel(count, *refs):
    grad_ref, square_ref = refs[:2]
    old, extra_in = refs[2:5], refs[5 : 5 + count]
    norm_ref, new_hbm, extra_out = refs[5 + count], refs[6 + count : 10 + count], refs[10 + count : 10 + 2 * count]
    new, sems = refs[10 + 2 * count : 14 + 2 * count], refs[-1]
    norm = jnp.sqrt(jnp.sum(square_ref[...], axis=(0, 1), keepdims=True))
    norm_ref[...] = norm
    factor = jnp.minimum(1.0, clip_limit / (norm + 1e-06))
    stores = {}

    def store(n, height, at):
        rows = pl.ds(at, height)
        stores[n, at] = pltpu.make_async_copy(new[n].at[rows], new_hbm[n].at[rows], sems.at[n, at // 8])
        stores[n, at].start()

    width = 1024
    for row in range(0, ROWS, 8):
        for begin in range(0, Q, width):
            at = (slice(row, row + 8), slice(begin, min(begin + width, Q)))
            clipped = grad_ref[at] * factor
            new_first = decay_first * old[1][at] + (1.0 - decay_first) * clipped
            new_second = decay_second * old[2][at] + (1.0 - decay_second) * clipped * clipped
            first_hat = new_first * (1.0 / (1.0 - decay_first**ADAM_STEP))
            second_hat = new_second * (1.0 / (1.0 - decay_second**ADAM_STEP))
            before = old[0][at]
            new[0][at] = before - learn_rate * (first_hat / (jnp.sqrt(second_hat) + adam_eps) + weight_decay * before)
            new[1][at] = new_first
            new[2][at] = new_second
        for n in range(3):
            store(n, 8, row)
        if row % 16:
            rows = slice(row - 8, row + 8)
            new[3][rows] = new[0][rows].astype(bf16)
            store(3, 16, row - 8)
    for source, target in zip(extra_in, extra_out):
        target[...] = source[...].reshape(target.shape)
    for copy in stores.values():
        copy.wait()


def adam(grads, squares, params, first, second, extras=(), extra_shapes=()):
    vmem = pl.BlockSpec(memory_space=pltpu.VMEM)
    hbm = pl.BlockSpec(memory_space=pl.ANY)
    shape = jax.ShapeDtypeStruct((ROWS, Q), f32)
    count = len(extras)
    return pl.pallas_call(
        functools.partial(adam_kernel, count),
        out_shape=(
            jax.ShapeDtypeStruct((1, 1), f32),
            shape, shape, shape, jax.ShapeDtypeStruct((ROWS, Q), bf16),
            *(jax.ShapeDtypeStruct(dims, v.dtype) for dims, v in zip(extra_shapes, extras)),
        ),
        in_specs=[vmem] * (5 + count),
        out_specs=(vmem,) + (hbm,) * 4 + (vmem,) * count,
        scratch_shapes=[pltpu.VMEM((ROWS, Q), f32)] * 3
        + [pltpu.VMEM((ROWS, Q), bf16), pltpu.SemaphoreType.DMA((4, ROWS // 8))],
        compiler_params=pltpu.CompilerParams(vmem_limit_bytes=30 << 20),
        name="adam",
    )(grads, squares, params, first, second, *extras)


def local_plain(noisy, action_mask, time_index, obs_embed, obs_slot, cotangent, params, first_moment, second_moment):
    rows = params.shape[0]
    padded = lambda v: jnp.pad(v, ((0, ROWS - rows), (0, 0))) if rows < ROWS else v
    if rows > ROWS:
        packed = [pack(params[r : r + ROWS]) for r in range(0, rows, ROWS)]
        own = jnp.concatenate([p[0].reshape(NB, ROWS, 256) for p in packed], axis=1)
        film_own = jnp.concatenate([p[1].reshape(4, ROWS, OBS) for p in packed], axis=1)
    else:
        own, film_own = pack(padded(params))
        own = own.reshape(NB, ROWS, 256)[:, :rows]
        film_own = film_own.reshape(4, ROWS, OBS)[:, :rows]
    weights = lax.all_gather(own, "wide", axis=1, tiled=True)
    film_rows = lax.all_gather(film_own, "wide", axis=1, tiled=True).reshape(4 * C, OBS)
    seen = lax.all_gather(obs_embed, "pair", axis=0, tiled=True).reshape(-1, OBS).astype(f32)
    cond, slope = mish_parts(seen)
    cond = cond.astype(bf16)
    seen_film = dot_nt(cond, film_rows).reshape(4, 4, 4, 8, 32).transpose(0, 3, 1, 2, 4).reshape(4, 8, 4, 128)
    seen_film = seen_film.reshape(4, 4, 8, 128)
    act, noisy_grad, grads, film_grad = train(
        weights, seen_film, obs_slot[None], noisy[0], action_mask, time_index, cotangent[0]
    )
    film_grad = film_grad.reshape(8, SAM, 4, 32).transpose(1, 2, 0, 3).reshape(SAM, 4 * C)
    film_total = lax.psum(dot_tn(film_grad, cond), ("pair", "wide")).reshape(4, C, OBS)
    back = lax.psum_scatter(
        (dot_nn(film_grad, film_rows) * slope).reshape(-1, obs_embed.shape[1], OBS),
        "pair", scatter_dimension=0, tiled=True,
    )
    total = lax.psum(grads.astype(f32), ("pair", "wide")).astype(bf16)
    squares = jnp.sum(jnp.square(total.astype(f32))) + jnp.sum(jnp.square(film_total))
    here = lax.axis_index("wide") * rows
    mine = lax.dynamic_slice_in_dim(total, here, rows, 1)
    film_mine = lax.dynamic_slice_in_dim(film_total, here, rows, 1)
    outs = []
    for r in range(0, rows, ROWS):
        take = lambda v: jnp.pad(v[:, r : r + ROWS], ((0, 0), (0, max(0, ROWS - rows)), (0, 0)))
        outs.append(
            adam(
                unpack(take(mine), take(film_mine).reshape(4 * ROWS, OBS)), squares.reshape(1, 1),
                *(padded(v)[r : r + ROWS] for v in (params, first_moment, second_moment)),
            )
        )
    new = [jnp.concatenate([o[k] for o in outs], axis=0)[:rows] for k in range(1, 5)]
    return (act[None], noisy_grad[None], back, outs[0][0].reshape(()), *new)


MESH = pl.DeviceIdType.MESH


class Place:
    def __init__(self):
        p = lax.axis_index("pair")
        w = lax.axis_index("wide")
        self.p, self.w = p, w
        self.x, self.y = lax.rem(p, 2), lax.div(p, 2)
        self.c, self.z = lax.rem(w, 2), lax.div(w, 2)
        turn = [1 - 2 * self.x, 2 - 4 * self.y]
        self.p_flip = [p, p + turn[0], p + turn[1], p + (turn[0] + turn[1])]
        z_turn = [1 - 2 * lax.rem(self.z, 2), 2 - 4 * lax.div(self.z, 2)]
        self.z_flip = [self.z, self.z + z_turn[0], self.z + z_turn[1], self.z + (z_turn[0] + z_turn[1])]
        self.w_flip = []
        for z in self.z_flip:
            self.w_flip += [2 * z + self.c, 2 * z + (1 - self.c)]
        self.w_flip[0] = w
        self.x_of = [lax.rem(v, 2) for v in self.p_flip]
        self.y_of = [lax.div(v, 2) for v in self.p_flip]

    def line(self, l):
        return (self.p, self.w_flip[l])

    def others(self):
        return [(self.p_flip[k], self.w_flip[l]) for k in range(1, 4) for l in range(1, 8)]

    def plane(self, k):
        return (self.p_flip[k], self.w)


def greet(me):
    barrier = pltpu.get_barrier_semaphore()
    for l in range(1, 8):
        pl.semaphore_signal(barrier, inc=1, device_id=me.line(l), device_id_type=MESH)
    for k in range(1, 4):
        pl.semaphore_signal(barrier, inc=1, device_id=me.plane(k), device_id_type=MESH)


def meet(me):
    pl.semaphore_wait(pltpu.get_barrier_semaphore(), 10)


def drain(size, semaphore):
    pltpu.make_async_copy(size, size, semaphore).wait()


class Pool:
    def __init__(self, ref):
        self.ref, self.used = ref, 0

    def new(self):
        self.used += 1
        return self.ref.at[self.used - 1]

    def several(self, keys):
        return {key: self.new() for key in keys}


class Lane:
    def __init__(self, pool):
        self.sent, self.bytes = pool.new(), 0

    def send(self, source, target, arrival, device):
        pltpu.make_async_remote_copy(
            src_ref=source, dst_ref=target, send_sem=self.sent, recv_sem=arrival,
            device_id=device, device_id_type=MESH,
        ).start()
        self.bytes += math.prod(source.shape) * source.dtype.itemsize

    def finish(self, size):
        assert math.prod(size.shape) * size.dtype.itemsize == self.bytes
        drain(size, self.sent)


def fold_rows(v):
    return jnp.concatenate([v[:, q * 256 : (q + 1) * 256] for q in range(4)], axis=0)


def unfold_rows(v):
    return jnp.concatenate([v[q * 4 : (q + 1) * 4] for q in range(4)], axis=1)


def quarter_rows(parts):
    quarter = (iota(parts[0].shape, 0) >> 2) & 3
    return sum(jnp.where(quarter == q, part, 0.0) for q, part in enumerate(parts))


class Gather:
    def __init__(self, me, own, weights, seen, obs_all, film, film_part, film_line, pool, local_sem):
        self.me, self.own, self.weights, self.seen, self.obs_all, self.film = me, own, weights, seen, obs_all, film
        self.film_part, self.film_line, self.local_sem = film_part, film_line, local_sem
        self.z, self.x, self.y, self.f, self.c, self.small = (Lane(pool) for _ in range(6))
        self.parts, self.films, self.more, self.narrow = (Lane(pool) for _ in range(4))
        pieces = [(g, k) for g in range(len(GATHER_GROUPS)) for k in range(1, 4)]
        self.z_in = pool.several(pieces)
        near = [(g, k) for g, k in pieces if g not in GATHER_DIRECT] + list(GATHER_DIRECT)
        self.x_in, self.y_in = pool.several(near), pool.several(near)
        self.f_in = pool.several(range(len(GATHER_GROUPS)))
        self.c_in = pool.several(range(len(GATHER_GROUPS)))
        self.obs_in, self.part_in, self.film_in, self.more_in = (pool.new() for _ in range(4))

    def start_obs(self):
        me = self.me
        piece = self.obs_all.at[me.p, me.w]
        for l in range(1, 8):
            self.small.send(piece, piece, self.obs_in, me.line(l))

    def start_rows(self, g):
        me = self.me
        lane = self.narrow if g == NARROW else self.z
        for k in range(1, 4):
            lane.send(
                self.own.at[gather_group(g), me.p, :, cols(g)],
                self.weights.at[gather_group(g), me.p, me.z, me.c, :, cols(g)],
                self.z_in[g, k], me.line(2 * k),
            )

    def start_local(self):
        self.local = pltpu.make_async_copy(self.own, self.weights.at[:, :, self.me.z, self.me.c], self.local_sem)
        self.local.start()

    def film_product(self):
        me = self.me
        drain(self.obs_all.at[0, 0:7], self.obs_in)
        cond = mish_parts(self.obs_all[me.p].reshape(128, 256).astype(f32))[0].astype(bf16)
        film = quarter_rows([dot_nt(cond, self.film[:, q * 256 : (q + 1) * 256]) for q in range(4)])
        row, col = iota((64, 128), 0), iota((64, 128), 1)
        pick = one_hot(((row >> 3) == (col >> 4)) & ((row & 7) == (col & 3)))
        self.film_part[...] = sum(dot_nn(pick, part) for part in split3(film)).reshape(8, 8, 128)
        for l in range(1, 8):
            self.parts.send(self.film_part.at[me.w_flip[l]], self.film_line.at[me.w], self.part_in, me.line(l))
        self.film_line[me.w] = self.film_part[me.w]

    def film_hop(self):
        me = self.me
        drain(self.film_line.at[0:7], self.part_in)
        for k in range(4):
            self.seen[me.p, k] = self.film_line[2 * k] + pltpu.roll(self.film_line[2 * k + 1], 4, 0)
        piece = self.seen.at[me.p]
        for k in range(1, 4):
            self.films.send(piece, piece, self.film_in, me.plane(k))

    def obs_hop(self):
        me = self.me
        piece = self.obs_all.at[me.p]
        for k in range(1, 4):
            self.more.send(piece, piece, self.more_in, me.plane(k))

    def film_done(self):
        drain(self.seen.at[0:3], self.film_in)

    def first_hop(self, g):
        me = self.me
        lanes = [self.narrow] * 3 if g == NARROW else [self.x, self.y, self.f]
        for k in range(1, 4):
            piece = self.weights.at[gather_group(g), me.p, me.z_flip[k], me.c, :, cols(g)]
            drain(piece, self.z_in[g, k])
            key = g if g in GATHER_DIRECT else (g, k)
            lanes[0].send(piece, piece, self.x_in[key], me.plane(1))
            lanes[1].send(piece, piece, self.y_in[key], me.plane(2))
            if g in GATHER_DIRECT:
                lanes[2].send(piece, piece, self.f_in[g], me.plane(3))

    def three(self, g):
        return self.weights.at[gather_group(g), 0, 0:3, 0, :, cols(g)]

    def second_hop(self, g):
        me = self.me
        if g in GATHER_DIRECT:
            drain(self.three(g), self.x_in[g])
            drain(self.three(g), self.y_in[g])
            return
        for k in range(1, 4):
            one = self.weights.at[gather_group(g), 0, 0, 0]
            drain(one, self.x_in[g, k])
            drain(one, self.y_in[g, k])
            along_y = (g + k) % 2 == 0
            piece = self.weights.at[gather_group(g), me.p_flip[1 if along_y else 2], me.z_flip[k], me.c]
            self.f.send(piece, piece, self.f_in[g], me.plane(2 if along_y else 1))

    def last_hop(self, g):
        if g == 0:
            self.local.wait()
        if g in GATHER_DIRECT:
            self.second_hop(g)
        drain(self.three(g), self.f_in[g])
        piece = self.weights.at[gather_group(g), :, :, self.me.c, :, cols(g)]
        (self.narrow if g == NARROW else self.c).send(piece, piece, self.c_in[g], self.me.line(1))

    def arrived(self, g):
        drain(self.weights.at[gather_group(g), :, :, 0, :, cols(g)], self.c_in[g])

    def obs_done(self):
        drain(self.obs_all.at[0:3], self.more_in)

    def finish(self):
        wide = pl.ds(0, GATHER_GROUPS[NARROW][0])
        for lane in (self.z, self.x, self.y, self.f):
            lane.finish(self.weights.at[wide, 0, 0:3, 0])
        self.c.finish(self.weights.at[wide, :, :, 0])
        self.narrow.finish(self.weights.at[0:7, :, 0, 0, :, cols(NARROW)])
        self.small.finish(self.obs_all.at[0, 0:7])
        self.parts.finish(self.film_line.at[0:7])
        self.films.finish(self.seen.at[0:3])
        self.more.finish(self.obs_all.at[0:3])


class Scatter:
    def __init__(self, me, grad, film_grad, obs_all, film, out, film_out, back, square, buffers, pool):
        self.me, self.grad, self.film_grad, self.obs_all, self.film = me, grad, film_grad, obs_all, film
        self.out, self.film_out, self.back, self.square = out, film_out, back, square
        (self.half, self.core, self.xb, self.yb, self.ub, self.vb, self.zb, self.zq, self.pq, self.db,
         self.film_all, self.back_part, self.back_line, self.cond, self.all_squares) = buffers
        self.c, self.x, self.y, self.u, self.v, self.z = (Lane(pool) for _ in range(6))
        self.zf, self.q, self.d, self.r, self.g, self.h, self.b, self.n = (Lane(pool) for _ in range(8))
        self.narrow, self.narrow_end = Lane(pool), Lane(pool)
        groups = range(len(GROUPS))
        self.staged = [g for g in groups if g != Z_FIRST and g not in PLANE_DIRECT]
        self.c_in = pool.several(groups)
        self.x_in, self.y_in, self.u_in, self.v_in = (pool.several(self.staged) for _ in range(4))
        self.d_in = pool.several(PLANE_DIRECT)
        self.z_in = pool.several(g for g in groups if g != Z_FIRST)
        self.zf_in, self.q_in, self.r_in, self.g_in, self.h_in, self.b_in, self.n_in = (pool.new() for _ in range(7))
        self.narrow_in, self.r_last = pool.new(), pool.new()
        self.squares = []

    def start(self, g):
        me = self.me
        lane = self.narrow if g == NARROW else self.c
        lane.send(
            self.grad.at[group(g), :, :, 1 - me.c, :, cols(g)], self.core.at[group(g), :, :, :, cols(g)],
            self.c_in[g], me.line(1),
        )

    def core_sum(self, g):
        me, half, (first, last) = self.me, self.half, GROUPS[g]
        drain(self.core.at[group(g), :, :, :, cols(g)], self.c_in[g])

        def add(i, _):
            j, q = first + i // 4, i % 4
            total = self.grad[j, q, :, me.c, :, cols(g)].astype(f32) + self.core[j, q, :, :, cols(g)].astype(f32)
            half[j, q // 2, q % 2, :, :, cols(g)] = total.astype(bf16)
            return 0

        lax.fori_loop(0, (last - first) * 4, add, 0)
        if g == Z_FIRST:
            self.z_send(g, 0)
        elif g in PLANE_DIRECT:
            for k in range(1, 4):
                piece = half.at[group(g), me.y_of[k], me.x_of[k]]
                self.d.send(piece, self.db.at[k - 1, group(g)], self.d_in[g], me.plane(k))
        else:
            lanes = [self.narrow] * 2 if g == NARROW else [self.x, self.y]
            lanes[0].send(
                half.at[group(g), :, 1 - me.x, LOW, :, cols(g)], self.xb.at[group(g), :, :, :, cols(g)],
                self.x_in[g], me.plane(1),
            )
            lanes[1].send(
                half.at[group(g), 1 - me.y, :, HIGH, :, cols(g)], self.yb.at[group(g), :, :, :, cols(g)],
                self.y_in[g], me.plane(2),
            )

    def z_send(self, g, n):
        me = self.me
        for k in range(1, 4):
            self.zf.send(
                self.half.at[GROUPS[g][0] + n, :, :, me.z_flip[k]], self.zq.at[k - 1, n], self.zf_in, me.line(2 * k)
            )

    def z_sum(self, g):
        me, half, (first, last) = self.me, self.half, GROUPS[g]
        drain(self.zq, self.zf_in)
        for j in range(first, last):
            total = half[j, :, :, me.z].astype(f32)
            for k in range(3):
                total = total + self.zq[k, j - first].astype(f32)
            half[j, :, :, me.z] = total.astype(bf16)
        for k in range(1, 4):
            piece = half.at[group(g), me.y_of[k], me.x_of[k], me.z]
            self.q.send(piece, self.pq.at[k - 1], self.q_in, me.plane(k))

    def plane_sum(self, g):
        drain(self.pq, self.q_in)
        self.finish_sum(g, [lambda j, k=k: self.pq[k, j - GROUPS[g][0]] for k in range(3)])

    def first_sum(self, g):
        me, half, (first, last) = self.me, self.half, GROUPS[g]
        lanes = [self.narrow] * 2 if g == NARROW else [self.u, self.v]
        drain(self.xb.at[group(g), :, :, :, cols(g)], self.x_in[g])

        def add_x(i, _):
            j, q = first + i // 2, i % 2
            total = half[j, q, me.x, LOW, :, cols(g)].astype(f32) + self.xb[j, q, :, :, cols(g)].astype(f32)
            half[j, q, me.x, LOW, :, cols(g)] = total.astype(bf16)
            return 0

        lax.fori_loop(0, (last - first) * 2, add_x, 0)
        lanes[0].send(
            half.at[group(g), 1 - me.y, me.x, LOW, :, cols(g)], self.ub.at[group(g), :, :, cols(g)],
            self.u_in[g], me.plane(2),
        )
        drain(self.yb.at[group(g), :, :, :, cols(g)], self.y_in[g])

        def add_y(i, _):
            j, q = first + i // 2, i % 2
            total = half[j, me.y, q, HIGH, :, cols(g)].astype(f32) + self.yb[j, q, :, :, cols(g)].astype(f32)
            half[j, me.y, q, HIGH, :, cols(g)] = total.astype(bf16)
            return 0

        lax.fori_loop(0, (last - first) * 2, add_y, 0)
        lanes[1].send(
            half.at[group(g), me.y, 1 - me.x, HIGH, :, cols(g)], self.vb.at[group(g), :, :, cols(g)],
            self.v_in[g], me.plane(1),
        )

    def direct_sum(self, g):
        me, half = self.me, self.half
        drain(self.db.at[:, group(g)], self.d_in[g])
        for j in range(*GROUPS[g]):
            total = half[j, me.y, me.x].astype(f32)
            for k in range(3):
                total = total + self.db[k, j].astype(f32)
            half[j, me.y, me.x] = total.astype(bf16)
        self.send_z(g)

    def second_sum(self, g):
        me, half = self.me, self.half
        drain(self.ub.at[group(g), :, :, cols(g)], self.u_in[g])
        drain(self.vb.at[group(g), :, :, cols(g)], self.v_in[g])
        for j in range(*GROUPS[g]):
            for part, more in ((LOW, self.ub), (HIGH, self.vb)):
                total = half[j, me.y, me.x, part, :, cols(g)].astype(f32) + more[j, :, :, cols(g)].astype(f32)
                half[j, me.y, me.x, part, :, cols(g)] = total.astype(bf16)
        self.send_z(g)

    def send_z(self, g):
        me = self.me
        lane = self.narrow_end if g == NARROW else self.z
        for k in range(1, 4):
            piece = self.half.at[group(g), me.y, me.x, me.z_flip[k], :, cols(g)]
            lane.send(piece, self.zb.at[k - 1, group(g), :, cols(g)], self.z_in[g], me.line(2 * k))

    def last_sum(self, g):
        drain(self.zb.at[:, group(g), :, cols(g)], self.z_in[g])
        self.finish_sum(g, [lambda j, k=k: self.zb[k, j, :, cols(g)] for k in range(3)])

    def finish_sum(self, g, terms):
        me = self.me
        for j in range(*GROUPS[g]):
            total = self.half[j, me.y, me.x, me.z, :, cols(g)].astype(f32)
            for term in terms:
                total = total + term(j).astype(f32)
            total = total.astype(bf16)
            self.out[j, me.p, :, cols(g)] = total
            self.count(jnp.square(total.astype(f32)))
        piece = self.out.at[group(g), me.p, :, cols(g)]
        lane, arrival = (self.narrow_end, self.narrow_in) if g == NARROW else (self.r, self.r_in)
        if g == 0:
            arrival = self.r_last
        for k in range(1, 4):
            lane.send(piece, piece, arrival, me.plane(k))

    def count(self, squares):
        folded = jnp.sum(squares.reshape(-1, 8, squares.shape[1]), axis=0)
        self.squares += [folded[:, i : i + 128] for i in range(0, squares.shape[1], 128)]

    def film_start(self):
        me = self.me
        self.film_all[me.p, me.w] = self.film_grad[me.w]
        for l in range(1, 8):
            self.g.send(self.film_grad.at[me.w_flip[l]], self.film_all.at[me.p, me.w], self.g_in, me.line(l))

    def film_hop(self):
        me = self.me
        drain(self.film_all.at[0, 0:7], self.g_in)
        piece = self.film_all.at[me.p]
        for k in range(1, 4):
            self.h.send(piece, piece, self.h_in, me.plane(k))

    def film_inputs(self):
        row, col = iota((128, 512), 0), iota((128, 512), 1)
        same = ((row >> 4) == ((col >> 4) & 7)) & (((row >> 2) & 3) == (col >> 7)) & ((row & 3) == (col & 3))
        seen_all = self.obs_all[...].reshape(512, 256)
        for q in range(4):
            pick = one_hot(same & (((col >> 2) & 3) == q))
            self.cond[q] = mish_parts(dot_nn(pick, seen_all))[0].astype(bf16)

    def film_products(self):
        me = self.me
        drain(self.film_all.at[0:3], self.h_in)
        copies = [self.film_all[k].reshape(128, 128).astype(f32) for k in range(4)]
        total = split2((copies[0] + copies[1]) + (copies[2] + copies[3]))
        row, col = iota((128, 128), 0), iota((128, 128), 1)
        mine = one_hot(((row >> 4) == (col >> 4)) & ((col & 15) == 4 * me.p + (row & 3)))
        rows = [dot_nn(mine, part).astype(bf16) for part in total]
        parts = [
            dot_nn(rows[0], self.film[:, q * 256 : (q + 1) * 256])
            + dot_nn(rows[1], self.film[:, q * 256 : (q + 1) * 256])
            for q in range(4)
        ]
        self.back_part[...] = quarter_rows(parts).astype(bf16).reshape(8, 16, 256)
        for l in range(1, 8):
            self.b.send(self.back_part.at[me.w_flip[l]], self.back_line.at[me.w], self.b_in, me.line(l))
        self.back_line[me.w] = self.back_part[me.w]
        turned = [part.T for part in total]
        for q in range(4):
            cond = self.cond[q]
            product = dot_nn(turned[0], cond) + dot_nn(turned[1], cond)
            self.film_out[:, q * 256 : (q + 1) * 256] = product
            self.count(0.25 * jnp.square(product))

    def film_back(self):
        me = self.me
        drain(self.back_line.at[0:7], self.b_in)
        total = jnp.sum(self.back_line[...].astype(f32), axis=0)
        slope = mish_parts(self.obs_all[me.p, me.w].astype(f32))[1]
        self.back[0] = unfold_rows(total * slope)

    def norm(self, hello, most, rest):
        me = self.me
        total = sum(self.squares)
        here = me.p * 8 + me.w
        piece = self.all_squares.at[here]
        self.all_squares[here] = jnp.sum(total, axis=0, keepdims=True)
        pl.semaphore_wait(hello, len(me.others()))
        for i in range(1, 32):
            self.n.send(piece, piece, self.n_in, (me.p_flip[i % 4], me.w_flip[i // 4]))
        drain(self.zb.at[:, GROUPS[0][1] : GROUPS[NARROW][0]], self.r_in)
        drain(self.zb.at[:, 0:1, :, cols(NARROW)], self.narrow_in)
        most()
        drain(self.zb.at[:, group(0)], self.r_last)
        rest()
        drain(self.all_squares.at[0:31], self.n_in)
        self.square[...] = jnp.sum(self.all_squares[...].reshape(32, 128), axis=0, keepdims=True)

    def finish(self):
        size = lambda gs: sum(GROUPS[g][1] - GROUPS[g][0] for g in gs if g != NARROW)
        staged, wide = size(self.staged), pl.ds(0, GROUPS[NARROW][0])
        self.c.finish(self.grad.at[wide, :, :, 0])
        self.x.finish(self.xb.at[0:staged])
        self.y.finish(self.yb.at[0:staged])
        self.u.finish(self.ub.at[0:staged])
        self.v.finish(self.vb.at[0:staged])
        self.d.finish(self.db.at[:, 0 : size(PLANE_DIRECT)])
        self.z.finish(self.zb.at[:, 0 : staged + size(PLANE_DIRECT)])
        self.zf.finish(self.zq)
        self.q.finish(self.pq)
        self.r.finish(self.zb.at[:, wide])
        self.narrow.finish(self.grad.at[0:7, :, 0, 0, :, cols(NARROW)])
        self.narrow_end.finish(self.zb.at[:, 0:2, :, cols(NARROW)])
        self.g.finish(self.film_all.at[0, 0:7])
        self.h.finish(self.film_all.at[0:3])
        self.b.finish(self.back_line.at[0:7])
        self.n.finish(self.all_squares.at[0:31])


GATHER_GROUPS = ((0, 1), (1, 3), (3, 5), (5, 7), (7, 8), (8, 9))
GATHER_DIRECT = (4, 5)
GROUPS = ((0, 1), (1, 3), (3, 5), (5, 7), (7, 8), (8, 9))
Z_FIRST = 3
PLANE_DIRECT = (0,)
SEMAPHORES = 125
LOW, HIGH = pl.ds(0, 2), pl.ds(2, 2)


NARROW = 5


def cols(g):
    return pl.ds(0, 128 if g == NARROW else 256)


def group(g):
    return pl.ds(GROUPS[g][0], GROUPS[g][1] - GROUPS[g][0])


def gather_group(g):
    return pl.ds(GATHER_GROUPS[g][0], GATHER_GROUPS[g][1] - GATHER_GROUPS[g][0])


def step_kernel(*refs):
    params_out = refs[16]
    targets = (params_out,) + refs[19:27]
    loads = [
        pltpu.make_async_copy(source, target, refs[-2].at[i])
        for i, (source, target) in enumerate(zip(refs[:11], targets + refs[17:19]))
    ]
    for i in (0, 2, 1, 3, 4, 5, 6, 7, 8):
        loads[i].start()
    refs = targets + refs[9:11] + refs[11:16] + refs[17:19] + refs[27:-2] + refs[-1:]
    (params, order, obs, slots, noisy, mask, levels, cotangent, table, first, second,
     act, noisy_grad, back, native, square, first_out, second_out,
     own, weights, seen, obs_all, film, film_part, film_line, grad, film_grad, out, film_out) = refs[:29]
    buffers, (semaphores, local_sem, hello) = refs[29:44], refs[44:]
    pool = Pool(semaphores)
    me = Place()
    gather = Gather(me, own, weights, seen, obs_all, film, film_part, film_line, pool, local_sem)
    scatter = Scatter(me, grad, film_grad, obs_all, film, out, film_out, back, square, buffers, pool)
    greet(me)
    loads[0].wait()
    loads[1].wait()
    pack_first(params, order, own)
    loads[2].wait()
    obs_all[me.p, me.w] = fold_rows(obs[0].astype(f32)).astype(bf16)
    meet(me)
    gather.start_rows(0)
    gather.start_obs()
    pack_rest(params, own, film)
    gather.start_local()
    gather.start_rows(1)
    for i in range(3, 9):
        loads[i].wait()

    def reach(point):
        if point == 0:
            gather.first_hop(0)
            gather.film_product()
            for g in range(2, len(GATHER_GROUPS)):
                gather.start_rows(g)
            gather.first_hop(1)
            gather.second_hop(0)
            gather.film_hop()
            gather.first_hop(2)
            gather.last_hop(0)
            gather.second_hop(1)
            for device in me.others():
                pl.semaphore_signal(hello, inc=1, device_id=device, device_id_type=MESH)
            gather.arrived(0)
        if point == 1:
            gather.first_hop(3)
            gather.second_hop(2)
            gather.last_hop(1)
            gather.film_done()
        if point == 2:
            gather.arrived(1)
            gather.first_hop(4)
        if point == 3:
            gather.last_hop(2)
            gather.second_hop(3)
            gather.arrived(2)
        if point == 4:
            gather.last_hop(3)
        if point == 5:
            gather.last_hop(4)
            gather.first_hop(5)
            gather.arrived(3)
        if point == 6:
            gather.obs_hop()
            loads[9].start()
            loads[10].start()
            gather.arrived(4)
        if point == 8:
            gather.last_hop(5)
            scatter.start(5)
            scatter.start(4)
        if point == 15:
            scatter.core_sum(5)
            scatter.core_sum(4)
        if point == 9:
            scatter.start(3)
            gather.arrived(5)
        if point == 10:
            scatter.core_sum(3)
        if point == 11:
            scatter.start(2)
        if point == 12:
            scatter.core_sum(2)
            scatter.first_sum(5)
            scatter.first_sum(4)
        if point == 13:
            scatter.film_start()
            scatter.z_send(Z_FIRST, 1)
            scatter.start(1)
        if point == 14:
            scatter.start(0)
            scatter.core_sum(1)
            scatter.second_sum(5)
            scatter.second_sum(4)
            scatter.core_sum(0)
            scatter.first_sum(2)

    train_body(
        Stacked(weights), seen, slots, noisy, mask, levels, cotangent, table,
        act, noisy_grad, Stacked(grad), film_grad, reach,
    )
    scatter.film_hop()
    scatter.first_sum(1)
    gather.obs_done()
    scatter.film_inputs()
    scatter.second_sum(2)
    scatter.z_sum(3)
    scatter.film_products()
    scatter.second_sum(1)
    scatter.direct_sum(0)
    scatter.plane_sum(3)
    scatter.last_sum(5)
    scatter.last_sum(4)
    scatter.last_sum(2)
    scatter.last_sum(1)
    scatter.film_back()
    scatter.last_sum(0)
    loads[9].wait()
    loads[10].wait()
    scatter.norm(
        hello,
        lambda: native_most(Blocks(out), film_out, native),
        lambda: native_rest(Blocks(out), order, native),
    )
    gather.finish()
    scatter.finish()
    assert pool.used <= SEMAPHORES


class Stacked:
    def __init__(self, ref):
        self.ref = ref

    def _split(self, key):
        if not isinstance(key, tuple):
            return key, slice(None)
        return key[0], key[2]

    def __getitem__(self, key):
        block, cols = self._split(key)
        value = self.ref[block // 4, block % 4, :, :, :, cols]
        return value.reshape(256, value.shape[-1])

    def __setitem__(self, key, value):
        block, cols = self._split(key)
        self.ref[block // 4, block % 4, :, :, :, cols] = value.reshape(4, 2, ROWS, value.shape[-1])


def step(params, obs, slots, noisy, mask, levels, cotangent, first, second):
    vmem = pl.BlockSpec(memory_space=pltpu.VMEM)
    n = NB // 4
    inputs = (
        params, jnp.asarray(first_order(), bf16), obs, slots, noisy, mask, levels, cotangent,
        jnp.asarray(level_table(), bf16), first, second,
    )
    inputs = tuple(pltpu.with_memory_space_constraint(v, pltpu.HBM) for v in inputs)
    low = lambda *shape: pltpu.VMEM(shape, bf16)
    return pl.pallas_call(
        step_kernel,
        out_shape=(
            jax.ShapeDtypeStruct((C, 256), bf16),
            jax.ShapeDtypeStruct((ADIM, 256), f32),
            jax.ShapeDtypeStruct((1, 4, OBS), f32),
            jax.ShapeDtypeStruct((ROWS, Q), f32),
            jax.ShapeDtypeStruct((1, 128), f32),
            *[jax.ShapeDtypeStruct((ROWS, Q), f32)] * 3,
        ),
        in_specs=[pl.BlockSpec(memory_space=pltpu.HBM)] * 11,
        out_specs=(vmem,) * 8,
        scratch_shapes=[
            *(pltpu.VMEM(v.shape, v.dtype) for v in inputs[1:9]),
            low(n, 4, ROWS, 256),
            low(n, 4, 4, 2, ROWS, 256),
            pltpu.VMEM((4, 4, 8, 128), f32),
            low(4, 8, 16, 256),
            low(4 * ROWS, OBS),
            pltpu.VMEM((8, 8, 128), f32),
            pltpu.VMEM((8, 8, 128), f32),
            low(n, 4, 4, 2, ROWS, 256),
            low(8, SAM, 128),
            low(n, 4, ROWS, 256),
            pltpu.VMEM((4 * ROWS, OBS), f32),
            low(n, 2, 2, 4, ROWS, 256),
            low(n, 4, 4, ROWS, 256),
            low(n, 2, 2, ROWS, 256),
            low(n, 2, 2, ROWS, 256),
            low(n, 2, ROWS, 256),
            low(n, 2, ROWS, 256),
            low(3, n, ROWS, 256),
            low(3, GROUPS[Z_FIRST][1] - GROUPS[Z_FIRST][0], 2, 2, ROWS, 256),
            low(3, GROUPS[Z_FIRST][1] - GROUPS[Z_FIRST][0], ROWS, 256),
            low(3, GROUPS[max(PLANE_DIRECT)][1], 4, ROWS, 256),
            low(4, 8, 16, 128),
            low(8, 16, 256),
            low(8, 16, 256),
            low(4, 128, 256),
            pltpu.VMEM((32, 1, 128), f32),
            pltpu.SemaphoreType.DMA((SEMAPHORES,)),
            pltpu.SemaphoreType.DMA,
            pltpu.SemaphoreType.DMA((11,)),
            pltpu.SemaphoreType.REGULAR,
        ],
        compiler_params=pltpu.CompilerParams(collective_id=0, has_side_effects=True, vmem_limit_bytes=34 << 20),
        cost_estimate=pl.CostEstimate(flops=3 * 10**9, bytes_accessed=200 * 10**6, transcendentals=10**6),
        name="step",
    )(*inputs)


def local_fast(noisy, action_mask, time_index, obs_embed, obs_slot, cotangent, params, first_moment, second_moment):
    act, noisy_grad, back, native, squares, params, first_moment, second_moment = step(
        params, obs_embed, obs_slot[None], noisy[0], action_mask, time_index, cotangent[0],
        first_moment, second_moment,
    )
    norm, *new, act, noisy_grad, back = adam(
        native, squares, params, first_moment, second_moment,
        (act, noisy_grad, back), ((1, C, 256), (ADIM, 1, 256), (1, 4, OBS)),
    )
    return (act, noisy_grad.transpose(1, 0, 2), back, norm.reshape(()), *new)


def solution(mesh):
    in_specs = (
        P("pair", None, "wide"),
        P(None, "wide"),
        P("pair", "wide"),
        P("pair", "wide", None),
        P("wide"),
        P("pair", None, "wide"),
        P("wide", None),
        P("wide", None),
        P("wide", None),
    )
    out_specs = (
        P("pair", None, "wide"),
        P("pair", None, "wide"),
        P("pair", "wide", None),
        P(),
        P("wide", None),
        P("wide", None),
        P("wide", None),
        P("wide", None),
    )
    fast = mesh.shape["pair"] == 4 and mesh.shape["wide"] == 8
    return jax.shard_map(local_fast if fast else local_plain, mesh=mesh, in_specs=in_specs, out_specs=out_specs, check_vma=False)
```

```python
import functools
import math

import jax
import jax.numpy as jnp
import numpy as np
from jax import lax
from jax.experimental import pallas as pl
from jax.experimental.pallas import tpu as pltpu
from jax.sharding import PartitionSpec as P

C = 256
OBS = 1024
TE = 128
TH = 512
ADIM = 10
FR = 16
LEVELS = 40
ADAM_STEP = 7
Q = 12627
SAM = 16
ROWS = 32
NB = 36

sigma_top = 80.0 ** (1.0 / 7.0)
sigma_low = 0.002 ** (1.0 / 7.0)
clip_limit = 1.0
learn_rate = 0.02
decay_first = 0.5
decay_second = 0.5
adam_eps = 1e-08
weight_decay = 0.01
norm_eps = 1e-05

f32 = jnp.float32
bf16 = jnp.bfloat16

AT_DOWN_RES = 1330
AT_TAIL = 12604
TAIL = 23
AT_FILM = (1340, 2492, 9788, 10940)
AT_TIME = (12092, 12348)
AT_UP_RES = 9276
B_MISC, B_INNER, B_OUTER, B_FILM = 0, 1, 2, 3
B_DS, B_POOL, B_SPREAD, B_UF, B_US, B_UR = 5, 10, 13, 17, 27, 32
LANE_TAIL = 64
CONVS = (
    (50, 5, 2, lambda t, h: B_DS + t),
    (5436, 5, 4, lambda t, h: B_UF + 2 * t + h // 2),
    (7996, 5, 2, lambda t, h: B_US + t),
    (3644, 3, 2, lambda t, h: B_POOL + t),
    (4412, 4, 2, lambda t, h: B_SPREAD + t),
)
(T_BIAS_A, T_BIAS_B, T_OUT, D_B1, D_G1, D_S1, D_FS, D_FO, D_B2, D_G2, D_S2, D_RB, PB, SB,
 U_B1, U_G1, U_S1, U_FS, U_FO, U_B2, U_G2, U_S2, U_RB) = range(TAIL)


def dot_nt(a, b):
    return lax.dot_general(a, b, (((1,), (1,)), ((), ())), preferred_element_type=f32)


def dot_nn(a, b):
    return lax.dot_general(a, b, (((1,), (0,)), ((), ())), preferred_element_type=f32)


def dot_tn(a, b):
    return lax.dot_general(a, b, (((0,), (0,)), ((), ())), preferred_element_type=f32)


def split2(v):
    high = v.astype(bf16)
    return high, (v - high.astype(f32)).astype(bf16)


def split3(v):
    high, rest = v.astype(bf16), None
    rest = v - high.astype(f32)
    mid = rest.astype(bf16)
    return high, mid, (rest - mid.astype(f32)).astype(bf16)


def iota(shape, dim):
    return lax.broadcasted_iota(jnp.int32, shape, dim)


def one_hot(condition):
    return jnp.where(condition, 1.0, 0.0).astype(bf16)


def tap_order(taps):
    n = 128 * taps
    row = lax.broadcasted_iota(jnp.int32, (n, n), 0)
    col = lax.broadcasted_iota(jnp.int32, (1, n), 1)
    source = (col & 127) * taps + (col >> 7)
    return jnp.where(row == source, 1.0, 0.0).astype(bf16)


def first_order():
    table = np.zeros((128, 128), np.float32)
    for i in range(ADIM):
        for t in range(5):
            table[i * 5 + t, t * ADIM + i] = 1.0
    return table


def level_table():
    levels = np.arange(LEVELS, dtype=np.float64)
    tau = 250.0 * 7.0 * np.log(sigma_top + levels / (LEVELS - 1) * (sigma_low - sigma_top))
    freq = np.exp(-math.log(10000.0) * np.arange(TE // 2) / (TE // 2 - 1))
    angles = tau[:, None] * freq[None, :]
    table = np.zeros((64, TE), np.float32)
    table[:LEVELS] = np.concatenate([np.sin(angles), np.cos(angles)], axis=1)
    return table


def pack_kernel(params_ref, order_ref, own_ref, film_ref):
    pack_rows(params_ref, order_ref, own_ref, film_ref)


class Blocks:
    def __init__(self, ref):
        self.ref = ref

    def _at(self, key):
        block, rest = (key[0], key[1:]) if isinstance(key, tuple) else (key, ())
        return (block // 4, block % 4) + rest

    def __getitem__(self, key):
        return self.ref[self._at(key)]

    def __setitem__(self, key, value):
        self.ref[self._at(key)] = value


def pack_rows(params_ref, order_ref, own_ref, film_ref):
    pack_first(params_ref, order_ref, own_ref)
    pack_rest(params_ref, own_ref, film_ref)


def pack_first(params_ref, order_ref, own_ref):
    own_ref = Blocks(own_ref)

    def low(start, width):
        return params_ref[:, start : start + width].astype(bf16)

    first = dot_nn(low(0, 128), order_ref[...])
    pieces = [
        first[:, :50],
        params_ref[:, AT_DOWN_RES : AT_DOWN_RES + ADIM],
        jnp.zeros((ROWS, LANE_TAIL - 60), f32),
        params_ref[:, AT_TAIL : AT_TAIL + TAIL],
        jnp.zeros((ROWS, 256 - LANE_TAIL - TAIL), f32),
    ]
    own_ref[B_MISC] = jnp.concatenate(pieces, axis=1).astype(bf16)
    own_ref[B_INNER] = low(AT_TIME[0], 256)
    own_ref[B_OUTER] = low(AT_TIME[1], 256)
    for q in range(4):
        own_ref[B_FILM + q // 2, :, (q % 2) * 128 : (q % 2) * 128 + 128] = low(AT_FILM[q] + OBS, TE)


def pack_rest(params_ref, own_ref, film_ref):
    own_ref = Blocks(own_ref)

    def low(start, width):
        return params_ref[:, start : start + width].astype(bf16)

    for q in range(4):
        film_ref[q * ROWS : (q + 1) * ROWS] = low(AT_FILM[q], OBS)
    for i in range(4):
        own_ref[B_UR + i, :, 0:128] = low(AT_UP_RES + i * 128, 128)
    for taps in (5, 3, 4):
        places = [(at, h, block) for at, k, groups, block in CONVS if k == taps for h in range(groups)]
        stacked = jnp.concatenate([low(at + h * 128 * taps, 128 * taps) for at, h, _ in places], axis=0)
        moved = dot_nn(stacked, tap_order(taps)).astype(bf16)
        for n, (_, h, block) in enumerate(places):
            for t in range(taps):
                own_ref[block(t, h), :, (h % 2) * 128 : (h % 2) * 128 + 128] = moved[
                    n * ROWS : (n + 1) * ROWS, t * 128 : (t + 1) * 128
                ]


def pack(params):
    vmem = pl.BlockSpec(memory_space=pltpu.VMEM)
    return pl.pallas_call(
        pack_kernel,
        out_shape=(
            jax.ShapeDtypeStruct((NB // 4, 4, ROWS, 256), bf16),
            jax.ShapeDtypeStruct((4 * ROWS, OBS), bf16),
        ),
        in_specs=[vmem, vmem],
        out_specs=(vmem, vmem),
        compiler_params=pltpu.CompilerParams(vmem_limit_bytes=40 << 20),
        name="pack",
    )(params, jnp.asarray(first_order(), bf16))


def mish_parts(v):
    e = jnp.exp(jnp.minimum(v, 20.0))
    n = e * (e + 2.0)
    r = 1.0 / (n + 2.0)
    t = n * r
    return v * t, t + 4.0 * v * (e * r) * ((e + 1.0) * r)


def step_frames(v, step):
    if step == 0:
        return v
    zeros = jnp.zeros((SAM * abs(step), v.shape[1]), v.dtype)
    if step > 0:
        return jnp.concatenate([v[SAM * step :], zeros], axis=0)
    return jnp.concatenate([zeros, v[: SAM * step]], axis=0)


def over_frames(v):
    return jnp.sum(v.reshape(-1, SAM, v.shape[1]), axis=0)


def each_frame(v, s):
    return v.reshape(-1, SAM, v.shape[1]), s[None]


def group_means(values, ones):
    parts = [p for v in values for p in split3(v)]
    sums = dot_nn(jnp.concatenate(parts, axis=0), ones)
    out = []
    for i in range(len(values)):
        a, b, c = (sums[(3 * i + k) * SAM : (3 * i + k + 1) * SAM] for k in range(3))
        out.append((a + (b + c)) * (1.0 / (32 * FR)))
    return out


def minus(v, s):
    a, b = each_frame(v, s)
    return (a - b).reshape(v.shape)


def times(v, s):
    a, b = each_frame(v, s)
    return (a * b).reshape(v.shape)


def plus(v, s):
    a, b = each_frame(v, s)
    return (a + b).reshape(v.shape)


def norm_forward(before, gain, shift, ones):
    center, square = group_means([over_frames(before), over_frames(before * before)], ones)
    scale = lax.rsqrt(jnp.maximum(square - center * center, 0.0) + norm_eps)
    away = minus(before, center)
    normal = times(away, scale)
    act, slope = mish_parts(normal * gain + shift)
    return act, normal, slope, scale


def norm_backward(grad_act, normal, slope, scale, gain, ones):
    grad_out = grad_act * slope
    shift_rows = over_frames(grad_out)
    gain_rows = over_frames(grad_out * normal)
    mean_grad, mean_both = group_means([shift_rows * gain, gain_rows * gain], ones)
    inner = minus(grad_out * gain, mean_grad) - times(normal, mean_both)
    return (
        times(inner, scale),
        jnp.sum(gain_rows, axis=0, keepdims=True),
        jnp.sum(shift_rows, axis=0, keepdims=True),
    )


def conv_forward(source, weight):
    total = dot_nt(step_frames(source, -2), weight(0))
    for t in range(1, 5):
        total = total + dot_nt(step_frames(source, t - 2), weight(t))
    return total


def conv_source(grad_low, weight):
    total = dot_nn(step_frames(grad_low, 2), weight(0))
    for t in range(1, 5):
        total = total + dot_nn(step_frames(grad_low, 2 - t), weight(t))
    return total


def row_sum(v):
    return jnp.sum(over_frames(v), axis=0, keepdims=True)


def halves(v):
    cube = v.reshape(FR // 2, 2, SAM, v.shape[1])
    return cube[:, 0].reshape(-1, v.shape[1]), cube[:, 1].reshape(-1, v.shape[1])


def interleave(even, odd):
    width = even.shape[1]
    pair = [v.reshape(FR // 2, 1, SAM, width) for v in (even, odd)]
    return jnp.concatenate(pair, axis=1).reshape(FR * SAM, width)


def train_kernel(*refs):
    for b in range(B_UR, NB):
        refs[10][b, :, 128:] = jnp.zeros((256, 128), bf16)
    train_body(*refs, lambda point: None)


def train_body(
    w_ref, seen_ref, slot_ref, noisy_ref, mask_ref, level_ref, cot_ref, table_ref,
    act_ref, noisy_grad_ref, grad_ref, film_grad_ref, reach,
):
    row = iota((256, 256), 0)
    col = iota((256, 256), 1)
    ones = jnp.where((row >> 5) == (col >> 5), 1.0, 0.0).astype(bf16)
    swap = jnp.where(col == ((row & 15) << 4) + (row >> 4), 1.0, 0.0).astype(bf16)
    spread_mask = one_hot((iota((SAM, 256), 1) >> 4) == iota((SAM, 256), 0))
    keep = dot_nn(mask_ref[...].astype(f32).astype(bf16), spread_mask)
    start_cols = noisy_ref[...].astype(f32) * keep
    start_cols = jnp.concatenate([start_cols, jnp.zeros((6, 256), f32)], axis=0).astype(bf16)
    start = dot_nt(swap, start_cols).astype(bf16)
    lane16 = iota((16, 128), 1)
    row16 = iota((16, 128), 0)
    inputs = jnp.zeros((256, 128), f32)
    for t in range(5):
        place = lane16 == row16 + t * ADIM
        if t == 2:
            place = place | (lane16 == row16 + 50)
        inputs = inputs + dot_nn(step_frames(start, t - 2), one_hot(place & (row16 < ADIM)))
    inputs = inputs.astype(bf16)
    cot_high, cot_low = split2(cot_ref[...])
    upstream = dot_nt(swap, cot_high) + dot_nt(swap, cot_low)
    upstream_low = upstream.astype(bf16)
    at_level = one_hot(iota((64, SAM), 0) == level_ref[...])
    feats = dot_tn(at_level, table_ref[...]).astype(bf16)
    reach(0)
    misc = w_ref[B_MISC, :, :128]
    lane = iota((256, 128), 1)
    misc_first = jnp.where(lane < 50, misc, jnp.zeros_like(misc))
    misc_res = jnp.where((lane >= 50) & (lane < 60), misc, jnp.zeros_like(misc))
    singles = misc.astype(f32).T[LANE_TAIL : LANE_TAIL + 32]
    vec = lambda k: singles[k : k + 1]

    inner = [w_ref[B_INNER, :, j * 128 : (j + 1) * 128] for j in range(2)]
    outer = [w_ref[B_OUTER, :, j * 128 : (j + 1) * 128] for j in range(2)]
    film_time = lambda q: w_ref[B_FILM + q // 2, :, (q % 2) * 128 : (q % 2) * 128 + 128]
    hidden = [mish_parts(dot_nt(feats, inner[j]) + vec(T_BIAS_A + j)) for j in range(2)]
    hidden_low = [h[0].astype(bf16) for h in hidden]
    embed = dot_nn(hidden_low[0], outer[0]) + dot_nn(hidden_low[1], outer[1]) + vec(T_OUT)[:, :TE]
    cond, cond_slope = mish_parts(embed)
    cond_low = cond.astype(bf16)
    pre = dot_nt(inputs, misc_first) + vec(D_B1)
    act_one, normal_one, slope_one, scale_one = norm_forward(pre, vec(D_G1), vec(D_S1), ones)
    reach(1)
    at_slot = one_hot(iota((SAM, SAM), 0) == slot_ref[...])
    line = iota((32, SAM), 0)
    seen_film = jnp.concatenate([seen_ref[:, k].reshape(32, 128) for k in range(4)], axis=1)
    seen_film = split3(seen_film)
    sides = []
    for side in range(2):
        at_line = one_hot(((line >> 3) * 4 + (line & 3) == slot_ref[...]) & ((line >> 2) & 1 == side))
        sides.append(sum(dot_tn(at_line, part) for part in seen_film))
    seen_film = jnp.concatenate(
        [sides[k % 2][:, (k // 2) * 128 : (k // 2) * 128 + 128] for k in range(8)], axis=1
    )
    spans = lambda v, q: jnp.concatenate([v[:, k * 128 + q * 32 : k * 128 + q * 32 + 32] for k in range(8)], axis=1)
    film_of = lambda q: spans(seen_film, q) + dot_nt(cond_low, film_time(q)) + vec((D_FS, D_FO, U_FS, U_FO)[q])
    film = [film_of(0), film_of(1)]
    mid_one = plus(times(act_one, film[0]), film[1]).astype(bf16)
    reach(2)
    down = lambda t: w_ref[B_DS + t]
    pre = conv_forward(mid_one, down) + vec(D_B2)
    act, normal_two, slope_two, scale_two = norm_forward(pre, vec(D_G2), vec(D_S2), ones)
    skip = (act + dot_nt(inputs, misc_res) + vec(D_RB)).astype(bf16)
    reach(3)
    even, odd = halves(skip)
    odd_prev = step_frames(odd, -1)
    pool_sources = (odd_prev, even, odd)
    pooled = sum(dot_nt(s, w_ref[B_POOL + t]) for t, s in enumerate(pool_sources)) + vec(PB)
    pooled = pooled.astype(bf16)
    reach(4)
    pooled_prev = step_frames(pooled, -1)
    pooled_next = step_frames(pooled, 1)
    even_out = dot_nt(pooled, w_ref[B_SPREAD + 1]) + dot_nt(pooled_prev, w_ref[B_SPREAD + 3])
    odd_out = dot_nt(pooled_next, w_ref[B_SPREAD]) + dot_nt(pooled, w_ref[B_SPREAD + 2])
    wide = (interleave(even_out, odd_out) + vec(SB)).astype(bf16)
    joined = (wide, skip)
    up_res = lambda h: jnp.concatenate([w_ref[B_UR + 2 * h + i, :, 0:128] for i in range(2)], axis=1)
    turned = upstream_low.T
    for h in range(2):
        product = dot_nn(turned, joined[h]).astype(bf16)
        for i in range(2):
            grad_ref[B_UR + 2 * h + i, :, 0:128] = product[:, i * 128 : (i + 1) * 128]
    reach(5)
    up_first = [lambda t, h=h: w_ref[B_UF + 2 * t + h] for h in range(2)]
    pre = conv_forward(wide, up_first[0]) + conv_forward(skip, up_first[1]) + vec(U_B1)
    act_three, normal_three, slope_three, scale_three = norm_forward(pre, vec(U_G1), vec(U_S1), ones)
    film += [film_of(2), film_of(3)]
    mid_three = plus(times(act_three, film[2]), film[3]).astype(bf16)
    reach(6)
    up = lambda t: w_ref[B_US + t]
    pre = conv_forward(mid_three, up) + vec(U_B2)
    act, normal_four, slope_four, scale_four = norm_forward(pre, vec(U_G2), vec(U_S2), ones)
    act_four = act

    single_grads = {}

    def film_weights(q, grad_low):
        columns = slice((q % 2) * 128, (q % 2) * 128 + 128)
        grad_ref[B_FILM + q // 2, :, columns] = dot_tn(grad_low, cond_low).astype(bf16)

    def conv_weights(grad_low, source, block):
        turned = grad_low.T
        for t in range(5):
            grad_ref[block(t)] = dot_nn(turned, step_frames(source, t - 2)).astype(bf16)

    reach(7)
    grad, single_grads[U_G2], single_grads[U_S2] = norm_backward(
        upstream, normal_four, slope_four, scale_four, vec(U_G2), ones
    )
    single_grads[U_B2] = row_sum(grad)
    low = grad.astype(bf16)
    conv_weights(low, mid_three, lambda t: B_US + t)
    reach(8)
    grad_mid = conv_source(low, up)
    shift_three = over_frames(grad_mid)
    gain_three = over_frames(grad_mid * act_three)
    grad, single_grads[U_G1], single_grads[U_S1] = norm_backward(
        times(grad_mid, film[2]), normal_three, slope_three, scale_three, vec(U_G1), ones
    )
    single_grads[U_B1] = row_sum(grad)
    low = grad.astype(bf16)
    reach(15)
    for h in range(2):
        conv_weights(low, joined[h], lambda t, h=h: B_UF + 2 * t + h)
    single_grads[U_RB] = row_sum(upstream)
    reach(9)
    grad_wide = conv_source(low, up_first[0]) + dot_nn(upstream_low, up_res(0))
    grad_skip = conv_source(low, up_first[1]) + dot_nn(upstream_low, up_res(1))
    single_grads[SB] = row_sum(grad_wide)
    low_even, low_odd = halves(grad_wide.astype(bf16))
    turned_even, turned_odd = low_even.T, low_odd.T
    grad_ref[B_SPREAD] = dot_nn(turned_odd, pooled_next).astype(bf16)
    grad_ref[B_SPREAD + 1] = dot_nn(turned_even, pooled).astype(bf16)
    grad_ref[B_SPREAD + 2] = dot_nn(turned_odd, pooled).astype(bf16)
    grad_ref[B_SPREAD + 3] = dot_nn(turned_even, pooled_prev).astype(bf16)
    reach(10)
    grad_pooled = dot_nn(low_even, w_ref[B_SPREAD + 1]) + dot_nn(low_odd, w_ref[B_SPREAD + 2])
    grad_pooled = grad_pooled + dot_nn(step_frames(low_even, 1), w_ref[B_SPREAD + 3])
    grad_pooled = grad_pooled + dot_nn(step_frames(low_odd, -1), w_ref[B_SPREAD])
    single_grads[PB] = row_sum(grad_pooled)
    low = grad_pooled.astype(bf16)
    turned = low.T
    for t in range(3):
        grad_ref[B_POOL + t] = dot_nn(turned, pool_sources[t]).astype(bf16)
    reach(11)
    grad_even = dot_nn(low, w_ref[B_POOL + 1])
    grad_odd = dot_nn(low, w_ref[B_POOL + 2]) + dot_nn(step_frames(low, 1), w_ref[B_POOL])
    grad_skip = grad_skip + interleave(grad_even, grad_odd)
    single_grads[D_RB] = row_sum(grad_skip)
    skip_low = grad_skip.astype(bf16)
    misc_grad = jnp.where(lane < 50, 0.0, dot_nn(skip_low.T, inputs))
    back = dot_nn(skip_low, misc_res)
    grad, single_grads[D_G2], single_grads[D_S2] = norm_backward(
        grad_skip, normal_two, slope_two, scale_two, vec(D_G2), ones
    )
    single_grads[D_B2] = row_sum(grad)
    low = grad.astype(bf16)
    conv_weights(low, mid_one, lambda t: B_DS + t)
    film_weights(2, gain_three.astype(bf16))
    film_weights(3, shift_three.astype(bf16))
    reach(12)
    grad_mid = conv_source(low, down)
    shift_one = over_frames(grad_mid)
    gain_one = over_frames(grad_mid * act_one)
    grad, single_grads[D_G1], single_grads[D_S1] = norm_backward(
        times(grad_mid, film[0]), normal_one, slope_one, scale_one, vec(D_G1), ones
    )
    single_grads[D_B1] = row_sum(grad)
    low = grad.astype(bf16)
    misc_grad = misc_grad + jnp.where(lane < 50, dot_nn(low.T, inputs), 0.0)
    film_grads = (gain_one, shift_one, gain_three, shift_three)
    film_low = [g.astype(bf16) for g in film_grads]
    back_cond = None
    for q in range(4):
        single_grads[(D_FS, D_FO, U_FS, U_FO)[q]] = jnp.sum(film_grads[q], axis=0, keepdims=True)
        if q < 2:
            film_weights(q, film_low[q])
        part = dot_nn(film_low[q], film_time(q))
        back_cond = part if back_cond is None else back_cond + part
    at_slots = [dot_nn(at_slot, v) for v in film_low]
    for k in range(8):
        film_grad_ref[k] = jnp.concatenate([v[:, k * 32 : (k + 1) * 32] for v in at_slots], axis=1).astype(bf16)
    reach(13)
    grad_embed = back_cond * cond_slope
    single_grads[T_OUT] = jnp.concatenate(
        [jnp.sum(grad_embed, axis=0, keepdims=True), jnp.zeros((1, C - TE), f32)], axis=1
    )
    embed_low = grad_embed.astype(bf16)
    for j in range(2):
        grad_ref[B_OUTER, :, j * 128 : (j + 1) * 128] = dot_tn(hidden_low[j], embed_low).astype(bf16)
        grad_hidden = dot_nt(embed_low, outer[j]) * hidden[j][1]
        single_grads[T_BIAS_A + j] = jnp.sum(grad_hidden, axis=0, keepdims=True)
        grad_ref[B_INNER, :, j * 128 : (j + 1) * 128] = dot_tn(grad_hidden.astype(bf16), feats).astype(bf16)
    stack = [jnp.zeros((LANE_TAIL, 256), f32)] + [single_grads[k] for k in range(TAIL)]
    stack = jnp.concatenate(stack + [jnp.zeros((128 - LANE_TAIL - TAIL, 256), f32)], axis=0)
    grad_ref[B_MISC, :, :128] = (misc_grad + stack.T).astype(bf16)
    grad_ref[B_MISC, :, 128:] = jnp.zeros((256, 128), bf16)
    reach(14)
    result = act_four + dot_nt(wide, up_res(0)) + dot_nt(skip, up_res(1)) + vec(U_RB)
    act_ref[...] = dot_tn(result.astype(bf16), swap).astype(bf16)
    back = back + dot_nn(low, misc_first)
    grad_start = back[:, 50:60]
    for t in range(5):
        grad_start = grad_start + step_frames(back[:, t * ADIM : (t + 1) * ADIM], 2 - t)
    grad_cols = sum(dot_tn(part, swap) for part in split3(jnp.concatenate([grad_start, jnp.zeros((256, 6), f32)], axis=1)))
    noisy_grad_ref[...] = grad_cols[:ADIM] * keep


def train(weights, seen_film, slots, noisy, mask, levels, cotangent):
    vmem = pl.BlockSpec(memory_space=pltpu.VMEM)
    return pl.pallas_call(
        train_kernel,
        out_shape=(
            jax.ShapeDtypeStruct((C, 256), bf16),
            jax.ShapeDtypeStruct((ADIM, 256), f32),
            jax.ShapeDtypeStruct((NB, 256, 256), bf16),
            jax.ShapeDtypeStruct((8, SAM, 128), bf16),
        ),
        in_specs=[vmem] * 8,
        out_specs=(vmem,) * 4,
        compiler_params=pltpu.CompilerParams(vmem_limit_bytes=48 << 20),
        name="train",
    )(weights, seen_film, slots, noisy, mask, levels, cotangent, jnp.asarray(level_table(), bf16))


HALF = ROWS // 2


def native_grads(own_ref, film_ref, order_ref, grad_ref):
    native_most(own_ref, film_ref, grad_ref)
    native_rest(own_ref, order_ref, grad_ref)


def native_rest(own_ref, order_ref, grad_ref):
    misc = own_ref[B_MISC]
    first = dot_nt(misc[:, :128], order_ref[...])
    misc = misc.astype(f32)
    grad_ref[:, 0:50] = first[:, :50]
    grad_ref[:, AT_DOWN_RES : AT_DOWN_RES + ADIM] = misc[:, 50:60]
    grad_ref[:, AT_TAIL : AT_TAIL + TAIL] = misc[:, LANE_TAIL : LANE_TAIL + TAIL]
    grad_ref[:, AT_TIME[0] : AT_TIME[0] + 256] = own_ref[B_INNER].astype(f32)
    grad_ref[:, AT_TIME[1] : AT_TIME[1] + 256] = own_ref[B_OUTER].astype(f32)
    native_film(own_ref, grad_ref, 0)


def native_film(own_ref, grad_ref, side):
    for q in (2 * side, 2 * side + 1):
        part = own_ref[B_FILM + side, :, (q % 2) * 128 : (q % 2) * 128 + 128]
        grad_ref[:, AT_FILM[q] + OBS : AT_FILM[q] + OBS + TE] = part.astype(f32)


def native_most(own_ref, film_ref, grad_ref):
    for q in range(4):
        grad_ref[:, AT_FILM[q] : AT_FILM[q] + OBS] = film_ref[q * ROWS : (q + 1) * ROWS]
    native_film(own_ref, grad_ref, 1)
    for i in range(4):
        begin = AT_UP_RES + i * 128
        grad_ref[:, begin : begin + 128] = own_ref[B_UR + i, :, 0:128].astype(f32)
    for taps in (5, 3, 4):
        places = [(at, h, block) for at, k, groups, block in CONVS if k == taps for h in range(groups)]
        stacked = jnp.concatenate(
            [
                jnp.concatenate(
                    [own_ref[block(t, h), :, (h % 2) * 128 : (h % 2) * 128 + 128] for t in range(taps)], axis=1
                )
                for _, h, block in places
            ],
            axis=0,
        )
        moved = dot_nt(stacked, tap_order(taps))
        for n, (at, h, _) in enumerate(places):
            begin = at + h * 128 * taps
            grad_ref[:, begin : begin + 128 * taps] = moved[n * ROWS : (n + 1) * ROWS]


def unpack_kernel(own_ref, film_ref, order_ref, grad_ref):
    native_grads(own_ref, film_ref, order_ref, grad_ref)


def unpack(own, film):
    vmem = pl.BlockSpec(memory_space=pltpu.VMEM)
    return pl.pallas_call(
        unpack_kernel,
        out_shape=jax.ShapeDtypeStruct((ROWS, Q), f32),
        in_specs=[vmem] * 3,
        out_specs=vmem,
        compiler_params=pltpu.CompilerParams(vmem_limit_bytes=30 << 20),
        name="unpack",
    )(own, film, jnp.asarray(first_order(), bf16))


def adam_kernel(count, *refs):
    grad_ref, square_ref = refs[:2]
    old, extra_in = refs[2:5], refs[5 : 5 + count]
    norm_ref, new_hbm, extra_out = refs[5 + count], refs[6 + count : 10 + count], refs[10 + count : 10 + 2 * count]
    new, sems = refs[10 + 2 * count : 14 + 2 * count], refs[-1]
    norm = jnp.sqrt(jnp.sum(square_ref[...], axis=(0, 1), keepdims=True))
    norm_ref[...] = norm
    factor = jnp.minimum(1.0, clip_limit / (norm + 1e-06))
    stores = {}

    def store(n, height, at):
        rows = pl.ds(at, height)
        stores[n, at] = pltpu.make_async_copy(new[n].at[rows], new_hbm[n].at[rows], sems.at[n, at // 8])
        stores[n, at].start()

    width = 1024
    for row in range(0, ROWS, 8):
        for begin in range(0, Q, width):
            at = (slice(row, row + 8), slice(begin, min(begin + width, Q)))
            clipped = grad_ref[at] * factor
            new_first = decay_first * old[1][at] + (1.0 - decay_first) * clipped
            new_second = decay_second * old[2][at] + (1.0 - decay_second) * clipped * clipped
            first_hat = new_first * (1.0 / (1.0 - decay_first**ADAM_STEP))
            second_hat = new_second * (1.0 / (1.0 - decay_second**ADAM_STEP))
            before = old[0][at]
            new[0][at] = before - learn_rate * (first_hat / (jnp.sqrt(second_hat) + adam_eps) + weight_decay * before)
            new[1][at] = new_first
            new[2][at] = new_second
        for n in range(3):
            store(n, 8, row)
        if row % 16:
            rows = slice(row - 8, row + 8)
            new[3][rows] = new[0][rows].astype(bf16)
            store(3, 16, row - 8)
    for source, target in zip(extra_in, extra_out):
        target[...] = source[...].reshape(target.shape)
    for copy in stores.values():
        copy.wait()


def adam(grads, squares, params, first, second, extras=(), extra_shapes=()):
    vmem = pl.BlockSpec(memory_space=pltpu.VMEM)
    hbm = pl.BlockSpec(memory_space=pl.ANY)
    shape = jax.ShapeDtypeStruct((ROWS, Q), f32)
    count = len(extras)
    return pl.pallas_call(
        functools.partial(adam_kernel, count),
        out_shape=(
            jax.ShapeDtypeStruct((1, 1), f32),
            shape, shape, shape, jax.ShapeDtypeStruct((ROWS, Q), bf16),
            *(jax.ShapeDtypeStruct(dims, v.dtype) for dims, v in zip(extra_shapes, extras)),
        ),
        in_specs=[vmem] * (5 + count),
        out_specs=(vmem,) + (hbm,) * 4 + (vmem,) * count,
        scratch_shapes=[pltpu.VMEM((ROWS, Q), f32)] * 3
        + [pltpu.VMEM((ROWS, Q), bf16), pltpu.SemaphoreType.DMA((4, ROWS // 8))],
        compiler_params=pltpu.CompilerParams(vmem_limit_bytes=30 << 20),
        name="adam",
    )(grads, squares, params, first, second, *extras)


def local_plain(noisy, action_mask, time_index, obs_embed, obs_slot, cotangent, params, first_moment, second_moment):
    rows = params.shape[0]
    padded = lambda v: jnp.pad(v, ((0, ROWS - rows), (0, 0))) if rows < ROWS else v
    if rows > ROWS:
        packed = [pack(params[r : r + ROWS]) for r in range(0, rows, ROWS)]
        own = jnp.concatenate([p[0].reshape(NB, ROWS, 256) for p in packed], axis=1)
        film_own = jnp.concatenate([p[1].reshape(4, ROWS, OBS) for p in packed], axis=1)
    else:
        own, film_own = pack(padded(params))
        own = own.reshape(NB, ROWS, 256)[:, :rows]
        film_own = film_own.reshape(4, ROWS, OBS)[:, :rows]
    weights = lax.all_gather(own, "wide", axis=1, tiled=True)
    film_rows = lax.all_gather(film_own, "wide", axis=1, tiled=True).reshape(4 * C, OBS)
    seen = lax.all_gather(obs_embed, "pair", axis=0, tiled=True).reshape(-1, OBS).astype(f32)
    cond, slope = mish_parts(seen)
    cond = cond.astype(bf16)
    seen_film = dot_nt(cond, film_rows).reshape(4, 4, 4, 8, 32).transpose(0, 3, 1, 2, 4).reshape(4, 8, 4, 128)
    seen_film = seen_film.reshape(4, 4, 8, 128)
    act, noisy_grad, grads, film_grad = train(
        weights, seen_film, obs_slot[None], noisy[0], action_mask, time_index, cotangent[0]
    )
    film_grad = film_grad.reshape(8, SAM, 4, 32).transpose(1, 2, 0, 3).reshape(SAM, 4 * C)
    film_total = lax.psum(dot_tn(film_grad, cond), ("pair", "wide")).reshape(4, C, OBS)
    back = lax.psum_scatter(
        (dot_nn(film_grad, film_rows) * slope).reshape(-1, obs_embed.shape[1], OBS),
        "pair", scatter_dimension=0, tiled=True,
    )
    total = lax.psum(grads.astype(f32), ("pair", "wide")).astype(bf16)
    squares = jnp.sum(jnp.square(total.astype(f32))) + jnp.sum(jnp.square(film_total))
    here = lax.axis_index("wide") * rows
    mine = lax.dynamic_slice_in_dim(total, here, rows, 1)
    film_mine = lax.dynamic_slice_in_dim(film_total, here, rows, 1)
    outs = []
    for r in range(0, rows, ROWS):
        take = lambda v: jnp.pad(v[:, r : r + ROWS], ((0, 0), (0, max(0, ROWS - rows)), (0, 0)))
        outs.append(
            adam(
                unpack(take(mine), take(film_mine).reshape(4 * ROWS, OBS)), squares.reshape(1, 1),
                *(padded(v)[r : r + ROWS] for v in (params, first_moment, second_moment)),
            )
        )
    new = [jnp.concatenate([o[k] for o in outs], axis=0)[:rows] for k in range(1, 5)]
    return (act[None], noisy_grad[None], back, outs[0][0].reshape(()), *new)


MESH = pl.DeviceIdType.MESH


class Place:
    def __init__(self):
        p = lax.axis_index("pair")
        w = lax.axis_index("wide")
        self.p, self.w = p, w
        self.x, self.y = lax.rem(p, 2), lax.div(p, 2)
        self.c, self.z = lax.rem(w, 2), lax.div(w, 2)
        turn = [1 - 2 * self.x, 2 - 4 * self.y]
        self.p_flip = [p, p + turn[0], p + turn[1], p + (turn[0] + turn[1])]
        z_turn = [1 - 2 * lax.rem(self.z, 2), 2 - 4 * lax.div(self.z, 2)]
        self.z_flip = [self.z, self.z + z_turn[0], self.z + z_turn[1], self.z + (z_turn[0] + z_turn[1])]
        self.w_flip = []
        for z in self.z_flip:
            self.w_flip += [2 * z + self.c, 2 * z + (1 - self.c)]
        self.w_flip[0] = w
        self.x_of = [lax.rem(v, 2) for v in self.p_flip]
        self.y_of = [lax.div(v, 2) for v in self.p_flip]

    def line(self, l):
        return (self.p, self.w_flip[l])

    def others(self):
        return [(self.p_flip[k], self.w_flip[l]) for k in range(1, 4) for l in range(1, 8)]

    def plane(self, k):
        return (self.p_flip[k], self.w)


def greet(me):
    barrier = pltpu.get_barrier_semaphore()
    for l in range(1, 8):
        pl.semaphore_signal(barrier, inc=1, device_id=me.line(l), device_id_type=MESH)
    for k in range(1, 4):
        pl.semaphore_signal(barrier, inc=1, device_id=me.plane(k), device_id_type=MESH)


def meet(me):
    pl.semaphore_wait(pltpu.get_barrier_semaphore(), 10)


def drain(size, semaphore):
    pltpu.make_async_copy(size, size, semaphore).wait()


class Pool:
    def __init__(self, ref):
        self.ref, self.used = ref, 0

    def new(self):
        self.used += 1
        return self.ref.at[self.used - 1]

    def several(self, keys):
        return {key: self.new() for key in keys}


class Lane:
    def __init__(self, pool):
        self.sent, self.bytes = pool.new(), 0

    def send(self, source, target, arrival, device):
        pltpu.make_async_remote_copy(
            src_ref=source, dst_ref=target, send_sem=self.sent, recv_sem=arrival,
            device_id=device, device_id_type=MESH,
        ).start()
        self.bytes += math.prod(source.shape) * source.dtype.itemsize

    def finish(self, size):
        assert math.prod(size.shape) * size.dtype.itemsize == self.bytes
        drain(size, self.sent)


def fold_rows(v):
    return jnp.concatenate([v[:, q * 256 : (q + 1) * 256] for q in range(4)], axis=0)


def unfold_rows(v):
    return jnp.concatenate([v[q * 4 : (q + 1) * 4] for q in range(4)], axis=1)


def quarter_rows(parts):
    quarter = (iota(parts[0].shape, 0) >> 2) & 3
    return sum(jnp.where(quarter == q, part, 0.0) for q, part in enumerate(parts))


class Gather:
    def __init__(self, me, own, weights, seen, obs_all, film, film_part, film_line, pool, local_sem):
        self.me, self.own, self.weights, self.seen, self.obs_all, self.film = me, own, weights, seen, obs_all, film
        self.film_part, self.film_line, self.local_sem = film_part, film_line, local_sem
        self.z, self.x, self.y, self.f, self.c, self.small = (Lane(pool) for _ in range(6))
        self.parts, self.films, self.more, self.narrow = (Lane(pool) for _ in range(4))
        pieces = [(g, k) for g in range(len(GATHER_GROUPS)) for k in range(1, 4)]
        self.z_in = pool.several(pieces)
        near = [(g, k) for g, k in pieces if g not in GATHER_DIRECT] + list(GATHER_DIRECT)
        self.x_in, self.y_in = pool.several(near), pool.several(near)
        self.f_in = pool.several(range(len(GATHER_GROUPS)))
        self.c_in = pool.several(range(len(GATHER_GROUPS)))
        self.obs_in, self.part_in, self.film_in, self.more_in = (pool.new() for _ in range(4))

    def start_obs(self):
        me = self.me
        piece = self.obs_all.at[me.p, me.w]
        for l in range(1, 8):
            self.small.send(piece, piece, self.obs_in, me.line(l))

    def start_rows(self, g):
        me = self.me
        lane = self.narrow if g == NARROW else self.z
        for k in range(1, 4):
            lane.send(
                self.own.at[gather_group(g), me.p, :, cols(g)],
                self.weights.at[gather_group(g), me.p, me.z, me.c, :, cols(g)],
                self.z_in[g, k], me.line(2 * k),
            )

    def start_local(self):
        self.local = pltpu.make_async_copy(self.own, self.weights.at[:, :, self.me.z, self.me.c], self.local_sem)
        self.local.start()

    def film_product(self):
        me = self.me
        drain(self.obs_all.at[0, 0:7], self.obs_in)
        cond = mish_parts(self.obs_all[me.p].reshape(128, 256).astype(f32))[0].astype(bf16)
        film = quarter_rows([dot_nt(cond, self.film[:, q * 256 : (q + 1) * 256]) for q in range(4)])
        row, col = iota((64, 128), 0), iota((64, 128), 1)
        pick = one_hot(((row >> 3) == (col >> 4)) & ((row & 7) == (col & 3)))
        self.film_part[...] = sum(dot_nn(pick, part) for part in split3(film)).reshape(8, 8, 128)
        for l in range(1, 8):
            self.parts.send(self.film_part.at[me.w_flip[l]], self.film_line.at[me.w], self.part_in, me.line(l))
        self.film_line[me.w] = self.film_part[me.w]

    def film_hop(self):
        me = self.me
        drain(self.film_line.at[0:7], self.part_in)
        for k in range(4):
            self.seen[me.p, k] = self.film_line[2 * k] + pltpu.roll(self.film_line[2 * k + 1], 4, 0)
        piece = self.seen.at[me.p]
        for k in range(1, 4):
            self.films.send(piece, piece, self.film_in, me.plane(k))

    def obs_hop(self):
        me = self.me
        piece = self.obs_all.at[me.p]
        for k in range(1, 4):
            self.more.send(piece, piece, self.more_in, me.plane(k))

    def film_done(self):
        drain(self.seen.at[0:3], self.film_in)

    def first_hop(self, g):
        me = self.me
        lanes = [self.narrow] * 3 if g == NARROW else [self.x, self.y, self.f]
        for k in range(1, 4):
            piece = self.weights.at[gather_group(g), me.p, me.z_flip[k], me.c, :, cols(g)]
            drain(piece, self.z_in[g, k])
            key = g if g in GATHER_DIRECT else (g, k)
            lanes[0].send(piece, piece, self.x_in[key], me.plane(1))
            lanes[1].send(piece, piece, self.y_in[key], me.plane(2))
            if g in GATHER_DIRECT:
                lanes[2].send(piece, piece, self.f_in[g], me.plane(3))

    def three(self, g):
        return self.weights.at[gather_group(g), 0, 0:3, 0, :, cols(g)]

    def second_hop(self, g):
        me = self.me
        if g in GATHER_DIRECT:
            drain(self.three(g), self.x_in[g])
            drain(self.three(g), self.y_in[g])
            return
        for k in range(1, 4):
            one = self.weights.at[gather_group(g), 0, 0, 0]
            drain(one, self.x_in[g, k])
            drain(one, self.y_in[g, k])
            along_y = (g + k) % 2 == 0
            piece = self.weights.at[gather_group(g), me.p_flip[1 if along_y else 2], me.z_flip[k], me.c]
            self.f.send(piece, piece, self.f_in[g], me.plane(2 if along_y else 1))

    def last_hop(self, g):
        if g == 0:
            self.local.wait()
        if g in GATHER_DIRECT:
            self.second_hop(g)
        drain(self.three(g), self.f_in[g])
        piece = self.weights.at[gather_group(g), :, :, self.me.c, :, cols(g)]
        (self.narrow if g == NARROW else self.c).send(piece, piece, self.c_in[g], self.me.line(1))

    def arrived(self, g):
        drain(self.weights.at[gather_group(g), :, :, 0, :, cols(g)], self.c_in[g])

    def obs_done(self):
        drain(self.obs_all.at[0:3], self.more_in)

    def finish(self):
        wide = pl.ds(0, GATHER_GROUPS[NARROW][0])
        for lane in (self.z, self.x, self.y, self.f):
            lane.finish(self.weights.at[wide, 0, 0:3, 0])
        self.c.finish(self.weights.at[wide, :, :, 0])
        self.narrow.finish(self.weights.at[0:7, :, 0, 0, :, cols(NARROW)])
        self.small.finish(self.obs_all.at[0, 0:7])
        self.parts.finish(self.film_line.at[0:7])
        self.films.finish(self.seen.at[0:3])
        self.more.finish(self.obs_all.at[0:3])


class Scatter:
    def __init__(self, me, grad, film_grad, obs_all, film, out, film_out, back, square, buffers, pool):
        self.me, self.grad, self.film_grad, self.obs_all, self.film = me, grad, film_grad, obs_all, film
        self.out, self.film_out, self.back, self.square = out, film_out, back, square
        (self.half, self.core, self.xb, self.yb, self.ub, self.vb, self.zb, self.zq, self.pq, self.db,
         self.film_all, self.back_part, self.back_line, self.cond, self.all_squares) = buffers
        self.c, self.x, self.y, self.u, self.v, self.z = (Lane(pool) for _ in range(6))
        self.zf, self.q, self.d, self.r, self.g, self.h, self.b, self.n = (Lane(pool) for _ in range(8))
        self.narrow, self.narrow_end = Lane(pool), Lane(pool)
        groups = range(len(GROUPS))
        self.staged = [g for g in groups if g != Z_FIRST and g not in PLANE_DIRECT]
        self.c_in = pool.several(groups)
        self.x_in, self.y_in, self.u_in, self.v_in = (pool.several(self.staged) for _ in range(4))
        self.d_in = pool.several(PLANE_DIRECT)
        self.z_in = pool.several(g for g in groups if g != Z_FIRST)
        self.zf_in, self.q_in, self.r_in, self.g_in, self.h_in, self.b_in, self.n_in = (pool.new() for _ in range(7))
        self.narrow_in, self.r_last = pool.new(), pool.new()
        self.squares = []

    def start(self, g):
        me = self.me
        lane = self.narrow if g == NARROW else self.c
        lane.send(
            self.grad.at[group(g), :, :, 1 - me.c, :, cols(g)], self.core.at[group(g), :, :, :, cols(g)],
            self.c_in[g], me.line(1),
        )

    def core_sum(self, g):
        me, half, (first, last) = self.me, self.half, GROUPS[g]
        drain(self.core.at[group(g), :, :, :, cols(g)], self.c_in[g])

        def add(i, _):
            j, q = first + i // 4, i % 4
            total = self.grad[j, q, :, me.c, :, cols(g)].astype(f32) + self.core[j, q, :, :, cols(g)].astype(f32)
            half[j, q // 2, q % 2, :, :, cols(g)] = total.astype(bf16)
            return 0

        lax.fori_loop(0, (last - first) * 4, add, 0)
        if g == Z_FIRST:
            self.z_send(g, 0)
        elif g in PLANE_DIRECT:
            for k in range(1, 4):
                piece = half.at[group(g), me.y_of[k], me.x_of[k]]
                self.d.send(piece, self.db.at[k - 1, group(g)], self.d_in[g], me.plane(k))
        else:
            lanes = [self.narrow] * 2 if g == NARROW else [self.x, self.y]
            lanes[0].send(
                half.at[group(g), :, 1 - me.x, LOW, :, cols(g)], self.xb.at[group(g), :, :, :, cols(g)],
                self.x_in[g], me.plane(1),
            )
            lanes[1].send(
                half.at[group(g), 1 - me.y, :, HIGH, :, cols(g)], self.yb.at[group(g), :, :, :, cols(g)],
                self.y_in[g], me.plane(2),
            )

    def z_send(self, g, n):
        me = self.me
        for k in range(1, 4):
            self.zf.send(
                self.half.at[GROUPS[g][0] + n, :, :, me.z_flip[k]], self.zq.at[k - 1, n], self.zf_in, me.line(2 * k)
            )

    def z_sum(self, g):
        me, half, (first, last) = self.me, self.half, GROUPS[g]
        drain(self.zq, self.zf_in)
        for j in range(first, last):
            total = half[j, :, :, me.z].astype(f32)
            for k in range(3):
                total = total + self.zq[k, j - first].astype(f32)
            half[j, :, :, me.z] = total.astype(bf16)
        for k in range(1, 4):
            piece = half.at[group(g), me.y_of[k], me.x_of[k], me.z]
            self.q.send(piece, self.pq.at[k - 1], self.q_in, me.plane(k))

    def plane_sum(self, g):
        drain(self.pq, self.q_in)
        self.finish_sum(g, [lambda j, k=k: self.pq[k, j - GROUPS[g][0]] for k in range(3)])

    def first_sum(self, g):
        me, half, (first, last) = self.me, self.half, GROUPS[g]
        lanes = [self.narrow] * 2 if g == NARROW else [self.u, self.v]
        drain(self.xb.at[group(g), :, :, :, cols(g)], self.x_in[g])

        def add_x(i, _):
            j, q = first + i // 2, i % 2
            total = half[j, q, me.x, LOW, :, cols(g)].astype(f32) + self.xb[j, q, :, :, cols(g)].astype(f32)
            half[j, q, me.x, LOW, :, cols(g)] = total.astype(bf16)
            return 0

        lax.fori_loop(0, (last - first) * 2, add_x, 0)
        lanes[0].send(
            half.at[group(g), 1 - me.y, me.x, LOW, :, cols(g)], self.ub.at[group(g), :, :, cols(g)],
            self.u_in[g], me.plane(2),
        )
        drain(self.yb.at[group(g), :, :, :, cols(g)], self.y_in[g])

        def add_y(i, _):
            j, q = first + i // 2, i % 2
            total = half[j, me.y, q, HIGH, :, cols(g)].astype(f32) + self.yb[j, q, :, :, cols(g)].astype(f32)
            half[j, me.y, q, HIGH, :, cols(g)] = total.astype(bf16)
            return 0

        lax.fori_loop(0, (last - first) * 2, add_y, 0)
        lanes[1].send(
            half.at[group(g), me.y, 1 - me.x, HIGH, :, cols(g)], self.vb.at[group(g), :, :, cols(g)],
            self.v_in[g], me.plane(1),
        )

    def direct_sum(self, g):
        me, half = self.me, self.half
        drain(self.db.at[:, group(g)], self.d_in[g])
        for j in range(*GROUPS[g]):
            total = half[j, me.y, me.x].astype(f32)
            for k in range(3):
                total = total + self.db[k, j].astype(f32)
            half[j, me.y, me.x] = total.astype(bf16)
        self.send_z(g)

    def second_sum(self, g):
        me, half = self.me, self.half
        drain(self.ub.at[group(g), :, :, cols(g)], self.u_in[g])
        drain(self.vb.at[group(g), :, :, cols(g)], self.v_in[g])
        for j in range(*GROUPS[g]):
            for part, more in ((LOW, self.ub), (HIGH, self.vb)):
                total = half[j, me.y, me.x, part, :, cols(g)].astype(f32) + more[j, :, :, cols(g)].astype(f32)
                half[j, me.y, me.x, part, :, cols(g)] = total.astype(bf16)
        self.send_z(g)

    def send_z(self, g):
        me = self.me
        lane = self.narrow_end if g == NARROW else self.z
        for k in range(1, 4):
            piece = self.half.at[group(g), me.y, me.x, me.z_flip[k], :, cols(g)]
            lane.send(piece, self.zb.at[k - 1, group(g), :, cols(g)], self.z_in[g], me.line(2 * k))

    def last_sum(self, g):
        drain(self.zb.at[:, group(g), :, cols(g)], self.z_in[g])
        self.finish_sum(g, [lambda j, k=k: self.zb[k, j, :, cols(g)] for k in range(3)])

    def finish_sum(self, g, terms):
        me = self.me
        for j in range(*GROUPS[g]):
            total = self.half[j, me.y, me.x, me.z, :, cols(g)].astype(f32)
            for term in terms:
                total = total + term(j).astype(f32)
            total = total.astype(bf16)
            self.out[j, me.p, :, cols(g)] = total
            self.count(jnp.square(total.astype(f32)))
        piece = self.out.at[group(g), me.p, :, cols(g)]
        lane, arrival = (self.narrow_end, self.narrow_in) if g == NARROW else (self.r, self.r_in)
        if g == 0:
            arrival = self.r_last
        for k in range(1, 4):
            lane.send(piece, piece, arrival, me.plane(k))

    def count(self, squares):
        folded = jnp.sum(squares.reshape(-1, 8, squares.shape[1]), axis=0)
        self.squares += [folded[:, i : i + 128] for i in range(0, squares.shape[1], 128)]

    def film_start(self):
        me = self.me
        self.film_all[me.p, me.w] = self.film_grad[me.w]
        for l in range(1, 8):
            self.g.send(self.film_grad.at[me.w_flip[l]], self.film_all.at[me.p, me.w], self.g_in, me.line(l))

    def film_hop(self):
        me = self.me
        drain(self.film_all.at[0, 0:7], self.g_in)
        piece = self.film_all.at[me.p]
        for k in range(1, 4):
            self.h.send(piece, piece, self.h_in, me.plane(k))

    def film_inputs(self):
        row, col = iota((128, 512), 0), iota((128, 512), 1)
        same = ((row >> 4) == ((col >> 4) & 7)) & (((row >> 2) & 3) == (col >> 7)) & ((row & 3) == (col & 3))
        seen_all = self.obs_all[...].reshape(512, 256)
        for q in range(4):
            pick = one_hot(same & (((col >> 2) & 3) == q))
            self.cond[q] = mish_parts(dot_nn(pick, seen_all))[0].astype(bf16)

    def film_products(self):
        me = self.me
        drain(self.film_all.at[0:3], self.h_in)
        copies = [self.film_all[k].reshape(128, 128).astype(f32) for k in range(4)]
        total = split2((copies[0] + copies[1]) + (copies[2] + copies[3]))
        row, col = iota((128, 128), 0), iota((128, 128), 1)
        mine = one_hot(((row >> 4) == (col >> 4)) & ((col & 15) == 4 * me.p + (row & 3)))
        rows = [dot_nn(mine, part).astype(bf16) for part in total]
        parts = [
            dot_nn(rows[0], self.film[:, q * 256 : (q + 1) * 256])
            + dot_nn(rows[1], self.film[:, q * 256 : (q + 1) * 256])
            for q in range(4)
        ]
        self.back_part[...] = quarter_rows(parts).astype(bf16).reshape(8, 16, 256)
        for l in range(1, 8):
            self.b.send(self.back_part.at[me.w_flip[l]], self.back_line.at[me.w], self.b_in, me.line(l))
        self.back_line[me.w] = self.back_part[me.w]
        turned = [part.T for part in total]
        for q in range(4):
            cond = self.cond[q]
            product = dot_nn(turned[0], cond) + dot_nn(turned[1], cond)
            self.film_out[:, q * 256 : (q + 1) * 256] = product
            self.count(0.25 * jnp.square(product))

    def film_back(self):
        me = self.me
        drain(self.back_line.at[0:7], self.b_in)
        total = jnp.sum(self.back_line[...].astype(f32), axis=0)
        slope = mish_parts(self.obs_all[me.p, me.w].astype(f32))[1]
        self.back[0] = unfold_rows(total * slope)

    def norm(self, hello, most, rest):
        me = self.me
        total = sum(self.squares)
        here = me.p * 8 + me.w
        piece = self.all_squares.at[here]
        self.all_squares[here] = jnp.sum(total, axis=0, keepdims=True)
        pl.semaphore_wait(hello, len(me.others()))
        for i in range(1, 32):
            self.n.send(piece, piece, self.n_in, (me.p_flip[i % 4], me.w_flip[i // 4]))
        drain(self.zb.at[:, GROUPS[0][1] : GROUPS[NARROW][0]], self.r_in)
        drain(self.zb.at[:, 0:1, :, cols(NARROW)], self.narrow_in)
        most()
        drain(self.zb.at[:, group(0)], self.r_last)
        rest()
        drain(self.all_squares.at[0:31], self.n_in)
        self.square[...] = jnp.sum(self.all_squares[...].reshape(32, 128), axis=0, keepdims=True)

    def finish(self):
        size = lambda gs: sum(GROUPS[g][1] - GROUPS[g][0] for g in gs if g != NARROW)
        staged, wide = size(self.staged), pl.ds(0, GROUPS[NARROW][0])
        self.c.finish(self.grad.at[wide, :, :, 0])
        self.x.finish(self.xb.at[0:staged])
        self.y.finish(self.yb.at[0:staged])
        self.u.finish(self.ub.at[0:staged])
        self.v.finish(self.vb.at[0:staged])
        self.d.finish(self.db.at[:, 0 : size(PLANE_DIRECT)])
        self.z.finish(self.zb.at[:, 0 : staged + size(PLANE_DIRECT)])
        self.zf.finish(self.zq)
        self.q.finish(self.pq)
        self.r.finish(self.zb.at[:, wide])
        self.narrow.finish(self.grad.at[0:7, :, 0, 0, :, cols(NARROW)])
        self.narrow_end.finish(self.zb.at[:, 0:2, :, cols(NARROW)])
        self.g.finish(self.film_all.at[0, 0:7])
        self.h.finish(self.film_all.at[0:3])
        self.b.finish(self.back_line.at[0:7])
        self.n.finish(self.all_squares.at[0:31])


GATHER_GROUPS = ((0, 1), (1, 3), (3, 5), (5, 7), (7, 8), (8, 9))
GATHER_DIRECT = (4, 5)
GROUPS = ((0, 1), (1, 3), (3, 5), (5, 7), (7, 8), (8, 9))
Z_FIRST = 3
PLANE_DIRECT = (0,)
SEMAPHORES = 125
LOW, HIGH = pl.ds(0, 2), pl.ds(2, 2)


NARROW = 5


def cols(g):
    return pl.ds(0, 128 if g == NARROW else 256)


def group(g):
    return pl.ds(GROUPS[g][0], GROUPS[g][1] - GROUPS[g][0])


def gather_group(g):
    return pl.ds(GATHER_GROUPS[g][0], GATHER_GROUPS[g][1] - GATHER_GROUPS[g][0])


def step_kernel(*refs):
    params_out = refs[16]
    targets = (params_out,) + refs[19:27]
    loads = [
        pltpu.make_async_copy(source, target, refs[-2].at[i])
        for i, (source, target) in enumerate(zip(refs[:11], targets + refs[17:19]))
    ]
    for i in (0, 2, 1, 3, 4, 5, 6, 7, 8):
        loads[i].start()
    refs = targets + refs[9:11] + refs[11:16] + refs[17:19] + refs[27:-2] + refs[-1:]
    (params, order, obs, slots, noisy, mask, levels, cotangent, table, first, second,
     act, noisy_grad, back, native, square, first_out, second_out,
     own, weights, seen, obs_all, film, film_part, film_line, grad, film_grad, out, film_out) = refs[:29]
    buffers, (semaphores, local_sem, hello) = refs[29:44], refs[44:]
    pool = Pool(semaphores)
    me = Place()
    gather = Gather(me, own, weights, seen, obs_all, film, film_part, film_line, pool, local_sem)
    scatter = Scatter(me, grad, film_grad, obs_all, film, out, film_out, back, square, buffers, pool)
    greet(me)
    loads[0].wait()
    loads[1].wait()
    pack_first(params, order, own)
    loads[2].wait()
    obs_all[me.p, me.w] = fold_rows(obs[0].astype(f32)).astype(bf16)
    meet(me)
    gather.start_rows(0)
    gather.start_obs()
    pack_rest(params, own, film)
    gather.start_local()
    gather.start_rows(1)
    for i in range(3, 9):
        loads[i].wait()

    def reach(point):
        if point == 0:
            gather.first_hop(0)
            gather.film_product()
            for g in range(2, len(GATHER_GROUPS)):
                gather.start_rows(g)
            gather.second_hop(0)
            gather.first_hop(1)
            gather.first_hop(2)
            gather.film_hop()
            gather.last_hop(0)
            gather.second_hop(1)
            for device in me.others():
                pl.semaphore_signal(hello, inc=1, device_id=device, device_id_type=MESH)
            gather.arrived(0)
        if point == 1:
            gather.first_hop(3)
            gather.second_hop(2)
            gather.last_hop(1)
            gather.film_done()
        if point == 2:
            gather.arrived(1)
            gather.first_hop(4)
        if point == 3:
            gather.last_hop(2)
            gather.second_hop(3)
            gather.arrived(2)
        if point == 4:
            gather.last_hop(3)
        if point == 5:
            gather.last_hop(4)
            gather.first_hop(5)
            gather.arrived(3)
        if point == 6:
            gather.obs_hop()
            loads[9].start()
            loads[10].start()
            gather.arrived(4)
        if point == 8:
            gather.last_hop(5)
            scatter.start(5)
            scatter.start(4)
        if point == 15:
            scatter.core_sum(5)
            scatter.core_sum(4)
        if point == 9:
            scatter.start(3)
            gather.arrived(5)
        if point == 10:
            scatter.core_sum(3)
        if point == 11:
            scatter.start(2)
        if point == 12:
            scatter.core_sum(2)
            scatter.first_sum(5)
            scatter.first_sum(4)
            scatter.start(1)
        if point == 13:
            scatter.film_start()
            scatter.z_send(Z_FIRST, 1)
        if point == 14:
            scatter.start(0)
            scatter.core_sum(1)
            scatter.second_sum(5)
            scatter.second_sum(4)
            scatter.first_sum(2)
            scatter.core_sum(0)

    train_body(
        Stacked(weights), seen, slots, noisy, mask, levels, cotangent, table,
        act, noisy_grad, Stacked(grad), film_grad, reach,
    )
    scatter.film_hop()
    scatter.first_sum(1)
    gather.obs_done()
    scatter.film_inputs()
    scatter.second_sum(2)
    scatter.z_sum(3)
    scatter.film_products()
    scatter.second_sum(1)
    scatter.direct_sum(0)
    scatter.plane_sum(3)
    scatter.last_sum(5)
    scatter.last_sum(4)
    scatter.last_sum(2)
    scatter.last_sum(1)
    scatter.film_back()
    scatter.last_sum(0)
    loads[9].wait()
    loads[10].wait()
    scatter.norm(
        hello,
        lambda: native_most(Blocks(out), film_out, native),
        lambda: native_rest(Blocks(out), order, native),
    )
    gather.finish()
    scatter.finish()
    assert pool.used <= SEMAPHORES


class Stacked:
    def __init__(self, ref):
        self.ref = ref

    def _split(self, key):
        if not isinstance(key, tuple):
            return key, slice(None)
        return key[0], key[2]

    def __getitem__(self, key):
        block, cols = self._split(key)
        value = self.ref[block // 4, block % 4, :, :, :, cols]
        return value.reshape(256, value.shape[-1])

    def __setitem__(self, key, value):
        block, cols = self._split(key)
        self.ref[block // 4, block % 4, :, :, :, cols] = value.reshape(4, 2, ROWS, value.shape[-1])


def step(params, obs, slots, noisy, mask, levels, cotangent, first, second):
    vmem = pl.BlockSpec(memory_space=pltpu.VMEM)
    n = NB // 4
    inputs = (
        params, jnp.asarray(first_order(), bf16), obs, slots, noisy, mask, levels, cotangent,
        jnp.asarray(level_table(), bf16), first, second,
    )
    inputs = tuple(pltpu.with_memory_space_constraint(v, pltpu.HBM) for v in inputs)
    low = lambda *shape: pltpu.VMEM(shape, bf16)
    return pl.pallas_call(
        step_kernel,
        out_shape=(
            jax.ShapeDtypeStruct((C, 256), bf16),
            jax.ShapeDtypeStruct((ADIM, 256), f32),
            jax.ShapeDtypeStruct((1, 4, OBS), f32),
            jax.ShapeDtypeStruct((ROWS, Q), f32),
            jax.ShapeDtypeStruct((1, 128), f32),
            *[jax.ShapeDtypeStruct((ROWS, Q), f32)] * 3,
        ),
        in_specs=[pl.BlockSpec(memory_space=pltpu.HBM)] * 11,
        out_specs=(vmem,) * 8,
        scratch_shapes=[
            *(pltpu.VMEM(v.shape, v.dtype) for v in inputs[1:9]),
            low(n, 4, ROWS, 256),
            low(n, 4, 4, 2, ROWS, 256),
            pltpu.VMEM((4, 4, 8, 128), f32),
            low(4, 8, 16, 256),
            low(4 * ROWS, OBS),
            pltpu.VMEM((8, 8, 128), f32),
            pltpu.VMEM((8, 8, 128), f32),
            low(n, 4, 4, 2, ROWS, 256),
            low(8, SAM, 128),
            low(n, 4, ROWS, 256),
            pltpu.VMEM((4 * ROWS, OBS), f32),
            low(n, 2, 2, 4, ROWS, 256),
            low(n, 4, 4, ROWS, 256),
            low(n, 2, 2, ROWS, 256),
            low(n, 2, 2, ROWS, 256),
            low(n, 2, ROWS, 256),
            low(n, 2, ROWS, 256),
            low(3, n, ROWS, 256),
            low(3, GROUPS[Z_FIRST][1] - GROUPS[Z_FIRST][0], 2, 2, ROWS, 256),
            low(3, GROUPS[Z_FIRST][1] - GROUPS[Z_FIRST][0], ROWS, 256),
            low(3, GROUPS[max(PLANE_DIRECT)][1], 4, ROWS, 256),
            low(4, 8, 16, 128),
            low(8, 16, 256),
            low(8, 16, 256),
            low(4, 128, 256),
            pltpu.VMEM((32, 1, 128), f32),
            pltpu.SemaphoreType.DMA((SEMAPHORES,)),
            pltpu.SemaphoreType.DMA,
            pltpu.SemaphoreType.DMA((11,)),
            pltpu.SemaphoreType.REGULAR,
        ],
        compiler_params=pltpu.CompilerParams(collective_id=0, has_side_effects=True, vmem_limit_bytes=34 << 20),
        cost_estimate=pl.CostEstimate(flops=3 * 10**9, bytes_accessed=200 * 10**6, transcendentals=10**6),
        name="step",
    )(*inputs)


def local_fast(noisy, action_mask, time_index, obs_embed, obs_slot, cotangent, params, first_moment, second_moment):
    act, noisy_grad, back, native, squares, params, first_moment, second_moment = step(
        params, obs_embed, obs_slot[None], noisy[0], action_mask, time_index, cotangent[0],
        first_moment, second_moment,
    )
    norm, *new, act, noisy_grad, back = adam(
        native, squares, params, first_moment, second_moment,
        (act, noisy_grad, back), ((1, C, 256), (ADIM, 1, 256), (1, 4, OBS)),
    )
    return (act, noisy_grad.transpose(1, 0, 2), back, norm.reshape(()), *new)


def solution(mesh):
    in_specs = (
        P("pair", None, "wide"),
        P(None, "wide"),
        P("pair", "wide"),
        P("pair", "wide", None),
        P("wide"),
        P("pair", None, "wide"),
        P("wide", None),
        P("wide", None),
        P("wide", None),
    )
    out_specs = (
        P("pair", None, "wide"),
        P("pair", None, "wide"),
        P("pair", "wide", None),
        P(),
        P("wide", None),
        P("wide", None),
        P("wide", None),
        P("wide", None),
    )
    fast = mesh.shape["pair"] == 4 and mesh.shape["wide"] == 8
    return jax.shard_map(local_fast if fast else local_plain, mesh=mesh, in_specs=in_specs, out_specs=out_specs, check_vma=False)
```

```python
import functools
import math

import jax
import jax.numpy as jnp
import numpy as np
from jax import lax
from jax.experimental import pallas as pl
from jax.experimental.pallas import tpu as pltpu
from jax.sharding import PartitionSpec as P

C = 256
OBS = 1024
TE = 128
TH = 512
ADIM = 10
FR = 16
LEVELS = 40
ADAM_STEP = 7
Q = 12627
SAM = 16
ROWS = 32
NB = 36

sigma_top = 80.0 ** (1.0 / 7.0)
sigma_low = 0.002 ** (1.0 / 7.0)
clip_limit = 1.0
learn_rate = 0.02
decay_first = 0.5
decay_second = 0.5
adam_eps = 1e-08
weight_decay = 0.01
norm_eps = 1e-05

f32 = jnp.float32
bf16 = jnp.bfloat16

AT_DOWN_RES = 1330
AT_TAIL = 12604
TAIL = 23
AT_FILM = (1340, 2492, 9788, 10940)
AT_TIME = (12092, 12348)
AT_UP_RES = 9276
B_MISC, B_INNER, B_OUTER, B_FILM = 0, 1, 2, 3
B_DS, B_POOL, B_SPREAD, B_UF, B_US, B_UR = 5, 10, 13, 17, 27, 32
LANE_TAIL = 64
CONVS = (
    (50, 5, 2, lambda t, h: B_DS + t),
    (5436, 5, 4, lambda t, h: B_UF + 2 * t + h // 2),
    (7996, 5, 2, lambda t, h: B_US + t),
    (3644, 3, 2, lambda t, h: B_POOL + t),
    (4412, 4, 2, lambda t, h: B_SPREAD + t),
)
(T_BIAS_A, T_BIAS_B, T_OUT, D_B1, D_G1, D_S1, D_FS, D_FO, D_B2, D_G2, D_S2, D_RB, PB, SB,
 U_B1, U_G1, U_S1, U_FS, U_FO, U_B2, U_G2, U_S2, U_RB) = range(TAIL)


def dot_nt(a, b):
    return lax.dot_general(a, b, (((1,), (1,)), ((), ())), preferred_element_type=f32)


def dot_nn(a, b):
    return lax.dot_general(a, b, (((1,), (0,)), ((), ())), preferred_element_type=f32)


def dot_tn(a, b):
    return lax.dot_general(a, b, (((0,), (0,)), ((), ())), preferred_element_type=f32)


def split2(v):
    high = v.astype(bf16)
    return high, (v - high.astype(f32)).astype(bf16)


def split3(v):
    high, rest = v.astype(bf16), None
    rest = v - high.astype(f32)
    mid = rest.astype(bf16)
    return high, mid, (rest - mid.astype(f32)).astype(bf16)


def iota(shape, dim):
    return lax.broadcasted_iota(jnp.int32, shape, dim)


def one_hot(condition):
    return jnp.where(condition, 1.0, 0.0).astype(bf16)


def tap_order(taps):
    n = 128 * taps
    row = lax.broadcasted_iota(jnp.int32, (n, n), 0)
    col = lax.broadcasted_iota(jnp.int32, (1, n), 1)
    source = (col & 127) * taps + (col >> 7)
    return jnp.where(row == source, 1.0, 0.0).astype(bf16)


def first_order():
    table = np.zeros((128, 128), np.float32)
    for i in range(ADIM):
        for t in range(5):
            table[i * 5 + t, t * ADIM + i] = 1.0
    return table


def level_table():
    levels = np.arange(LEVELS, dtype=np.float64)
    tau = 250.0 * 7.0 * np.log(sigma_top + levels / (LEVELS - 1) * (sigma_low - sigma_top))
    freq = np.exp(-math.log(10000.0) * np.arange(TE // 2) / (TE // 2 - 1))
    angles = tau[:, None] * freq[None, :]
    table = np.zeros((64, TE), np.float32)
    table[:LEVELS] = np.concatenate([np.sin(angles), np.cos(angles)], axis=1)
    return table


def pack_kernel(params_ref, order_ref, own_ref, film_ref):
    pack_rows(params_ref, order_ref, own_ref, film_ref)


class Blocks:
    def __init__(self, ref):
        self.ref = ref

    def _at(self, key):
        block, rest = (key[0], key[1:]) if isinstance(key, tuple) else (key, ())
        return (block // 4, block % 4) + rest

    def __getitem__(self, key):
        return self.ref[self._at(key)]

    def __setitem__(self, key, value):
        self.ref[self._at(key)] = value


def pack_rows(params_ref, order_ref, own_ref, film_ref):
    pack_first(params_ref, order_ref, own_ref)
    pack_rest(params_ref, own_ref, film_ref)


def pack_first(params_ref, order_ref, own_ref):
    own_ref = Blocks(own_ref)

    def low(start, width):
        return params_ref[:, start : start + width].astype(bf16)

    first = dot_nn(low(0, 128), order_ref[...])
    pieces = [
        first[:, :50],
        params_ref[:, AT_DOWN_RES : AT_DOWN_RES + ADIM],
        jnp.zeros((ROWS, LANE_TAIL - 60), f32),
        params_ref[:, AT_TAIL : AT_TAIL + TAIL],
        jnp.zeros((ROWS, 256 - LANE_TAIL - TAIL), f32),
    ]
    own_ref[B_MISC] = jnp.concatenate(pieces, axis=1).astype(bf16)
    own_ref[B_INNER] = low(AT_TIME[0], 256)
    own_ref[B_OUTER] = low(AT_TIME[1], 256)
    for q in range(4):
        own_ref[B_FILM + q // 2, :, (q % 2) * 128 : (q % 2) * 128 + 128] = low(AT_FILM[q] + OBS, TE)


def pack_rest(params_ref, own_ref, film_ref):
    own_ref = Blocks(own_ref)

    def low(start, width):
        return params_ref[:, start : start + width].astype(bf16)

    for q in range(4):
        film_ref[q * ROWS : (q + 1) * ROWS] = low(AT_FILM[q], OBS)
    for i in range(4):
        own_ref[B_UR + i, :, 0:128] = low(AT_UP_RES + i * 128, 128)
    for taps in (5, 3, 4):
        places = [(at, h, block) for at, k, groups, block in CONVS if k == taps for h in range(groups)]
        stacked = jnp.concatenate([low(at + h * 128 * taps, 128 * taps) for at, h, _ in places], axis=0)
        moved = dot_nn(stacked, tap_order(taps)).astype(bf16)
        for n, (_, h, block) in enumerate(places):
            for t in range(taps):
                own_ref[block(t, h), :, (h % 2) * 128 : (h % 2) * 128 + 128] = moved[
                    n * ROWS : (n + 1) * ROWS, t * 128 : (t + 1) * 128
                ]


def pack(params):
    vmem = pl.BlockSpec(memory_space=pltpu.VMEM)
    return pl.pallas_call(
        pack_kernel,
        out_shape=(
            jax.ShapeDtypeStruct((NB // 4, 4, ROWS, 256), bf16),
            jax.ShapeDtypeStruct((4 * ROWS, OBS), bf16),
        ),
        in_specs=[vmem, vmem],
        out_specs=(vmem, vmem),
        compiler_params=pltpu.CompilerParams(vmem_limit_bytes=40 << 20),
        name="pack",
    )(params, jnp.asarray(first_order(), bf16))


def mish_parts(v):
    e = jnp.exp(jnp.minimum(v, 20.0))
    n = e * (e + 2.0)
    r = 1.0 / (n + 2.0)
    t = n * r
    return v * t, t + 4.0 * v * (e * r) * ((e + 1.0) * r)


def step_frames(v, step):
    if step == 0:
        return v
    zeros = jnp.zeros((SAM * abs(step), v.shape[1]), v.dtype)
    if step > 0:
        return jnp.concatenate([v[SAM * step :], zeros], axis=0)
    return jnp.concatenate([zeros, v[: SAM * step]], axis=0)


def over_frames(v):
    return jnp.sum(v.reshape(-1, SAM, v.shape[1]), axis=0)


def each_frame(v, s):
    return v.reshape(-1, SAM, v.shape[1]), s[None]


def group_means(values, ones):
    parts = [p for v in values for p in split3(v)]
    sums = dot_nn(jnp.concatenate(parts, axis=0), ones)
    out = []
    for i in range(len(values)):
        a, b, c = (sums[(3 * i + k) * SAM : (3 * i + k + 1) * SAM] for k in range(3))
        out.append((a + (b + c)) * (1.0 / (32 * FR)))
    return out


def minus(v, s):
    a, b = each_frame(v, s)
    return (a - b).reshape(v.shape)


def times(v, s):
    a, b = each_frame(v, s)
    return (a * b).reshape(v.shape)


def plus(v, s):
    a, b = each_frame(v, s)
    return (a + b).reshape(v.shape)


def norm_forward(before, gain, shift, ones):
    center, square = group_means([over_frames(before), over_frames(before * before)], ones)
    scale = lax.rsqrt(jnp.maximum(square - center * center, 0.0) + norm_eps)
    away = minus(before, center)
    normal = times(away, scale)
    act, slope = mish_parts(normal * gain + shift)
    return act, normal, slope, scale


def norm_backward(grad_act, normal, slope, scale, gain, ones):
    grad_out = grad_act * slope
    shift_rows = over_frames(grad_out)
    gain_rows = over_frames(grad_out * normal)
    mean_grad, mean_both = group_means([shift_rows * gain, gain_rows * gain], ones)
    inner = minus(grad_out * gain, mean_grad) - times(normal, mean_both)
    return (
        times(inner, scale),
        jnp.sum(gain_rows, axis=0, keepdims=True),
        jnp.sum(shift_rows, axis=0, keepdims=True),
    )


def conv_forward(source, weight):
    total = dot_nt(step_frames(source, -2), weight(0))
    for t in range(1, 5):
        total = total + dot_nt(step_frames(source, t - 2), weight(t))
    return total


def conv_source(grad_low, weight):
    total = dot_nn(step_frames(grad_low, 2), weight(0))
    for t in range(1, 5):
        total = total + dot_nn(step_frames(grad_low, 2 - t), weight(t))
    return total


def row_sum(v):
    return jnp.sum(over_frames(v), axis=0, keepdims=True)


def halves(v):
    cube = v.reshape(FR // 2, 2, SAM, v.shape[1])
    return cube[:, 0].reshape(-1, v.shape[1]), cube[:, 1].reshape(-1, v.shape[1])


def interleave(even, odd):
    width = even.shape[1]
    pair = [v.reshape(FR // 2, 1, SAM, width) for v in (even, odd)]
    return jnp.concatenate(pair, axis=1).reshape(FR * SAM, width)


def train_kernel(*refs):
    for b in range(B_UR, NB):
        refs[10][b, :, 128:] = jnp.zeros((256, 128), bf16)
    train_body(*refs, lambda point: None)()


def train_body(
    w_ref, seen_ref, slot_ref, noisy_ref, mask_ref, level_ref, cot_ref, table_ref,
    act_ref, noisy_grad_ref, grad_ref, film_grad_ref, reach,
):
    row = iota((256, 256), 0)
    col = iota((256, 256), 1)
    ones = jnp.where((row >> 5) == (col >> 5), 1.0, 0.0).astype(bf16)
    swap = jnp.where(col == ((row & 15) << 4) + (row >> 4), 1.0, 0.0).astype(bf16)
    spread_mask = one_hot((iota((SAM, 256), 1) >> 4) == iota((SAM, 256), 0))
    keep = dot_nn(mask_ref[...].astype(f32).astype(bf16), spread_mask)
    start_cols = noisy_ref[...].astype(f32) * keep
    start_cols = jnp.concatenate([start_cols, jnp.zeros((6, 256), f32)], axis=0).astype(bf16)
    start = dot_nt(swap, start_cols).astype(bf16)
    lane16 = iota((16, 128), 1)
    row16 = iota((16, 128), 0)
    inputs = jnp.zeros((256, 128), f32)
    for t in range(5):
        place = lane16 == row16 + t * ADIM
        if t == 2:
            place = place | (lane16 == row16 + 50)
        inputs = inputs + dot_nn(step_frames(start, t - 2), one_hot(place & (row16 < ADIM)))
    inputs = inputs.astype(bf16)
    cot_high, cot_low = split2(cot_ref[...])
    upstream = dot_nt(swap, cot_high) + dot_nt(swap, cot_low)
    upstream_low = upstream.astype(bf16)
    at_level = one_hot(iota((64, SAM), 0) == level_ref[...])
    feats = dot_tn(at_level, table_ref[...]).astype(bf16)
    reach(0)
    misc = w_ref[B_MISC, :, :128]
    lane = iota((256, 128), 1)
    misc_first = jnp.where(lane < 50, misc, jnp.zeros_like(misc))
    misc_res = jnp.where((lane >= 50) & (lane < 60), misc, jnp.zeros_like(misc))
    singles = misc.astype(f32).T[LANE_TAIL : LANE_TAIL + 32]
    vec = lambda k: singles[k : k + 1]

    inner = [w_ref[B_INNER, :, j * 128 : (j + 1) * 128] for j in range(2)]
    outer = [w_ref[B_OUTER, :, j * 128 : (j + 1) * 128] for j in range(2)]
    film_time = lambda q: w_ref[B_FILM + q // 2, :, (q % 2) * 128 : (q % 2) * 128 + 128]
    hidden = [mish_parts(dot_nt(feats, inner[j]) + vec(T_BIAS_A + j)) for j in range(2)]
    hidden_low = [h[0].astype(bf16) for h in hidden]
    embed = dot_nn(hidden_low[0], outer[0]) + dot_nn(hidden_low[1], outer[1]) + vec(T_OUT)[:, :TE]
    cond, cond_slope = mish_parts(embed)
    cond_low = cond.astype(bf16)
    pre = dot_nt(inputs, misc_first) + vec(D_B1)
    act_one, normal_one, slope_one, scale_one = norm_forward(pre, vec(D_G1), vec(D_S1), ones)
    reach(1)
    at_slot = one_hot(iota((SAM, SAM), 0) == slot_ref[...])
    line = iota((32, SAM), 0)
    seen_film = jnp.concatenate([seen_ref[:, k].reshape(32, 128) for k in range(4)], axis=1)
    seen_film = split3(seen_film)
    sides = []
    for side in range(2):
        at_line = one_hot(((line >> 3) * 4 + (line & 3) == slot_ref[...]) & ((line >> 2) & 1 == side))
        sides.append(sum(dot_tn(at_line, part) for part in seen_film))
    seen_film = jnp.concatenate(
        [sides[k % 2][:, (k // 2) * 128 : (k // 2) * 128 + 128] for k in range(8)], axis=1
    )
    spans = lambda v, q: jnp.concatenate([v[:, k * 128 + q * 32 : k * 128 + q * 32 + 32] for k in range(8)], axis=1)
    film_of = lambda q: spans(seen_film, q) + dot_nt(cond_low, film_time(q)) + vec((D_FS, D_FO, U_FS, U_FO)[q])
    film = [film_of(0), film_of(1)]
    mid_one = plus(times(act_one, film[0]), film[1]).astype(bf16)
    reach(2)
    down = lambda t: w_ref[B_DS + t]
    pre = conv_forward(mid_one, down) + vec(D_B2)
    act, normal_two, slope_two, scale_two = norm_forward(pre, vec(D_G2), vec(D_S2), ones)
    skip = (act + dot_nt(inputs, misc_res) + vec(D_RB)).astype(bf16)
    reach(3)
    even, odd = halves(skip)
    odd_prev = step_frames(odd, -1)
    pool_sources = (odd_prev, even, odd)
    pooled = sum(dot_nt(s, w_ref[B_POOL + t]) for t, s in enumerate(pool_sources)) + vec(PB)
    pooled = pooled.astype(bf16)
    reach(4)
    pooled_prev = step_frames(pooled, -1)
    pooled_next = step_frames(pooled, 1)
    even_out = dot_nt(pooled, w_ref[B_SPREAD + 1]) + dot_nt(pooled_prev, w_ref[B_SPREAD + 3])
    odd_out = dot_nt(pooled_next, w_ref[B_SPREAD]) + dot_nt(pooled, w_ref[B_SPREAD + 2])
    wide = (interleave(even_out, odd_out) + vec(SB)).astype(bf16)
    joined = (wide, skip)
    up_res = lambda h: jnp.concatenate([w_ref[B_UR + 2 * h + i, :, 0:128] for i in range(2)], axis=1)
    turned = upstream_low.T
    for h in range(2):
        product = dot_nn(turned, joined[h]).astype(bf16)
        for i in range(2):
            grad_ref[B_UR + 2 * h + i, :, 0:128] = product[:, i * 128 : (i + 1) * 128]
    reach(5)
    up_first = [lambda t, h=h: w_ref[B_UF + 2 * t + h] for h in range(2)]
    pre = conv_forward(wide, up_first[0]) + conv_forward(skip, up_first[1]) + vec(U_B1)
    act_three, normal_three, slope_three, scale_three = norm_forward(pre, vec(U_G1), vec(U_S1), ones)
    film += [film_of(2), film_of(3)]
    mid_three = plus(times(act_three, film[2]), film[3]).astype(bf16)
    reach(6)
    up = lambda t: w_ref[B_US + t]
    pre = conv_forward(mid_three, up) + vec(U_B2)
    act, normal_four, slope_four, scale_four = norm_forward(pre, vec(U_G2), vec(U_S2), ones)
    act_four = act

    single_grads = {}

    def film_weights(q, grad_low):
        columns = slice((q % 2) * 128, (q % 2) * 128 + 128)
        grad_ref[B_FILM + q // 2, :, columns] = dot_tn(grad_low, cond_low).astype(bf16)

    def conv_weights(grad_low, source, block):
        turned = grad_low.T
        for t in range(5):
            grad_ref[block(t)] = dot_nn(turned, step_frames(source, t - 2)).astype(bf16)

    reach(7)
    grad, single_grads[U_G2], single_grads[U_S2] = norm_backward(
        upstream, normal_four, slope_four, scale_four, vec(U_G2), ones
    )
    single_grads[U_B2] = row_sum(grad)
    low = grad.astype(bf16)
    conv_weights(low, mid_three, lambda t: B_US + t)
    reach(8)
    grad_mid = conv_source(low, up)
    shift_three = over_frames(grad_mid)
    gain_three = over_frames(grad_mid * act_three)
    grad, single_grads[U_G1], single_grads[U_S1] = norm_backward(
        times(grad_mid, film[2]), normal_three, slope_three, scale_three, vec(U_G1), ones
    )
    single_grads[U_B1] = row_sum(grad)
    low = grad.astype(bf16)
    reach(15)
    for h in range(2):
        conv_weights(low, joined[h], lambda t, h=h: B_UF + 2 * t + h)
    single_grads[U_RB] = row_sum(upstream)
    reach(9)
    grad_wide = conv_source(low, up_first[0]) + dot_nn(upstream_low, up_res(0))
    grad_skip = conv_source(low, up_first[1]) + dot_nn(upstream_low, up_res(1))
    single_grads[SB] = row_sum(grad_wide)
    low_even, low_odd = halves(grad_wide.astype(bf16))
    turned_even, turned_odd = low_even.T, low_odd.T
    grad_ref[B_SPREAD] = dot_nn(turned_odd, pooled_next).astype(bf16)
    grad_ref[B_SPREAD + 1] = dot_nn(turned_even, pooled).astype(bf16)
    grad_ref[B_SPREAD + 2] = dot_nn(turned_odd, pooled).astype(bf16)
    grad_ref[B_SPREAD + 3] = dot_nn(turned_even, pooled_prev).astype(bf16)
    reach(10)
    grad_pooled = dot_nn(low_even, w_ref[B_SPREAD + 1]) + dot_nn(low_odd, w_ref[B_SPREAD + 2])
    grad_pooled = grad_pooled + dot_nn(step_frames(low_even, 1), w_ref[B_SPREAD + 3])
    grad_pooled = grad_pooled + dot_nn(step_frames(low_odd, -1), w_ref[B_SPREAD])
    single_grads[PB] = row_sum(grad_pooled)
    low = grad_pooled.astype(bf16)
    turned = low.T
    for t in range(3):
        grad_ref[B_POOL + t] = dot_nn(turned, pool_sources[t]).astype(bf16)
    reach(11)
    grad_even = dot_nn(low, w_ref[B_POOL + 1])
    grad_odd = dot_nn(low, w_ref[B_POOL + 2]) + dot_nn(step_frames(low, 1), w_ref[B_POOL])
    grad_skip = grad_skip + interleave(grad_even, grad_odd)
    single_grads[D_RB] = row_sum(grad_skip)
    skip_low = grad_skip.astype(bf16)
    misc_grad = jnp.where(lane < 50, 0.0, dot_nn(skip_low.T, inputs))
    back = dot_nn(skip_low, misc_res)
    grad, single_grads[D_G2], single_grads[D_S2] = norm_backward(
        grad_skip, normal_two, slope_two, scale_two, vec(D_G2), ones
    )
    single_grads[D_B2] = row_sum(grad)
    low = grad.astype(bf16)
    conv_weights(low, mid_one, lambda t: B_DS + t)
    film_weights(2, gain_three.astype(bf16))
    film_weights(3, shift_three.astype(bf16))
    reach(12)
    grad_mid = conv_source(low, down)
    shift_one = over_frames(grad_mid)
    gain_one = over_frames(grad_mid * act_one)
    grad, single_grads[D_G1], single_grads[D_S1] = norm_backward(
        times(grad_mid, film[0]), normal_one, slope_one, scale_one, vec(D_G1), ones
    )
    single_grads[D_B1] = row_sum(grad)
    low = grad.astype(bf16)
    misc_grad = misc_grad + jnp.where(lane < 50, dot_nn(low.T, inputs), 0.0)
    film_grads = (gain_one, shift_one, gain_three, shift_three)
    film_low = [g.astype(bf16) for g in film_grads]
    back_cond = None
    for q in range(4):
        single_grads[(D_FS, D_FO, U_FS, U_FO)[q]] = jnp.sum(film_grads[q], axis=0, keepdims=True)
        if q < 2:
            film_weights(q, film_low[q])
        part = dot_nn(film_low[q], film_time(q))
        back_cond = part if back_cond is None else back_cond + part
    at_slots = [dot_nn(at_slot, v) for v in film_low]
    for k in range(8):
        film_grad_ref[k] = jnp.concatenate([v[:, k * 32 : (k + 1) * 32] for v in at_slots], axis=1).astype(bf16)
    reach(13)
    grad_embed = back_cond * cond_slope
    single_grads[T_OUT] = jnp.concatenate(
        [jnp.sum(grad_embed, axis=0, keepdims=True), jnp.zeros((1, C - TE), f32)], axis=1
    )
    embed_low = grad_embed.astype(bf16)
    for j in range(2):
        grad_ref[B_OUTER, :, j * 128 : (j + 1) * 128] = dot_tn(hidden_low[j], embed_low).astype(bf16)
        grad_hidden = dot_nt(embed_low, outer[j]) * hidden[j][1]
        single_grads[T_BIAS_A + j] = jnp.sum(grad_hidden, axis=0, keepdims=True)
        grad_ref[B_INNER, :, j * 128 : (j + 1) * 128] = dot_tn(grad_hidden.astype(bf16), feats).astype(bf16)
    stack = [jnp.zeros((LANE_TAIL, 256), f32)] + [single_grads[k] for k in range(TAIL)]
    stack = jnp.concatenate(stack + [jnp.zeros((128 - LANE_TAIL - TAIL, 256), f32)], axis=0)
    grad_ref[B_MISC, :, :128] = (misc_grad + stack.T).astype(bf16)
    grad_ref[B_MISC, :, 128:] = jnp.zeros((256, 128), bf16)
    reach(14)

    def outputs():
        result = act_four + dot_nt(wide, up_res(0)) + dot_nt(skip, up_res(1)) + vec(U_RB)
        act_ref[...] = dot_tn(result.astype(bf16), swap).astype(bf16)
        total = back + dot_nn(low, misc_first)
        grad_start = total[:, 50:60]
        for t in range(5):
            grad_start = grad_start + step_frames(total[:, t * ADIM : (t + 1) * ADIM], 2 - t)
        grad_cols = sum(dot_tn(part, swap) for part in split3(jnp.concatenate([grad_start, jnp.zeros((256, 6), f32)], axis=1)))
        noisy_grad_ref[...] = grad_cols[:ADIM] * keep

    return outputs


def train(weights, seen_film, slots, noisy, mask, levels, cotangent):
    vmem = pl.BlockSpec(memory_space=pltpu.VMEM)
    return pl.pallas_call(
        train_kernel,
        out_shape=(
            jax.ShapeDtypeStruct((C, 256), bf16),
            jax.ShapeDtypeStruct((ADIM, 256), f32),
            jax.ShapeDtypeStruct((NB, 256, 256), bf16),
            jax.ShapeDtypeStruct((8, SAM, 128), bf16),
        ),
        in_specs=[vmem] * 8,
        out_specs=(vmem,) * 4,
        compiler_params=pltpu.CompilerParams(vmem_limit_bytes=48 << 20),
        name="train",
    )(weights, seen_film, slots, noisy, mask, levels, cotangent, jnp.asarray(level_table(), bf16))


HALF = ROWS // 2


def native_grads(own_ref, film_ref, order_ref, grad_ref):
    native_most(own_ref, film_ref, grad_ref)
    native_rest(own_ref, order_ref, grad_ref)


def native_rest(own_ref, order_ref, grad_ref):
    misc = own_ref[B_MISC]
    first = dot_nt(misc[:, :128], order_ref[...])
    misc = misc.astype(f32)
    grad_ref[:, 0:50] = first[:, :50]
    grad_ref[:, AT_DOWN_RES : AT_DOWN_RES + ADIM] = misc[:, 50:60]
    grad_ref[:, AT_TAIL : AT_TAIL + TAIL] = misc[:, LANE_TAIL : LANE_TAIL + TAIL]
    grad_ref[:, AT_TIME[0] : AT_TIME[0] + 256] = own_ref[B_INNER].astype(f32)
    grad_ref[:, AT_TIME[1] : AT_TIME[1] + 256] = own_ref[B_OUTER].astype(f32)
    native_film(own_ref, grad_ref, 0)


def native_film(own_ref, grad_ref, side):
    for q in (2 * side, 2 * side + 1):
        part = own_ref[B_FILM + side, :, (q % 2) * 128 : (q % 2) * 128 + 128]
        grad_ref[:, AT_FILM[q] + OBS : AT_FILM[q] + OBS + TE] = part.astype(f32)


def native_most(own_ref, film_ref, grad_ref):
    for q in range(4):
        grad_ref[:, AT_FILM[q] : AT_FILM[q] + OBS] = film_ref[q * ROWS : (q + 1) * ROWS]
    native_film(own_ref, grad_ref, 1)
    for i in range(4):
        begin = AT_UP_RES + i * 128
        grad_ref[:, begin : begin + 128] = own_ref[B_UR + i, :, 0:128].astype(f32)
    for taps in (5, 3, 4):
        places = [(at, h, block) for at, k, groups, block in CONVS if k == taps for h in range(groups)]
        stacked = jnp.concatenate(
            [
                jnp.concatenate(
                    [own_ref[block(t, h), :, (h % 2) * 128 : (h % 2) * 128 + 128] for t in range(taps)], axis=1
                )
                for _, h, block in places
            ],
            axis=0,
        )
        moved = dot_nt(stacked, tap_order(taps))
        for n, (at, h, _) in enumerate(places):
            begin = at + h * 128 * taps
            grad_ref[:, begin : begin + 128 * taps] = moved[n * ROWS : (n + 1) * ROWS]


def unpack_kernel(own_ref, film_ref, order_ref, grad_ref):
    native_grads(own_ref, film_ref, order_ref, grad_ref)


def unpack(own, film):
    vmem = pl.BlockSpec(memory_space=pltpu.VMEM)
    return pl.pallas_call(
        unpack_kernel,
        out_shape=jax.ShapeDtypeStruct((ROWS, Q), f32),
        in_specs=[vmem] * 3,
        out_specs=vmem,
        compiler_params=pltpu.CompilerParams(vmem_limit_bytes=30 << 20),
        name="unpack",
    )(own, film, jnp.asarray(first_order(), bf16))


def adam_kernel(count, *refs):
    grad_ref, square_ref = refs[:2]
    old, extra_in = refs[2:5], refs[5 : 5 + count]
    norm_ref, new_hbm, extra_out = refs[5 + count], refs[6 + count : 10 + count], refs[10 + count : 10 + 2 * count]
    new, sems = refs[10 + 2 * count : 14 + 2 * count], refs[-1]
    norm = jnp.sqrt(jnp.sum(square_ref[...], axis=(0, 1), keepdims=True))
    norm_ref[...] = norm
    factor = jnp.minimum(1.0, clip_limit / (norm + 1e-06))
    stores = {}

    def store(n, height, at):
        rows = pl.ds(at, height)
        stores[n, at] = pltpu.make_async_copy(new[n].at[rows], new_hbm[n].at[rows], sems.at[n, at // 8])
        stores[n, at].start()

    width = 1024
    for row in range(0, ROWS, 8):
        for begin in range(0, Q, width):
            at = (slice(row, row + 8), slice(begin, min(begin + width, Q)))
            clipped = grad_ref[at] * factor
            new_first = decay_first * old[1][at] + (1.0 - decay_first) * clipped
            new_second = decay_second * old[2][at] + (1.0 - decay_second) * clipped * clipped
            first_hat = new_first * (1.0 / (1.0 - decay_first**ADAM_STEP))
            second_hat = new_second * (1.0 / (1.0 - decay_second**ADAM_STEP))
            before = old[0][at]
            new[0][at] = before - learn_rate * (first_hat / (jnp.sqrt(second_hat) + adam_eps) + weight_decay * before)
            new[1][at] = new_first
            new[2][at] = new_second
        for n in range(3):
            store(n, 8, row)
        if row % 16:
            rows = slice(row - 8, row + 8)
            new[3][rows] = new[0][rows].astype(bf16)
            store(3, 16, row - 8)
    for source, target in zip(extra_in, extra_out):
        target[...] = source[...].reshape(target.shape)
    for copy in stores.values():
        copy.wait()


def adam(grads, squares, params, first, second, extras=(), extra_shapes=()):
    vmem = pl.BlockSpec(memory_space=pltpu.VMEM)
    hbm = pl.BlockSpec(memory_space=pl.ANY)
    shape = jax.ShapeDtypeStruct((ROWS, Q), f32)
    count = len(extras)
    return pl.pallas_call(
        functools.partial(adam_kernel, count),
        out_shape=(
            jax.ShapeDtypeStruct((1, 1), f32),
            shape, shape, shape, jax.ShapeDtypeStruct((ROWS, Q), bf16),
            *(jax.ShapeDtypeStruct(dims, v.dtype) for dims, v in zip(extra_shapes, extras)),
        ),
        in_specs=[vmem] * (5 + count),
        out_specs=(vmem,) + (hbm,) * 4 + (vmem,) * count,
        scratch_shapes=[pltpu.VMEM((ROWS, Q), f32)] * 3
        + [pltpu.VMEM((ROWS, Q), bf16), pltpu.SemaphoreType.DMA((4, ROWS // 8))],
        compiler_params=pltpu.CompilerParams(vmem_limit_bytes=30 << 20),
        name="adam",
    )(grads, squares, params, first, second, *extras)


def local_plain(noisy, action_mask, time_index, obs_embed, obs_slot, cotangent, params, first_moment, second_moment):
    rows = params.shape[0]
    padded = lambda v: jnp.pad(v, ((0, ROWS - rows), (0, 0))) if rows < ROWS else v
    if rows > ROWS:
        packed = [pack(params[r : r + ROWS]) for r in range(0, rows, ROWS)]
        own = jnp.concatenate([p[0].reshape(NB, ROWS, 256) for p in packed], axis=1)
        film_own = jnp.concatenate([p[1].reshape(4, ROWS, OBS) for p in packed], axis=1)
    else:
        own, film_own = pack(padded(params))
        own = own.reshape(NB, ROWS, 256)[:, :rows]
        film_own = film_own.reshape(4, ROWS, OBS)[:, :rows]
    weights = lax.all_gather(own, "wide", axis=1, tiled=True)
    film_rows = lax.all_gather(film_own, "wide", axis=1, tiled=True).reshape(4 * C, OBS)
    seen = lax.all_gather(obs_embed, "pair", axis=0, tiled=True).reshape(-1, OBS).astype(f32)
    cond, slope = mish_parts(seen)
    cond = cond.astype(bf16)
    seen_film = dot_nt(cond, film_rows).reshape(4, 4, 4, 8, 32).transpose(0, 3, 1, 2, 4).reshape(4, 8, 4, 128)
    seen_film = seen_film.reshape(4, 4, 8, 128)
    act, noisy_grad, grads, film_grad = train(
        weights, seen_film, obs_slot[None], noisy[0], action_mask, time_index, cotangent[0]
    )
    film_grad = film_grad.reshape(8, SAM, 4, 32).transpose(1, 2, 0, 3).reshape(SAM, 4 * C)
    film_total = lax.psum(dot_tn(film_grad, cond), ("pair", "wide")).reshape(4, C, OBS)
    back = lax.psum_scatter(
        (dot_nn(film_grad, film_rows) * slope).reshape(-1, obs_embed.shape[1], OBS),
        "pair", scatter_dimension=0, tiled=True,
    )
    total = lax.psum(grads.astype(f32), ("pair", "wide")).astype(bf16)
    squares = jnp.sum(jnp.square(total.astype(f32))) + jnp.sum(jnp.square(film_total))
    here = lax.axis_index("wide") * rows
    mine = lax.dynamic_slice_in_dim(total, here, rows, 1)
    film_mine = lax.dynamic_slice_in_dim(film_total, here, rows, 1)
    outs = []
    for r in range(0, rows, ROWS):
        take = lambda v: jnp.pad(v[:, r : r + ROWS], ((0, 0), (0, max(0, ROWS - rows)), (0, 0)))
        outs.append(
            adam(
                unpack(take(mine), take(film_mine).reshape(4 * ROWS, OBS)), squares.reshape(1, 1),
                *(padded(v)[r : r + ROWS] for v in (params, first_moment, second_moment)),
            )
        )
    new = [jnp.concatenate([o[k] for o in outs], axis=0)[:rows] for k in range(1, 5)]
    return (act[None], noisy_grad[None], back, outs[0][0].reshape(()), *new)


MESH = pl.DeviceIdType.MESH


class Place:
    def __init__(self):
        p = lax.axis_index("pair")
        w = lax.axis_index("wide")
        self.p, self.w = p, w
        self.x, self.y = lax.rem(p, 2), lax.div(p, 2)
        self.c, self.z = lax.rem(w, 2), lax.div(w, 2)
        turn = [1 - 2 * self.x, 2 - 4 * self.y]
        self.p_flip = [p, p + turn[0], p + turn[1], p + (turn[0] + turn[1])]
        z_turn = [1 - 2 * lax.rem(self.z, 2), 2 - 4 * lax.div(self.z, 2)]
        self.z_flip = [self.z, self.z + z_turn[0], self.z + z_turn[1], self.z + (z_turn[0] + z_turn[1])]
        self.w_flip = []
        for z in self.z_flip:
            self.w_flip += [2 * z + self.c, 2 * z + (1 - self.c)]
        self.w_flip[0] = w
        self.x_of = [lax.rem(v, 2) for v in self.p_flip]
        self.y_of = [lax.div(v, 2) for v in self.p_flip]

    def line(self, l):
        return (self.p, self.w_flip[l])

    def others(self):
        return [(self.p_flip[k], self.w_flip[l]) for k in range(1, 4) for l in range(1, 8)]

    def plane(self, k):
        return (self.p_flip[k], self.w)


def greet(me):
    barrier = pltpu.get_barrier_semaphore()
    for l in range(1, 8):
        pl.semaphore_signal(barrier, inc=1, device_id=me.line(l), device_id_type=MESH)
    for k in range(1, 4):
        pl.semaphore_signal(barrier, inc=1, device_id=me.plane(k), device_id_type=MESH)


def meet(me):
    pl.semaphore_wait(pltpu.get_barrier_semaphore(), 10)


def drain(size, semaphore):
    pltpu.make_async_copy(size, size, semaphore).wait()


class Pool:
    def __init__(self, ref):
        self.ref, self.used = ref, 0

    def new(self):
        self.used += 1
        return self.ref.at[self.used - 1]

    def several(self, keys):
        return {key: self.new() for key in keys}


class Lane:
    def __init__(self, pool):
        self.sent, self.bytes = pool.new(), 0

    def send(self, source, target, arrival, device):
        pltpu.make_async_remote_copy(
            src_ref=source, dst_ref=target, send_sem=self.sent, recv_sem=arrival,
            device_id=device, device_id_type=MESH,
        ).start()
        self.bytes += math.prod(source.shape) * source.dtype.itemsize

    def finish(self, size):
        assert math.prod(size.shape) * size.dtype.itemsize == self.bytes
        drain(size, self.sent)


def fold_rows(v):
    return jnp.concatenate([v[:, q * 256 : (q + 1) * 256] for q in range(4)], axis=0)


def unfold_rows(v):
    return jnp.concatenate([v[q * 4 : (q + 1) * 4] for q in range(4)], axis=1)


def quarter_rows(parts):
    quarter = (iota(parts[0].shape, 0) >> 2) & 3
    return sum(jnp.where(quarter == q, part, 0.0) for q, part in enumerate(parts))


class Gather:
    def __init__(self, me, own, weights, seen, obs_all, film, film_part, film_line, pool, local_sem):
        self.me, self.own, self.weights, self.seen, self.obs_all, self.film = me, own, weights, seen, obs_all, film
        self.film_part, self.film_line, self.local_sem = film_part, film_line, local_sem
        self.z, self.x, self.y, self.f, self.c, self.small = (Lane(pool) for _ in range(6))
        self.parts, self.films, self.more, self.narrow = (Lane(pool) for _ in range(4))
        pieces = [(g, k) for g in range(len(GATHER_GROUPS)) for k in range(1, 4)]
        self.z_in = pool.several(pieces)
        near = [(g, k) for g, k in pieces if g not in GATHER_DIRECT] + list(GATHER_DIRECT)
        self.x_in, self.y_in = pool.several(near), pool.several(near)
        self.f_in = pool.several(range(len(GATHER_GROUPS)))
        self.c_in = pool.several(range(len(GATHER_GROUPS)))
        self.obs_in, self.part_in, self.film_in, self.more_in = (pool.new() for _ in range(4))

    def start_obs(self):
        me = self.me
        piece = self.obs_all.at[me.p, me.w]
        for l in range(1, 8):
            self.small.send(piece, piece, self.obs_in, me.line(l))

    def start_rows(self, g):
        me = self.me
        lane = self.narrow if g == NARROW else self.z
        for k in range(1, 4):
            lane.send(
                self.own.at[gather_group(g), me.p, :, cols(g)],
                self.weights.at[gather_group(g), me.p, me.z, me.c, :, cols(g)],
                self.z_in[g, k], me.line(2 * k),
            )

    def start_local(self):
        self.local = pltpu.make_async_copy(self.own, self.weights.at[:, :, self.me.z, self.me.c], self.local_sem)
        self.local.start()

    def film_product(self):
        me = self.me
        drain(self.obs_all.at[0, 0:7], self.obs_in)
        cond = mish_parts(self.obs_all[me.p].reshape(128, 256).astype(f32))[0].astype(bf16)
        film = quarter_rows([dot_nt(cond, self.film[:, q * 256 : (q + 1) * 256]) for q in range(4)])
        row, col = iota((64, 128), 0), iota((64, 128), 1)
        pick = one_hot(((row >> 3) == (col >> 4)) & ((row & 7) == (col & 3)))
        self.film_part[...] = sum(dot_nn(pick, part) for part in split3(film)).reshape(8, 8, 128)
        for l in range(1, 8):
            self.parts.send(self.film_part.at[me.w_flip[l]], self.film_line.at[me.w], self.part_in, me.line(l))
        self.film_line[me.w] = self.film_part[me.w]

    def film_hop(self):
        me = self.me
        drain(self.film_line.at[0:7], self.part_in)
        for k in range(4):
            self.seen[me.p, k] = self.film_line[2 * k] + pltpu.roll(self.film_line[2 * k + 1], 4, 0)
        piece = self.seen.at[me.p]
        for k in range(1, 4):
            self.films.send(piece, piece, self.film_in, me.plane(k))

    def obs_hop(self):
        me = self.me
        piece = self.obs_all.at[me.p]
        for k in range(1, 4):
            self.more.send(piece, piece, self.more_in, me.plane(k))

    def film_done(self):
        drain(self.seen.at[0:3], self.film_in)

    def first_hop(self, g):
        me = self.me
        lanes = [self.narrow] * 3 if g == NARROW else [self.x, self.y, self.f]
        for k in range(1, 4):
            piece = self.weights.at[gather_group(g), me.p, me.z_flip[k], me.c, :, cols(g)]
            drain(piece, self.z_in[g, k])
            key = g if g in GATHER_DIRECT else (g, k)
            lanes[0].send(piece, piece, self.x_in[key], me.plane(1))
            lanes[1].send(piece, piece, self.y_in[key], me.plane(2))
            if g in GATHER_DIRECT:
                lanes[2].send(piece, piece, self.f_in[g], me.plane(3))

    def three(self, g):
        return self.weights.at[gather_group(g), 0, 0:3, 0, :, cols(g)]

    def second_hop(self, g):
        me = self.me
        if g in GATHER_DIRECT:
            drain(self.three(g), self.x_in[g])
            drain(self.three(g), self.y_in[g])
            return
        for k in range(1, 4):
            one = self.weights.at[gather_group(g), 0, 0, 0]
            drain(one, self.x_in[g, k])
            drain(one, self.y_in[g, k])
            along_y = (g + k) % 2 == 0
            piece = self.weights.at[gather_group(g), me.p_flip[1 if along_y else 2], me.z_flip[k], me.c]
            self.f.send(piece, piece, self.f_in[g], me.plane(2 if along_y else 1))

    def last_hop(self, g):
        if g == 0:
            self.local.wait()
        if g in GATHER_DIRECT:
            self.second_hop(g)
        drain(self.three(g), self.f_in[g])
        piece = self.weights.at[gather_group(g), :, :, self.me.c, :, cols(g)]
        (self.narrow if g == NARROW else self.c).send(piece, piece, self.c_in[g], self.me.line(1))

    def arrived(self, g):
        drain(self.weights.at[gather_group(g), :, :, 0, :, cols(g)], self.c_in[g])

    def obs_done(self):
        drain(self.obs_all.at[0:3], self.more_in)

    def finish(self):
        wide = pl.ds(0, GATHER_GROUPS[NARROW][0])
        for lane in (self.z, self.x, self.y, self.f):
            lane.finish(self.weights.at[wide, 0, 0:3, 0])
        self.c.finish(self.weights.at[wide, :, :, 0])
        self.narrow.finish(self.weights.at[0:7, :, 0, 0, :, cols(NARROW)])
        self.small.finish(self.obs_all.at[0, 0:7])
        self.parts.finish(self.film_line.at[0:7])
        self.films.finish(self.seen.at[0:3])
        self.more.finish(self.obs_all.at[0:3])


class Scatter:
    def __init__(self, me, grad, film_grad, obs_all, film, out, film_out, back, square, buffers, pool):
        self.me, self.grad, self.film_grad, self.obs_all, self.film = me, grad, film_grad, obs_all, film
        self.out, self.film_out, self.back, self.square = out, film_out, back, square
        (self.half, self.core, self.xb, self.yb, self.ub, self.vb, self.zb, self.zq, self.pq, self.db,
         self.film_all, self.back_part, self.back_line, self.cond, self.all_squares) = buffers
        self.c, self.x, self.y, self.u, self.v, self.z = (Lane(pool) for _ in range(6))
        self.zf, self.q, self.d, self.r, self.g, self.h, self.b, self.n = (Lane(pool) for _ in range(8))
        self.narrow, self.narrow_end = Lane(pool), Lane(pool)
        groups = range(len(GROUPS))
        self.staged = [g for g in groups if g != Z_FIRST and g not in PLANE_DIRECT]
        self.c_in = pool.several(groups)
        self.x_in, self.y_in, self.u_in, self.v_in = (pool.several(self.staged) for _ in range(4))
        self.d_in = pool.several(PLANE_DIRECT)
        self.z_in = pool.several(g for g in groups if g != Z_FIRST)
        self.zf_in, self.q_in, self.r_in, self.g_in, self.h_in, self.b_in, self.n_in = (pool.new() for _ in range(7))
        self.narrow_in, self.r_last = pool.new(), pool.new()
        self.squares = []

    def start(self, g):
        me = self.me
        lane = self.narrow if g == NARROW else self.c
        lane.send(
            self.grad.at[group(g), :, :, 1 - me.c, :, cols(g)], self.core.at[group(g), :, :, :, cols(g)],
            self.c_in[g], me.line(1),
        )

    def core_sum(self, g):
        me, half, (first, last) = self.me, self.half, GROUPS[g]
        drain(self.core.at[group(g), :, :, :, cols(g)], self.c_in[g])

        def add(i, _):
            j, q = first + i // 4, i % 4
            total = self.grad[j, q, :, me.c, :, cols(g)].astype(f32) + self.core[j, q, :, :, cols(g)].astype(f32)
            half[j, q // 2, q % 2, :, :, cols(g)] = total.astype(bf16)
            return 0

        lax.fori_loop(0, (last - first) * 4, add, 0)
        if g == Z_FIRST:
            self.z_send(g, 0)
        elif g in PLANE_DIRECT:
            for k in range(1, 4):
                piece = half.at[group(g), me.y_of[k], me.x_of[k]]
                self.d.send(piece, self.db.at[k - 1, group(g)], self.d_in[g], me.plane(k))
        else:
            lanes = [self.narrow] * 2 if g == NARROW else [self.x, self.y]
            lanes[0].send(
                half.at[group(g), :, 1 - me.x, LOW, :, cols(g)], self.xb.at[group(g), :, :, :, cols(g)],
                self.x_in[g], me.plane(1),
            )
            lanes[1].send(
                half.at[group(g), 1 - me.y, :, HIGH, :, cols(g)], self.yb.at[group(g), :, :, :, cols(g)],
                self.y_in[g], me.plane(2),
            )

    def z_send(self, g, n):
        me = self.me
        for k in range(1, 4):
            self.zf.send(
                self.half.at[GROUPS[g][0] + n, :, :, me.z_flip[k]], self.zq.at[k - 1, n], self.zf_in, me.line(2 * k)
            )

    def z_sum(self, g):
        me, half, (first, last) = self.me, self.half, GROUPS[g]
        drain(self.zq, self.zf_in)
        for j in range(first, last):
            total = half[j, :, :, me.z].astype(f32)
            for k in range(3):
                total = total + self.zq[k, j - first].astype(f32)
            half[j, :, :, me.z] = total.astype(bf16)
        for k in range(1, 4):
            piece = half.at[group(g), me.y_of[k], me.x_of[k], me.z]
            self.q.send(piece, self.pq.at[k - 1], self.q_in, me.plane(k))

    def plane_sum(self, g):
        drain(self.pq, self.q_in)
        self.finish_sum(g, [lambda j, k=k: self.pq[k, j - GROUPS[g][0]] for k in range(3)])

    def first_sum(self, g):
        me, half, (first, last) = self.me, self.half, GROUPS[g]
        lanes = [self.narrow] * 2 if g == NARROW else [self.u, self.v]
        drain(self.xb.at[group(g), :, :, :, cols(g)], self.x_in[g])

        def add_x(i, _):
            j, q = first + i // 2, i % 2
            total = half[j, q, me.x, LOW, :, cols(g)].astype(f32) + self.xb[j, q, :, :, cols(g)].astype(f32)
            half[j, q, me.x, LOW, :, cols(g)] = total.astype(bf16)
            return 0

        lax.fori_loop(0, (last - first) * 2, add_x, 0)
        lanes[0].send(
            half.at[group(g), 1 - me.y, me.x, LOW, :, cols(g)], self.ub.at[group(g), :, :, cols(g)],
            self.u_in[g], me.plane(2),
        )
        drain(self.yb.at[group(g), :, :, :, cols(g)], self.y_in[g])

        def add_y(i, _):
            j, q = first + i // 2, i % 2
            total = half[j, me.y, q, HIGH, :, cols(g)].astype(f32) + self.yb[j, q, :, :, cols(g)].astype(f32)
            half[j, me.y, q, HIGH, :, cols(g)] = total.astype(bf16)
            return 0

        lax.fori_loop(0, (last - first) * 2, add_y, 0)
        lanes[1].send(
            half.at[group(g), me.y, 1 - me.x, HIGH, :, cols(g)], self.vb.at[group(g), :, :, cols(g)],
            self.v_in[g], me.plane(1),
        )

    def direct_sum(self, g):
        me, half = self.me, self.half
        drain(self.db.at[:, group(g)], self.d_in[g])
        for j in range(*GROUPS[g]):
            total = half[j, me.y, me.x].astype(f32)
            for k in range(3):
                total = total + self.db[k, j].astype(f32)
            half[j, me.y, me.x] = total.astype(bf16)
        self.send_z(g)

    def second_sum(self, g):
        me, half = self.me, self.half
        drain(self.ub.at[group(g), :, :, cols(g)], self.u_in[g])
        drain(self.vb.at[group(g), :, :, cols(g)], self.v_in[g])
        for j in range(*GROUPS[g]):
            for part, more in ((LOW, self.ub), (HIGH, self.vb)):
                total = half[j, me.y, me.x, part, :, cols(g)].astype(f32) + more[j, :, :, cols(g)].astype(f32)
                half[j, me.y, me.x, part, :, cols(g)] = total.astype(bf16)
        self.send_z(g)

    def send_z(self, g):
        me = self.me
        lane = self.narrow_end if g == NARROW else self.z
        for k in range(1, 4):
            piece = self.half.at[group(g), me.y, me.x, me.z_flip[k], :, cols(g)]
            lane.send(piece, self.zb.at[k - 1, group(g), :, cols(g)], self.z_in[g], me.line(2 * k))

    def last_sum(self, g):
        drain(self.zb.at[:, group(g), :, cols(g)], self.z_in[g])
        self.finish_sum(g, [lambda j, k=k: self.zb[k, j, :, cols(g)] for k in range(3)])

    def finish_sum(self, g, terms):
        me = self.me
        for j in range(*GROUPS[g]):
            total = self.half[j, me.y, me.x, me.z, :, cols(g)].astype(f32)
            for term in terms:
                total = total + term(j).astype(f32)
            total = total.astype(bf16)
            self.out[j, me.p, :, cols(g)] = total
            self.count(jnp.square(total.astype(f32)))
        piece = self.out.at[group(g), me.p, :, cols(g)]
        lane, arrival = (self.narrow_end, self.narrow_in) if g == NARROW else (self.r, self.r_in)
        if g == 0:
            arrival = self.r_last
        for k in range(1, 4):
            lane.send(piece, piece, arrival, me.plane(k))

    def count(self, squares):
        folded = jnp.sum(squares.reshape(-1, 8, squares.shape[1]), axis=0)
        self.squares += [folded[:, i : i + 128] for i in range(0, squares.shape[1], 128)]

    def film_start(self):
        me = self.me
        self.film_all[me.p, me.w] = self.film_grad[me.w]
        for l in range(1, 8):
            self.g.send(self.film_grad.at[me.w_flip[l]], self.film_all.at[me.p, me.w], self.g_in, me.line(l))

    def film_hop(self):
        me = self.me
        drain(self.film_all.at[0, 0:7], self.g_in)
        piece = self.film_all.at[me.p]
        for k in range(1, 4):
            self.h.send(piece, piece, self.h_in, me.plane(k))

    def film_inputs(self):
        row, col = iota((128, 512), 0), iota((128, 512), 1)
        same = ((row >> 4) == ((col >> 4) & 7)) & (((row >> 2) & 3) == (col >> 7)) & ((row & 3) == (col & 3))
        seen_all = self.obs_all[...].reshape(512, 256)
        for q in range(4):
            pick = one_hot(same & (((col >> 2) & 3) == q))
            self.cond[q] = mish_parts(dot_nn(pick, seen_all))[0].astype(bf16)

    def film_products(self):
        me = self.me
        drain(self.film_all.at[0:3], self.h_in)
        copies = [self.film_all[k].reshape(128, 128).astype(f32) for k in range(4)]
        total = split2((copies[0] + copies[1]) + (copies[2] + copies[3]))
        row, col = iota((128, 128), 0), iota((128, 128), 1)
        mine = one_hot(((row >> 4) == (col >> 4)) & ((col & 15) == 4 * me.p + (row & 3)))
        rows = [dot_nn(mine, part).astype(bf16) for part in total]
        parts = [
            dot_nn(rows[0], self.film[:, q * 256 : (q + 1) * 256])
            + dot_nn(rows[1], self.film[:, q * 256 : (q + 1) * 256])
            for q in range(4)
        ]
        self.back_part[...] = quarter_rows(parts).astype(bf16).reshape(8, 16, 256)
        for l in range(1, 8):
            self.b.send(self.back_part.at[me.w_flip[l]], self.back_line.at[me.w], self.b_in, me.line(l))
        self.back_line[me.w] = self.back_part[me.w]
        turned = [part.T for part in total]
        for q in range(4):
            cond = self.cond[q]
            product = dot_nn(turned[0], cond) + dot_nn(turned[1], cond)
            self.film_out[:, q * 256 : (q + 1) * 256] = product
            self.count(0.25 * jnp.square(product))

    def film_back(self):
        me = self.me
        drain(self.back_line.at[0:7], self.b_in)
        total = jnp.sum(self.back_line[...].astype(f32), axis=0)
        slope = mish_parts(self.obs_all[me.p, me.w].astype(f32))[1]
        self.back[0] = unfold_rows(total * slope)

    def norm(self, hello, most, rest):
        me = self.me
        total = sum(self.squares)
        here = me.p * 8 + me.w
        piece = self.all_squares.at[here]
        self.all_squares[here] = jnp.sum(total, axis=0, keepdims=True)
        pl.semaphore_wait(hello, len(me.others()))
        for i in range(1, 32):
            self.n.send(piece, piece, self.n_in, (me.p_flip[i % 4], me.w_flip[i // 4]))
        drain(self.zb.at[:, GROUPS[0][1] : GROUPS[NARROW][0]], self.r_in)
        drain(self.zb.at[:, 0:1, :, cols(NARROW)], self.narrow_in)
        most()
        drain(self.zb.at[:, group(0)], self.r_last)
        rest()
        drain(self.all_squares.at[0:31], self.n_in)
        self.square[...] = jnp.sum(self.all_squares[...].reshape(32, 128), axis=0, keepdims=True)

    def finish(self):
        size = lambda gs: sum(GROUPS[g][1] - GROUPS[g][0] for g in gs if g != NARROW)
        staged, wide = size(self.staged), pl.ds(0, GROUPS[NARROW][0])
        self.c.finish(self.grad.at[wide, :, :, 0])
        self.x.finish(self.xb.at[0:staged])
        self.y.finish(self.yb.at[0:staged])
        self.u.finish(self.ub.at[0:staged])
        self.v.finish(self.vb.at[0:staged])
        self.d.finish(self.db.at[:, 0 : size(PLANE_DIRECT)])
        self.z.finish(self.zb.at[:, 0 : staged + size(PLANE_DIRECT)])
        self.zf.finish(self.zq)
        self.q.finish(self.pq)
        self.r.finish(self.zb.at[:, wide])
        self.narrow.finish(self.grad.at[0:7, :, 0, 0, :, cols(NARROW)])
        self.narrow_end.finish(self.zb.at[:, 0:2, :, cols(NARROW)])
        self.g.finish(self.film_all.at[0, 0:7])
        self.h.finish(self.film_all.at[0:3])
        self.b.finish(self.back_line.at[0:7])
        self.n.finish(self.all_squares.at[0:31])


GATHER_GROUPS = ((0, 1), (1, 3), (3, 5), (5, 7), (7, 8), (8, 9))
GATHER_DIRECT = (4, 5)
GROUPS = ((0, 1), (1, 3), (3, 5), (5, 7), (7, 8), (8, 9))
Z_FIRST = 3
PLANE_DIRECT = (0,)
SEMAPHORES = 125
LOW, HIGH = pl.ds(0, 2), pl.ds(2, 2)


NARROW = 5


def cols(g):
    return pl.ds(0, 128 if g == NARROW else 256)


def group(g):
    return pl.ds(GROUPS[g][0], GROUPS[g][1] - GROUPS[g][0])


def gather_group(g):
    return pl.ds(GATHER_GROUPS[g][0], GATHER_GROUPS[g][1] - GATHER_GROUPS[g][0])


def step_kernel(*refs):
    params_out = refs[16]
    targets = (params_out,) + refs[19:27]
    targets = targets[:2] + (refs[2],) + targets[3:4] + (refs[4],) + targets[5:]
    loads = [
        pltpu.make_async_copy(source, target, refs[-2].at[i])
        for i, (source, target) in enumerate(zip(refs[:11], targets + refs[17:19]))
    ]
    for i in (0, 1, 3, 5, 6, 7, 8):
        loads[i].start()
    refs = targets + refs[9:11] + refs[11:16] + refs[17:19] + refs[27:-2] + refs[-1:]
    (params, order, obs, slots, noisy, mask, levels, cotangent, table, first, second,
     act, noisy_grad, back, native, square, first_out, second_out,
     own, weights, seen, obs_all, film, film_part, film_line, grad, film_grad, out, film_out) = refs[:29]
    buffers, (semaphores, local_sem, hello) = refs[29:44], refs[44:]
    pool = Pool(semaphores)
    me = Place()
    gather = Gather(me, own, weights, seen, obs_all, film, film_part, film_line, pool, local_sem)
    scatter = Scatter(me, grad, film_grad, obs_all, film, out, film_out, back, square, buffers, pool)
    greet(me)
    loads[0].wait()
    loads[1].wait()
    pack_first(params, order, own)
    obs_all[me.p, me.w] = fold_rows(obs[0].astype(f32)).astype(bf16)
    meet(me)
    gather.start_rows(0)
    gather.start_obs()
    pack_rest(params, own, film)
    gather.start_local()
    gather.start_rows(1)
    for i in (3, 5, 6, 7, 8):
        loads[i].wait()

    def reach(point):
        if point == 0:
            gather.first_hop(0)
            gather.film_product()
            for g in range(2, len(GATHER_GROUPS)):
                gather.start_rows(g)
            gather.second_hop(0)
            gather.first_hop(1)
            gather.first_hop(2)
            gather.film_hop()
            gather.last_hop(0)
            gather.second_hop(1)
            for device in me.others():
                pl.semaphore_signal(hello, inc=1, device_id=device, device_id_type=MESH)
            gather.arrived(0)
        if point == 1:
            gather.first_hop(3)
            gather.second_hop(2)
            gather.last_hop(1)
            gather.film_done()
        if point == 2:
            gather.arrived(1)
            gather.first_hop(4)
        if point == 3:
            gather.last_hop(2)
            gather.second_hop(3)
            gather.arrived(2)
        if point == 4:
            gather.last_hop(3)
        if point == 5:
            gather.last_hop(4)
            gather.first_hop(5)
            gather.arrived(3)
        if point == 6:
            gather.obs_hop()
            loads[9].start()
            loads[10].start()
            gather.arrived(4)
        if point == 8:
            gather.last_hop(5)
            scatter.start(5)
            scatter.start(4)
        if point == 15:
            scatter.core_sum(5)
            scatter.core_sum(4)
        if point == 9:
            scatter.start(3)
            gather.arrived(5)
        if point == 10:
            scatter.core_sum(3)
        if point == 11:
            scatter.start(2)
        if point == 12:
            scatter.core_sum(2)
            scatter.first_sum(5)
            scatter.first_sum(4)
            scatter.start(1)
        if point == 13:
            scatter.film_start()
            scatter.z_send(Z_FIRST, 1)
        if point == 14:
            scatter.start(0)
            scatter.core_sum(1)
            scatter.second_sum(5)
            scatter.second_sum(4)
            scatter.first_sum(2)
            scatter.core_sum(0)

    outputs = train_body(
        Stacked(weights), seen, slots, noisy, mask, levels, cotangent, table,
        act, noisy_grad, Stacked(grad), film_grad, reach,
    )
    scatter.film_hop()
    scatter.first_sum(1)
    gather.obs_done()
    scatter.film_inputs()
    scatter.second_sum(2)
    scatter.z_sum(3)
    scatter.film_products()
    scatter.second_sum(1)
    scatter.direct_sum(0)
    scatter.plane_sum(3)
    scatter.last_sum(5)
    scatter.last_sum(4)
    scatter.last_sum(2)
    outputs()
    scatter.last_sum(1)
    scatter.film_back()
    scatter.last_sum(0)
    loads[9].wait()
    loads[10].wait()
    scatter.norm(
        hello,
        lambda: native_most(Blocks(out), film_out, native),
        lambda: native_rest(Blocks(out), order, native),
    )
    gather.finish()
    scatter.finish()
    assert pool.used <= SEMAPHORES


class Stacked:
    def __init__(self, ref):
        self.ref = ref

    def _split(self, key):
        if not isinstance(key, tuple):
            return key, slice(None)
        return key[0], key[2]

    def __getitem__(self, key):
        block, cols = self._split(key)
        value = self.ref[block // 4, block % 4, :, :, :, cols]
        return value.reshape(256, value.shape[-1])

    def __setitem__(self, key, value):
        block, cols = self._split(key)
        self.ref[block // 4, block % 4, :, :, :, cols] = value.reshape(4, 2, ROWS, value.shape[-1])


def step(params, obs, slots, noisy, mask, levels, cotangent, first, second):
    vmem = pl.BlockSpec(memory_space=pltpu.VMEM)
    n = NB // 4
    inputs = (
        params, jnp.asarray(first_order(), bf16), obs, slots, noisy, mask, levels, cotangent,
        jnp.asarray(level_table(), bf16), first, second,
    )
    inputs = tuple(pltpu.with_memory_space_constraint(v, pltpu.HBM) for v in inputs)
    low = lambda *shape: pltpu.VMEM(shape, bf16)
    return pl.pallas_call(
        step_kernel,
        out_shape=(
            jax.ShapeDtypeStruct((C, 256), bf16),
            jax.ShapeDtypeStruct((ADIM, 256), f32),
            jax.ShapeDtypeStruct((1, 4, OBS), f32),
            jax.ShapeDtypeStruct((ROWS, Q), f32),
            jax.ShapeDtypeStruct((1, 128), f32),
            *[jax.ShapeDtypeStruct((ROWS, Q), f32)] * 3,
        ),
        in_specs=[vmem if i in (2, 4) else pl.BlockSpec(memory_space=pltpu.HBM) for i in range(11)],
        out_specs=(vmem,) * 8,
        scratch_shapes=[
            *(pltpu.VMEM(v.shape, v.dtype) for v in inputs[1:9]),
            low(n, 4, ROWS, 256),
            low(n, 4, 4, 2, ROWS, 256),
            pltpu.VMEM((4, 4, 8, 128), f32),
            low(4, 8, 16, 256),
            low(4 * ROWS, OBS),
            pltpu.VMEM((8, 8, 128), f32),
            pltpu.VMEM((8, 8, 128), f32),
            low(n, 4, 4, 2, ROWS, 256),
            low(8, SAM, 128),
            low(n, 4, ROWS, 256),
            pltpu.VMEM((4 * ROWS, OBS), f32),
            low(n, 2, 2, 4, ROWS, 256),
            low(n, 4, 4, ROWS, 256),
            low(n, 2, 2, ROWS, 256),
            low(n, 2, 2, ROWS, 256),
            low(n, 2, ROWS, 256),
            low(n, 2, ROWS, 256),
            low(3, n, ROWS, 256),
            low(3, GROUPS[Z_FIRST][1] - GROUPS[Z_FIRST][0], 2, 2, ROWS, 256),
            low(3, GROUPS[Z_FIRST][1] - GROUPS[Z_FIRST][0], ROWS, 256),
            low(3, GROUPS[max(PLANE_DIRECT)][1], 4, ROWS, 256),
            low(4, 8, 16, 128),
            low(8, 16, 256),
            low(8, 16, 256),
            low(4, 128, 256),
            pltpu.VMEM((32, 1, 128), f32),
            pltpu.SemaphoreType.DMA((SEMAPHORES,)),
            pltpu.SemaphoreType.DMA,
            pltpu.SemaphoreType.DMA((11,)),
            pltpu.SemaphoreType.REGULAR,
        ],
        compiler_params=pltpu.CompilerParams(collective_id=0, has_side_effects=True, vmem_limit_bytes=34 << 20),
        cost_estimate=pl.CostEstimate(flops=3 * 10**9, bytes_accessed=200 * 10**6, transcendentals=10**6),
        name="step",
    )(*inputs)


def local_fast(noisy, action_mask, time_index, obs_embed, obs_slot, cotangent, params, first_moment, second_moment):
    act, noisy_grad, back, native, squares, params, first_moment, second_moment = step(
        params, obs_embed, obs_slot[None], noisy[0], action_mask, time_index, cotangent[0],
        first_moment, second_moment,
    )
    norm, *new, act, noisy_grad, back = adam(
        native, squares, params, first_moment, second_moment,
        (act, noisy_grad, back), ((1, C, 256), (ADIM, 1, 256), (1, 4, OBS)),
    )
    return (act, noisy_grad.transpose(1, 0, 2), back, norm.reshape(()), *new)


def solution(mesh):
    in_specs = (
        P("pair", None, "wide"),
        P(None, "wide"),
        P("pair", "wide"),
        P("pair", "wide", None),
        P("wide"),
        P("pair", None, "wide"),
        P("wide", None),
        P("wide", None),
        P("wide", None),
    )
    out_specs = (
        P("pair", None, "wide"),
        P("pair", None, "wide"),
        P("pair", "wide", None),
        P(),
        P("wide", None),
        P("wide", None),
        P("wide", None),
        P("wide", None),
    )
    fast = mesh.shape["pair"] == 4 and mesh.shape["wide"] == 8
    return jax.shard_map(local_fast if fast else local_plain, mesh=mesh, in_specs=in_specs, out_specs=out_specs, check_vma=False)
```
